32 devices in a mesh: span: 16 (over z, x, core), elem: 2 (over y).
Axes of the slice: x: 2, y: 2, z: 4, core: 2. Of those that a mesh axis runs over, the one named last changes fastest.
Arguments:
- current_block: float32 [16, 64, 20480], P('span', None, 'elem'), may hold values from -6 to 6
- search_block: float32 [16, 64, 20480], P('span', None, 'elem'), may hold values from -6 to 6
- previous_block: float32 [16, 64, 20480], P('span', None, 'elem'), may hold values from -6 to 6
- ground_spring: float32 [20480], P('elem'), may hold values from 1 to 18
- wire_tension: float32 [20480], P('elem'), may hold values from 0.3 to 13.5
- dropper_stiff: float32 [20480], P('elem'), may hold values from 0.3 to 3
- dropper_offset: int32 [20480], P('elem'), may hold values from 1 to 8
- span_link: float32 [20480], P('elem'), may hold values from 0.1 to 0.4
- ritz_rotation: float32 [16, 192, 64], P('span'), may hold values from -0.4375 to 0.4375
Outputs:
- next_block: float32 [16, 64, 20480], P('span', None, 'elem')
- next_residual: float32 [16, 64, 20480], P('span', None, 'elem')
- ritz_values: float32 [16, 64], P('span')
The draws below stay inside these ranges and needn't reach their ends.
Inputs may be any that keep to these rules, and one draw needn't show every extreme that they name: `dropper_offset`: 20480 * i is joined by a dropper to 20480 * i + dropper_offset_i; droppers that would reach past 20480 20480 - 1 are absent.
All inputs are finite; a program needn't handle non-finite values.
Results may differ from the reference program's by a relative error of at most 0.00016.
Values sent between devices are 32-bit elements; how exact they have to be, the bound alone decides.
No kernel may reach another device: no remote copies, remote signals or barrier semaphores. Data moves between devices by JAX's collectives and lax.ppermute only.
A program may use at most 192 MiB of HBM per device.

```python
import math
import jax
import jax.numpy as jnp
from jax import lax

DOF = 20480
M = 64
REACH = 8
SPANS = 16


def rising_draw(key, low, high):
    position = jnp.arange(DOF).astype(jnp.float32)
    rise = 3.0
    factor = jnp.exp(math.log(rise) * position / (DOF - 1))
    noise = jax.random.uniform(key, (DOF,), jnp.float32, low, high)
    return noise * factor


def draw_ground_spring(key, part):
    return rising_draw(jax.random.fold_in(key, 11), 1.0, 2.0)


def draw_wire_tension(key, part):
    return rising_draw(jax.random.fold_in(key, 23), 0.3, 1.5)


def set_ends(array, stream_key, least, largest):
    longest = array.shape.index(max(array.shape))
    spots = []
    for shift in (0, 1):
        where = [jax.random.randint(jax.random.fold_in(stream_key, axis), (), 0, length) for axis, length in enumerate(array.shape)]
        where[longest] = (where[longest] + shift) % array.shape[longest]
        spots.append(tuple(where))
    return array.at[spots[0]].set(least).at[spots[1]].set(largest)


def block_levels(stream_key, dims, split, least, largest):
    def one(axis_at, shards_of):
        draws = jax.random.uniform(jax.random.fold_in(jax.random.fold_in(stream_key, 6), axis_at), (shards_of,), jnp.float32, least / len(split), largest / len(split))
        return jnp.repeat(jnp.exp(draws), dims[axis_at] // shards_of).reshape((-1,) + (1,) * (len(dims) - axis_at - 1))

    gain = one(*split[0])
    for cut in split[1:]:
        gain = gain * one(*cut)
    return gain


def bell_draw(stream_key, extent, scale, most, split=(), dtype=jnp.bfloat16):
    array = scale * jax.random.normal(stream_key, extent, jnp.float32)
    if split:
        array = array * block_levels(stream_key, extent, split, -0.22, 0.18)
    return jnp.clip(array, -most, most).astype(dtype)


def setup_inputs(seed: int = 0) -> dict:
    streams_of = jax.random.split(jax.random.key(seed), 10)
    current_block = bell_draw(streams_of[0], (SPANS, M, DOF), 1.0, 6.0, ((0, 16), (2, 2)), jnp.float32)
    search_block = bell_draw(streams_of[1], (SPANS, M, DOF), 1.0, 6.0, ((0, 16), (2, 2)), jnp.float32)
    previous_block = bell_draw(streams_of[2], (SPANS, M, DOF), 1.0, 6.0, ((0, 16), (2, 2)), jnp.float32)
    ground_spring = draw_ground_spring(jax.random.fold_in(streams_of[9], 71), 0)
    wire_tension = draw_wire_tension(jax.random.fold_in(streams_of[9], 71), 0)
    dropper_stiff = jnp.clip(jnp.exp(math.log(3.0) - 2.3025851 * jax.random.uniform(streams_of[5], (DOF,), jnp.float32) ** block_levels(streams_of[5], (DOF,), ((0, 2),), -0.2, 0.2)), 0.3, 3.0)
    dropper_offset = set_ends(jax.random.randint(streams_of[6], (DOF,), 1, REACH + 1), jax.random.fold_in(streams_of[6], 1), 1, REACH).astype(jnp.int32)
    span_link = jnp.clip(0.1 + 0.3 * jax.random.uniform(streams_of[7], (DOF,), jnp.float32) ** block_levels(streams_of[7], (DOF,), ((0, 2),), -0.2, 0.2), 0.1, 0.4)
    ritz_rotation = bell_draw(streams_of[8], (SPANS, 3 * M, M), (3 * M) ** -0.5, 0.4375, ((0, 16),), jnp.float32)
    return dict(current_block=current_block, search_block=search_block, previous_block=previous_block, ground_spring=ground_spring, wire_tension=wire_tension, dropper_stiff=dropper_stiff, dropper_offset=dropper_offset, span_link=span_link, ritz_rotation=ritz_rotation)


def fourier_rows(count):
    row = jnp.arange(count)[:, None]
    col = jnp.arange(count)[None, :]
    half = count // 2
    wave = jnp.where(row <= half, row, row - half)
    phase = (wave * col % count).astype(jnp.float32) * (2.0 * math.pi / count)
    scaled = jnp.where(row <= half, jnp.cos(phase), jnp.sin(phase)) * math.sqrt(2.0 / count)
    edge = (row == 0) | (row == half)
    matrix = jnp.where(edge, jnp.cos(phase) * math.sqrt(1.0 / count), scaled)
    slots = jnp.arange(count)
    slot_wave = jnp.where(slots <= half, slots, slots - half)
    cosines = jnp.cos(slot_wave.astype(jnp.float32) * (2.0 * math.pi / count))
    return (matrix, cosines)

def along_spans(matrix, block):
    shape = block.shape
    flat = block.reshape(shape[0], -1)
    return jnp.dot(matrix, flat, precision=lax.Precision.HIGHEST).reshape(shape)

def shift_up(field, distance):
    return jnp.concatenate([field[:, distance:], jnp.zeros_like(field[:, :distance])], 1)

def shift_down(field, distance):
    return jnp.concatenate([jnp.zeros_like(field[:, :distance]), field[:, :-distance]], 1)

def apply_span(field, ground, tension, dropper_rows, link_term):
    flux = tension * (field - shift_up(field, 1))
    applied = ground * field + flux - shift_down(flux, 1)
    for distance in range(1, REACH + 1):
        flux = dropper_rows[distance - 1] * (field - shift_up(field, distance))
        applied = applied + flux - shift_down(flux, distance)
    return applied + link_term * field

def reference(current_block, search_block, previous_block, ground_spring, wire_tension, dropper_stiff, dropper_offset, span_link, ritz_rotation):
    matrix, cosines = fourier_rows(SPANS)
    position = jnp.arange(DOF).astype(jnp.int32)
    tension = jnp.where(position < DOF - 1, wire_tension, jnp.zeros_like(wire_tension))
    dropper_rows = jnp.stack([jnp.where((dropper_offset == distance) & (position + distance < DOF), dropper_stiff, jnp.zeros_like(dropper_stiff)) for distance in range(1, REACH + 1)])
    link_terms = 2.0 * (1.0 - cosines)
    slot_x = along_spans(matrix, current_block)
    slot_w = along_spans(matrix, search_block)
    slot_p = along_spans(matrix, previous_block)

    def one_slot(items):
        field_x, field_w, field_p, rotation, link_term = items
        stacked = jnp.concatenate([field_x, field_w, field_p], 0)
        applied = apply_span(stacked, ground_spring, tension, dropper_rows, link_term * span_link)
        projected = jnp.dot(rotation.T, stacked, precision=lax.Precision.HIGHEST)
        stiff_projected = jnp.dot(rotation.T, applied, precision=lax.Precision.HIGHEST)
        energy = lax.optimization_barrier(jnp.sum(projected * stiff_projected, axis=1))
        weight_sum = lax.optimization_barrier(jnp.sum(projected * projected, axis=1))
        ritz = energy / (weight_sum + 1e-06)
        residual = stiff_projected - ritz[:, None] * projected
        return (projected, residual, ritz)
    projected, residual, ritz = lax.map(one_slot, (slot_x, slot_w, slot_p, ritz_rotation, link_terms))
    return (along_spans(matrix.T, projected), along_spans(matrix.T, residual), ritz)
```

```python
import math

import jax
import jax.numpy as jnp
from jax import lax
from jax.sharding import PartitionSpec as P

REACH = 8
HIGHEST = lax.Precision.HIGHEST


def fourier_rows(count):
    row = jnp.arange(count)[:, None]
    col = jnp.arange(count)[None, :]
    half = count // 2
    wave = jnp.where(row <= half, row, row - half)
    phase = (wave * col % count).astype(jnp.float32) * (2.0 * math.pi / count)
    scaled = jnp.where(row <= half, jnp.cos(phase), jnp.sin(phase)) * math.sqrt(2.0 / count)
    edge = (row == 0) | (row == half)
    matrix = jnp.where(edge, jnp.cos(phase) * math.sqrt(1.0 / count), scaled)
    slots = jnp.arange(count)
    slot_wave = jnp.where(slots <= half, slots, slots - half)
    cosines = jnp.cos(slot_wave.astype(jnp.float32) * (2.0 * math.pi / count))
    return (matrix, cosines)


def along_spans(matrix, block):
    shape = block.shape
    flat = block.reshape(shape[0], -1)
    return jnp.dot(matrix, flat, precision=HIGHEST).reshape(shape)


def spread(block, count):
    rows, dofs = block.shape
    return block.reshape(rows, count, dofs // count).transpose(1, 0, 2)


def collect(pieces):
    count, rows, dofs = pieces.shape
    return pieces.transpose(1, 0, 2).reshape(1, rows, count * dofs)


def exchange(pieces):
    return lax.all_to_all(pieces, "span", split_axis=0, concat_axis=0, tiled=True)


def to_next(cells, step):
    count, parts = lax.axis_size("span"), lax.axis_size("elem")
    line = [s * parts + e for e in range(parts) for s in range(count)]
    pairs = list(zip(line, line[1:]))
    if step < 0:
        pairs = [(b, a) for a, b in pairs]
    return lax.ppermute(cells, ("span", "elem"), pairs)


def coefficients(ground, tension, stiff, offset, link, count, dofs):
    dof_dev = ground.shape[0]
    start = lax.axis_index("span") * dofs
    elem = lax.axis_index("elem")
    dof_all = dof_dev * lax.axis_size("elem")
    position = elem * dof_dev + jnp.arange(dof_dev)
    distance = jnp.arange(1, REACH + 1)[:, None]
    weights = jnp.where((offset == distance) & (position + distance < dof_all), stiff, 0.0)
    wire = jnp.where((distance == 1) & (position < dof_all - 1), tension, 0.0)
    weights = weights + wire
    pairs = [(i, i + 1) for i in range(lax.axis_size("elem") - 1)]
    left = lax.ppermute(weights[:, dof_dev - REACH :], "elem", pairs)
    weights = jnp.concatenate([left, weights], 1)
    weights = lax.dynamic_slice_in_dim(weights, start, dofs + REACH, 1)
    ground = lax.dynamic_slice_in_dim(ground, start, dofs, 0)
    link = lax.dynamic_slice_in_dim(link, start, dofs, 0)
    return weights, ground, link


def on_device(
    current_block,
    search_block,
    previous_block,
    ground_spring,
    wire_tension,
    dropper_stiff,
    dropper_offset,
    span_link,
    ritz_rotation,
):
    count = lax.axis_size("span")
    dof_dev = current_block.shape[2]
    dofs = dof_dev // count
    matrix, cosines = fourier_rows(count)
    blocks = (current_block, search_block, previous_block)
    stacked = exchange(jnp.concatenate([spread(b[0], count) for b in blocks], 1))
    rotation = lax.all_gather(ritz_rotation, "span", axis=0, tiled=True)
    weights, ground, link = coefficients(
        ground_spring, wire_tension, dropper_stiff, dropper_offset, span_link, count, dofs
    )
    slots = along_spans(matrix, stacked)
    projected = jnp.einsum("jvm,jvd->jmd", rotation, slots, precision=HIGHEST)
    back = matrix.T
    next_block = collect(exchange(along_spans(back, projected)))
    before = to_next(projected[:, :, dofs - REACH :], 1)
    after = to_next(projected[:, :, :REACH], -1)
    wide = jnp.concatenate([before, projected, after], 2)
    stiff = ground * projected
    near = wide[:, :, : REACH + dofs]
    for distance in range(1, REACH + 1):
        flux = weights[distance - 1] * (near - wide[:, :, distance : distance + REACH + dofs])
        stiff = stiff + flux[:, :, REACH:] - flux[:, :, REACH - distance : REACH - distance + dofs]
    stiff = stiff + (2.0 * (1.0 - cosines))[:, None, None] * link * projected
    sums = jnp.stack([jnp.sum(projected * stiff, 2), jnp.sum(projected * projected, 2)])
    sums = lax.psum(sums, ("elem", "span"))
    ritz = sums[0] / (sums[1] + 1e-06)
    residual = stiff - ritz[:, :, None] * projected
    next_residual = collect(exchange(along_spans(back, residual)))
    my_ritz = lax.dynamic_slice_in_dim(ritz, lax.axis_index("span"), 1, 0)
    return (next_block, next_residual, my_ritz)


def solution(mesh):
    return jax.shard_map(
        on_device,
        mesh=mesh,
        in_specs=(
            P("span", None, "elem"),
            P("span", None, "elem"),
            P("span", None, "elem"),
            P("elem"),
            P("elem"),
            P("elem"),
            P("elem"),
            P("elem"),
            P("span", None, None),
        ),
        out_specs=(P("span", None, "elem"), P("span", None, "elem"), P("span", None)),
        check_vma=False,
    )
```

```python
import math

import jax
import jax.numpy as jnp
from jax import lax
from jax.experimental import pallas as pl
from jax.experimental.pallas import tpu as pltpu
from jax.sharding import PartitionSpec as P

REACH = 8
LANES = 128
ROWS = 8
VMEM_LIMIT = 40 * 1024 * 1024
HIGHEST = lax.Precision.HIGHEST


def fourier_rows(count):
    row = jnp.arange(count)[:, None]
    col = jnp.arange(count)[None, :]
    half = count // 2
    wave = jnp.where(row <= half, row, row - half)
    phase = (wave * col % count).astype(jnp.float32) * (2.0 * math.pi / count)
    scaled = jnp.where(row <= half, jnp.cos(phase), jnp.sin(phase)) * math.sqrt(2.0 / count)
    edge = (row == 0) | (row == half)
    matrix = jnp.where(edge, jnp.cos(phase) * math.sqrt(1.0 / count), scaled)
    slots = jnp.arange(count)
    slot_wave = jnp.where(slots <= half, slots, slots - half)
    cosines = jnp.cos(slot_wave.astype(jnp.float32) * (2.0 * math.pi / count))
    return (matrix, cosines)


def along_spans(matrix, block):
    shape = block.shape
    flat = block.reshape(shape[0], -1)
    return jnp.dot(matrix, flat, precision=HIGHEST).reshape(shape)


def spread(block, count):
    rows, dofs = block.shape
    return block.reshape(rows, count, dofs // count).transpose(1, 0, 2)


def collect(pieces):
    count, rows, dofs = pieces.shape
    return pieces.transpose(1, 0, 2).reshape(1, rows, count * dofs)


def exchange(pieces):
    return lax.all_to_all(pieces, "span", split_axis=0, concat_axis=0, tiled=True)


def to_next(cells, step):
    count, parts = lax.axis_size("span"), lax.axis_size("elem")
    line = [s * parts + e for e in range(parts) for s in range(count)]
    pairs = list(zip(line, line[1:]))
    if step < 0:
        pairs = [(b, a) for a, b in pairs]
    return lax.ppermute(cells, ("span", "elem"), pairs)


def coefficients(ground, tension, stiff, offset, link, count, dofs):
    dof_dev = ground.shape[0]
    start = lax.axis_index("span") * dofs
    elem = lax.axis_index("elem")
    dof_all = dof_dev * lax.axis_size("elem")
    position = elem * dof_dev + jnp.arange(dof_dev)
    distance = jnp.arange(1, REACH + 1)[:, None]
    weights = jnp.where((offset == distance) & (position + distance < dof_all), stiff, 0.0)
    wire = jnp.where((distance == 1) & (position < dof_all - 1), tension, 0.0)
    weights = weights + wire
    pairs = [(i, i + 1) for i in range(lax.axis_size("elem") - 1)]
    left = lax.ppermute(weights[:, dof_dev - REACH :], "elem", pairs)
    weights = jnp.concatenate([left, weights], 1)
    weights = lax.dynamic_slice_in_dim(weights, start, dofs + REACH, 1)
    ground = lax.dynamic_slice_in_dim(ground, start, dofs, 0)
    link = lax.dynamic_slice_in_dim(link, start, dofs, 0)
    return weights, ground, link


def add_up(terms):
    total = terms[0]
    for term in terms[1:]:
        total = total + term
    return total


def scaled(factor, value):
    if abs(factor - 1.0) < 1e-12:
        return value
    return value * factor


def cosine_sums(a):
    n = len(a) - 1
    if n == 1:
        return [a[0] + a[1], a[0] - a[1]]
    half = n // 2
    even = cosine_sums([a[s] + a[n - s] for s in range(half)] + [a[half]])
    diff = [a[s] - a[n - s] for s in range(half)]
    out = [None] * (n + 1)
    out[0::2] = even
    for j in range(1, n, 2):
        out[j] = add_up([scaled(math.cos(math.pi * j * s / n), diff[s]) for s in range(half)])
    return out


def sine_sums(b):
    n = len(b) + 1
    if n == 1:
        return []
    half = n // 2
    at = [None] + list(b)
    even = sine_sums([at[s] - at[n - s] for s in range(1, half)])
    total = [None] + [at[s] + at[n - s] for s in range(1, half)] + [at[half]]
    out = [None] * (n + 1)
    for k, value in enumerate(even):
        out[2 * k + 2] = value
    for j in range(1, n, 2):
        terms = [(math.sin(math.pi * j * s / n), total[s]) for s in range(1, half + 1)]
        terms = [scaled(abs(f), t) if f > 0 else -scaled(abs(f), t) for f, t in terms]
        out[j] = add_up(terms)
    return out[1:n]


def slot_scales(count):
    edge, inner = math.sqrt(1.0 / count), math.sqrt(2.0 / count)
    return [edge if j in (0, count // 2) else inner for j in range(count)]


def to_slots(x):
    n = len(x)
    half = n // 2
    plus = [x[0]] + [x[s] + x[n - s] for s in range(1, half)] + [x[half]]
    minus = [x[s] - x[n - s] for s in range(1, half)]
    return cosine_sums(plus) + sine_sums(minus)


def to_spans(y):
    n = len(y)
    half = n // 2
    even = cosine_sums(y[: half + 1])
    odd = [None] + sine_sums(y[half + 1 :])
    out = [None] * n
    out[0], out[half] = even[0], even[half]
    for s in range(1, half):
        out[s] = even[s] + odd[s]
        out[n - s] = even[s] - odd[s]
    return out


def params(**kw):
    return pltpu.CompilerParams(vmem_limit_bytes=VMEM_LIMIT, **kw)


def spread_blocks(blocks, count):
    _, rows, dof_dev = blocks[0].shape
    dofs = dof_dev // count
    kinds = len(blocks)

    def kernel(*refs):
        out = refs[-1]
        for k in range(kinds):
            out[0, k * rows : (k + 1) * rows, :] = refs[k][0]

    return pl.pallas_call(
        kernel,
        grid=(count,),
        in_specs=[pl.BlockSpec((1, rows, dofs), lambda i: (0, 0, i))] * kinds,
        out_specs=pl.BlockSpec((1, kinds * rows, dofs), lambda i: (i, 0, 0)),
        out_shape=jax.ShapeDtypeStruct((count, kinds * rows, dofs), jnp.float32),
        compiler_params=params(),
        name="spread_blocks",
    )(*blocks)


def collect_block(pieces):
    count, rows, dofs = pieces.shape

    def kernel(piece, out):
        out[...] = piece[...]

    return pl.pallas_call(
        kernel,
        grid=(count,),
        in_specs=[pl.BlockSpec((1, rows, dofs), lambda i: (i, 0, 0))],
        out_specs=pl.BlockSpec((1, rows, dofs), lambda i: (0, 0, i)),
        out_shape=jax.ShapeDtypeStruct((1, rows, count * dofs), jnp.float32),
        compiler_params=params(),
        name="collect_block",
    )(pieces)


def project(stacked, rotation):
    count, wide, dofs = stacked.shape
    rows = rotation.shape[1]
    tiles = dofs // LANES
    scales = slot_scales(count)
    groups = -(-count * REACH // LANES)
    per = LANES // REACH

    def kernel(x, rot, proj, back, head, tail, slots):
        tile = pl.program_id(0)

        def transform(r, carry):
            at = pl.ds(pl.multiple_of(r * ROWS, ROWS), ROWS)
            out = to_slots([x[s, at, :] for s in range(count)])
            for j in range(count):
                slots[j, at, :] = out[j]
            return carry

        lax.fori_loop(0, wide // ROWS, transform, 0)
        for j in range(count):
            proj[j] = jnp.dot(
                rot[j], slots[j], precision=HIGHEST, preferred_element_type=jnp.float32
            )

        def inverse(r, carry):
            at = pl.ds(pl.multiple_of(r * ROWS, ROWS), ROWS)
            out = to_spans([proj[j, at, :] * scales[j] for j in range(count)])
            for s in range(count):
                back[s, at, :] = out[s]
            return carry

        lax.fori_loop(0, rows // ROWS, inverse, 0)
        lane = lax.broadcasted_iota(jnp.int32, (rows, LANES), 1)

        def pack(ref, start):
            for g in range(groups):
                packed = jnp.zeros((rows, LANES), jnp.float32)
                for k in range(min(per, count - g * per)):
                    turn = (k * REACH - start) % LANES
                    value = proj[g * per + k]
                    value = pltpu.roll(value, turn, 1) if turn else value
                    packed = jnp.where(lane // REACH == k, value, packed)
                ref[g] = packed

        @pl.when(tile == 0)
        def _():
            pack(head, 0)

        @pl.when(tile == tiles - 1)
        def _():
            pack(tail, LANES - REACH)

    cell = pl.BlockSpec((count, rows, LANES), lambda t: (0, 0, t))
    edge = pl.BlockSpec((groups, rows, LANES), lambda t: (0, 0, 0))
    field = jax.ShapeDtypeStruct((count, rows, dofs), jnp.float32)
    edges = jax.ShapeDtypeStruct((groups, rows, LANES), jnp.float32)
    return pl.pallas_call(
        kernel,
        grid=(tiles,),
        in_specs=[
            pl.BlockSpec((count, wide, LANES), lambda t: (0, 0, t)),
            pl.BlockSpec((count, rows, wide), lambda t: (0, 0, 0)),
        ],
        out_specs=[cell, cell, edge, edge],
        out_shape=[field, field, edges, edges],
        scratch_shapes=[pltpu.VMEM((count, wide, LANES), jnp.float32)],
        compiler_params=params(),
        name="project",
    )(stacked, rotation)


def stiffness(projected, before, after, bands, links):
    count, rows, dofs = projected.shape
    per = LANES // REACH
    strips = rows // ROWS

    def kernel(x, left, right, band, lam, stiff, sums, energy, norm):
        def strip(it, carry):
            j, r = it // strips, it % strips
            at = pl.ds(pl.multiple_of(r * ROWS, ROWS), ROWS)
            to = pl.ds(pl.multiple_of(it * ROWS, ROWS), ROWS)
            g, k = j // per, j % per
            here = x[j, at, :]
            low = pltpu.roll(left[g, at, :], (2 * LANES - REACH - REACH * k) % LANES, 1)
            high = pltpu.roll(right[g, at, :], (LANES - REACH * k) % LANES, 1)
            full = jnp.concatenate([low, here, high], 1)
            size = dofs + 2 * LANES
            total = (band[16:17, :] + lam[j] * band[17:18, :]) * here
            for d in range(1, REACH + 1):
                up = pltpu.roll(full, size - d, 1)[:, LANES : LANES + dofs]
                down = pltpu.roll(full, d, 1)[:, LANES : LANES + dofs]
                total = total - band[d - 1 : d, :] * up
                total = total - band[REACH + d - 1 : REACH + d, :] * down
            stiff[j, at, :] = total
            both, own = total * here, here * here
            tiles = [slice(t * LANES, (t + 1) * LANES) for t in range(dofs // LANES)]
            energy[to, :] = add_up([both[:, t] for t in tiles])
            norm[to, :] = add_up([own[:, t] for t in tiles])
            return carry

        lax.fori_loop(0, count * strips, strip, 0)
        ones = jnp.ones((ROWS, LANES), jnp.float32)
        for row, part in enumerate((energy, norm)):
            line = lax.dot_general(
                ones,
                part[...],
                (((1,), (1,)), ((), ())),
                precision=HIGHEST,
                preferred_element_type=jnp.float32,
            )
            sums[row : row + 1, :] = line[:1]

    vmem = pl.BlockSpec(memory_space=pltpu.VMEM)
    return pl.pallas_call(
        kernel,
        in_specs=[vmem, vmem, vmem, vmem, pl.BlockSpec(memory_space=pltpu.SMEM)],
        out_specs=[vmem, vmem],
        out_shape=[
            jax.ShapeDtypeStruct((count, rows, dofs), jnp.float32),
            jax.ShapeDtypeStruct((2, count * rows), jnp.float32),
        ],
        scratch_shapes=[pltpu.VMEM((count * rows, LANES), jnp.float32)] * 2,
        compiler_params=params(),
        name="stiffness",
    )(projected, before, after, bands, links)


def residual_back(projected, stiff, sums):
    count, rows, dofs = projected.shape
    scales = slot_scales(count)

    def kernel(x, kx, total, back, ritz, wide):
        @pl.when(pl.program_id(0) == 0)
        def _():
            value = total[0:1, :] / (total[1:2, :] + 1e-06)
            ritz[...] = value
            row = lax.broadcasted_iota(jnp.int32, (ROWS, count * rows), 0)
            first = jnp.where(row == 0, value, 0.0)
            ones = jnp.ones((ROWS, LANES), jnp.float32)
            spread_out = lax.dot_general(
                first,
                ones,
                (((0,), (0,)), ((), ())),
                precision=HIGHEST,
                preferred_element_type=jnp.float32,
            )
            wide[...] = spread_out

        def strip(r, carry):
            at = pl.ds(pl.multiple_of(r * ROWS, ROWS), ROWS)
            terms = []
            for j in range(count):
                to = pl.ds(pl.multiple_of(j * rows + r * ROWS, ROWS), ROWS)
                terms.append((kx[j, at, :] - wide[to, :] * x[j, at, :]) * scales[j])
            out = to_spans(terms)
            for s in range(count):
                back[s, at, :] = out[s]
            return carry

        lax.fori_loop(0, rows // ROWS, strip, 0)

    cell = pl.BlockSpec((count, rows, LANES), lambda t: (0, 0, t))
    return pl.pallas_call(
        kernel,
        grid=(dofs // LANES,),
        in_specs=[cell, cell, pl.BlockSpec((2, count * rows), lambda t: (0, 0))],
        out_specs=[cell, pl.BlockSpec((1, count * rows), lambda t: (0, 0))],
        out_shape=[
            jax.ShapeDtypeStruct((count, rows, dofs), jnp.float32),
            jax.ShapeDtypeStruct((1, count * rows), jnp.float32),
        ],
        scratch_shapes=[pltpu.VMEM((count * rows, LANES), jnp.float32)],
        compiler_params=params(),
        name="residual_back",
    )(projected, stiff, sums)


def sum_over_all(value):
    for axis in ("elem", "span"):
        size = lax.axis_size(axis)
        step = 1
        while step < size:
            value = value + lax.ppermute(value, axis, [(i, i ^ step) for i in range(size)])
            step *= 2
    return value


def tiled_device(
    current_block,
    search_block,
    previous_block,
    ground_spring,
    wire_tension,
    dropper_stiff,
    dropper_offset,
    span_link,
    ritz_rotation,
):
    count = lax.axis_size("span")
    dofs = current_block.shape[2] // count
    rows = current_block.shape[1]
    stacked = exchange(spread_blocks((current_block, search_block, previous_block), count))
    scales = jnp.array(slot_scales(count), jnp.float32)[:, None, None]
    rotation = lax.all_gather(ritz_rotation.transpose(0, 2, 1), "span", axis=0, tiled=True)
    weights, ground, link = coefficients(
        ground_spring, wire_tension, dropper_stiff, dropper_offset, span_link, count, dofs
    )
    up = weights[:, REACH:]
    down = [weights[d - 1, REACH - d : REACH - d + dofs] for d in range(1, REACH + 1)]
    down = jnp.stack(down)
    diagonal = ground + jnp.sum(up, 0) + jnp.sum(down, 0)
    bands = jnp.concatenate([up, down, diagonal[None], link[None]])
    links = 2.0 * (1.0 - fourier_rows(count)[1])
    projected, spans, head, tail = project(stacked, rotation * scales)
    next_block = collect_block(exchange(spans))
    before, after = to_next(tail, 1), to_next(head, -1)
    stiff, sums = stiffness(projected, before, after, bands, links)
    spans, ritz = residual_back(projected, stiff, sum_over_all(sums))
    next_residual = collect_block(exchange(spans))
    ritz = lax.dynamic_slice_in_dim(ritz, lax.axis_index("span") * rows, rows, 1)
    return (next_block, next_residual, ritz)


def on_device(
    current_block,
    search_block,
    previous_block,
    ground_spring,
    wire_tension,
    dropper_stiff,
    dropper_offset,
    span_link,
    ritz_rotation,
):
    count = lax.axis_size("span")
    dof_dev = current_block.shape[2]
    dofs = dof_dev // count
    matrix, cosines = fourier_rows(count)
    blocks = (current_block, search_block, previous_block)
    stacked = exchange(jnp.concatenate([spread(b[0], count) for b in blocks], 1))
    rotation = lax.all_gather(ritz_rotation, "span", axis=0, tiled=True)
    weights, ground, link = coefficients(
        ground_spring, wire_tension, dropper_stiff, dropper_offset, span_link, count, dofs
    )
    slots = along_spans(matrix, stacked)
    projected = jnp.einsum("jvm,jvd->jmd", rotation, slots, precision=HIGHEST)
    back = matrix.T
    next_block = collect(exchange(along_spans(back, projected)))
    before = to_next(projected[:, :, dofs - REACH :], 1)
    after = to_next(projected[:, :, :REACH], -1)
    wide = jnp.concatenate([before, projected, after], 2)
    stiff = ground * projected
    near = wide[:, :, : REACH + dofs]
    for distance in range(1, REACH + 1):
        flux = weights[distance - 1] * (near - wide[:, :, distance : distance + REACH + dofs])
        stiff = stiff + flux[:, :, REACH:] - flux[:, :, REACH - distance : REACH - distance + dofs]
    stiff = stiff + (2.0 * (1.0 - cosines))[:, None, None] * link * projected
    sums = jnp.stack([jnp.sum(projected * stiff, 2), jnp.sum(projected * projected, 2)])
    sums = lax.psum(sums, ("elem", "span"))
    ritz = sums[0] / (sums[1] + 1e-06)
    residual = stiff - ritz[:, :, None] * projected
    next_residual = collect(exchange(along_spans(back, residual)))
    my_ritz = lax.dynamic_slice_in_dim(ritz, lax.axis_index("span"), 1, 0)
    return (next_block, next_residual, my_ritz)


def by_shape(*args):
    count, dof_dev = lax.axis_size("span"), args[0].shape[2]
    halves = count & (count - 1) == 0 and lax.axis_size("elem") in (1, 2, 4, 8, 16)
    if halves and count > 1 and dof_dev % (count * LANES) == 0:
        return tiled_device(*args)
    return on_device(*args)


def solution(mesh):
    return jax.shard_map(
        by_shape,
        mesh=mesh,
        in_specs=(
            P("span", None, "elem"),
            P("span", None, "elem"),
            P("span", None, "elem"),
            P("elem"),
            P("elem"),
            P("elem"),
            P("elem"),
            P("elem"),
            P("span", None, None),
        ),
        out_specs=(P("span", None, "elem"), P("span", None, "elem"), P("span", None)),
        check_vma=False,
    )
```

```python
import math

import jax
import jax.numpy as jnp
from jax import lax
from jax.experimental import pallas as pl
from jax.experimental.pallas import tpu as pltpu
from jax.sharding import PartitionSpec as P

REACH = 8
LANES = 128
ROWS = 8
VMEM_LIMIT = 40 * 1024 * 1024
HIGHEST = lax.Precision.HIGHEST


def fourier_rows(count):
    row = jnp.arange(count)[:, None]
    col = jnp.arange(count)[None, :]
    half = count // 2
    wave = jnp.where(row <= half, row, row - half)
    phase = (wave * col % count).astype(jnp.float32) * (2.0 * math.pi / count)
    scaled = jnp.where(row <= half, jnp.cos(phase), jnp.sin(phase)) * math.sqrt(2.0 / count)
    edge = (row == 0) | (row == half)
    matrix = jnp.where(edge, jnp.cos(phase) * math.sqrt(1.0 / count), scaled)
    slots = jnp.arange(count)
    slot_wave = jnp.where(slots <= half, slots, slots - half)
    cosines = jnp.cos(slot_wave.astype(jnp.float32) * (2.0 * math.pi / count))
    return (matrix, cosines)


def along_spans(matrix, block):
    shape = block.shape
    flat = block.reshape(shape[0], -1)
    return jnp.dot(matrix, flat, precision=HIGHEST).reshape(shape)


def spread(block, count):
    rows, dofs = block.shape
    return block.reshape(rows, count, dofs // count).transpose(1, 0, 2)


def collect(pieces):
    count, rows, dofs = pieces.shape
    return pieces.transpose(1, 0, 2).reshape(1, rows, count * dofs)


def exchange(pieces):
    return lax.all_to_all(pieces, "span", split_axis=0, concat_axis=0, tiled=True)


def to_next(cells, step):
    count, parts = lax.axis_size("span"), lax.axis_size("elem")
    line = [s * parts + e for e in range(parts) for s in range(count)]
    pairs = list(zip(line, line[1:]))
    if step < 0:
        pairs = [(b, a) for a, b in pairs]
    return lax.ppermute(cells, ("span", "elem"), pairs)


def coefficients(ground, tension, stiff, offset, link, count, dofs):
    dof_dev = ground.shape[0]
    start = lax.axis_index("span") * dofs
    elem = lax.axis_index("elem")
    dof_all = dof_dev * lax.axis_size("elem")
    position = elem * dof_dev + jnp.arange(dof_dev)
    distance = jnp.arange(1, REACH + 1)[:, None]
    weights = jnp.where((offset == distance) & (position + distance < dof_all), stiff, 0.0)
    wire = jnp.where((distance == 1) & (position < dof_all - 1), tension, 0.0)
    weights = weights + wire
    pairs = [(i, i + 1) for i in range(lax.axis_size("elem") - 1)]
    left = lax.ppermute(weights[:, dof_dev - REACH :], "elem", pairs)
    weights = jnp.concatenate([left, weights], 1)
    weights = lax.dynamic_slice_in_dim(weights, start, dofs + REACH, 1)
    ground = lax.dynamic_slice_in_dim(ground, start, dofs, 0)
    link = lax.dynamic_slice_in_dim(link, start, dofs, 0)
    return weights, ground, link


def add_up(terms):
    total = terms[0]
    for term in terms[1:]:
        total = total + term
    return total


def scaled(factor, value):
    if abs(factor - 1.0) < 1e-12:
        return value
    return value * factor


def cosine_sums(a):
    n = len(a) - 1
    if n == 1:
        return [a[0] + a[1], a[0] - a[1]]
    half = n // 2
    even = cosine_sums([a[s] + a[n - s] for s in range(half)] + [a[half]])
    diff = [a[s] - a[n - s] for s in range(half)]
    out = [None] * (n + 1)
    out[0::2] = even
    for j in range(1, n, 2):
        out[j] = add_up([scaled(math.cos(math.pi * j * s / n), diff[s]) for s in range(half)])
    return out


def sine_sums(b):
    n = len(b) + 1
    if n == 1:
        return []
    half = n // 2
    at = [None] + list(b)
    even = sine_sums([at[s] - at[n - s] for s in range(1, half)])
    total = [None] + [at[s] + at[n - s] for s in range(1, half)] + [at[half]]
    out = [None] * (n + 1)
    for k, value in enumerate(even):
        out[2 * k + 2] = value
    for j in range(1, n, 2):
        terms = [(math.sin(math.pi * j * s / n), total[s]) for s in range(1, half + 1)]
        terms = [scaled(abs(f), t) if f > 0 else -scaled(abs(f), t) for f, t in terms]
        out[j] = add_up(terms)
    return out[1:n]


def slot_scales(count):
    edge, inner = math.sqrt(1.0 / count), math.sqrt(2.0 / count)
    return [edge if j in (0, count // 2) else inner for j in range(count)]


def to_slots(x):
    n = len(x)
    half = n // 2
    plus = [x[0]] + [x[s] + x[n - s] for s in range(1, half)] + [x[half]]
    minus = [x[s] - x[n - s] for s in range(1, half)]
    return cosine_sums(plus) + sine_sums(minus)


def to_spans(y):
    n = len(y)
    half = n // 2
    even = cosine_sums(y[: half + 1])
    odd = [None] + sine_sums(y[half + 1 :])
    out = [None] * n
    out[0], out[half] = even[0], even[half]
    for s in range(1, half):
        out[s] = even[s] + odd[s]
        out[n - s] = even[s] - odd[s]
    return out


def params(**kw):
    return pltpu.CompilerParams(vmem_limit_bytes=VMEM_LIMIT, **kw)


def spread_blocks(blocks, count):
    _, rows, dof_dev = blocks[0].shape
    dofs = dof_dev // count
    kinds = len(blocks)
    cuts = 2 if rows % (2 * ROWS) == 0 else 1
    strip = rows // cuts

    def kernel(*refs):
        out, held, come, go = refs[kinds:]
        arrivals = []
        for c in range(cuts):
            for k in range(kinds):
                at = slice(c * strip, (c + 1) * strip)
                copy = pltpu.make_async_copy(
                    refs[k].at[0, at, :], held.at[k, at, :], come.at[c * kinds + k]
                )
                copy.start()
                arrivals.append((c, k, copy))
        leaving = []
        for c, k, copy in arrivals:
            copy.wait()
            for i in range(count):
                piece = pltpu.make_async_copy(
                    held.at[k, c * strip : (c + 1) * strip, i * dofs : (i + 1) * dofs],
                    out.at[i, k * rows + c * strip : k * rows + (c + 1) * strip, :],
                    go.at[(c * kinds + k) * count + i],
                )
                piece.start()
                leaving.append(piece)
        for piece in leaving:
            piece.wait()

    whole = pl.BlockSpec(memory_space=pltpu.HBM)
    return pl.pallas_call(
        kernel,
        in_specs=[whole] * kinds,
        out_specs=whole,
        out_shape=pltpu.HBM((count, kinds * rows, dofs), jnp.float32),
        scratch_shapes=[
            pltpu.VMEM((kinds, rows, dof_dev), jnp.float32),
            pltpu.SemaphoreType.DMA((cuts * kinds,)),
            pltpu.SemaphoreType.DMA((cuts * kinds * count,)),
        ],
        compiler_params=pltpu.CompilerParams(vmem_limit_bytes=60 * 1024 * 1024),
        name="spread_blocks",
    )(*blocks)


def collect_block(pieces):
    count, rows, dofs = pieces.shape
    many = max(n for n in (1, 2, 4, 8) if count % n == 0)

    def kernel(piece, out):
        for i in range(many):
            out[0, :, i * dofs : (i + 1) * dofs] = piece[i]

    return pl.pallas_call(
        kernel,
        grid=(count // many,),
        in_specs=[pl.BlockSpec((many, rows, dofs), lambda i: (i, 0, 0))],
        out_specs=pl.BlockSpec((1, rows, many * dofs), lambda i: (0, 0, i)),
        out_shape=pltpu.HBM((1, rows, count * dofs), jnp.float32),
        compiler_params=params(),
        name="collect_block",
    )(pieces)


def project(stacked, rotation):
    count, wide, dofs = stacked.shape
    rows = rotation.shape[1]
    tiles = dofs // LANES
    scales = slot_scales(count)
    groups = -(-count * REACH // LANES)
    per = LANES // REACH

    def kernel(x, rot, proj, back, head, tail, slots):
        tile = pl.program_id(0)

        def transform(r, carry):
            at = pl.ds(pl.multiple_of(r * ROWS, ROWS), ROWS)
            out = to_slots([x[s, at, :] for s in range(count)])
            for j in range(count):
                slots[j, at, :] = out[j]
            return carry

        lax.fori_loop(0, wide // ROWS, transform, 0)
        for j in range(count):
            proj[j] = jnp.dot(
                rot[j], slots[j], precision=HIGHEST, preferred_element_type=jnp.float32
            )

        def inverse(r, carry):
            at = pl.ds(pl.multiple_of(r * ROWS, ROWS), ROWS)
            out = to_spans([proj[j, at, :] * scales[j] for j in range(count)])
            for s in range(count):
                back[s, at, :] = out[s]
            return carry

        lax.fori_loop(0, rows // ROWS, inverse, 0)
        lane = lax.broadcasted_iota(jnp.int32, (rows, LANES), 1)

        def pack(ref, start):
            for g in range(groups):
                packed = jnp.zeros((rows, LANES), jnp.float32)
                for k in range(min(per, count - g * per)):
                    turn = (k * REACH - start) % LANES
                    value = proj[g * per + k]
                    value = pltpu.roll(value, turn, 1) if turn else value
                    packed = jnp.where(lane // REACH == k, value, packed)
                ref[g] = packed

        @pl.when(tile == 0)
        def _():
            pack(head, 0)

        @pl.when(tile == tiles - 1)
        def _():
            pack(tail, LANES - REACH)

    cell = pl.BlockSpec((count, rows, LANES), lambda t: (0, 0, t))
    edge = pl.BlockSpec((groups, rows, LANES), lambda t: (0, 0, 0))
    field = pltpu.HBM((count, rows, dofs), jnp.float32)
    edges = jax.ShapeDtypeStruct((groups, rows, LANES), jnp.float32)
    return pl.pallas_call(
        kernel,
        grid=(tiles,),
        in_specs=[
            pl.BlockSpec((count, wide, LANES), lambda t: (0, 0, t)),
            pl.BlockSpec((count, rows, wide), lambda t: (0, 0, 0)),
        ],
        out_specs=[cell, cell, edge, edge],
        out_shape=[field, field, edges, edges],
        scratch_shapes=[pltpu.VMEM((count, wide, LANES), jnp.float32)],
        compiler_params=params(),
        name="project",
    )(stacked, rotation)


def stiffness(projected, before, after, bands, links):
    count, rows, dofs = projected.shape
    per = LANES // REACH
    tiles = dofs // LANES

    def kernel(x, left, right, band, lam, stiff, sums, energy, norm, matrix):
        row = lax.broadcasted_iota(jnp.int32, (LANES, LANES), 0)
        gap = row - lax.broadcasted_iota(jnp.int32, (LANES, LANES), 1)
        for t in range(tiles):
            at = slice(t * LANES, (t + 1) * LANES)
            here = jnp.where(gap == 0, band[16:17, at], 0.0)
            halo = jnp.zeros((LANES, LANES), jnp.float32)
            for d in range(1, REACH + 1):
                up, down = band[d - 1 : d, at], band[REACH + d - 1 : REACH + d, at]
                here = jnp.where(gap == d, -up, here)
                here = jnp.where(gap == -d, -down, here)
                halo = jnp.where(gap == d - LANES, -up, halo)
                halo = jnp.where(gap == LANES - d, -down, halo)
            matrix[t, :LANES, :] = here
            matrix[t, LANES:, :] = halo
        lane = lax.broadcasted_iota(jnp.int32, (rows, LANES), 1)

        def slot(j, carry):
            to = pl.ds(pl.multiple_of(j * rows, rows), rows)
            g, k = j // per, j % per
            low = pltpu.roll(left[g], (2 * LANES - REACH - REACH * k) % LANES, 1)
            high = pltpu.roll(right[g], (LANES - REACH * k) % LANES, 1)
            work = jnp.zeros((rows, LANES), jnp.float32)
            size = jnp.zeros((rows, LANES), jnp.float32)
            for t in range(tiles):
                at = slice(t * LANES, (t + 1) * LANES)
                here = x[j, :, at]
                previous = low if t == 0 else x[j, :, (t - 1) * LANES : t * LANES]
                following = high if t == tiles - 1 else x[j, :, (t + 1) * LANES : (t + 2) * LANES]
                halo = jnp.where(lane < LANES // 2, following, previous)
                total = jnp.dot(
                    jnp.concatenate([here, halo], 1),
                    matrix[t],
                    precision=HIGHEST,
                    preferred_element_type=jnp.float32,
                )
                total = total + (lam[j] * band[17:18, at]) * here
                stiff[j, :, at] = total
                work = work + total * here
                size = size + here * here
            energy[to, :] = work
            norm[to, :] = size
            return carry

        lax.fori_loop(0, count, slot, 0)
        ones = jnp.ones((ROWS, LANES), jnp.float32)
        for r, part in enumerate((energy, norm)):
            line = lax.dot_general(
                ones,
                part[...],
                (((1,), (1,)), ((), ())),
                precision=HIGHEST,
                preferred_element_type=jnp.float32,
            )
            sums[r : r + 1, :] = line[:1]

    vmem = pl.BlockSpec(memory_space=pltpu.VMEM)
    return pl.pallas_call(
        kernel,
        in_specs=[vmem, vmem, vmem, vmem, pl.BlockSpec(memory_space=pltpu.SMEM)],
        out_specs=[vmem, vmem],
        out_shape=[
            jax.ShapeDtypeStruct((count, rows, dofs), jnp.float32),
            jax.ShapeDtypeStruct((2, count * rows), jnp.float32),
        ],
        scratch_shapes=[
            pltpu.VMEM((count * rows, LANES), jnp.float32),
            pltpu.VMEM((count * rows, LANES), jnp.float32),
            pltpu.VMEM((tiles, 2 * LANES, LANES), jnp.float32),
        ],
        compiler_params=params(),
        name="stiffness",
    )(projected, before, after, bands, links)


def residual_back(projected, stiff, sums):
    count, rows, dofs = projected.shape
    scales = slot_scales(count)

    def kernel(x, kx, total, back, ritz, wide):
        @pl.when(pl.program_id(0) == 0)
        def _():
            value = total[0:1, :] / (total[1:2, :] + 1e-06)
            ritz[...] = value
            row = lax.broadcasted_iota(jnp.int32, (ROWS, count * rows), 0)
            first = jnp.where(row == 0, value, 0.0)
            ones = jnp.ones((ROWS, LANES), jnp.float32)
            spread_out = lax.dot_general(
                first,
                ones,
                (((0,), (0,)), ((), ())),
                precision=HIGHEST,
                preferred_element_type=jnp.float32,
            )
            wide[...] = spread_out

        def strip(r, carry):
            at = pl.ds(pl.multiple_of(r * ROWS, ROWS), ROWS)
            terms = []
            for j in range(count):
                to = pl.ds(pl.multiple_of(j * rows + r * ROWS, ROWS), ROWS)
                terms.append((kx[j, at, :] - wide[to, :] * x[j, at, :]) * scales[j])
            out = to_spans(terms)
            for s in range(count):
                back[s, at, :] = out[s]
            return carry

        lax.fori_loop(0, rows // ROWS, strip, 0)

    cell = pl.BlockSpec((count, rows, LANES), lambda t: (0, 0, t))
    return pl.pallas_call(
        kernel,
        grid=(dofs // LANES,),
        in_specs=[cell, cell, pl.BlockSpec((2, count * rows), lambda t: (0, 0))],
        out_specs=[cell, pl.BlockSpec((1, count * rows), lambda t: (0, 0))],
        out_shape=[
            pltpu.HBM((count, rows, dofs), jnp.float32),
            jax.ShapeDtypeStruct((1, count * rows), jnp.float32),
        ],
        scratch_shapes=[pltpu.VMEM((count * rows, LANES), jnp.float32)],
        compiler_params=params(),
        name="residual_back",
    )(projected, stiff, sums)


def halvings(axis):
    step = lax.axis_size(axis) // 2
    while step:
        yield step, [(i, i ^ step) for i in range(lax.axis_size(axis))]
        step //= 2


def sum_over_all(value):
    for axis in ("span", "elem"):
        for _, pairs in halvings(axis):
            value = value + lax.ppermute(value, axis, pairs)
    return value


def gather_spans(value):
    tail = value.shape[1:]
    held, bits = value.reshape(tail), 0
    for step, pairs in halvings("span"):
        other = lax.ppermute(held, "span", pairs)
        upper = (lax.axis_index("span") & step) != 0
        held = jnp.stack([jnp.where(upper, other, held), jnp.where(upper, held, other)])
        bits += 1
    order = tuple(range(bits))[::-1] + tuple(range(bits, bits + len(tail)))
    return held.transpose(order).reshape((-1,) + tail)


def tiled_device(
    current_block,
    search_block,
    previous_block,
    ground_spring,
    wire_tension,
    dropper_stiff,
    dropper_offset,
    span_link,
    ritz_rotation,
):
    count = lax.axis_size("span")
    dofs = current_block.shape[2] // count
    rows = current_block.shape[1]
    stacked = exchange(spread_blocks((current_block, search_block, previous_block), count))
    scales = jnp.array(slot_scales(count), jnp.float32)[:, None, None]
    rotation = gather_spans(ritz_rotation.transpose(0, 2, 1))
    weights, ground, link = coefficients(
        ground_spring, wire_tension, dropper_stiff, dropper_offset, span_link, count, dofs
    )
    up = weights[:, REACH:]
    down = [weights[d - 1, REACH - d : REACH - d + dofs] for d in range(1, REACH + 1)]
    down = jnp.stack(down)
    diagonal = ground + jnp.sum(up, 0) + jnp.sum(down, 0)
    bands = jnp.concatenate([up, down, diagonal[None], link[None]])
    links = 2.0 * (1.0 - fourier_rows(count)[1])
    projected, spans, head, tail = project(stacked, rotation * scales)
    before, after = to_next(tail, 1), to_next(head, -1)
    spans, before, after = lax.optimization_barrier((spans, before, after))
    next_block = collect_block(exchange(spans))
    stiff, sums = stiffness(projected, before, after, bands, links)
    spans, ritz = residual_back(projected, stiff, sum_over_all(sums))
    next_residual = collect_block(exchange(spans))
    ritz = lax.dynamic_slice_in_dim(ritz, lax.axis_index("span") * rows, rows, 1)
    return (next_block, next_residual, ritz)


def on_device(
    current_block,
    search_block,
    previous_block,
    ground_spring,
    wire_tension,
    dropper_stiff,
    dropper_offset,
    span_link,
    ritz_rotation,
):
    count = lax.axis_size("span")
    dof_dev = current_block.shape[2]
    dofs = dof_dev // count
    matrix, cosines = fourier_rows(count)
    blocks = (current_block, search_block, previous_block)
    stacked = exchange(jnp.concatenate([spread(b[0], count) for b in blocks], 1))
    rotation = lax.all_gather(ritz_rotation, "span", axis=0, tiled=True)
    weights, ground, link = coefficients(
        ground_spring, wire_tension, dropper_stiff, dropper_offset, span_link, count, dofs
    )
    slots = along_spans(matrix, stacked)
    projected = jnp.einsum("jvm,jvd->jmd", rotation, slots, precision=HIGHEST)
    back = matrix.T
    next_block = collect(exchange(along_spans(back, projected)))
    before = to_next(projected[:, :, dofs - REACH :], 1)
    after = to_next(projected[:, :, :REACH], -1)
    wide = jnp.concatenate([before, projected, after], 2)
    stiff = ground * projected
    near = wide[:, :, : REACH + dofs]
    for distance in range(1, REACH + 1):
        flux = weights[distance - 1] * (near - wide[:, :, distance : distance + REACH + dofs])
        stiff = stiff + flux[:, :, REACH:] - flux[:, :, REACH - distance : REACH - distance + dofs]
    stiff = stiff + (2.0 * (1.0 - cosines))[:, None, None] * link * projected
    sums = jnp.stack([jnp.sum(projected * stiff, 2), jnp.sum(projected * projected, 2)])
    sums = lax.psum(sums, ("elem", "span"))
    ritz = sums[0] / (sums[1] + 1e-06)
    residual = stiff - ritz[:, :, None] * projected
    next_residual = collect(exchange(along_spans(back, residual)))
    my_ritz = lax.dynamic_slice_in_dim(ritz, lax.axis_index("span"), 1, 0)
    return (next_block, next_residual, my_ritz)


def by_shape(*args):
    count, dof_dev = lax.axis_size("span"), args[0].shape[2]
    halves = count & (count - 1) == 0 and lax.axis_size("elem") in (1, 2, 4, 8, 16)
    if halves and count > 1 and dof_dev % (count * LANES) == 0:
        return tiled_device(*args)
    return on_device(*args)


def solution(mesh):
    return jax.shard_map(
        by_shape,
        mesh=mesh,
        in_specs=(
            P("span", None, "elem"),
            P("span", None, "elem"),
            P("span", None, "elem"),
            P("elem"),
            P("elem"),
            P("elem"),
            P("elem"),
            P("elem"),
            P("span", None, None),
        ),
        out_specs=(P("span", None, "elem"), P("span", None, "elem"), P("span", None)),
        check_vma=False,
    )
```

```python
import math

import jax
import jax.numpy as jnp
from jax import lax
from jax.experimental import pallas as pl
from jax.experimental.pallas import tpu as pltpu
from jax.sharding import PartitionSpec as P

REACH = 8
LANES = 128
ROWS = 8
VMEM_LIMIT = 40 * 1024 * 1024
HIGHEST = lax.Precision.HIGHEST


def fourier_rows(count):
    row = jnp.arange(count)[:, None]
    col = jnp.arange(count)[None, :]
    half = count // 2
    wave = jnp.where(row <= half, row, row - half)
    phase = (wave * col % count).astype(jnp.float32) * (2.0 * math.pi / count)
    scaled = jnp.where(row <= half, jnp.cos(phase), jnp.sin(phase)) * math.sqrt(2.0 / count)
    edge = (row == 0) | (row == half)
    matrix = jnp.where(edge, jnp.cos(phase) * math.sqrt(1.0 / count), scaled)
    slots = jnp.arange(count)
    slot_wave = jnp.where(slots <= half, slots, slots - half)
    cosines = jnp.cos(slot_wave.astype(jnp.float32) * (2.0 * math.pi / count))
    return (matrix, cosines)


def along_spans(matrix, block):
    shape = block.shape
    flat = block.reshape(shape[0], -1)
    return jnp.dot(matrix, flat, precision=HIGHEST).reshape(shape)


def spread(block, count):
    rows, dofs = block.shape
    return block.reshape(rows, count, dofs // count).transpose(1, 0, 2)


def collect(pieces):
    count, rows, dofs = pieces.shape
    return pieces.transpose(1, 0, 2).reshape(1, rows, count * dofs)


def exchange(pieces):
    return lax.all_to_all(pieces, "span", split_axis=0, concat_axis=0, tiled=True)


def to_next(cells, step):
    count, parts = lax.axis_size("span"), lax.axis_size("elem")
    line = [s * parts + e for e in range(parts) for s in range(count)]
    pairs = list(zip(line, line[1:]))
    if step < 0:
        pairs = [(b, a) for a, b in pairs]
    return lax.ppermute(cells, ("span", "elem"), pairs)


def coefficients(ground, tension, stiff, offset, link, count, dofs):
    dof_dev = ground.shape[0]
    start = lax.axis_index("span") * dofs
    elem = lax.axis_index("elem")
    dof_all = dof_dev * lax.axis_size("elem")
    position = elem * dof_dev + jnp.arange(dof_dev)
    distance = jnp.arange(1, REACH + 1)[:, None]
    weights = jnp.where((offset == distance) & (position + distance < dof_all), stiff, 0.0)
    wire = jnp.where((distance == 1) & (position < dof_all - 1), tension, 0.0)
    weights = weights + wire
    pairs = [(i, i + 1) for i in range(lax.axis_size("elem") - 1)]
    left = lax.ppermute(weights[:, dof_dev - REACH :], "elem", pairs)
    weights = jnp.concatenate([left, weights], 1)
    weights = lax.dynamic_slice_in_dim(weights, start, dofs + REACH, 1)
    ground = lax.dynamic_slice_in_dim(ground, start, dofs, 0)
    link = lax.dynamic_slice_in_dim(link, start, dofs, 0)
    return weights, ground, link


def add_up(terms):
    total = terms[0]
    for term in terms[1:]:
        total = total + term
    return total


def scaled(factor, value):
    if abs(factor - 1.0) < 1e-12:
        return value
    return value * factor


def cosine_sums(a):
    n = len(a) - 1
    if n == 1:
        return [a[0] + a[1], a[0] - a[1]]
    half = n // 2
    even = cosine_sums([a[s] + a[n - s] for s in range(half)] + [a[half]])
    diff = [a[s] - a[n - s] for s in range(half)]
    out = [None] * (n + 1)
    out[0::2] = even
    for j in range(1, n, 2):
        out[j] = add_up([scaled(math.cos(math.pi * j * s / n), diff[s]) for s in range(half)])
    return out


def sine_sums(b):
    n = len(b) + 1
    if n == 1:
        return []
    half = n // 2
    at = [None] + list(b)
    even = sine_sums([at[s] - at[n - s] for s in range(1, half)])
    total = [None] + [at[s] + at[n - s] for s in range(1, half)] + [at[half]]
    out = [None] * (n + 1)
    for k, value in enumerate(even):
        out[2 * k + 2] = value
    for j in range(1, n, 2):
        terms = [(math.sin(math.pi * j * s / n), total[s]) for s in range(1, half + 1)]
        terms = [scaled(abs(f), t) if f > 0 else -scaled(abs(f), t) for f, t in terms]
        out[j] = add_up(terms)
    return out[1:n]


def slot_scales(count):
    edge, inner = math.sqrt(1.0 / count), math.sqrt(2.0 / count)
    return [edge if j in (0, count // 2) else inner for j in range(count)]


def to_slots(x):
    n = len(x)
    half = n // 2
    plus = [x[0]] + [x[s] + x[n - s] for s in range(1, half)] + [x[half]]
    minus = [x[s] - x[n - s] for s in range(1, half)]
    return cosine_sums(plus) + sine_sums(minus)


def to_spans(y):
    n = len(y)
    half = n // 2
    even = cosine_sums(y[: half + 1])
    odd = [None] + sine_sums(y[half + 1 :])
    out = [None] * n
    out[0], out[half] = even[0], even[half]
    for s in range(1, half):
        out[s] = even[s] + odd[s]
        out[n - s] = even[s] - odd[s]
    return out


def params(**kw):
    return pltpu.CompilerParams(vmem_limit_bytes=VMEM_LIMIT, **kw)


def spread_blocks(blocks, count):
    _, rows, dof_dev = blocks[0].shape
    dofs = dof_dev // count
    kinds = len(blocks)
    cuts = 2 if rows % (2 * ROWS) == 0 else 1
    strip = rows // cuts

    def kernel(*refs):
        out, held, come, go = refs[kinds:]
        arrivals = []
        for c in range(cuts):
            for k in range(kinds):
                at = slice(c * strip, (c + 1) * strip)
                copy = pltpu.make_async_copy(
                    refs[k].at[0, at, :], held.at[k, at, :], come.at[c * kinds + k]
                )
                copy.start()
                arrivals.append((c, k, copy))
        leaving = []
        for c, k, copy in arrivals:
            copy.wait()
            for i in range(count):
                piece = pltpu.make_async_copy(
                    held.at[k, c * strip : (c + 1) * strip, i * dofs : (i + 1) * dofs],
                    out.at[i, k * rows + c * strip : k * rows + (c + 1) * strip, :],
                    go.at[(c * kinds + k) * count + i],
                )
                piece.start()
                leaving.append(piece)
        for piece in leaving:
            piece.wait()

    whole = pl.BlockSpec(memory_space=pltpu.HBM)
    return pl.pallas_call(
        kernel,
        in_specs=[whole] * kinds,
        out_specs=whole,
        out_shape=pltpu.HBM((count, kinds * rows, dofs), jnp.float32),
        scratch_shapes=[
            pltpu.VMEM((kinds, rows, dof_dev), jnp.float32),
            pltpu.SemaphoreType.DMA((cuts * kinds,)),
            pltpu.SemaphoreType.DMA((cuts * kinds * count,)),
        ],
        compiler_params=pltpu.CompilerParams(vmem_limit_bytes=60 * 1024 * 1024),
        name="spread_blocks",
    )(*blocks)


def collect_block(pieces):
    count, rows, dofs = pieces.shape
    many = max(n for n in (1, 2, 4, 8) if count % n == 0)

    def kernel(piece, out):
        for i in range(many):
            out[0, :, i * dofs : (i + 1) * dofs] = piece[i]

    return pl.pallas_call(
        kernel,
        grid=(count // many,),
        in_specs=[pl.BlockSpec((many, rows, dofs), lambda i: (i, 0, 0))],
        out_specs=pl.BlockSpec((1, rows, many * dofs), lambda i: (0, 0, i)),
        out_shape=pltpu.HBM((1, rows, count * dofs), jnp.float32),
        compiler_params=params(),
        name="collect_block",
    )(pieces)


def project(stacked, rotation):
    count, wide, dofs = stacked.shape
    rows = rotation.shape[1]
    tiles = dofs // LANES
    scales = slot_scales(count)
    groups = -(-count * REACH // LANES)
    per = LANES // REACH

    def kernel(x, rot, proj, back, head, tail, slots):
        tile = pl.program_id(0)

        def transform(r, carry):
            at = pl.ds(pl.multiple_of(r * ROWS, ROWS), ROWS)
            out = to_slots([x[s, at, :] for s in range(count)])
            for j in range(count):
                slots[j, at, :] = out[j]
            return carry

        lax.fori_loop(0, wide // ROWS, transform, 0)
        for j in range(count):
            proj[j] = jnp.dot(
                rot[j], slots[j], precision=HIGHEST, preferred_element_type=jnp.float32
            )

        def inverse(r, carry):
            at = pl.ds(pl.multiple_of(r * ROWS, ROWS), ROWS)
            out = to_spans([proj[j, at, :] * scales[j] for j in range(count)])
            for s in range(count):
                back[s, at, :] = out[s]
            return carry

        lax.fori_loop(0, rows // ROWS, inverse, 0)
        lane = lax.broadcasted_iota(jnp.int32, (rows, LANES), 1)

        def pack(ref, start):
            for g in range(groups):
                packed = jnp.zeros((rows, LANES), jnp.float32)
                for k in range(min(per, count - g * per)):
                    turn = (k * REACH - start) % LANES
                    value = proj[g * per + k]
                    value = pltpu.roll(value, turn, 1) if turn else value
                    packed = jnp.where(lane // REACH == k, value, packed)
                ref[g] = packed

        @pl.when(tile == 0)
        def _():
            pack(head, 0)

        @pl.when(tile == tiles - 1)
        def _():
            pack(tail, LANES - REACH)

    cell = pl.BlockSpec((count, rows, LANES), lambda t: (0, 0, t))
    edge = pl.BlockSpec((groups, rows, LANES), lambda t: (0, 0, 0))
    field = pltpu.HBM((count, rows, dofs), jnp.float32)
    edges = jax.ShapeDtypeStruct((groups, rows, LANES), jnp.float32)
    return pl.pallas_call(
        kernel,
        grid=(tiles,),
        in_specs=[
            pl.BlockSpec((count, wide, LANES), lambda t: (0, 0, t)),
            pl.BlockSpec((count, rows, wide), lambda t: (0, 0, 0)),
        ],
        out_specs=[cell, cell, edge, edge],
        out_shape=[field, field, edges, edges],
        scratch_shapes=[pltpu.VMEM((count, wide, LANES), jnp.float32)],
        compiler_params=params(),
        name="project",
    )(stacked, rotation)


def stiffness(projected, before, after, bands, links):
    count, rows, dofs = projected.shape
    per = LANES // REACH
    tiles = dofs // LANES

    def kernel(x, left, right, band, lam, stiff, sums, energy, norm, matrix):
        row = lax.broadcasted_iota(jnp.int32, (LANES, LANES), 0)
        gap = row - lax.broadcasted_iota(jnp.int32, (LANES, LANES), 1)
        for t in range(tiles):
            at = slice(t * LANES, (t + 1) * LANES)
            here = jnp.where(gap == 0, band[16:17, at], 0.0)
            halo = jnp.zeros((LANES, LANES), jnp.float32)
            for d in range(1, REACH + 1):
                up, down = band[d - 1 : d, at], band[REACH + d - 1 : REACH + d, at]
                here = jnp.where(gap == d, -up, here)
                here = jnp.where(gap == -d, -down, here)
                halo = jnp.where(gap == d - LANES, -up, halo)
                halo = jnp.where(gap == LANES - d, -down, halo)
            matrix[t, :LANES, :] = here
            matrix[t, LANES:, :] = halo
        lane = lax.broadcasted_iota(jnp.int32, (rows, LANES), 1)

        def slot(j, carry):
            to = pl.ds(pl.multiple_of(j * rows, rows), rows)
            g, k = j // per, j % per
            low = pltpu.roll(left[g], (2 * LANES - REACH - REACH * k) % LANES, 1)
            high = pltpu.roll(right[g], (LANES - REACH * k) % LANES, 1)
            work = jnp.zeros((rows, LANES), jnp.float32)
            size = jnp.zeros((rows, LANES), jnp.float32)
            for t in range(tiles):
                at = slice(t * LANES, (t + 1) * LANES)
                here = x[j, :, at]
                previous = low if t == 0 else x[j, :, (t - 1) * LANES : t * LANES]
                following = high if t == tiles - 1 else x[j, :, (t + 1) * LANES : (t + 2) * LANES]
                halo = jnp.where(lane < LANES // 2, following, previous)
                total = jnp.dot(
                    jnp.concatenate([here, halo], 1),
                    matrix[t],
                    precision=HIGHEST,
                    preferred_element_type=jnp.float32,
                )
                total = total + (lam[j] * band[17:18, at]) * here
                stiff[j, :, at] = total
                work = work + total * here
                size = size + here * here
            energy[to, :] = work
            norm[to, :] = size
            return carry

        lax.fori_loop(0, count, slot, 0)
        ones = jnp.ones((ROWS, LANES), jnp.float32)
        for r, part in enumerate((energy, norm)):
            line = lax.dot_general(
                ones,
                part[...],
                (((1,), (1,)), ((), ())),
                precision=HIGHEST,
                preferred_element_type=jnp.float32,
            )
            sums[r : r + 1, :] = line[:1]

    vmem = pl.BlockSpec(memory_space=pltpu.VMEM)
    return pl.pallas_call(
        kernel,
        in_specs=[vmem, vmem, vmem, vmem, pl.BlockSpec(memory_space=pltpu.SMEM)],
        out_specs=[vmem, vmem],
        out_shape=[
            jax.ShapeDtypeStruct((count, rows, dofs), jnp.float32),
            jax.ShapeDtypeStruct((2, count * rows), jnp.float32),
        ],
        scratch_shapes=[
            pltpu.VMEM((count * rows, LANES), jnp.float32),
            pltpu.VMEM((count * rows, LANES), jnp.float32),
            pltpu.VMEM((tiles, 2 * LANES, LANES), jnp.float32),
        ],
        compiler_params=params(),
        name="stiffness",
    )(projected, before, after, bands, links)


def residual_back(projected, stiff, sums):
    count, rows, dofs = projected.shape
    scales = slot_scales(count)

    def kernel(x, kx, total, back, ritz, wide):
        @pl.when(pl.program_id(0) == 0)
        def _():
            value = total[0:1, :] / (total[1:2, :] + 1e-06)
            ritz[...] = value
            row = lax.broadcasted_iota(jnp.int32, (ROWS, count * rows), 0)
            first = jnp.where(row == 0, value, 0.0)
            ones = jnp.ones((ROWS, LANES), jnp.float32)
            spread_out = lax.dot_general(
                first,
                ones,
                (((0,), (0,)), ((), ())),
                precision=HIGHEST,
                preferred_element_type=jnp.float32,
            )
            wide[...] = spread_out

        def strip(r, carry):
            at = pl.ds(pl.multiple_of(r * ROWS, ROWS), ROWS)
            terms = []
            for j in range(count):
                to = pl.ds(pl.multiple_of(j * rows + r * ROWS, ROWS), ROWS)
                terms.append((kx[j, at, :] - wide[to, :] * x[j, at, :]) * scales[j])
            out = to_spans(terms)
            for s in range(count):
                back[s, at, :] = out[s]
            return carry

        lax.fori_loop(0, rows // ROWS, strip, 0)

    cell = pl.BlockSpec((count, rows, LANES), lambda t: (0, 0, t))
    return pl.pallas_call(
        kernel,
        grid=(dofs // LANES,),
        in_specs=[cell, cell, pl.BlockSpec((2, count * rows), lambda t: (0, 0))],
        out_specs=[cell, pl.BlockSpec((1, count * rows), lambda t: (0, 0))],
        out_shape=[
            pltpu.HBM((count, rows, dofs), jnp.float32),
            jax.ShapeDtypeStruct((1, count * rows), jnp.float32),
        ],
        scratch_shapes=[pltpu.VMEM((count * rows, LANES), jnp.float32)],
        compiler_params=params(),
        name="residual_back",
    )(projected, stiff, sums)


def halvings(axis):
    step = lax.axis_size(axis) // 2
    while step:
        yield step, [(i, i ^ step) for i in range(lax.axis_size(axis))]
        step //= 2


def exchange_step(held, step, pairs):
    other = lax.ppermute(held, "span", pairs)
    upper = (lax.axis_index("span") & step) != 0
    return jnp.stack([jnp.where(upper, other, held), jnp.where(upper, held, other)])


def in_order(held, bits):
    order = tuple(range(bits))[::-1] + tuple(range(bits, held.ndim))
    held = held.transpose(order)
    return held.reshape((-1,) + held.shape[bits:])


def tiled_device(
    current_block,
    search_block,
    previous_block,
    ground_spring,
    wire_tension,
    dropper_stiff,
    dropper_offset,
    span_link,
    ritz_rotation,
):
    count = lax.axis_size("span")
    dofs = current_block.shape[2] // count
    rows = current_block.shape[1]
    steps = list(halvings("span"))
    far, near = steps[: len(steps) // 2], steps[len(steps) // 2 :]
    rotation = ritz_rotation[0].T
    for step, pairs in far:
        rotation = exchange_step(rotation, step, pairs)
    pieces = spread_blocks((current_block, search_block, previous_block), count)
    pieces, rotation = lax.optimization_barrier((pieces, rotation))
    stacked = exchange(pieces)
    for step, pairs in near:
        rotation = exchange_step(rotation, step, pairs)
    rotation = in_order(rotation, len(steps))
    scales = jnp.array(slot_scales(count), jnp.float32)[:, None, None]
    weights, ground, link = coefficients(
        ground_spring, wire_tension, dropper_stiff, dropper_offset, span_link, count, dofs
    )
    up = weights[:, REACH:]
    down = [weights[d - 1, REACH - d : REACH - d + dofs] for d in range(1, REACH + 1)]
    down = jnp.stack(down)
    diagonal = ground + jnp.sum(up, 0) + jnp.sum(down, 0)
    bands = jnp.concatenate([up, down, diagonal[None], link[None]])
    links = 2.0 * (1.0 - fourier_rows(count)[1])
    projected, spans, head, tail = project(stacked, rotation * scales)
    before, after = to_next(tail, 1), to_next(head, -1)
    stiff, sums = stiffness(projected, before, after, bands, links)
    for _, pairs in far:
        sums = sums + lax.ppermute(sums, "span", pairs)
    spans, sums = lax.optimization_barrier((spans, sums))
    next_block = collect_block(exchange(spans))
    for _, pairs in near:
        sums = sums + lax.ppermute(sums, "span", pairs)
    for _, pairs in halvings("elem"):
        sums = sums + lax.ppermute(sums, "elem", pairs)
    spans, ritz = residual_back(projected, stiff, sums)
    next_residual = collect_block(exchange(spans))
    ritz = lax.dynamic_slice_in_dim(ritz, lax.axis_index("span") * rows, rows, 1)
    return (next_block, next_residual, ritz)


def on_device(
    current_block,
    search_block,
    previous_block,
    ground_spring,
    wire_tension,
    dropper_stiff,
    dropper_offset,
    span_link,
    ritz_rotation,
):
    count = lax.axis_size("span")
    dof_dev = current_block.shape[2]
    dofs = dof_dev // count
    matrix, cosines = fourier_rows(count)
    blocks = (current_block, search_block, previous_block)
    stacked = exchange(jnp.concatenate([spread(b[0], count) for b in blocks], 1))
    rotation = lax.all_gather(ritz_rotation, "span", axis=0, tiled=True)
    weights, ground, link = coefficients(
        ground_spring, wire_tension, dropper_stiff, dropper_offset, span_link, count, dofs
    )
    slots = along_spans(matrix, stacked)
    projected = jnp.einsum("jvm,jvd->jmd", rotation, slots, precision=HIGHEST)
    back = matrix.T
    next_block = collect(exchange(along_spans(back, projected)))
    before = to_next(projected[:, :, dofs - REACH :], 1)
    after = to_next(projected[:, :, :REACH], -1)
    wide = jnp.concatenate([before, projected, after], 2)
    stiff = ground * projected
    near = wide[:, :, : REACH + dofs]
    for distance in range(1, REACH + 1):
        flux = weights[distance - 1] * (near - wide[:, :, distance : distance + REACH + dofs])
        stiff = stiff + flux[:, :, REACH:] - flux[:, :, REACH - distance : REACH - distance + dofs]
    stiff = stiff + (2.0 * (1.0 - cosines))[:, None, None] * link * projected
    sums = jnp.stack([jnp.sum(projected * stiff, 2), jnp.sum(projected * projected, 2)])
    sums = lax.psum(sums, ("elem", "span"))
    ritz = sums[0] / (sums[1] + 1e-06)
    residual = stiff - ritz[:, :, None] * projected
    next_residual = collect(exchange(along_spans(back, residual)))
    my_ritz = lax.dynamic_slice_in_dim(ritz, lax.axis_index("span"), 1, 0)
    return (next_block, next_residual, my_ritz)


def by_shape(*args):
    count, dof_dev = lax.axis_size("span"), args[0].shape[2]
    halves = count & (count - 1) == 0 and lax.axis_size("elem") in (1, 2, 4, 8, 16)
    if halves and count > 1 and dof_dev % (count * LANES) == 0:
        return tiled_device(*args)
    return on_device(*args)


def solution(mesh):
    return jax.shard_map(
        by_shape,
        mesh=mesh,
        in_specs=(
            P("span", None, "elem"),
            P("span", None, "elem"),
            P("span", None, "elem"),
            P("elem"),
            P("elem"),
            P("elem"),
            P("elem"),
            P("elem"),
            P("span", None, None),
        ),
        out_specs=(P("span", None, "elem"), P("span", None, "elem"), P("span", None)),
        check_vma=False,
    )
```

```python
import math

import jax
import jax.numpy as jnp
from jax import lax
from jax.experimental import pallas as pl
from jax.experimental.pallas import tpu as pltpu
from jax.sharding import PartitionSpec as P

REACH = 8
LANES = 128
ROWS = 8
VMEM_LIMIT = 20 * 1024 * 1024
HIGHEST = lax.Precision.HIGHEST


def fourier_rows(count):
    row = jnp.arange(count)[:, None]
    col = jnp.arange(count)[None, :]
    half = count // 2
    wave = jnp.where(row <= half, row, row - half)
    phase = (wave * col % count).astype(jnp.float32) * (2.0 * math.pi / count)
    scaled = jnp.where(row <= half, jnp.cos(phase), jnp.sin(phase)) * math.sqrt(2.0 / count)
    edge = (row == 0) | (row == half)
    matrix = jnp.where(edge, jnp.cos(phase) * math.sqrt(1.0 / count), scaled)
    slots = jnp.arange(count)
    slot_wave = jnp.where(slots <= half, slots, slots - half)
    cosines = jnp.cos(slot_wave.astype(jnp.float32) * (2.0 * math.pi / count))
    return (matrix, cosines)


def along_spans(matrix, block):
    shape = block.shape
    flat = block.reshape(shape[0], -1)
    return jnp.dot(matrix, flat, precision=HIGHEST).reshape(shape)


def spread(block, count):
    rows, dofs = block.shape
    return block.reshape(rows, count, dofs // count).transpose(1, 0, 2)


def collect(pieces):
    count, rows, dofs = pieces.shape
    return pieces.transpose(1, 0, 2).reshape(1, rows, count * dofs)


def exchange(pieces):
    return lax.all_to_all(pieces, "span", split_axis=0, concat_axis=0, tiled=True)


def to_next(cells, step):
    count, parts = lax.axis_size("span"), lax.axis_size("elem")
    line = [s * parts + e for e in range(parts) for s in range(count)]
    pairs = list(zip(line, line[1:]))
    if step < 0:
        pairs = [(b, a) for a, b in pairs]
    return lax.ppermute(cells, ("span", "elem"), pairs)


def coefficients(ground, tension, stiff, offset, link, count, dofs):
    dof_dev = ground.shape[0]
    start = lax.axis_index("span") * dofs
    elem = lax.axis_index("elem")
    dof_all = dof_dev * lax.axis_size("elem")
    position = elem * dof_dev + jnp.arange(dof_dev)
    distance = jnp.arange(1, REACH + 1)[:, None]
    weights = jnp.where((offset == distance) & (position + distance < dof_all), stiff, 0.0)
    wire = jnp.where((distance == 1) & (position < dof_all - 1), tension, 0.0)
    weights = weights + wire
    pairs = [(i, i + 1) for i in range(lax.axis_size("elem") - 1)]
    left = lax.ppermute(weights[:, dof_dev - REACH :], "elem", pairs)
    weights = jnp.concatenate([left, weights], 1)
    weights = lax.dynamic_slice_in_dim(weights, start, dofs + REACH, 1)
    ground = lax.dynamic_slice_in_dim(ground, start, dofs, 0)
    link = lax.dynamic_slice_in_dim(link, start, dofs, 0)
    return weights, ground, link


def add_up(terms):
    total = terms[0]
    for term in terms[1:]:
        total = total + term
    return total


def scaled(factor, value):
    if abs(factor - 1.0) < 1e-12:
        return value
    return value * factor


def cosine_sums(a):
    n = len(a) - 1
    if n == 1:
        return [a[0] + a[1], a[0] - a[1]]
    half = n // 2
    even = cosine_sums([a[s] + a[n - s] for s in range(half)] + [a[half]])
    diff = [a[s] - a[n - s] for s in range(half)]
    out = [None] * (n + 1)
    out[0::2] = even
    for j in range(1, n, 2):
        out[j] = add_up([scaled(math.cos(math.pi * j * s / n), diff[s]) for s in range(half)])
    return out


def sine_sums(b):
    n = len(b) + 1
    if n == 1:
        return []
    half = n // 2
    at = [None] + list(b)
    even = sine_sums([at[s] - at[n - s] for s in range(1, half)])
    total = [None] + [at[s] + at[n - s] for s in range(1, half)] + [at[half]]
    out = [None] * (n + 1)
    for k, value in enumerate(even):
        out[2 * k + 2] = value
    for j in range(1, n, 2):
        terms = [(math.sin(math.pi * j * s / n), total[s]) for s in range(1, half + 1)]
        terms = [scaled(abs(f), t) if f > 0 else -scaled(abs(f), t) for f, t in terms]
        out[j] = add_up(terms)
    return out[1:n]


def slot_scales(count):
    edge, inner = math.sqrt(1.0 / count), math.sqrt(2.0 / count)
    return [edge if j in (0, count // 2) else inner for j in range(count)]


def to_slots(x):
    n = len(x)
    half = n // 2
    plus = [x[0]] + [x[s] + x[n - s] for s in range(1, half)] + [x[half]]
    minus = [x[s] - x[n - s] for s in range(1, half)]
    return cosine_sums(plus) + sine_sums(minus)


def to_spans(y):
    n = len(y)
    half = n // 2
    even = cosine_sums(y[: half + 1])
    odd = [None] + sine_sums(y[half + 1 :])
    out = [None] * n
    out[0], out[half] = even[0], even[half]
    for s in range(1, half):
        out[s] = even[s] + odd[s]
        out[n - s] = even[s] - odd[s]
    return out


def params(**kw):
    return pltpu.CompilerParams(vmem_limit_bytes=VMEM_LIMIT, **kw)


def spread_blocks(blocks, count):
    _, rows, dof_dev = blocks[0].shape
    dofs = dof_dev // count
    kinds = len(blocks)
    cuts = 2 if rows % (2 * ROWS) == 0 else 1
    strip = rows // cuts

    def kernel(*refs):
        out, held, come, go = refs[kinds:]
        arrivals = []
        for c in range(cuts):
            for k in range(kinds):
                at = slice(c * strip, (c + 1) * strip)
                copy = pltpu.make_async_copy(
                    refs[k].at[0, at, :], held.at[k, at, :], come.at[c * kinds + k]
                )
                copy.start()
                arrivals.append((c, k, copy))
        leaving = []
        for c, k, copy in arrivals:
            copy.wait()
            for i in range(count):
                piece = pltpu.make_async_copy(
                    held.at[k, c * strip : (c + 1) * strip, i * dofs : (i + 1) * dofs],
                    out.at[i, k * rows + c * strip : k * rows + (c + 1) * strip, :],
                    go.at[(c * kinds + k) * count + i],
                )
                piece.start()
                leaving.append(piece)
        for piece in leaving:
            piece.wait()

    whole = pl.BlockSpec(memory_space=pltpu.HBM)
    return pl.pallas_call(
        kernel,
        in_specs=[whole] * kinds,
        out_specs=whole,
        out_shape=pltpu.HBM((count, kinds * rows, dofs), jnp.float32),
        scratch_shapes=[
            pltpu.VMEM((kinds, rows, dof_dev), jnp.float32),
            pltpu.SemaphoreType.DMA((cuts * kinds,)),
            pltpu.SemaphoreType.DMA((cuts * kinds * count,)),
        ],
        compiler_params=pltpu.CompilerParams(vmem_limit_bytes=60 * 1024 * 1024),
        name="spread_blocks",
    )(*blocks)


def collect_blocks(pieces):
    count, rows, dofs = pieces[0].shape
    many = max(n for n in (1, 2, 4, 8) if count % n == 0)
    kinds = len(pieces)

    def kernel(*refs):
        for piece, out in zip(refs[:kinds], refs[kinds:]):
            for i in range(many):
                out[0, :, i * dofs : (i + 1) * dofs] = piece[i]

    return pl.pallas_call(
        kernel,
        grid=(count // many,),
        in_specs=[pl.BlockSpec((many, rows, dofs), lambda i: (i, 0, 0))] * kinds,
        out_specs=[pl.BlockSpec((1, rows, many * dofs), lambda i: (0, 0, i))] * kinds,
        out_shape=[pltpu.HBM((1, rows, count * dofs), jnp.float32)] * kinds,
        compiler_params=params(),
        name="collect_blocks",
    )(*pieces)


PARTS = 3


def bf16_parts(value):
    parts = []
    for i in range(PARTS):
        parts.append(value.astype(jnp.bfloat16))
        if i < PARTS - 1:
            value = value - parts[i].astype(jnp.float32)
    return parts


def project(stacked, rotation):
    count, wide, dofs = stacked.shape
    rows = rotation.shape[1]
    tiles = dofs // LANES
    scales = slot_scales(count)
    groups = -(-count * REACH // LANES)
    per = LANES // REACH

    strip = 2 * ROWS

    def kernel(x, rot, proj, back, head, tail, split_rot, *split_slots):
        tile = pl.program_id(0)

        @pl.when(tile == 0)
        def _():
            def one(j, carry):
                for i, part in enumerate(bf16_parts(rot[j])):
                    split_rot[j, i * rows : (i + 1) * rows, :] = part
                return carry

            lax.fori_loop(0, count, one, 0)

        def transform(r, carry):
            at = pl.ds(pl.multiple_of(r * strip, strip), strip)
            halves = []
            for h in range(2):
                own = pl.ds(pl.multiple_of(r * strip + h * ROWS, ROWS), ROWS)
                halves.append(to_slots([x[s, own, :] for s in range(count)]))
            for j in range(count):
                value = jnp.concatenate([half[j] for half in halves], 0)
                for part, ref in zip(bf16_parts(value), split_slots):
                    ref[j, at, :] = part
            return carry

        lax.fori_loop(0, wide // strip, transform, 0)
        for j in range(count):
            total = None
            for i in range(PARTS - 1, -1, -1):
                terms = PARTS - i
                stacked_terms = jnp.dot(
                    split_rot[j, : terms * rows, :],
                    split_slots[i][j],
                    preferred_element_type=jnp.float32,
                )
                for q in range(terms - 1, -1, -1):
                    term = stacked_terms[q * rows : (q + 1) * rows]
                    total = term if total is None else total + term
            proj[j] = total

        def inverse(r, carry):
            at = pl.ds(pl.multiple_of(r * ROWS, ROWS), ROWS)
            out = to_spans([proj[j, at, :] * scales[j] for j in range(count)])
            for s in range(count):
                back[s, at, :] = out[s]
            return carry

        lax.fori_loop(0, rows // ROWS, inverse, 0)
        lane = lax.broadcasted_iota(jnp.int32, (rows, LANES), 1)

        def pack(ref, start):
            for g in range(groups):
                packed = jnp.zeros((rows, LANES), jnp.float32)
                for k in range(min(per, count - g * per)):
                    turn = (k * REACH - start) % LANES
                    value = proj[g * per + k]
                    value = pltpu.roll(value, turn, 1) if turn else value
                    packed = jnp.where(lane // REACH == k, value, packed)
                ref[g] = packed

        @pl.when(tile == 0)
        def _():
            pack(head, 0)

        @pl.when(tile == tiles - 1)
        def _():
            pack(tail, LANES - REACH)

    cell = pl.BlockSpec((count, rows, LANES), lambda t: (0, 0, t))
    edge = pl.BlockSpec((groups, rows, LANES), lambda t: (0, 0, 0))
    field = pltpu.HBM((count, rows, dofs), jnp.float32)
    edges = jax.ShapeDtypeStruct((groups, rows, LANES), jnp.float32)
    return pl.pallas_call(
        kernel,
        grid=(tiles,),
        in_specs=[
            pl.BlockSpec((count, wide, LANES), lambda t: (0, 0, t)),
            pl.BlockSpec((count, rows, wide), lambda t: (0, 0, 0)),
        ],
        out_specs=[cell, cell, edge, edge],
        out_shape=[jax.ShapeDtypeStruct(field.shape, jnp.float32), field, edges, edges],
        scratch_shapes=[pltpu.VMEM((count, PARTS * rows, wide), jnp.bfloat16)]
        + [pltpu.VMEM((count, wide, LANES), jnp.bfloat16)] * PARTS,
        compiler_params=params(),
        name="project",
    )(stacked, rotation)


def stiffness(projected, before, after, bands, links):
    count, rows, dofs = projected.shape
    per = LANES // REACH
    tiles = dofs // LANES

    def kernel(x, left, right, band, lam, stiff, sums, energy, norm, matrix):
        row = lax.broadcasted_iota(jnp.int32, (LANES, LANES), 0)
        gap = row - lax.broadcasted_iota(jnp.int32, (LANES, LANES), 1)
        for t in range(tiles):
            at = slice(t * LANES, (t + 1) * LANES)
            here = jnp.where(gap == 0, band[16:17, at], 0.0)
            halo = jnp.zeros((LANES, LANES), jnp.float32)
            for d in range(1, REACH + 1):
                up, down = band[d - 1 : d, at], band[REACH + d - 1 : REACH + d, at]
                here = jnp.where(gap == d, -up, here)
                here = jnp.where(gap == -d, -down, here)
                halo = jnp.where(gap == d - LANES, -up, halo)
                halo = jnp.where(gap == LANES - d, -down, halo)
            matrix[t, :LANES, :] = here
            matrix[t, LANES:, :] = halo
        lane = lax.broadcasted_iota(jnp.int32, (rows, LANES), 1)

        def slot(j, carry):
            to = pl.ds(pl.multiple_of(j * rows, rows), rows)
            g, k = j // per, j % per
            low = pltpu.roll(left[g], (2 * LANES - REACH - REACH * k) % LANES, 1)
            high = pltpu.roll(right[g], (LANES - REACH * k) % LANES, 1)
            work = jnp.zeros((rows, LANES), jnp.float32)
            size = jnp.zeros((rows, LANES), jnp.float32)
            for t in range(tiles):
                at = slice(t * LANES, (t + 1) * LANES)
                here = x[j, :, at]
                previous = low if t == 0 else x[j, :, (t - 1) * LANES : t * LANES]
                following = high if t == tiles - 1 else x[j, :, (t + 1) * LANES : (t + 2) * LANES]
                halo = jnp.where(lane < LANES // 2, following, previous)
                total = jnp.dot(
                    jnp.concatenate([here, halo], 1),
                    matrix[t],
                    precision=HIGHEST,
                    preferred_element_type=jnp.float32,
                )
                total = total + (lam[j] * band[17:18, at]) * here
                stiff[j, :, at] = total
                work = work + total * here
                size = size + here * here
            energy[to, :] = work
            norm[to, :] = size
            return carry

        lax.fori_loop(0, count, slot, 0)
        ones = jnp.ones((ROWS, LANES), jnp.float32)
        for r, part in enumerate((energy, norm)):
            line = lax.dot_general(
                ones,
                part[...],
                (((1,), (1,)), ((), ())),
                precision=HIGHEST,
                preferred_element_type=jnp.float32,
            )
            sums[r : r + 1, :] = line[:1]

    vmem = pl.BlockSpec(memory_space=pltpu.VMEM)
    return pl.pallas_call(
        kernel,
        in_specs=[vmem, vmem, vmem, vmem, pl.BlockSpec(memory_space=pltpu.SMEM)],
        out_specs=[vmem, vmem],
        out_shape=[
            jax.ShapeDtypeStruct((count, rows, dofs), jnp.float32),
            jax.ShapeDtypeStruct((2, count * rows), jnp.float32),
        ],
        scratch_shapes=[
            pltpu.VMEM((count * rows, LANES), jnp.float32),
            pltpu.VMEM((count * rows, LANES), jnp.float32),
            pltpu.VMEM((tiles, 2 * LANES, LANES), jnp.float32),
        ],
        compiler_params=params(),
        name="stiffness",
    )(projected, before, after, bands, links)


def residual_back(projected, stiff, sums):
    count, rows, dofs = projected.shape
    scales = slot_scales(count)

    def kernel(x, kx, total, back, ritz, wide):
        @pl.when(pl.program_id(0) == 0)
        def _():
            value = total[0:1, :] / (total[1:2, :] + 1e-06)
            ritz[...] = value
            row = lax.broadcasted_iota(jnp.int32, (ROWS, count * rows), 0)
            first = jnp.where(row == 0, value, 0.0)
            ones = jnp.ones((ROWS, LANES), jnp.float32)
            spread_out = lax.dot_general(
                first,
                ones,
                (((0,), (0,)), ((), ())),
                precision=HIGHEST,
                preferred_element_type=jnp.float32,
            )
            wide[...] = spread_out

        def strip(r, carry):
            at = pl.ds(pl.multiple_of(r * ROWS, ROWS), ROWS)
            terms = []
            for j in range(count):
                to = pl.ds(pl.multiple_of(j * rows + r * ROWS, ROWS), ROWS)
                terms.append((kx[j, at, :] - wide[to, :] * x[j, at, :]) * scales[j])
            out = to_spans(terms)
            for s in range(count):
                back[s, at, :] = out[s]
            return carry

        lax.fori_loop(0, rows // ROWS, strip, 0)

    cell = pl.BlockSpec((count, rows, LANES), lambda t: (0, 0, t))
    return pl.pallas_call(
        kernel,
        grid=(dofs // LANES,),
        in_specs=[cell, cell, pl.BlockSpec((2, count * rows), lambda t: (0, 0))],
        out_specs=[cell, pl.BlockSpec((1, count * rows), lambda t: (0, 0))],
        out_shape=[
            pltpu.HBM((count, rows, dofs), jnp.float32),
            jax.ShapeDtypeStruct((1, count * rows), jnp.float32),
        ],
        scratch_shapes=[pltpu.VMEM((count * rows, LANES), jnp.float32)],
        compiler_params=params(),
        name="residual_back",
    )(projected, stiff, sums)


def halvings(axis):
    step = lax.axis_size(axis) // 2
    while step:
        yield step, [(i, i ^ step) for i in range(lax.axis_size(axis))]
        step //= 2


def exchange_step(held, step, pairs):
    other = lax.ppermute(held, "span", pairs)
    upper = (lax.axis_index("span") & step) != 0
    return jnp.stack([jnp.where(upper, other, held), jnp.where(upper, held, other)])


def in_order(held, bits):
    order = tuple(range(bits))[::-1] + tuple(range(bits, held.ndim))
    held = held.transpose(order)
    return held.reshape((-1,) + held.shape[bits:])


def tiled_device(
    current_block,
    search_block,
    previous_block,
    ground_spring,
    wire_tension,
    dropper_stiff,
    dropper_offset,
    span_link,
    ritz_rotation,
):
    count = lax.axis_size("span")
    dofs = current_block.shape[2] // count
    rows = current_block.shape[1]
    steps = list(halvings("span"))
    far, near = steps[: len(steps) // 2], steps[len(steps) // 2 :]
    rotation = ritz_rotation[0].T
    for step, pairs in far:
        rotation = exchange_step(rotation, step, pairs)
    pieces = spread_blocks((current_block, search_block, previous_block), count)
    pieces, rotation = lax.optimization_barrier((pieces, rotation))
    stacked = exchange(pieces)
    for step, pairs in near:
        rotation = exchange_step(rotation, step, pairs)
    rotation = in_order(rotation, len(steps))
    scales = jnp.array(slot_scales(count), jnp.float32)[:, None, None]
    weights, ground, link = coefficients(
        ground_spring, wire_tension, dropper_stiff, dropper_offset, span_link, count, dofs
    )
    up = weights[:, REACH:]
    down = [weights[d - 1, REACH - d : REACH - d + dofs] for d in range(1, REACH + 1)]
    down = jnp.stack(down)
    diagonal = ground + jnp.sum(up, 0) + jnp.sum(down, 0)
    bands = jnp.concatenate([up, down, diagonal[None], link[None]])
    links = 2.0 * (1.0 - fourier_rows(count)[1])
    projected, spans, head, tail = project(stacked, rotation * scales)
    before, after = to_next(tail, 1), to_next(head, -1)
    stiff, sums = stiffness(projected, before, after, bands, links)
    for _, pairs in far:
        sums = sums + lax.ppermute(sums, "span", pairs)
    spans, sums = lax.optimization_barrier((spans, sums))
    block_pieces = exchange(spans)
    for _, pairs in near:
        sums = sums + lax.ppermute(sums, "span", pairs)
    for _, pairs in halvings("elem"):
        sums = sums + lax.ppermute(sums, "elem", pairs)
    spans, ritz = residual_back(projected, stiff, sums)
    next_block, next_residual = collect_blocks([block_pieces, exchange(spans)])
    ritz = lax.dynamic_slice_in_dim(ritz, lax.axis_index("span") * rows, rows, 1)
    return (next_block, next_residual, ritz)


def on_device(
    current_block,
    search_block,
    previous_block,
    ground_spring,
    wire_tension,
    dropper_stiff,
    dropper_offset,
    span_link,
    ritz_rotation,
):
    count = lax.axis_size("span")
    dof_dev = current_block.shape[2]
    dofs = dof_dev // count
    matrix, cosines = fourier_rows(count)
    blocks = (current_block, search_block, previous_block)
    stacked = exchange(jnp.concatenate([spread(b[0], count) for b in blocks], 1))
    rotation = lax.all_gather(ritz_rotation, "span", axis=0, tiled=True)
    weights, ground, link = coefficients(
        ground_spring, wire_tension, dropper_stiff, dropper_offset, span_link, count, dofs
    )
    slots = along_spans(matrix, stacked)
    projected = jnp.einsum("jvm,jvd->jmd", rotation, slots, precision=HIGHEST)
    back = matrix.T
    next_block = collect(exchange(along_spans(back, projected)))
    before = to_next(projected[:, :, dofs - REACH :], 1)
    after = to_next(projected[:, :, :REACH], -1)
    wide = jnp.concatenate([before, projected, after], 2)
    stiff = ground * projected
    near = wide[:, :, : REACH + dofs]
    for distance in range(1, REACH + 1):
        flux = weights[distance - 1] * (near - wide[:, :, distance : distance + REACH + dofs])
        stiff = stiff + flux[:, :, REACH:] - flux[:, :, REACH - distance : REACH - distance + dofs]
    stiff = stiff + (2.0 * (1.0 - cosines))[:, None, None] * link * projected
    sums = jnp.stack([jnp.sum(projected * stiff, 2), jnp.sum(projected * projected, 2)])
    sums = lax.psum(sums, ("elem", "span"))
    ritz = sums[0] / (sums[1] + 1e-06)
    residual = stiff - ritz[:, :, None] * projected
    next_residual = collect(exchange(along_spans(back, residual)))
    my_ritz = lax.dynamic_slice_in_dim(ritz, lax.axis_index("span"), 1, 0)
    return (next_block, next_residual, my_ritz)


def by_shape(*args):
    count, dof_dev = lax.axis_size("span"), args[0].shape[2]
    halves = count & (count - 1) == 0 and lax.axis_size("elem") in (1, 2, 4, 8, 16)
    if halves and count > 1 and dof_dev % (count * LANES) == 0:
        return tiled_device(*args)
    return on_device(*args)


def solution(mesh):
    return jax.shard_map(
        by_shape,
        mesh=mesh,
        in_specs=(
            P("span", None, "elem"),
            P("span", None, "elem"),
            P("span", None, "elem"),
            P("elem"),
            P("elem"),
            P("elem"),
            P("elem"),
            P("elem"),
            P("span", None, None),
        ),
        out_specs=(P("span", None, "elem"), P("span", None, "elem"), P("span", None)),
        check_vma=False,
    )
```

```python
import math

import jax
import jax.numpy as jnp
from jax import lax
from jax.experimental import pallas as pl
from jax.experimental.pallas import tpu as pltpu
from jax.sharding import PartitionSpec as P

REACH = 8
LANES = 128
ROWS = 8
VMEM_LIMIT = 20 * 1024 * 1024
HIGHEST = lax.Precision.HIGHEST


def fourier_rows(count):
    row = jnp.arange(count)[:, None]
    col = jnp.arange(count)[None, :]
    half = count // 2
    wave = jnp.where(row <= half, row, row - half)
    phase = (wave * col % count).astype(jnp.float32) * (2.0 * math.pi / count)
    scaled = jnp.where(row <= half, jnp.cos(phase), jnp.sin(phase)) * math.sqrt(2.0 / count)
    edge = (row == 0) | (row == half)
    matrix = jnp.where(edge, jnp.cos(phase) * math.sqrt(1.0 / count), scaled)
    slots = jnp.arange(count)
    slot_wave = jnp.where(slots <= half, slots, slots - half)
    cosines = jnp.cos(slot_wave.astype(jnp.float32) * (2.0 * math.pi / count))
    return (matrix, cosines)


def along_spans(matrix, block):
    shape = block.shape
    flat = block.reshape(shape[0], -1)
    return jnp.dot(matrix, flat, precision=HIGHEST).reshape(shape)


def spread(block, count):
    rows, dofs = block.shape
    return block.reshape(rows, count, dofs // count).transpose(1, 0, 2)


def collect(pieces):
    count, rows, dofs = pieces.shape
    return pieces.transpose(1, 0, 2).reshape(1, rows, count * dofs)


def exchange(pieces):
    return lax.all_to_all(pieces, "span", split_axis=0, concat_axis=0, tiled=True)


def to_next(cells, step):
    count, parts = lax.axis_size("span"), lax.axis_size("elem")
    line = [s * parts + e for e in range(parts) for s in range(count)]
    pairs = list(zip(line, line[1:]))
    if step < 0:
        pairs = [(b, a) for a, b in pairs]
    return lax.ppermute(cells, ("span", "elem"), pairs)


def coefficients(ground, tension, stiff, offset, link, count, dofs):
    dof_dev = ground.shape[0]
    start = lax.axis_index("span") * dofs
    elem = lax.axis_index("elem")
    dof_all = dof_dev * lax.axis_size("elem")
    position = elem * dof_dev + jnp.arange(dof_dev)
    distance = jnp.arange(1, REACH + 1)[:, None]
    weights = jnp.where((offset == distance) & (position + distance < dof_all), stiff, 0.0)
    wire = jnp.where((distance == 1) & (position < dof_all - 1), tension, 0.0)
    weights = weights + wire
    pairs = [(i, i + 1) for i in range(lax.axis_size("elem") - 1)]
    left = lax.ppermute(weights[:, dof_dev - REACH :], "elem", pairs)
    weights = jnp.concatenate([left, weights], 1)
    weights = lax.dynamic_slice_in_dim(weights, start, dofs + REACH, 1)
    ground = lax.dynamic_slice_in_dim(ground, start, dofs, 0)
    link = lax.dynamic_slice_in_dim(link, start, dofs, 0)
    return weights, ground, link


def add_up(terms):
    total = terms[0]
    for term in terms[1:]:
        total = total + term
    return total


def scaled(factor, value):
    if abs(factor - 1.0) < 1e-12:
        return value
    return value * factor


def cosine_sums(a):
    n = len(a) - 1
    if n == 1:
        return [a[0] + a[1], a[0] - a[1]]
    half = n // 2
    even = cosine_sums([a[s] + a[n - s] for s in range(half)] + [a[half]])
    diff = [a[s] - a[n - s] for s in range(half)]
    out = [None] * (n + 1)
    out[0::2] = even
    for j in range(1, n, 2):
        out[j] = add_up([scaled(math.cos(math.pi * j * s / n), diff[s]) for s in range(half)])
    return out


def sine_sums(b):
    n = len(b) + 1
    if n == 1:
        return []
    half = n // 2
    at = [None] + list(b)
    even = sine_sums([at[s] - at[n - s] for s in range(1, half)])
    total = [None] + [at[s] + at[n - s] for s in range(1, half)] + [at[half]]
    out = [None] * (n + 1)
    for k, value in enumerate(even):
        out[2 * k + 2] = value
    for j in range(1, n, 2):
        terms = [(math.sin(math.pi * j * s / n), total[s]) for s in range(1, half + 1)]
        terms = [scaled(abs(f), t) if f > 0 else -scaled(abs(f), t) for f, t in terms]
        out[j] = add_up(terms)
    return out[1:n]


def slot_scales(count):
    edge, inner = math.sqrt(1.0 / count), math.sqrt(2.0 / count)
    return [edge if j in (0, count // 2) else inner for j in range(count)]


def to_slots(x):
    n = len(x)
    half = n // 2
    plus = [x[0]] + [x[s] + x[n - s] for s in range(1, half)] + [x[half]]
    minus = [x[s] - x[n - s] for s in range(1, half)]
    return cosine_sums(plus) + sine_sums(minus)


def to_spans(y):
    n = len(y)
    half = n // 2
    even = cosine_sums(y[: half + 1])
    odd = [None] + sine_sums(y[half + 1 :])
    out = [None] * n
    out[0], out[half] = even[0], even[half]
    for s in range(1, half):
        out[s] = even[s] + odd[s]
        out[n - s] = even[s] - odd[s]
    return out


def params(**kw):
    return pltpu.CompilerParams(vmem_limit_bytes=VMEM_LIMIT, **kw)


def spread_blocks(blocks, count):
    _, rows, dof_dev = blocks[0].shape
    dofs = dof_dev // count
    kinds = len(blocks)
    cuts = 2 if rows % (2 * ROWS) == 0 else 1
    strip = rows // cuts

    def kernel(*refs):
        out, held, come, go = refs[kinds:]
        arrivals = []
        for c in range(cuts):
            for k in range(kinds):
                at = slice(c * strip, (c + 1) * strip)
                copy = pltpu.make_async_copy(
                    refs[k].at[0, at, :], held.at[k, at, :], come.at[c * kinds + k]
                )
                copy.start()
                arrivals.append((c, k, copy))
        leaving = []
        for c, k, copy in arrivals:
            copy.wait()
            for i in range(count):
                piece = pltpu.make_async_copy(
                    held.at[k, c * strip : (c + 1) * strip, i * dofs : (i + 1) * dofs],
                    out.at[i, k * rows + c * strip : k * rows + (c + 1) * strip, :],
                    go.at[(c * kinds + k) * count + i],
                )
                piece.start()
                leaving.append(piece)
        for piece in leaving:
            piece.wait()

    whole = pl.BlockSpec(memory_space=pltpu.HBM)
    return pl.pallas_call(
        kernel,
        in_specs=[whole] * kinds,
        out_specs=whole,
        out_shape=pltpu.HBM((count, kinds * rows, dofs), jnp.float32),
        scratch_shapes=[
            pltpu.VMEM((kinds, rows, dof_dev), jnp.float32),
            pltpu.SemaphoreType.DMA((cuts * kinds,)),
            pltpu.SemaphoreType.DMA((cuts * kinds * count,)),
        ],
        compiler_params=pltpu.CompilerParams(vmem_limit_bytes=60 * 1024 * 1024),
        name="spread_blocks",
    )(*blocks)


def collect_blocks(pieces):
    count, rows, dofs = pieces[0].shape
    many = max(n for n in (1, 2, 4, 8) if count % n == 0)
    kinds = len(pieces)

    def kernel(*refs):
        for piece, out in zip(refs[:kinds], refs[kinds:]):
            for i in range(many):
                out[0, :, i * dofs : (i + 1) * dofs] = piece[i]

    return pl.pallas_call(
        kernel,
        grid=(count // many,),
        in_specs=[pl.BlockSpec((many, rows, dofs), lambda i: (i, 0, 0))] * kinds,
        out_specs=[pl.BlockSpec((1, rows, many * dofs), lambda i: (0, 0, i))] * kinds,
        out_shape=[pltpu.HBM((1, rows, count * dofs), jnp.float32)] * kinds,
        compiler_params=params(),
        name="collect_blocks",
    )(*pieces)


PARTS = 3


def bf16_parts(value):
    parts = []
    for i in range(PARTS):
        parts.append(value.astype(jnp.bfloat16))
        if i < PARTS - 1:
            value = value - parts[i].astype(jnp.float32)
    return parts


def project(stacked, rotation):
    count, wide, dofs = stacked.shape
    rows = rotation.shape[1]
    tiles = dofs // LANES
    scales = slot_scales(count)
    groups = -(-count * REACH // LANES)
    per = LANES // REACH

    strip = 2 * ROWS

    def kernel(x, rot, proj, back, head, tail, split_rot, *split_slots):
        tile = pl.program_id(0)

        @pl.when(tile == 0)
        def _():
            def one(j, carry):
                for i, part in enumerate(bf16_parts(rot[j])):
                    split_rot[j, i * rows : (i + 1) * rows, :] = part
                return carry

            lax.fori_loop(0, count, one, 0)

        def transform(r, carry):
            at = pl.ds(pl.multiple_of(r * strip, strip), strip)
            halves = []
            for h in range(2):
                own = pl.ds(pl.multiple_of(r * strip + h * ROWS, ROWS), ROWS)
                halves.append(to_slots([x[s, own, :] for s in range(count)]))
            for j in range(count):
                value = jnp.concatenate([half[j] for half in halves], 0)
                for part, ref in zip(bf16_parts(value), split_slots):
                    ref[j, at, :] = part
            return carry

        lax.fori_loop(0, wide // strip, transform, 0)
        for j in range(count):
            total = None
            for i in range(PARTS - 1, -1, -1):
                terms = PARTS - i
                stacked_terms = jnp.dot(
                    split_rot[j, : terms * rows, :],
                    split_slots[i][j],
                    preferred_element_type=jnp.float32,
                )
                for q in range(terms - 1, -1, -1):
                    term = stacked_terms[q * rows : (q + 1) * rows]
                    total = term if total is None else total + term
            proj[j] = total

        def inverse(r, carry):
            at = pl.ds(pl.multiple_of(r * ROWS, ROWS), ROWS)
            out = to_spans([proj[j, at, :] * scales[j] for j in range(count)])
            for s in range(count):
                back[s, at, :] = out[s]
            return carry

        lax.fori_loop(0, rows // ROWS, inverse, 0)
        lane = lax.broadcasted_iota(jnp.int32, (rows, LANES), 1)

        def pack(ref, start):
            for g in range(groups):
                packed = jnp.zeros((rows, LANES), jnp.float32)
                for k in range(min(per, count - g * per)):
                    turn = (k * REACH - start) % LANES
                    value = proj[g * per + k]
                    value = pltpu.roll(value, turn, 1) if turn else value
                    packed = jnp.where(lane // REACH == k, value, packed)
                ref[g] = packed

        @pl.when(tile == 0)
        def _():
            pack(head, 0)

        @pl.when(tile == tiles - 1)
        def _():
            pack(tail, LANES - REACH)

    cell = pl.BlockSpec((count, rows, LANES), lambda t: (0, 0, t))
    edge = pl.BlockSpec((groups, rows, LANES), lambda t: (0, 0, 0))
    field = pltpu.HBM((count, rows, dofs), jnp.float32)
    edges = jax.ShapeDtypeStruct((groups, rows, LANES), jnp.float32)
    return pl.pallas_call(
        kernel,
        grid=(tiles,),
        in_specs=[
            pl.BlockSpec((count, wide, LANES), lambda t: (0, 0, t)),
            pl.BlockSpec((count, rows, wide), lambda t: (0, 0, 0)),
        ],
        out_specs=[cell, cell, edge, edge],
        out_shape=[jax.ShapeDtypeStruct(field.shape, jnp.float32), field, edges, edges],
        scratch_shapes=[pltpu.VMEM((count, PARTS * rows, wide), jnp.bfloat16)]
        + [pltpu.VMEM((count, wide, LANES), jnp.bfloat16)] * PARTS,
        compiler_params=params(),
        name="project",
    )(stacked, rotation)


def stiffness(projected, before, after, bands, links):
    count, rows, dofs = projected.shape
    per = LANES // REACH
    tiles = dofs // LANES

    def kernel(x, left, right, band, lam, stiff, sums, energy, norm, matrix):
        row = lax.broadcasted_iota(jnp.int32, (LANES, LANES), 0)
        gap = row - lax.broadcasted_iota(jnp.int32, (LANES, LANES), 1)
        for t in range(tiles):
            at = slice(t * LANES, (t + 1) * LANES)
            here = jnp.where(gap == 0, band[16:17, at], 0.0)
            halo = jnp.zeros((LANES, LANES), jnp.float32)
            for d in range(1, REACH + 1):
                up, down = band[d - 1 : d, at], band[REACH + d - 1 : REACH + d, at]
                here = jnp.where(gap == d, -up, here)
                here = jnp.where(gap == -d, -down, here)
                halo = jnp.where(gap == d - LANES, -up, halo)
                halo = jnp.where(gap == LANES - d, -down, halo)
            matrix[t, :LANES, :] = here
            matrix[t, LANES:, :] = halo
        lane = lax.broadcasted_iota(jnp.int32, (rows, LANES), 1)

        def slot(j, carry):
            to = pl.ds(pl.multiple_of(j * rows, rows), rows)
            g, k = j // per, j % per
            low = pltpu.roll(left[g], (2 * LANES - REACH - REACH * k) % LANES, 1)
            high = pltpu.roll(right[g], (LANES - REACH * k) % LANES, 1)
            work = jnp.zeros((rows, LANES), jnp.float32)
            size = jnp.zeros((rows, LANES), jnp.float32)
            for t in range(tiles):
                at = slice(t * LANES, (t + 1) * LANES)
                here = x[j, :, at]
                previous = low if t == 0 else x[j, :, (t - 1) * LANES : t * LANES]
                following = high if t == tiles - 1 else x[j, :, (t + 1) * LANES : (t + 2) * LANES]
                halo = jnp.where(lane < LANES // 2, following, previous)
                total = jnp.dot(
                    jnp.concatenate([here, halo], 1),
                    matrix[t],
                    precision=HIGHEST,
                    preferred_element_type=jnp.float32,
                )
                total = total + (lam[j] * band[17:18, at]) * here
                stiff[j, :, at] = total
                work = work + total * here
                size = size + here * here
            energy[to, :] = work
            norm[to, :] = size
            return carry

        lax.fori_loop(0, count, slot, 0)
        ones = jnp.ones((ROWS, LANES), jnp.float32)
        for r, part in enumerate((energy, norm)):
            line = lax.dot_general(
                ones,
                part[...],
                (((1,), (1,)), ((), ())),
                precision=HIGHEST,
                preferred_element_type=jnp.float32,
            )
            sums[r : r + 1, :] = line[:1]

    vmem = pl.BlockSpec(memory_space=pltpu.VMEM)
    return pl.pallas_call(
        kernel,
        in_specs=[vmem, vmem, vmem, vmem, pl.BlockSpec(memory_space=pltpu.SMEM)],
        out_specs=[vmem, vmem],
        out_shape=[
            jax.ShapeDtypeStruct((count, rows, dofs), jnp.float32),
            jax.ShapeDtypeStruct((2, count * rows), jnp.float32),
        ],
        scratch_shapes=[
            pltpu.VMEM((count * rows, LANES), jnp.float32),
            pltpu.VMEM((count * rows, LANES), jnp.float32),
            pltpu.VMEM((tiles, 2 * LANES, LANES), jnp.float32),
        ],
        compiler_params=params(),
        name="stiffness",
    )(projected, before, after, bands, links)


def residual_back(projected, stiff, sums):
    count, rows, dofs = projected.shape
    scales = slot_scales(count)

    def kernel(x, kx, total, back, ritz, wide):
        @pl.when(pl.program_id(0) == 0)
        def _():
            value = total[0:1, :] / (total[1:2, :] + 1e-06)
            ritz[...] = value
            row = lax.broadcasted_iota(jnp.int32, (ROWS, count * rows), 0)
            first = jnp.where(row == 0, value, 0.0)
            ones = jnp.ones((ROWS, LANES), jnp.float32)
            spread_out = lax.dot_general(
                first,
                ones,
                (((0,), (0,)), ((), ())),
                precision=HIGHEST,
                preferred_element_type=jnp.float32,
            )
            wide[...] = spread_out

        def strip(r, carry):
            at = pl.ds(pl.multiple_of(r * ROWS, ROWS), ROWS)
            terms = []
            for j in range(count):
                to = pl.ds(pl.multiple_of(j * rows + r * ROWS, ROWS), ROWS)
                terms.append((kx[j, at, :] - wide[to, :] * x[j, at, :]) * scales[j])
            out = to_spans(terms)
            for s in range(count):
                back[s, at, :] = out[s]
            return carry

        lax.fori_loop(0, rows // ROWS, strip, 0)

    cell = pl.BlockSpec((count, rows, LANES), lambda t: (0, 0, t))
    return pl.pallas_call(
        kernel,
        grid=(dofs // LANES,),
        in_specs=[cell, cell, pl.BlockSpec((2, count * rows), lambda t: (0, 0))],
        out_specs=[cell, pl.BlockSpec((1, count * rows), lambda t: (0, 0))],
        out_shape=[
            pltpu.HBM((count, rows, dofs), jnp.float32),
            jax.ShapeDtypeStruct((1, count * rows), jnp.float32),
        ],
        scratch_shapes=[pltpu.VMEM((count * rows, LANES), jnp.float32)],
        compiler_params=params(),
        name="residual_back",
    )(projected, stiff, sums)


def halvings(axis):
    step = lax.axis_size(axis) // 2
    while step:
        yield step, [(i, i ^ step) for i in range(lax.axis_size(axis))]
        step //= 2


def exchange_step(held, step, pairs):
    other = lax.ppermute(held, "span", pairs)
    upper = (lax.axis_index("span") & step) != 0
    return jnp.stack([jnp.where(upper, other, held), jnp.where(upper, held, other)])


def in_order(held, steps):
    bits = [step for step, _ in steps][::-1]
    order = tuple(sorted(range(len(bits)), key=lambda d: -bits[d]))
    held = held.transpose(order + tuple(range(len(bits), held.ndim)))
    return held.reshape((-1,) + held.shape[len(bits) :])


def tiled_device(
    current_block,
    search_block,
    previous_block,
    ground_spring,
    wire_tension,
    dropper_stiff,
    dropper_offset,
    span_link,
    ritz_rotation,
):
    count = lax.axis_size("span")
    dofs = current_block.shape[2] // count
    rows = current_block.shape[1]
    steps = list(halvings("span"))
    rotation = exchange_step(ritz_rotation[0].T, *steps[0])
    pieces = spread_blocks((current_block, search_block, previous_block), count)
    pieces, rotation = lax.optimization_barrier((pieces, rotation))
    stacked = exchange(pieces)
    order = steps[2:] + steps[1:2]
    for step, pairs in order:
        rotation = exchange_step(rotation, step, pairs)
    rotation = in_order(rotation, [steps[0]] + order)
    scales = jnp.array(slot_scales(count), jnp.float32)[:, None, None]
    weights, ground, link = coefficients(
        ground_spring, wire_tension, dropper_stiff, dropper_offset, span_link, count, dofs
    )
    up = weights[:, REACH:]
    down = [weights[d - 1, REACH - d : REACH - d + dofs] for d in range(1, REACH + 1)]
    down = jnp.stack(down)
    diagonal = ground + jnp.sum(up, 0) + jnp.sum(down, 0)
    bands = jnp.concatenate([up, down, diagonal[None], link[None]])
    links = 2.0 * (1.0 - fourier_rows(count)[1])
    projected, spans, head, tail = project(stacked, rotation * scales)
    before, after = to_next(tail, 1), to_next(head, -1)
    spans, before, after = lax.optimization_barrier((spans, before, after))
    block_pieces = exchange(spans)
    stiff, sums = stiffness(projected, before, after, bands, links)
    for _, pairs in halvings("elem"):
        sums = sums + lax.ppermute(sums, "elem", pairs)
    for _, pairs in steps[::-1]:
        sums = sums + lax.ppermute(sums, "span", pairs)
    spans, ritz = residual_back(projected, stiff, sums)
    next_block, next_residual = collect_blocks([block_pieces, exchange(spans)])
    ritz = lax.dynamic_slice_in_dim(ritz, lax.axis_index("span") * rows, rows, 1)
    return (next_block, next_residual, ritz)


def on_device(
    current_block,
    search_block,
    previous_block,
    ground_spring,
    wire_tension,
    dropper_stiff,
    dropper_offset,
    span_link,
    ritz_rotation,
):
    count = lax.axis_size("span")
    dof_dev = current_block.shape[2]
    dofs = dof_dev // count
    matrix, cosines = fourier_rows(count)
    blocks = (current_block, search_block, previous_block)
    stacked = exchange(jnp.concatenate([spread(b[0], count) for b in blocks], 1))
    rotation = lax.all_gather(ritz_rotation, "span", axis=0, tiled=True)
    weights, ground, link = coefficients(
        ground_spring, wire_tension, dropper_stiff, dropper_offset, span_link, count, dofs
    )
    slots = along_spans(matrix, stacked)
    projected = jnp.einsum("jvm,jvd->jmd", rotation, slots, precision=HIGHEST)
    back = matrix.T
    next_block = collect(exchange(along_spans(back, projected)))
    before = to_next(projected[:, :, dofs - REACH :], 1)
    after = to_next(projected[:, :, :REACH], -1)
    wide = jnp.concatenate([before, projected, after], 2)
    stiff = ground * projected
    near = wide[:, :, : REACH + dofs]
    for distance in range(1, REACH + 1):
        flux = weights[distance - 1] * (near - wide[:, :, distance : distance + REACH + dofs])
        stiff = stiff + flux[:, :, REACH:] - flux[:, :, REACH - distance : REACH - distance + dofs]
    stiff = stiff + (2.0 * (1.0 - cosines))[:, None, None] * link * projected
    sums = jnp.stack([jnp.sum(projected * stiff, 2), jnp.sum(projected * projected, 2)])
    sums = lax.psum(sums, ("elem", "span"))
    ritz = sums[0] / (sums[1] + 1e-06)
    residual = stiff - ritz[:, :, None] * projected
    next_residual = collect(exchange(along_spans(back, residual)))
    my_ritz = lax.dynamic_slice_in_dim(ritz, lax.axis_index("span"), 1, 0)
    return (next_block, next_residual, my_ritz)


def by_shape(*args):
    count, dof_dev = lax.axis_size("span"), args[0].shape[2]
    halves = count & (count - 1) == 0 and lax.axis_size("elem") in (1, 2, 4, 8, 16)
    if halves and count > 1 and dof_dev % (count * LANES) == 0:
        return tiled_device(*args)
    return on_device(*args)


def solution(mesh):
    return jax.shard_map(
        by_shape,
        mesh=mesh,
        in_specs=(
            P("span", None, "elem"),
            P("span", None, "elem"),
            P("span", None, "elem"),
            P("elem"),
            P("elem"),
            P("elem"),
            P("elem"),
            P("elem"),
            P("span", None, None),
        ),
        out_specs=(P("span", None, "elem"), P("span", None, "elem"), P("span", None)),
        check_vma=False,
    )
```

```python
import math

import jax
import jax.numpy as jnp
from jax import lax
from jax.experimental import pallas as pl
from jax.experimental.pallas import tpu as pltpu
from jax.sharding import PartitionSpec as P

REACH = 8
LANES = 128
ROWS = 8
VMEM_LIMIT = 20 * 1024 * 1024
HIGHEST = lax.Precision.HIGHEST


def fourier_rows(count):
    row = jnp.arange(count)[:, None]
    col = jnp.arange(count)[None, :]
    half = count // 2
    wave = jnp.where(row <= half, row, row - half)
    phase = (wave * col % count).astype(jnp.float32) * (2.0 * math.pi / count)
    scaled = jnp.where(row <= half, jnp.cos(phase), jnp.sin(phase)) * math.sqrt(2.0 / count)
    edge = (row == 0) | (row == half)
    matrix = jnp.where(edge, jnp.cos(phase) * math.sqrt(1.0 / count), scaled)
    slots = jnp.arange(count)
    slot_wave = jnp.where(slots <= half, slots, slots - half)
    cosines = jnp.cos(slot_wave.astype(jnp.float32) * (2.0 * math.pi / count))
    return (matrix, cosines)


def along_spans(matrix, block):
    shape = block.shape
    flat = block.reshape(shape[0], -1)
    return jnp.dot(matrix, flat, precision=HIGHEST).reshape(shape)


def spread(block, count):
    rows, dofs = block.shape
    return block.reshape(rows, count, dofs // count).transpose(1, 0, 2)


def collect(pieces):
    count, rows, dofs = pieces.shape
    return pieces.transpose(1, 0, 2).reshape(1, rows, count * dofs)


def exchange(pieces):
    return lax.all_to_all(pieces, "span", split_axis=0, concat_axis=0, tiled=True)


def to_next(cells, step):
    count, parts = lax.axis_size("span"), lax.axis_size("elem")
    line = [s * parts + e for e in range(parts) for s in range(count)]
    pairs = list(zip(line, line[1:]))
    if step < 0:
        pairs = [(b, a) for a, b in pairs]
    return lax.ppermute(cells, ("span", "elem"), pairs)


def exchange_half(pieces):
    count = lax.axis_size("span")
    half = count // 2
    groups = [list(range(half)), list(range(half, count))]
    return lax.all_to_all(
        pieces, "span", split_axis=0, concat_axis=0, tiled=True, axis_index_groups=groups
    )


def coefficients(ground, tension, stiff, offset, link, count, dofs):
    dof_dev = ground.shape[0]
    start = lax.axis_index("span") * dofs
    elem = lax.axis_index("elem")
    dof_all = dof_dev * lax.axis_size("elem")
    position = elem * dof_dev + jnp.arange(dof_dev)
    distance = jnp.arange(1, REACH + 1)[:, None]
    weights = jnp.where((offset == distance) & (position + distance < dof_all), stiff, 0.0)
    wire = jnp.where((distance == 1) & (position < dof_all - 1), tension, 0.0)
    weights = weights + wire
    pairs = [(i, i + 1) for i in range(lax.axis_size("elem") - 1)]
    left = lax.ppermute(weights[:, dof_dev - REACH :], "elem", pairs)
    weights = jnp.concatenate([left, weights], 1)
    weights = lax.dynamic_slice_in_dim(weights, start, dofs + REACH, 1)
    ground = lax.dynamic_slice_in_dim(ground, start, dofs, 0)
    link = lax.dynamic_slice_in_dim(link, start, dofs, 0)
    return weights, ground, link


def add_up(terms):
    total = terms[0]
    for term in terms[1:]:
        total = total + term
    return total


def scaled(factor, value):
    if abs(factor - 1.0) < 1e-12:
        return value
    return value * factor


def plus(a, b):
    return a if b is None else a + b


def minus(a, b):
    return a if b is None else a - b


def cosine_sums(a):
    n = len(a) - 1
    if n == 1:
        return [plus(a[0], a[1]), minus(a[0], a[1])]
    half = n // 2
    even = cosine_sums([plus(a[s], a[n - s]) for s in range(half)] + [a[half]])
    diff = [minus(a[s], a[n - s]) for s in range(half)]
    out = [None] * (n + 1)
    out[0::2] = even
    for j in range(1, n, 2):
        out[j] = add_up([scaled(math.cos(math.pi * j * s / n), diff[s]) for s in range(half)])
    return out


def sine_sums(b):
    n = len(b) + 1
    if n == 1:
        return []
    half = n // 2
    at = [None] + list(b)
    even = sine_sums([at[s] - at[n - s] for s in range(1, half)])
    total = [None] + [at[s] + at[n - s] for s in range(1, half)] + [at[half]]
    out = [None] * (n + 1)
    for k, value in enumerate(even):
        out[2 * k + 2] = value
    for j in range(1, n, 2):
        terms = [(math.sin(math.pi * j * s / n), total[s]) for s in range(1, half + 1)]
        terms = [scaled(abs(f), t) if f > 0 else -scaled(abs(f), t) for f, t in terms]
        out[j] = add_up(terms)
    return out[1:n]


def slot_scales(count):
    edge, inner = math.sqrt(1.0 / count), math.sqrt(2.0 / count)
    return [edge if j in (0, count // 2) else inner for j in range(count)]


def to_slots(x):
    return cosine_sums(list(x) + [None]) + sine_sums(x[1:])


def half_signs(count):
    half = count // 2
    return [-1.0 if (j if j <= half else j - half) % 2 else 1.0 for j in range(count)]


def to_spans(y):
    n = len(y)
    half = n // 2
    even = cosine_sums(y[: half + 1])
    odd = [None] + sine_sums(y[half + 1 :])
    out = [None] * n
    out[0], out[half] = even[0], even[half]
    for s in range(1, half):
        out[s] = even[s] + odd[s]
        out[n - s] = even[s] - odd[s]
    return out


def params(**kw):
    return pltpu.CompilerParams(vmem_limit_bytes=VMEM_LIMIT, **kw)


def spread_blocks(blocks, bases, dofs, many, cuts):
    rows = blocks[0].shape[1]
    kinds = len(blocks)

    def kernel(base, *refs):
        outs = refs[kinds : kinds + len(cuts)]
        held = refs[kinds + len(cuts) : kinds + 2 * len(cuts)]
        come, go = refs[-2:]
        arrivals = []
        for c, (which, first, width) in enumerate(cuts):
            for q in range(many):
                group = []
                for k in range(kinds):
                    start = pl.multiple_of(base[which] + (q * dofs + first), LANES)
                    copy = pltpu.make_async_copy(
                        refs[k].at[0, :, pl.ds(start, width)],
                        held[c].at[q, k * rows : (k + 1) * rows, :],
                        come.at[(c * many + q) * kinds + k],
                    )
                    copy.start()
                    group.append(copy)
                arrivals.append((c, q, group))
        leaving = []
        for c, q, group in arrivals:
            for copy in group:
                copy.wait()
            piece = pltpu.make_async_copy(held[c].at[q], outs[c].at[q], go.at[c * many + q])
            piece.start()
            leaving.append(piece)
        for piece in leaving:
            piece.wait()

    whole = pl.BlockSpec(memory_space=pltpu.HBM)
    shapes = [(many, kinds * rows, width) for _, _, width in cuts]
    return pl.pallas_call(
        kernel,
        in_specs=[pl.BlockSpec(memory_space=pltpu.SMEM)] + [whole] * kinds,
        out_specs=[whole] * len(cuts),
        out_shape=[pltpu.HBM(shape, jnp.float32) for shape in shapes],
        scratch_shapes=[pltpu.VMEM(shape, jnp.float32) for shape in shapes]
        + [
            pltpu.SemaphoreType.DMA((len(cuts) * many * kinds,)),
            pltpu.SemaphoreType.DMA((len(cuts) * many,)),
        ],
        compiler_params=pltpu.CompilerParams(vmem_limit_bytes=60 * 1024 * 1024),
        name="spread_blocks",
    )(bases, *blocks)


def collect_blocks(pieces):
    count, rows, dofs = pieces[0].shape
    many = max(n for n in (1, 2, 4, 8) if count % n == 0)
    kinds = len(pieces)

    def kernel(*refs):
        for piece, out in zip(refs[:kinds], refs[kinds:]):
            for i in range(many):
                out[0, :, i * dofs : (i + 1) * dofs] = piece[i]

    return pl.pallas_call(
        kernel,
        grid=(count // many,),
        in_specs=[pl.BlockSpec((many, rows, dofs), lambda i: (i, 0, 0))] * kinds,
        out_specs=[pl.BlockSpec((1, rows, many * dofs), lambda i: (0, 0, i))] * kinds,
        out_shape=[pltpu.HBM((1, rows, count * dofs), jnp.float32)] * kinds,
        compiler_params=params(),
        name="collect_blocks",
    )(*pieces)


PARTS = 3


def bf16_parts(value):
    parts = []
    for i in range(PARTS):
        parts.append(value.astype(jnp.bfloat16))
        if i < PARTS - 1:
            value = value - parts[i].astype(jnp.float32)
    return parts


def project(stacked, rotation):
    spans, wide, dofs = stacked.shape
    count, rows = rotation.shape[:2]
    strip = 2 * ROWS

    def kernel(x, rot, proj, split_rot, *split_slots):
        @pl.when(pl.program_id(0) == 0)
        def _():
            def one(j, carry):
                for i, part in enumerate(bf16_parts(rot[j])):
                    split_rot[j, i * rows : (i + 1) * rows, :] = part
                return carry

            lax.fori_loop(0, count, one, 0)

        def transform(r, carry):
            at = pl.ds(pl.multiple_of(r * strip, strip), strip)
            halves = []
            for h in range(2):
                own = pl.ds(pl.multiple_of(r * strip + h * ROWS, ROWS), ROWS)
                halves.append(to_slots([x[s, own, :] for s in range(spans)]))
            for j in range(count):
                value = jnp.concatenate([half[j] for half in halves], 0)
                for part, ref in zip(bf16_parts(value), split_slots):
                    ref[j, at, :] = part
            return carry

        lax.fori_loop(0, wide // strip, transform, 0)
        for j in range(count):
            total = None
            for i in range(PARTS - 1, -1, -1):
                terms = PARTS - i
                stacked_terms = jnp.dot(
                    split_rot[j, : terms * rows, :],
                    split_slots[i][j],
                    preferred_element_type=jnp.float32,
                )
                for q in range(terms - 1, -1, -1):
                    term = stacked_terms[q * rows : (q + 1) * rows]
                    total = term if total is None else total + term
            proj[j] = total

    return pl.pallas_call(
        kernel,
        grid=(dofs // LANES,),
        in_specs=[
            pl.BlockSpec((spans, wide, LANES), lambda t: (0, 0, t)),
            pl.BlockSpec((count, rows, wide), lambda t: (0, 0, 0)),
        ],
        out_specs=pl.BlockSpec((count, rows, LANES), lambda t: (0, 0, t)),
        out_shape=pltpu.HBM((count, rows, dofs), jnp.float32),
        scratch_shapes=[pltpu.VMEM((count, PARTS * rows, wide), jnp.bfloat16)]
        + [pltpu.VMEM((count, wide, LANES), jnp.bfloat16)] * PARTS,
        compiler_params=params(),
        name="project",
    )(stacked, rotation)


def combine(own, others):
    count, rows, dofs = own.shape
    tiles = dofs // LANES
    scales = slot_scales(count)
    groups = -(-count * REACH // LANES)
    per = LANES // REACH
    sizes = [other.shape[2] // LANES for other in others]
    firsts = [sum(sizes[:c]) for c in range(len(sizes))]

    def kernel(*refs):
        x, parts = refs[0], refs[1 : 1 + len(others)]
        proj, back, head, tail = refs[1 + len(others) :]
        tile = pl.program_id(0)

        def strip_of(part):
            def strip(r, carry):
                at = pl.ds(pl.multiple_of(r * ROWS, ROWS), ROWS)
                terms = []
                for j in range(count):
                    value = x[j, at, :] + part[j, at, :]
                    proj[j, at, :] = value
                    terms.append(value * scales[j])
                out = to_spans(terms)
                for s in range(count):
                    back[s, at, :] = out[s]
                return carry

            return strip

        for first, size, part in zip(firsts, sizes, parts):

            @pl.when((tile >= first) & (tile < first + size))
            def _(part=part):
                lax.fori_loop(0, rows // ROWS, strip_of(part), 0)

        lane = lax.broadcasted_iota(jnp.int32, (rows, LANES), 1)

        def pack(ref, start):
            for g in range(groups):
                packed = jnp.zeros((rows, LANES), jnp.float32)
                for k in range(min(per, count - g * per)):
                    turn = (k * REACH - start) % LANES
                    value = proj[g * per + k]
                    value = pltpu.roll(value, turn, 1) if turn else value
                    packed = jnp.where(lane // REACH == k, value, packed)
                ref[g] = packed

        @pl.when(tile == 0)
        def _():
            pack(head, 0)

        @pl.when(tile == tiles - 1)
        def _():
            pack(tail, LANES - REACH)

    def cell(first, size):
        return pl.BlockSpec(
            (count, rows, LANES), lambda t: (0, 0, jnp.clip(t - first, 0, size - 1))
        )

    plain = pl.BlockSpec((count, rows, LANES), lambda t: (0, 0, t))
    edge = pl.BlockSpec((groups, rows, LANES), lambda t: (0, 0, 0))
    edges = jax.ShapeDtypeStruct((groups, rows, LANES), jnp.float32)
    return pl.pallas_call(
        kernel,
        grid=(tiles,),
        in_specs=[plain] + [cell(f, z) for f, z in zip(firsts, sizes)],
        out_specs=[plain, plain, edge, edge],
        out_shape=[
            jax.ShapeDtypeStruct((count, rows, dofs), jnp.float32),
            pltpu.HBM((count, rows, dofs), jnp.float32),
            edges,
            edges,
        ],
        compiler_params=params(),
        name="combine",
    )(own, *others)


def stiffness(projected, before, after, bands, links):
    count, rows, dofs = projected.shape
    per = LANES // REACH
    tiles = dofs // LANES

    def kernel(x, left, right, band, lam, stiff, sums, energy, norm, matrix):
        row = lax.broadcasted_iota(jnp.int32, (LANES, LANES), 0)
        gap = row - lax.broadcasted_iota(jnp.int32, (LANES, LANES), 1)
        for t in range(tiles):
            at = slice(t * LANES, (t + 1) * LANES)
            here = jnp.where(gap == 0, band[16:17, at], 0.0)
            halo = jnp.zeros((LANES, LANES), jnp.float32)
            for d in range(1, REACH + 1):
                up, down = band[d - 1 : d, at], band[REACH + d - 1 : REACH + d, at]
                here = jnp.where(gap == d, -up, here)
                here = jnp.where(gap == -d, -down, here)
                halo = jnp.where(gap == d - LANES, -up, halo)
                halo = jnp.where(gap == LANES - d, -down, halo)
            matrix[t, :LANES, :] = here
            matrix[t, LANES:, :] = halo
        lane = lax.broadcasted_iota(jnp.int32, (rows, LANES), 1)

        def slot(j, carry):
            to = pl.ds(pl.multiple_of(j * rows, rows), rows)
            g, k = j // per, j % per
            low = pltpu.roll(left[g], (2 * LANES - REACH - REACH * k) % LANES, 1)
            high = pltpu.roll(right[g], (LANES - REACH * k) % LANES, 1)
            work = jnp.zeros((rows, LANES), jnp.float32)
            size = jnp.zeros((rows, LANES), jnp.float32)
            for t in range(tiles):
                at = slice(t * LANES, (t + 1) * LANES)
                here = x[j, :, at]
                previous = low if t == 0 else x[j, :, (t - 1) * LANES : t * LANES]
                following = high if t == tiles - 1 else x[j, :, (t + 1) * LANES : (t + 2) * LANES]
                halo = jnp.where(lane < LANES // 2, following, previous)
                total = jnp.dot(
                    jnp.concatenate([here, halo], 1),
                    matrix[t],
                    precision=HIGHEST,
                    preferred_element_type=jnp.float32,
                )
                total = total + (lam[j] * band[17:18, at]) * here
                stiff[j, :, at] = total
                work = work + total * here
                size = size + here * here
            energy[to, :] = work
            norm[to, :] = size
            return carry

        lax.fori_loop(0, count, slot, 0)
        ones = jnp.ones((ROWS, LANES), jnp.float32)
        for r, part in enumerate((energy, norm)):
            line = lax.dot_general(
                ones,
                part[...],
                (((1,), (1,)), ((), ())),
                precision=HIGHEST,
                preferred_element_type=jnp.float32,
            )
            sums[r : r + 1, :] = line[:1]

    vmem = pl.BlockSpec(memory_space=pltpu.VMEM)
    return pl.pallas_call(
        kernel,
        in_specs=[vmem, vmem, vmem, vmem, pl.BlockSpec(memory_space=pltpu.SMEM)],
        out_specs=[vmem, vmem],
        out_shape=[
            jax.ShapeDtypeStruct((count, rows, dofs), jnp.float32),
            jax.ShapeDtypeStruct((2, count * rows), jnp.float32),
        ],
        scratch_shapes=[
            pltpu.VMEM((count * rows, LANES), jnp.float32),
            pltpu.VMEM((count * rows, LANES), jnp.float32),
            pltpu.VMEM((tiles, 2 * LANES, LANES), jnp.float32),
        ],
        compiler_params=params(),
        name="stiffness",
    )(projected, before, after, bands, links)


def residual_back(projected, stiff, sums):
    count, rows, dofs = projected.shape
    scales = slot_scales(count)

    def kernel(x, kx, total, back, ritz, wide):
        @pl.when(pl.program_id(0) == 0)
        def _():
            value = total[0:1, :] / (total[1:2, :] + 1e-06)
            ritz[...] = value
            row = lax.broadcasted_iota(jnp.int32, (ROWS, count * rows), 0)
            first = jnp.where(row == 0, value, 0.0)
            ones = jnp.ones((ROWS, LANES), jnp.float32)
            spread_out = lax.dot_general(
                first,
                ones,
                (((0,), (0,)), ((), ())),
                precision=HIGHEST,
                preferred_element_type=jnp.float32,
            )
            wide[...] = spread_out

        def strip(r, carry):
            at = pl.ds(pl.multiple_of(r * ROWS, ROWS), ROWS)
            terms = []
            for j in range(count):
                to = pl.ds(pl.multiple_of(j * rows + r * ROWS, ROWS), ROWS)
                terms.append((kx[j, at, :] - wide[to, :] * x[j, at, :]) * scales[j])
            out = to_spans(terms)
            for s in range(count):
                back[s, at, :] = out[s]
            return carry

        lax.fori_loop(0, rows // ROWS, strip, 0)

    cell = pl.BlockSpec((count, rows, LANES), lambda t: (0, 0, t))
    return pl.pallas_call(
        kernel,
        grid=(dofs // LANES,),
        in_specs=[cell, cell, pl.BlockSpec((2, count * rows), lambda t: (0, 0))],
        out_specs=[cell, pl.BlockSpec((1, count * rows), lambda t: (0, 0))],
        out_shape=[
            pltpu.HBM((count, rows, dofs), jnp.float32),
            jax.ShapeDtypeStruct((1, count * rows), jnp.float32),
        ],
        scratch_shapes=[pltpu.VMEM((count * rows, LANES), jnp.float32)],
        compiler_params=params(),
        name="residual_back",
    )(projected, stiff, sums)


def halvings(axis):
    step = lax.axis_size(axis) // 2
    while step:
        yield step, [(i, i ^ step) for i in range(lax.axis_size(axis))]
        step //= 2


def exchange_step(held, step, pairs):
    other = lax.ppermute(held, "span", pairs)
    upper = (lax.axis_index("span") & step) != 0
    return jnp.stack([jnp.where(upper, other, held), jnp.where(upper, held, other)])


def in_order(held, steps):
    bits = [step for step, _ in steps][::-1]
    order = tuple(sorted(range(len(bits)), key=lambda d: -bits[d]))
    held = held.transpose(order + tuple(range(len(bits), held.ndim)))
    return held.reshape((-1,) + held.shape[len(bits) :])


def tiled_device(
    current_block,
    search_block,
    previous_block,
    ground_spring,
    wire_tension,
    dropper_stiff,
    dropper_offset,
    span_link,
    ritz_rotation,
):
    count = lax.axis_size("span")
    dofs = current_block.shape[2] // count
    rows = current_block.shape[1]
    steps = list(halvings("span"))
    half = count // 2
    me = lax.axis_index("span")
    upper = me >= half
    blocks = (current_block, search_block, previous_block)
    bases = jnp.stack([jnp.where(upper, 0, half * dofs), jnp.where(upper, half * dofs, 0)])
    tiles = dofs // LANES
    first = tiles * 2 // 5 * LANES
    chunks = [(0, 0, first), (0, first, dofs - first)] if first else [(0, 0, dofs)]
    rotation = ritz_rotation[0].T
    for step, pairs in steps[:2]:
        rotation = exchange_step(rotation, step, pairs)
    (pieces,) = spread_blocks(blocks, bases, dofs, half, chunks[:1])
    pieces, rotation = lax.optimization_barrier((pieces, rotation))
    arrived = [exchange_half(pieces)]
    for step, pairs in steps[2:]:
        rotation = exchange_step(rotation, step, pairs)
    rotation = in_order(rotation, steps)
    signs = [scale * sign for scale, sign in zip(slot_scales(count), half_signs(count))]
    scales = jnp.where(
        upper, jnp.array(signs, jnp.float32), jnp.array(slot_scales(count), jnp.float32)
    )
    rotation = rotation * scales[:, None, None]
    rest = spread_blocks(blocks, bases, dofs, half, chunks[1:] + [(1, 0, dofs)])
    swap = [(i, (i + half) % count) for i in range(count)]
    others = []
    for pieces in rest:
        part = project(arrived[-1], rotation)
        if others:
            part, others[-1] = lax.optimization_barrier((part, others[-1]))
        others.append(lax.ppermute(part, "span", swap))
        pieces, _ = lax.optimization_barrier((pieces, arrived[-1]))
        arrived.append(exchange_half(pieces))
    own = project(arrived[-1], rotation)
    projected, spans, head, tail = combine(own, others)
    weights, ground, link = coefficients(
        ground_spring, wire_tension, dropper_stiff, dropper_offset, span_link, count, dofs
    )
    up = weights[:, REACH:]
    down = [weights[d - 1, REACH - d : REACH - d + dofs] for d in range(1, REACH + 1)]
    down = jnp.stack(down)
    diagonal = ground + jnp.sum(up, 0) + jnp.sum(down, 0)
    bands = jnp.concatenate([up, down, diagonal[None], link[None]])
    links = 2.0 * (1.0 - fourier_rows(count)[1])
    before, after = to_next(tail, 1), to_next(head, -1)
    spans, before, after = lax.optimization_barrier((spans, before, after))
    block_pieces = exchange(spans)
    stiff, sums = stiffness(projected, before, after, bands, links)
    for _, pairs in halvings("elem"):
        sums = sums + lax.ppermute(sums, "elem", pairs)
    for _, pairs in steps[::-1]:
        sums = sums + lax.ppermute(sums, "span", pairs)
    spans, ritz = residual_back(projected, stiff, sums)
    next_block, next_residual = collect_blocks([block_pieces, exchange(spans)])
    ritz = lax.dynamic_slice_in_dim(ritz, lax.axis_index("span") * rows, rows, 1)
    return (next_block, next_residual, ritz)


def on_device(
    current_block,
    search_block,
    previous_block,
    ground_spring,
    wire_tension,
    dropper_stiff,
    dropper_offset,
    span_link,
    ritz_rotation,
):
    count = lax.axis_size("span")
    dof_dev = current_block.shape[2]
    dofs = dof_dev // count
    matrix, cosines = fourier_rows(count)
    blocks = (current_block, search_block, previous_block)
    stacked = exchange(jnp.concatenate([spread(b[0], count) for b in blocks], 1))
    rotation = lax.all_gather(ritz_rotation, "span", axis=0, tiled=True)
    weights, ground, link = coefficients(
        ground_spring, wire_tension, dropper_stiff, dropper_offset, span_link, count, dofs
    )
    slots = along_spans(matrix, stacked)
    projected = jnp.einsum("jvm,jvd->jmd", rotation, slots, precision=HIGHEST)
    back = matrix.T
    next_block = collect(exchange(along_spans(back, projected)))
    before = to_next(projected[:, :, dofs - REACH :], 1)
    after = to_next(projected[:, :, :REACH], -1)
    wide = jnp.concatenate([before, projected, after], 2)
    stiff = ground * projected
    near = wide[:, :, : REACH + dofs]
    for distance in range(1, REACH + 1):
        flux = weights[distance - 1] * (near - wide[:, :, distance : distance + REACH + dofs])
        stiff = stiff + flux[:, :, REACH:] - flux[:, :, REACH - distance : REACH - distance + dofs]
    stiff = stiff + (2.0 * (1.0 - cosines))[:, None, None] * link * projected
    sums = jnp.stack([jnp.sum(projected * stiff, 2), jnp.sum(projected * projected, 2)])
    sums = lax.psum(sums, ("elem", "span"))
    ritz = sums[0] / (sums[1] + 1e-06)
    residual = stiff - ritz[:, :, None] * projected
    next_residual = collect(exchange(along_spans(back, residual)))
    my_ritz = lax.dynamic_slice_in_dim(ritz, lax.axis_index("span"), 1, 0)
    return (next_block, next_residual, my_ritz)


def by_shape(*args):
    count, dof_dev = lax.axis_size("span"), args[0].shape[2]
    halves = count & (count - 1) == 0 and lax.axis_size("elem") in (1, 2, 4, 8, 16)
    if halves and count > 2 and dof_dev % (count * LANES) == 0:
        return tiled_device(*args)
    return on_device(*args)


def solution(mesh):
    return jax.shard_map(
        by_shape,
        mesh=mesh,
        in_specs=(
            P("span", None, "elem"),
            P("span", None, "elem"),
            P("span", None, "elem"),
            P("elem"),
            P("elem"),
            P("elem"),
            P("elem"),
            P("elem"),
            P("span", None, None),
        ),
        out_specs=(P("span", None, "elem"), P("span", None, "elem"), P("span", None)),
        check_vma=False,
    )
```

```python
import math

import jax
import jax.numpy as jnp
from jax import lax
from jax.experimental import pallas as pl
from jax.experimental.pallas import tpu as pltpu
from jax.sharding import PartitionSpec as P

REACH = 8
LANES = 128
ROWS = 8
VMEM_LIMIT = 20 * 1024 * 1024
HIGHEST = lax.Precision.HIGHEST


def fourier_rows(count):
    row = jnp.arange(count)[:, None]
    col = jnp.arange(count)[None, :]
    half = count // 2
    wave = jnp.where(row <= half, row, row - half)
    phase = (wave * col % count).astype(jnp.float32) * (2.0 * math.pi / count)
    scaled = jnp.where(row <= half, jnp.cos(phase), jnp.sin(phase)) * math.sqrt(2.0 / count)
    edge = (row == 0) | (row == half)
    matrix = jnp.where(edge, jnp.cos(phase) * math.sqrt(1.0 / count), scaled)
    slots = jnp.arange(count)
    slot_wave = jnp.where(slots <= half, slots, slots - half)
    cosines = jnp.cos(slot_wave.astype(jnp.float32) * (2.0 * math.pi / count))
    return (matrix, cosines)


def along_spans(matrix, block):
    shape = block.shape
    flat = block.reshape(shape[0], -1)
    return jnp.dot(matrix, flat, precision=HIGHEST).reshape(shape)


def spread(block, count):
    rows, dofs = block.shape
    return block.reshape(rows, count, dofs // count).transpose(1, 0, 2)


def collect(pieces):
    count, rows, dofs = pieces.shape
    return pieces.transpose(1, 0, 2).reshape(1, rows, count * dofs)


def exchange(pieces):
    return lax.all_to_all(pieces, "span", split_axis=0, concat_axis=0, tiled=True)


def to_next(cells, step):
    count, parts = lax.axis_size("span"), lax.axis_size("elem")
    line = [s * parts + e for e in range(parts) for s in range(count)]
    pairs = list(zip(line, line[1:]))
    if step < 0:
        pairs = [(b, a) for a, b in pairs]
    return lax.ppermute(cells, ("span", "elem"), pairs)


def exchange_half(pieces):
    count = lax.axis_size("span")
    half = count // 2
    groups = [list(range(half)), list(range(half, count))]
    return lax.all_to_all(
        pieces, "span", split_axis=0, concat_axis=0, tiled=True, axis_index_groups=groups
    )


def coefficients(ground, tension, stiff, offset, link, count, dofs):
    dof_dev = ground.shape[0]
    start = lax.axis_index("span") * dofs
    elem = lax.axis_index("elem")
    dof_all = dof_dev * lax.axis_size("elem")
    position = elem * dof_dev + jnp.arange(dof_dev)
    distance = jnp.arange(1, REACH + 1)[:, None]
    weights = jnp.where((offset == distance) & (position + distance < dof_all), stiff, 0.0)
    wire = jnp.where((distance == 1) & (position < dof_all - 1), tension, 0.0)
    weights = weights + wire
    pairs = [(i, i + 1) for i in range(lax.axis_size("elem") - 1)]
    left = lax.ppermute(weights[:, dof_dev - REACH :], "elem", pairs)
    weights = jnp.concatenate([left, weights], 1)
    weights = lax.dynamic_slice_in_dim(weights, start, dofs + REACH, 1)
    ground = lax.dynamic_slice_in_dim(ground, start, dofs, 0)
    link = lax.dynamic_slice_in_dim(link, start, dofs, 0)
    return weights, ground, link


def add_up(terms):
    total = terms[0]
    for term in terms[1:]:
        total = total + term
    return total


def scaled(factor, value):
    if abs(factor - 1.0) < 1e-12:
        return value
    return value * factor


def plus(a, b):
    return a if b is None else a + b


def minus(a, b):
    return a if b is None else a - b


def cosine_sums(a):
    n = len(a) - 1
    if n == 1:
        return [plus(a[0], a[1]), minus(a[0], a[1])]
    half = n // 2
    even = cosine_sums([plus(a[s], a[n - s]) for s in range(half)] + [a[half]])
    diff = [minus(a[s], a[n - s]) for s in range(half)]
    out = [None] * (n + 1)
    out[0::2] = even
    for j in range(1, n, 2):
        out[j] = add_up([scaled(math.cos(math.pi * j * s / n), diff[s]) for s in range(half)])
    return out


def sine_sums(b):
    n = len(b) + 1
    if n == 1:
        return []
    half = n // 2
    at = [None] + list(b)
    even = sine_sums([at[s] - at[n - s] for s in range(1, half)])
    total = [None] + [at[s] + at[n - s] for s in range(1, half)] + [at[half]]
    out = [None] * (n + 1)
    for k, value in enumerate(even):
        out[2 * k + 2] = value
    for j in range(1, n, 2):
        terms = [(math.sin(math.pi * j * s / n), total[s]) for s in range(1, half + 1)]
        terms = [scaled(abs(f), t) if f > 0 else -scaled(abs(f), t) for f, t in terms]
        out[j] = add_up(terms)
    return out[1:n]


def slot_scales(count):
    edge, inner = math.sqrt(1.0 / count), math.sqrt(2.0 / count)
    return [edge if j in (0, count // 2) else inner for j in range(count)]


def to_slots(x):
    return cosine_sums(list(x) + [None]) + sine_sums(x[1:])


def half_signs(count):
    half = count // 2
    return [-1.0 if (j if j <= half else j - half) % 2 else 1.0 for j in range(count)]


def to_spans(y):
    n = len(y)
    half = n // 2
    even = cosine_sums(y[: half + 1])
    odd = [None] + sine_sums(y[half + 1 :])
    out = [None] * n
    out[0], out[half] = even[0], even[half]
    for s in range(1, half):
        out[s] = even[s] + odd[s]
        out[n - s] = even[s] - odd[s]
    return out


def params(**kw):
    return pltpu.CompilerParams(vmem_limit_bytes=VMEM_LIMIT, **kw)


def spread_blocks(blocks, bases, dofs, many, cuts):
    rows = blocks[0].shape[1]
    kinds = len(blocks)

    def kernel(base, *refs):
        outs = refs[kinds : kinds + len(cuts)]
        held = refs[kinds + len(cuts) : kinds + 2 * len(cuts)]
        come, go = refs[-2:]
        arrivals = []
        for c, (which, first, width) in enumerate(cuts):
            for q in range(many):
                group = []
                for k in range(kinds):
                    start = pl.multiple_of(base[which] + (q * dofs + first), LANES)
                    copy = pltpu.make_async_copy(
                        refs[k].at[0, :, pl.ds(start, width)],
                        held[c].at[q, k * rows : (k + 1) * rows, :],
                        come.at[(c * many + q) * kinds + k],
                    )
                    copy.start()
                    group.append(copy)
                arrivals.append((c, q, group))
        leaving = []
        for c, q, group in arrivals:
            for copy in group:
                copy.wait()
            piece = pltpu.make_async_copy(held[c].at[q], outs[c].at[q], go.at[c * many + q])
            piece.start()
            leaving.append(piece)
        for piece in leaving:
            piece.wait()

    whole = pl.BlockSpec(memory_space=pltpu.HBM)
    shapes = [(many, kinds * rows, width) for _, _, width in cuts]
    return pl.pallas_call(
        kernel,
        in_specs=[pl.BlockSpec(memory_space=pltpu.SMEM)] + [whole] * kinds,
        out_specs=[whole] * len(cuts),
        out_shape=[pltpu.HBM(shape, jnp.float32) for shape in shapes],
        scratch_shapes=[pltpu.VMEM(shape, jnp.float32) for shape in shapes]
        + [
            pltpu.SemaphoreType.DMA((len(cuts) * many * kinds,)),
            pltpu.SemaphoreType.DMA((len(cuts) * many,)),
        ],
        compiler_params=pltpu.CompilerParams(vmem_limit_bytes=60 * 1024 * 1024),
        name="spread_blocks",
    )(bases, *blocks)


def collect_blocks(pieces):
    count, rows, dofs = pieces[0].shape
    many = max(n for n in (1, 2, 4, 8) if count % n == 0)
    kinds = len(pieces)

    def kernel(*refs):
        for piece, out in zip(refs[:kinds], refs[kinds:]):
            for i in range(many):
                out[0, :, i * dofs : (i + 1) * dofs] = piece[i]

    return pl.pallas_call(
        kernel,
        grid=(count // many,),
        in_specs=[pl.BlockSpec((many, rows, dofs), lambda i: (i, 0, 0))] * kinds,
        out_specs=[pl.BlockSpec((1, rows, many * dofs), lambda i: (0, 0, i))] * kinds,
        out_shape=[pltpu.HBM((1, rows, count * dofs), jnp.float32)] * kinds,
        compiler_params=params(),
        name="collect_blocks",
    )(*pieces)


PARTS = 3


def bf16_parts(value):
    parts = []
    for i in range(PARTS):
        parts.append(value.astype(jnp.bfloat16))
        if i < PARTS - 1:
            value = value - parts[i].astype(jnp.float32)
    return parts


def project(stacked, rotation):
    spans, wide, dofs = stacked.shape
    count, rows = rotation.shape[:2]
    strip = 2 * ROWS

    def kernel(x, rot, proj, split_rot, *split_slots):
        @pl.when(pl.program_id(0) == 0)
        def _():
            def one(j, carry):
                for i, part in enumerate(bf16_parts(rot[j])):
                    split_rot[j, i * rows : (i + 1) * rows, :] = part
                return carry

            lax.fori_loop(0, count, one, 0)

        def transform(r, carry):
            at = pl.ds(pl.multiple_of(r * strip, strip), strip)
            halves = []
            for h in range(2):
                own = pl.ds(pl.multiple_of(r * strip + h * ROWS, ROWS), ROWS)
                halves.append(to_slots([x[s, own, :] for s in range(spans)]))
            for j in range(count):
                value = jnp.concatenate([half[j] for half in halves], 0)
                for part, ref in zip(bf16_parts(value), split_slots):
                    ref[j, at, :] = part
            return carry

        lax.fori_loop(0, wide // strip, transform, 0)
        for j in range(count):
            total = None
            for i in range(PARTS - 1, -1, -1):
                terms = PARTS - i
                stacked_terms = jnp.dot(
                    split_rot[j, : terms * rows, :],
                    split_slots[i][j],
                    preferred_element_type=jnp.float32,
                )
                for q in range(terms - 1, -1, -1):
                    term = stacked_terms[q * rows : (q + 1) * rows]
                    total = term if total is None else total + term
            proj[j] = total

    return pl.pallas_call(
        kernel,
        grid=(dofs // LANES,),
        in_specs=[
            pl.BlockSpec((spans, wide, LANES), lambda t: (0, 0, t)),
            pl.BlockSpec((count, rows, wide), lambda t: (0, 0, 0)),
        ],
        out_specs=pl.BlockSpec((count, rows, LANES), lambda t: (0, 0, t)),
        out_shape=pltpu.HBM((count, rows, dofs), jnp.float32),
        scratch_shapes=[pltpu.VMEM((count, PARTS * rows, wide), jnp.bfloat16)]
        + [pltpu.VMEM((count, wide, LANES), jnp.bfloat16)] * PARTS,
        compiler_params=params(),
        name="project",
    )(stacked, rotation)


def combine(own, others):
    count, rows, dofs = own.shape
    tiles = dofs // LANES
    scales = slot_scales(count)
    groups = -(-count * REACH // LANES)
    per = LANES // REACH
    sizes = [other.shape[2] // LANES for other in others]
    firsts = [sum(sizes[:c]) for c in range(len(sizes))]

    def kernel(*refs):
        x, parts = refs[0], refs[1 : 1 + len(others)]
        proj, back, head, tail = refs[1 + len(others) :]
        tile = pl.program_id(0)

        def strip_of(part):
            def strip(r, carry):
                at = pl.ds(pl.multiple_of(r * ROWS, ROWS), ROWS)
                terms = []
                for j in range(count):
                    value = x[j, at, :] + part[j, at, :]
                    proj[j, at, :] = value
                    terms.append(value * scales[j])
                out = to_spans(terms)
                for s in range(count):
                    back[s, at, :] = out[s]
                return carry

            return strip

        for first, size, part in zip(firsts, sizes, parts):

            @pl.when((tile >= first) & (tile < first + size))
            def _(part=part):
                lax.fori_loop(0, rows // ROWS, strip_of(part), 0)

        lane = lax.broadcasted_iota(jnp.int32, (rows, LANES), 1)

        def pack(ref, start):
            for g in range(groups):
                packed = jnp.zeros((rows, LANES), jnp.float32)
                for k in range(min(per, count - g * per)):
                    turn = (k * REACH - start) % LANES
                    value = proj[g * per + k]
                    value = pltpu.roll(value, turn, 1) if turn else value
                    packed = jnp.where(lane // REACH == k, value, packed)
                ref[g] = packed

        @pl.when(tile == 0)
        def _():
            pack(head, 0)

        @pl.when(tile == tiles - 1)
        def _():
            pack(tail, LANES - REACH)

    def cell(first, size):
        return pl.BlockSpec(
            (count, rows, LANES), lambda t: (0, 0, jnp.clip(t - first, 0, size - 1))
        )

    plain = pl.BlockSpec((count, rows, LANES), lambda t: (0, 0, t))
    edge = pl.BlockSpec((groups, rows, LANES), lambda t: (0, 0, 0))
    edges = jax.ShapeDtypeStruct((groups, rows, LANES), jnp.float32)
    return pl.pallas_call(
        kernel,
        grid=(tiles,),
        in_specs=[plain] + [cell(f, z) for f, z in zip(firsts, sizes)],
        out_specs=[plain, plain, edge, edge],
        out_shape=[
            jax.ShapeDtypeStruct((count, rows, dofs), jnp.float32),
            pltpu.HBM((count, rows, dofs), jnp.float32),
            edges,
            edges,
        ],
        compiler_params=params(),
        name="combine",
    )(own, *others)


def stiffness(projected, before, after, bands, links):
    count, rows, dofs = projected.shape
    per = LANES // REACH
    tiles = dofs // LANES

    def kernel(x, left, right, band, lam, stiff, sums, energy, norm, matrix):
        row = lax.broadcasted_iota(jnp.int32, (LANES, LANES), 0)
        gap = row - lax.broadcasted_iota(jnp.int32, (LANES, LANES), 1)
        for t in range(tiles):
            at = slice(t * LANES, (t + 1) * LANES)
            here = jnp.where(gap == 0, band[16:17, at], 0.0)
            halo = jnp.zeros((LANES, LANES), jnp.float32)
            for d in range(1, REACH + 1):
                up, down = band[d - 1 : d, at], band[REACH + d - 1 : REACH + d, at]
                here = jnp.where(gap == d, -up, here)
                here = jnp.where(gap == -d, -down, here)
                halo = jnp.where(gap == d - LANES, -up, halo)
                halo = jnp.where(gap == LANES - d, -down, halo)
            matrix[t, :LANES, :] = here
            matrix[t, LANES:, :] = halo
        lane = lax.broadcasted_iota(jnp.int32, (rows, LANES), 1)

        def slot(j, carry):
            to = pl.ds(pl.multiple_of(j * rows, rows), rows)
            g, k = j // per, j % per
            low = pltpu.roll(left[g], (2 * LANES - REACH - REACH * k) % LANES, 1)
            high = pltpu.roll(right[g], (LANES - REACH * k) % LANES, 1)
            work = jnp.zeros((rows, LANES), jnp.float32)
            size = jnp.zeros((rows, LANES), jnp.float32)
            for t in range(tiles):
                at = slice(t * LANES, (t + 1) * LANES)
                here = x[j, :, at]
                previous = low if t == 0 else x[j, :, (t - 1) * LANES : t * LANES]
                following = high if t == tiles - 1 else x[j, :, (t + 1) * LANES : (t + 2) * LANES]
                halo = jnp.where(lane < LANES // 2, following, previous)
                total = jnp.dot(
                    jnp.concatenate([here, halo], 1),
                    matrix[t],
                    precision=HIGHEST,
                    preferred_element_type=jnp.float32,
                )
                total = total + (lam[j] * band[17:18, at]) * here
                stiff[j, :, at] = total
                work = work + total * here
                size = size + here * here
            energy[to, :] = work
            norm[to, :] = size
            return carry

        lax.fori_loop(0, count, slot, 0)
        ones = jnp.ones((ROWS, LANES), jnp.float32)
        for r, part in enumerate((energy, norm)):
            line = lax.dot_general(
                ones,
                part[...],
                (((1,), (1,)), ((), ())),
                precision=HIGHEST,
                preferred_element_type=jnp.float32,
            )
            sums[r : r + 1, :] = line[:1]

    vmem = pl.BlockSpec(memory_space=pltpu.VMEM)
    return pl.pallas_call(
        kernel,
        in_specs=[vmem, vmem, vmem, vmem, pl.BlockSpec(memory_space=pltpu.SMEM)],
        out_specs=[vmem, vmem],
        out_shape=[
            jax.ShapeDtypeStruct((count, rows, dofs), jnp.float32),
            jax.ShapeDtypeStruct((2, count * rows), jnp.float32),
        ],
        scratch_shapes=[
            pltpu.VMEM((count * rows, LANES), jnp.float32),
            pltpu.VMEM((count * rows, LANES), jnp.float32),
            pltpu.VMEM((tiles, 2 * LANES, LANES), jnp.float32),
        ],
        compiler_params=params(),
        name="stiffness",
    )(projected, before, after, bands, links)


def residual_back(projected, stiff, sums):
    count, rows, dofs = projected.shape
    scales = slot_scales(count)

    def kernel(x, kx, total, back, ritz, wide):
        @pl.when(pl.program_id(0) == 0)
        def _():
            value = total[0:1, :] / (total[1:2, :] + 1e-06)
            ritz[...] = value
            row = lax.broadcasted_iota(jnp.int32, (ROWS, count * rows), 0)
            first = jnp.where(row == 0, value, 0.0)
            ones = jnp.ones((ROWS, LANES), jnp.float32)
            spread_out = lax.dot_general(
                first,
                ones,
                (((0,), (0,)), ((), ())),
                precision=HIGHEST,
                preferred_element_type=jnp.float32,
            )
            wide[...] = spread_out

        def strip(r, carry):
            at = pl.ds(pl.multiple_of(r * ROWS, ROWS), ROWS)
            terms = []
            for j in range(count):
                to = pl.ds(pl.multiple_of(j * rows + r * ROWS, ROWS), ROWS)
                terms.append((kx[j, at, :] - wide[to, :] * x[j, at, :]) * scales[j])
            out = to_spans(terms)
            for s in range(count):
                back[s, at, :] = out[s]
            return carry

        lax.fori_loop(0, rows // ROWS, strip, 0)

    cell = pl.BlockSpec((count, rows, LANES), lambda t: (0, 0, t))
    return pl.pallas_call(
        kernel,
        grid=(dofs // LANES,),
        in_specs=[cell, cell, pl.BlockSpec((2, count * rows), lambda t: (0, 0))],
        out_specs=[cell, pl.BlockSpec((1, count * rows), lambda t: (0, 0))],
        out_shape=[
            pltpu.HBM((count, rows, dofs), jnp.float32),
            jax.ShapeDtypeStruct((1, count * rows), jnp.float32),
        ],
        scratch_shapes=[pltpu.VMEM((count * rows, LANES), jnp.float32)],
        compiler_params=params(),
        name="residual_back",
    )(projected, stiff, sums)


def halvings(axis):
    step = lax.axis_size(axis) // 2
    while step:
        yield step, [(i, i ^ step) for i in range(lax.axis_size(axis))]
        step //= 2


def exchange_step(held, step, pairs):
    other = lax.ppermute(held, "span", pairs)
    upper = (lax.axis_index("span") & step) != 0
    return jnp.stack([jnp.where(upper, other, held), jnp.where(upper, held, other)])


def in_order(held, steps):
    bits = [step for step, _ in steps][::-1]
    order = tuple(sorted(range(len(bits)), key=lambda d: -bits[d]))
    held = held.transpose(order + tuple(range(len(bits), held.ndim)))
    return held.reshape((-1,) + held.shape[len(bits) :])


def tiled_device(
    current_block,
    search_block,
    previous_block,
    ground_spring,
    wire_tension,
    dropper_stiff,
    dropper_offset,
    span_link,
    ritz_rotation,
):
    count = lax.axis_size("span")
    dofs = current_block.shape[2] // count
    rows = current_block.shape[1]
    steps = list(halvings("span"))
    half = count // 2
    me = lax.axis_index("span")
    upper = me >= half
    blocks = (current_block, search_block, previous_block)
    bases = jnp.stack([jnp.where(upper, 0, half * dofs), jnp.where(upper, half * dofs, 0)])
    tiles = dofs // LANES
    first = tiles * 2 // 5 * LANES
    chunks = [(0, 0, first), (0, first, dofs - first)] if first else [(0, 0, dofs)]
    rotation = ritz_rotation[0].T
    for step, pairs in steps[:2]:
        rotation = exchange_step(rotation, step, pairs)
    (pieces,) = spread_blocks(blocks, bases, dofs, half, chunks[:1])
    pieces, rotation = lax.optimization_barrier((pieces, rotation))
    arrived = [exchange_half(pieces)]
    for step, pairs in steps[2:]:
        rotation = exchange_step(rotation, step, pairs)
    rotation = in_order(rotation, steps)
    signs = [scale * sign for scale, sign in zip(slot_scales(count), half_signs(count))]
    scales = jnp.where(
        upper, jnp.array(signs, jnp.float32), jnp.array(slot_scales(count), jnp.float32)
    )
    rotation = rotation * scales[:, None, None]
    rest = spread_blocks(blocks, bases, dofs, half, chunks[1:] + [(1, 0, dofs)])
    swap = [(i, (i + half) % count) for i in range(count)]
    others = []
    for pieces in rest:
        part = project(arrived[-1], rotation)
        if others:
            part, others[-1] = lax.optimization_barrier((part, others[-1]))
            pieces, arrived[-1] = lax.optimization_barrier((pieces, arrived[-1]))
        else:
            pieces, part = lax.optimization_barrier((pieces, part))
        others.append(lax.ppermute(part, "span", swap))
        arrived.append(exchange_half(pieces))
    own = project(arrived[-1], rotation)
    projected, spans, head, tail = combine(own, others)
    weights, ground, link = coefficients(
        ground_spring, wire_tension, dropper_stiff, dropper_offset, span_link, count, dofs
    )
    up = weights[:, REACH:]
    down = [weights[d - 1, REACH - d : REACH - d + dofs] for d in range(1, REACH + 1)]
    down = jnp.stack(down)
    diagonal = ground + jnp.sum(up, 0) + jnp.sum(down, 0)
    bands = jnp.concatenate([up, down, diagonal[None], link[None]])
    links = 2.0 * (1.0 - fourier_rows(count)[1])
    before, after = to_next(tail, 1), to_next(head, -1)
    spans, before, after = lax.optimization_barrier((spans, before, after))
    block_pieces = exchange(spans)
    stiff, sums = stiffness(projected, before, after, bands, links)
    for _, pairs in halvings("elem"):
        sums = sums + lax.ppermute(sums, "elem", pairs)
    for _, pairs in steps[::-1]:
        sums = sums + lax.ppermute(sums, "span", pairs)
    spans, ritz = residual_back(projected, stiff, sums)
    next_block, next_residual = collect_blocks([block_pieces, exchange(spans)])
    ritz = lax.dynamic_slice_in_dim(ritz, lax.axis_index("span") * rows, rows, 1)
    return (next_block, next_residual, ritz)


def on_device(
    current_block,
    search_block,
    previous_block,
    ground_spring,
    wire_tension,
    dropper_stiff,
    dropper_offset,
    span_link,
    ritz_rotation,
):
    count = lax.axis_size("span")
    dof_dev = current_block.shape[2]
    dofs = dof_dev // count
    matrix, cosines = fourier_rows(count)
    blocks = (current_block, search_block, previous_block)
    stacked = exchange(jnp.concatenate([spread(b[0], count) for b in blocks], 1))
    rotation = lax.all_gather(ritz_rotation, "span", axis=0, tiled=True)
    weights, ground, link = coefficients(
        ground_spring, wire_tension, dropper_stiff, dropper_offset, span_link, count, dofs
    )
    slots = along_spans(matrix, stacked)
    projected = jnp.einsum("jvm,jvd->jmd", rotation, slots, precision=HIGHEST)
    back = matrix.T
    next_block = collect(exchange(along_spans(back, projected)))
    before = to_next(projected[:, :, dofs - REACH :], 1)
    after = to_next(projected[:, :, :REACH], -1)
    wide = jnp.concatenate([before, projected, after], 2)
    stiff = ground * projected
    near = wide[:, :, : REACH + dofs]
    for distance in range(1, REACH + 1):
        flux = weights[distance - 1] * (near - wide[:, :, distance : distance + REACH + dofs])
        stiff = stiff + flux[:, :, REACH:] - flux[:, :, REACH - distance : REACH - distance + dofs]
    stiff = stiff + (2.0 * (1.0 - cosines))[:, None, None] * link * projected
    sums = jnp.stack([jnp.sum(projected * stiff, 2), jnp.sum(projected * projected, 2)])
    sums = lax.psum(sums, ("elem", "span"))
    ritz = sums[0] / (sums[1] + 1e-06)
    residual = stiff - ritz[:, :, None] * projected
    next_residual = collect(exchange(along_spans(back, residual)))
    my_ritz = lax.dynamic_slice_in_dim(ritz, lax.axis_index("span"), 1, 0)
    return (next_block, next_residual, my_ritz)


def by_shape(*args):
    count, dof_dev = lax.axis_size("span"), args[0].shape[2]
    halves = count & (count - 1) == 0 and lax.axis_size("elem") in (1, 2, 4, 8, 16)
    if halves and count > 2 and dof_dev % (count * LANES) == 0:
        return tiled_device(*args)
    return on_device(*args)


def solution(mesh):
    return jax.shard_map(
        by_shape,
        mesh=mesh,
        in_specs=(
            P("span", None, "elem"),
            P("span", None, "elem"),
            P("span", None, "elem"),
            P("elem"),
            P("elem"),
            P("elem"),
            P("elem"),
            P("elem"),
            P("span", None, None),
        ),
        out_specs=(P("span", None, "elem"), P("span", None, "elem"), P("span", None)),
        check_vma=False,
    )
```

```python
import math

import jax
import jax.numpy as jnp
from jax import lax
from jax.experimental import pallas as pl
from jax.experimental.pallas import tpu as pltpu
from jax.sharding import PartitionSpec as P

REACH = 8
LANES = 128
ROWS = 8
VMEM_LIMIT = 24 * 1024 * 1024
HIGHEST = lax.Precision.HIGHEST


def fourier_rows(count):
    row = jnp.arange(count)[:, None]
    col = jnp.arange(count)[None, :]
    half = count // 2
    wave = jnp.where(row <= half, row, row - half)
    phase = (wave * col % count).astype(jnp.float32) * (2.0 * math.pi / count)
    scaled = jnp.where(row <= half, jnp.cos(phase), jnp.sin(phase)) * math.sqrt(2.0 / count)
    edge = (row == 0) | (row == half)
    matrix = jnp.where(edge, jnp.cos(phase) * math.sqrt(1.0 / count), scaled)
    slots = jnp.arange(count)
    slot_wave = jnp.where(slots <= half, slots, slots - half)
    cosines = jnp.cos(slot_wave.astype(jnp.float32) * (2.0 * math.pi / count))
    return (matrix, cosines)


def along_spans(matrix, block):
    shape = block.shape
    flat = block.reshape(shape[0], -1)
    return jnp.dot(matrix, flat, precision=HIGHEST).reshape(shape)


def spread(block, count):
    rows, dofs = block.shape
    return block.reshape(rows, count, dofs // count).transpose(1, 0, 2)


def collect(pieces):
    count, rows, dofs = pieces.shape
    return pieces.transpose(1, 0, 2).reshape(1, rows, count * dofs)


def exchange(pieces):
    return lax.all_to_all(pieces, "span", split_axis=0, concat_axis=0, tiled=True)


def to_next(cells, step):
    count, parts = lax.axis_size("span"), lax.axis_size("elem")
    line = [s * parts + e for e in range(parts) for s in range(count)]
    pairs = list(zip(line, line[1:]))
    if step < 0:
        pairs = [(b, a) for a, b in pairs]
    return lax.ppermute(cells, ("span", "elem"), pairs)


def coefficients(ground, tension, stiff, offset, link, count, dofs):
    dof_dev = ground.shape[0]
    start = lax.axis_index("span") * dofs
    elem = lax.axis_index("elem")
    dof_all = dof_dev * lax.axis_size("elem")
    position = elem * dof_dev + jnp.arange(dof_dev)
    distance = jnp.arange(1, REACH + 1)[:, None]
    weights = jnp.where((offset == distance) & (position + distance < dof_all), stiff, 0.0)
    wire = jnp.where((distance == 1) & (position < dof_all - 1), tension, 0.0)
    weights = weights + wire
    pairs = [(i, i + 1) for i in range(lax.axis_size("elem") - 1)]
    left = lax.ppermute(weights[:, dof_dev - REACH :], "elem", pairs)
    weights = jnp.concatenate([left, weights], 1)
    weights = lax.dynamic_slice_in_dim(weights, start, dofs + REACH, 1)
    ground = lax.dynamic_slice_in_dim(ground, start, dofs, 0)
    link = lax.dynamic_slice_in_dim(link, start, dofs, 0)
    return weights, ground, link


def add_up(terms):
    total = terms[0]
    for term in terms[1:]:
        total = total + term
    return total


def scaled(factor, value):
    if abs(factor - 1.0) < 1e-12:
        return value
    return value * factor


def cosine_sums(a):
    n = len(a) - 1
    if n == 1:
        return [a[0] + a[1], a[0] - a[1]]
    half = n // 2
    even = cosine_sums([a[s] + a[n - s] for s in range(half)] + [a[half]])
    diff = [a[s] - a[n - s] for s in range(half)]
    out = [None] * (n + 1)
    out[0::2] = even
    for j in range(1, n, 2):
        out[j] = add_up([scaled(math.cos(math.pi * j * s / n), diff[s]) for s in range(half)])
    return out


def sine_sums(b):
    n = len(b) + 1
    if n == 1:
        return []
    half = n // 2
    at = [None] + list(b)
    even = sine_sums([at[s] - at[n - s] for s in range(1, half)])
    total = [None] + [at[s] + at[n - s] for s in range(1, half)] + [at[half]]
    out = [None] * (n + 1)
    for k, value in enumerate(even):
        out[2 * k + 2] = value
    for j in range(1, n, 2):
        terms = [(math.sin(math.pi * j * s / n), total[s]) for s in range(1, half + 1)]
        terms = [scaled(abs(f), t) if f > 0 else -scaled(abs(f), t) for f, t in terms]
        out[j] = add_up(terms)
    return out[1:n]


def slot_scales(count):
    edge, inner = math.sqrt(1.0 / count), math.sqrt(2.0 / count)
    return [edge if j in (0, count // 2) else inner for j in range(count)]


def to_slots(x):
    n = len(x)
    half = n // 2
    plus = [x[0]] + [x[s] + x[n - s] for s in range(1, half)] + [x[half]]
    minus = [x[s] - x[n - s] for s in range(1, half)]
    return cosine_sums(plus) + sine_sums(minus)


def to_spans(y):
    n = len(y)
    half = n // 2
    even = cosine_sums(y[: half + 1])
    odd = [None] + sine_sums(y[half + 1 :])
    out = [None] * n
    out[0], out[half] = even[0], even[half]
    for s in range(1, half):
        out[s] = even[s] + odd[s]
        out[n - s] = even[s] - odd[s]
    return out


def params(**kw):
    return pltpu.CompilerParams(vmem_limit_bytes=VMEM_LIMIT, **kw)


def spread_blocks(blocks, count):
    _, rows, dof_dev = blocks[0].shape
    dofs = dof_dev // count
    kinds = len(blocks)
    cuts = 2 if rows % (2 * ROWS) == 0 else 1
    strip = rows // cuts

    def kernel(*refs):
        out, held, come, go = refs[kinds:]
        arrivals = []
        for c in range(cuts):
            for k in range(kinds):
                at = slice(c * strip, (c + 1) * strip)
                copy = pltpu.make_async_copy(
                    refs[k].at[0, at, :], held.at[k, at, :], come.at[c * kinds + k]
                )
                copy.start()
                arrivals.append((c, k, copy))
        leaving = []
        for c, k, copy in arrivals:
            copy.wait()
            for i in range(count):
                piece = pltpu.make_async_copy(
                    held.at[k, c * strip : (c + 1) * strip, i * dofs : (i + 1) * dofs],
                    out.at[i, k * rows + c * strip : k * rows + (c + 1) * strip, :],
                    go.at[(c * kinds + k) * count + i],
                )
                piece.start()
                leaving.append(piece)
        for piece in leaving:
            piece.wait()

    whole = pl.BlockSpec(memory_space=pltpu.HBM)
    return pl.pallas_call(
        kernel,
        in_specs=[whole] * kinds,
        out_specs=whole,
        out_shape=pltpu.HBM((count, kinds * rows, dofs), jnp.float32),
        scratch_shapes=[
            pltpu.VMEM((kinds, rows, dof_dev), jnp.float32),
            pltpu.SemaphoreType.DMA((cuts * kinds,)),
            pltpu.SemaphoreType.DMA((cuts * kinds * count,)),
        ],
        compiler_params=pltpu.CompilerParams(vmem_limit_bytes=60 * 1024 * 1024),
        name="spread_blocks",
    )(*blocks)


def collect_blocks(pieces):
    count, rows, dofs = pieces[0].shape
    many = max(n for n in (1, 2, 4, 8) if count % n == 0)
    kinds = len(pieces)

    def kernel(*refs):
        for piece, out in zip(refs[:kinds], refs[kinds:]):
            for i in range(many):
                out[0, :, i * dofs : (i + 1) * dofs] = piece[i]

    return pl.pallas_call(
        kernel,
        grid=(count // many,),
        in_specs=[pl.BlockSpec((many, rows, dofs), lambda i: (i, 0, 0))] * kinds,
        out_specs=[pl.BlockSpec((1, rows, many * dofs), lambda i: (0, 0, i))] * kinds,
        out_shape=[pltpu.HBM((1, rows, count * dofs), jnp.float32)] * kinds,
        compiler_params=params(),
        name="collect_blocks",
    )(*pieces)


PARTS = 3


def bf16_parts(value):
    parts = []
    for i in range(PARTS):
        parts.append(value.astype(jnp.bfloat16))
        if i < PARTS - 1:
            value = value - parts[i].astype(jnp.float32)
    return parts


def project(stacked, rotation, tiles, prior=None):
    count, wide, dofs = stacked.shape
    rows = rotation.shape[1]
    width = len(tiles) * LANES
    scales = slot_scales(count)
    groups = -(-count * REACH // LANES)
    per = LANES // REACH
    strip = 2 * ROWS

    def kernel(x, rot, *refs):
        refs = refs[2:] if prior is not None else refs
        proj, back = refs[:2]
        edges, scratch = (refs[2:4], refs[4:]) if prior is None else ((), refs[2:])
        held, split_rot, mine, sent, come, go = scratch[:6]
        split_slots = scratch[6:]
        arrivals = []
        for c, t in enumerate(tiles):
            copy = pltpu.make_async_copy(
                x.at[:, :, t * LANES : (t + 1) * LANES], held.at[c], come.at[c]
            )
            copy.start()
            arrivals.append(copy)

        def one(j, carry):
            for i, part in enumerate(bf16_parts(rot[j])):
                split_rot[j, i * rows : (i + 1) * rows, :] = part
            return carry

        lax.fori_loop(0, count, one, 0)
        for c, copy in enumerate(arrivals):
            copy.wait()

            def transform(r, carry, c=c):
                at = pl.ds(pl.multiple_of(r * strip, strip), strip)
                halves = []
                for h in range(2):
                    own = pl.ds(pl.multiple_of(r * strip + h * ROWS, ROWS), ROWS)
                    halves.append(to_slots([held[c, s, own, :] for s in range(count)]))
                for j in range(count):
                    value = jnp.concatenate([half[j] for half in halves], 0)
                    for part, ref in zip(bf16_parts(value), split_slots):
                        ref[j, at, c * LANES : (c + 1) * LANES] = part
                return carry

            lax.fori_loop(0, wide // strip, transform, 0)
        for j in range(count):
            total = None
            for i in range(PARTS - 1, -1, -1):
                terms = PARTS - i
                stacked_terms = jnp.dot(
                    split_rot[j, : terms * rows, :],
                    split_slots[i][j],
                    preferred_element_type=jnp.float32,
                )
                for q in range(terms - 1, -1, -1):
                    term = stacked_terms[q * rows : (q + 1) * rows]
                    total = term if total is None else total + term
            mine[j] = total
        leaving = []

        def leave(source, target, c, t, at):
            copy = pltpu.make_async_copy(
                source.at[:, :, c * LANES : (c + 1) * LANES],
                target.at[:, :, t * LANES : (t + 1) * LANES],
                go.at[at],
            )
            copy.start()
            leaving.append(copy)

        for c, t in enumerate(tiles):
            leave(mine, proj, c, t, c)
        for c, t in enumerate(tiles):
            lanes = slice(c * LANES, (c + 1) * LANES)

            def inverse(r, carry, lanes=lanes):
                at = pl.ds(pl.multiple_of(r * ROWS, ROWS), ROWS)
                out = to_spans([mine[j, at, lanes] * scales[j] for j in range(count)])
                for s in range(count):
                    sent[s, at, lanes] = out[s]
                return carry

            lax.fori_loop(0, rows // ROWS, inverse, 0)
            leave(sent, back, c, t, len(tiles) + c)
        lane = lax.broadcasted_iota(jnp.int32, (rows, LANES), 1)
        ends = ((0, 0), (len(tiles) - 1, LANES - REACH))
        for ref, (c, start) in zip(edges, ends):
            for g in range(groups):
                packed = jnp.zeros((rows, LANES), jnp.float32)
                for k in range(min(per, count - g * per)):
                    turn = (k * REACH - start) % LANES
                    value = mine[g * per + k, :, c * LANES : (c + 1) * LANES]
                    value = pltpu.roll(value, turn, 1) if turn else value
                    packed = jnp.where(lane // REACH == k, value, packed)
                ref[g] = packed
        for copy in leaving:
            copy.wait()

    whole = pl.BlockSpec(memory_space=pltpu.HBM)
    vmem = pl.BlockSpec(memory_space=pltpu.VMEM)
    field = pltpu.HBM((count, rows, dofs), jnp.float32)
    edge = jax.ShapeDtypeStruct((groups, rows, LANES), jnp.float32)
    first = prior is None
    return pl.pallas_call(
        kernel,
        in_specs=[whole, vmem] + ([] if first else [whole, whole]),
        out_specs=[whole, whole] + ([vmem, vmem] if first else []),
        out_shape=[field, field] + ([edge, edge] if first else []),
        input_output_aliases={} if first else {2: 0, 3: 1},
        scratch_shapes=[
            pltpu.VMEM((len(tiles), count, wide, LANES), jnp.float32),
            pltpu.VMEM((count, PARTS * rows, wide), jnp.bfloat16),
            pltpu.VMEM((count, rows, width), jnp.float32),
            pltpu.VMEM((count, rows, width), jnp.float32),
            pltpu.SemaphoreType.DMA((len(tiles),)),
            pltpu.SemaphoreType.DMA((2 * len(tiles),)),
        ]
        + [pltpu.VMEM((count, wide, width), jnp.bfloat16)] * PARTS,
        compiler_params=params(),
        name="project",
    )(stacked, rotation, *(() if first else prior))


def stiffness(projected, before, after, bands, links):
    count, rows, dofs = projected.shape
    per = LANES // REACH
    tiles = dofs // LANES

    def kernel(x, left, right, band, lam, stiff, sums, energy, norm, matrix):
        row = lax.broadcasted_iota(jnp.int32, (LANES, LANES), 0)
        gap = row - lax.broadcasted_iota(jnp.int32, (LANES, LANES), 1)
        for t in range(tiles):
            at = slice(t * LANES, (t + 1) * LANES)
            here = jnp.where(gap == 0, band[16:17, at], 0.0)
            halo = jnp.zeros((LANES, LANES), jnp.float32)
            for d in range(1, REACH + 1):
                up, down = band[d - 1 : d, at], band[REACH + d - 1 : REACH + d, at]
                here = jnp.where(gap == d, -up, here)
                here = jnp.where(gap == -d, -down, here)
                halo = jnp.where(gap == d - LANES, -up, halo)
                halo = jnp.where(gap == LANES - d, -down, halo)
            matrix[t, :LANES, :] = here
            matrix[t, LANES:, :] = halo
        lane = lax.broadcasted_iota(jnp.int32, (rows, LANES), 1)

        def slot(j, carry):
            to = pl.ds(pl.multiple_of(j * rows, rows), rows)
            g, k = j // per, j % per
            low = pltpu.roll(left[g], (2 * LANES - REACH - REACH * k) % LANES, 1)
            high = pltpu.roll(right[g], (LANES - REACH * k) % LANES, 1)
            work = jnp.zeros((rows, LANES), jnp.float32)
            size = jnp.zeros((rows, LANES), jnp.float32)
            for t in range(tiles):
                at = slice(t * LANES, (t + 1) * LANES)
                here = x[j, :, at]
                previous = low if t == 0 else x[j, :, (t - 1) * LANES : t * LANES]
                following = high if t == tiles - 1 else x[j, :, (t + 1) * LANES : (t + 2) * LANES]
                halo = jnp.where(lane < LANES // 2, following, previous)
                total = jnp.dot(
                    jnp.concatenate([here, halo], 1),
                    matrix[t],
                    precision=HIGHEST,
                    preferred_element_type=jnp.float32,
                )
                total = total + (lam[j] * band[17:18, at]) * here
                stiff[j, :, at] = total
                work = work + total * here
                size = size + here * here
            energy[to, :] = work
            norm[to, :] = size
            return carry

        lax.fori_loop(0, count, slot, 0)
        ones = jnp.ones((ROWS, LANES), jnp.float32)
        for r, part in enumerate((energy, norm)):
            line = lax.dot_general(
                ones,
                part[...],
                (((1,), (1,)), ((), ())),
                precision=HIGHEST,
                preferred_element_type=jnp.float32,
            )
            sums[r : r + 1, :] = line[:1]

    vmem = pl.BlockSpec(memory_space=pltpu.VMEM)
    return pl.pallas_call(
        kernel,
        in_specs=[vmem, vmem, vmem, vmem, pl.BlockSpec(memory_space=pltpu.SMEM)],
        out_specs=[vmem, vmem],
        out_shape=[
            jax.ShapeDtypeStruct((count, rows, dofs), jnp.float32),
            jax.ShapeDtypeStruct((2, count * rows), jnp.float32),
        ],
        scratch_shapes=[
            pltpu.VMEM((count * rows, LANES), jnp.float32),
            pltpu.VMEM((count * rows, LANES), jnp.float32),
            pltpu.VMEM((tiles, 2 * LANES, LANES), jnp.float32),
        ],
        compiler_params=params(),
        name="stiffness",
    )(projected, before, after, bands, links)


def residual_back(projected, stiff, sums):
    count, rows, dofs = projected.shape
    scales = slot_scales(count)

    def kernel(x, kx, total, back, ritz, wide):
        @pl.when(pl.program_id(0) == 0)
        def _():
            value = total[0:1, :] / (total[1:2, :] + 1e-06)
            ritz[...] = value
            row = lax.broadcasted_iota(jnp.int32, (ROWS, count * rows), 0)
            first = jnp.where(row == 0, value, 0.0)
            ones = jnp.ones((ROWS, LANES), jnp.float32)
            spread_out = lax.dot_general(
                first,
                ones,
                (((0,), (0,)), ((), ())),
                precision=HIGHEST,
                preferred_element_type=jnp.float32,
            )
            wide[...] = spread_out

        def strip(r, carry):
            at = pl.ds(pl.multiple_of(r * ROWS, ROWS), ROWS)
            terms = []
            for j in range(count):
                to = pl.ds(pl.multiple_of(j * rows + r * ROWS, ROWS), ROWS)
                terms.append((kx[j, at, :] - wide[to, :] * x[j, at, :]) * scales[j])
            out = to_spans(terms)
            for s in range(count):
                back[s, at, :] = out[s]
            return carry

        lax.fori_loop(0, rows // ROWS, strip, 0)

    cell = pl.BlockSpec((count, rows, LANES), lambda t: (0, 0, t))
    return pl.pallas_call(
        kernel,
        grid=(dofs // LANES,),
        in_specs=[cell, cell, pl.BlockSpec((2, count * rows), lambda t: (0, 0))],
        out_specs=[cell, pl.BlockSpec((1, count * rows), lambda t: (0, 0))],
        out_shape=[
            pltpu.HBM((count, rows, dofs), jnp.float32),
            jax.ShapeDtypeStruct((1, count * rows), jnp.float32),
        ],
        scratch_shapes=[pltpu.VMEM((count * rows, LANES), jnp.float32)],
        compiler_params=params(),
        name="residual_back",
    )(projected, stiff, sums)


def halvings(axis):
    step = lax.axis_size(axis) // 2
    while step:
        yield step, [(i, i ^ step) for i in range(lax.axis_size(axis))]
        step //= 2


def exchange_step(held, step, pairs):
    other = lax.ppermute(held, "span", pairs)
    upper = (lax.axis_index("span") & step) != 0
    return jnp.stack([jnp.where(upper, other, held), jnp.where(upper, held, other)])


def in_order(held, steps):
    bits = [step for step, _ in steps][::-1]
    order = tuple(sorted(range(len(bits)), key=lambda d: -bits[d]))
    held = held.transpose(order + tuple(range(len(bits), held.ndim)))
    return held.reshape((-1,) + held.shape[len(bits) :])


def tiled_device(
    current_block,
    search_block,
    previous_block,
    ground_spring,
    wire_tension,
    dropper_stiff,
    dropper_offset,
    span_link,
    ritz_rotation,
):
    count = lax.axis_size("span")
    dofs = current_block.shape[2] // count
    rows = current_block.shape[1]
    steps = list(halvings("span"))
    rotation = exchange_step(ritz_rotation[0].T, *steps[0])
    pieces = spread_blocks((current_block, search_block, previous_block), count)
    pieces, rotation = lax.optimization_barrier((pieces, rotation))
    stacked = exchange(pieces)
    order = steps[2:] + steps[1:2]
    for step, pairs in order:
        rotation = exchange_step(rotation, step, pairs)
    rotation = in_order(rotation, [steps[0]] + order)
    scales = jnp.array(slot_scales(count), jnp.float32)[:, None, None]
    weights, ground, link = coefficients(
        ground_spring, wire_tension, dropper_stiff, dropper_offset, span_link, count, dofs
    )
    up = weights[:, REACH:]
    down = [weights[d - 1, REACH - d : REACH - d + dofs] for d in range(1, REACH + 1)]
    down = jnp.stack(down)
    diagonal = ground + jnp.sum(up, 0) + jnp.sum(down, 0)
    bands = jnp.concatenate([up, down, diagonal[None], link[None]])
    links = 2.0 * (1.0 - fourier_rows(count)[1])
    rotation = rotation * scales
    tiles = list(range(dofs // LANES))
    outer, inner = sorted({0, tiles[-1]}), tiles[1:-1]
    projected, spans, head, tail = project(stacked, rotation, outer)
    if inner:
        projected, spans = project(stacked, rotation, inner, (projected, spans))
    before, after = to_next(tail, 1), to_next(head, -1)
    spans, before, after = lax.optimization_barrier((spans, before, after))
    block_pieces = exchange(spans)
    stiff, sums = stiffness(projected, before, after, bands, links)
    for _, pairs in halvings("elem"):
        sums = sums + lax.ppermute(sums, "elem", pairs)
    for _, pairs in steps[::-1]:
        sums = sums + lax.ppermute(sums, "span", pairs)
    spans, ritz = residual_back(projected, stiff, sums)
    (next_block,) = collect_blocks([block_pieces])
    (next_residual,) = collect_blocks([exchange(spans)])
    ritz = lax.dynamic_slice_in_dim(ritz, lax.axis_index("span") * rows, rows, 1)
    return (next_block, next_residual, ritz)


def on_device(
    current_block,
    search_block,
    previous_block,
    ground_spring,
    wire_tension,
    dropper_stiff,
    dropper_offset,
    span_link,
    ritz_rotation,
):
    count = lax.axis_size("span")
    dof_dev = current_block.shape[2]
    dofs = dof_dev // count
    matrix, cosines = fourier_rows(count)
    blocks = (current_block, search_block, previous_block)
    stacked = exchange(jnp.concatenate([spread(b[0], count) for b in blocks], 1))
    rotation = lax.all_gather(ritz_rotation, "span", axis=0, tiled=True)
    weights, ground, link = coefficients(
        ground_spring, wire_tension, dropper_stiff, dropper_offset, span_link, count, dofs
    )
    slots = along_spans(matrix, stacked)
    projected = jnp.einsum("jvm,jvd->jmd", rotation, slots, precision=HIGHEST)
    back = matrix.T
    next_block = collect(exchange(along_spans(back, projected)))
    before = to_next(projected[:, :, dofs - REACH :], 1)
    after = to_next(projected[:, :, :REACH], -1)
    wide = jnp.concatenate([before, projected, after], 2)
    stiff = ground * projected
    near = wide[:, :, : REACH + dofs]
    for distance in range(1, REACH + 1):
        flux = weights[distance - 1] * (near - wide[:, :, distance : distance + REACH + dofs])
        stiff = stiff + flux[:, :, REACH:] - flux[:, :, REACH - distance : REACH - distance + dofs]
    stiff = stiff + (2.0 * (1.0 - cosines))[:, None, None] * link * projected
    sums = jnp.stack([jnp.sum(projected * stiff, 2), jnp.sum(projected * projected, 2)])
    sums = lax.psum(sums, ("elem", "span"))
    ritz = sums[0] / (sums[1] + 1e-06)
    residual = stiff - ritz[:, :, None] * projected
    next_residual = collect(exchange(along_spans(back, residual)))
    my_ritz = lax.dynamic_slice_in_dim(ritz, lax.axis_index("span"), 1, 0)
    return (next_block, next_residual, my_ritz)


def by_shape(*args):
    count, dof_dev = lax.axis_size("span"), args[0].shape[2]
    halves = count & (count - 1) == 0 and lax.axis_size("elem") in (1, 2, 4, 8, 16)
    if halves and count > 1 and dof_dev % (count * LANES) == 0:
        return tiled_device(*args)
    return on_device(*args)


def solution(mesh):
    return jax.shard_map(
        by_shape,
        mesh=mesh,
        in_specs=(
            P("span", None, "elem"),
            P("span", None, "elem"),
            P("span", None, "elem"),
            P("elem"),
            P("elem"),
            P("elem"),
            P("elem"),
            P("elem"),
            P("span", None, None),
        ),
        out_specs=(P("span", None, "elem"), P("span", None, "elem"), P("span", None)),
        check_vma=False,
    )
```

```python
import math

import jax
import jax.numpy as jnp
from jax import lax
from jax.experimental import pallas as pl
from jax.experimental.pallas import tpu as pltpu
from jax.sharding import PartitionSpec as P

REACH = 8
LANES = 128
ROWS = 8
VMEM_LIMIT = 24 * 1024 * 1024
HIGHEST = lax.Precision.HIGHEST


def fourier_rows(count):
    row = jnp.arange(count)[:, None]
    col = jnp.arange(count)[None, :]
    half = count // 2
    wave = jnp.where(row <= half, row, row - half)
    phase = (wave * col % count).astype(jnp.float32) * (2.0 * math.pi / count)
    scaled = jnp.where(row <= half, jnp.cos(phase), jnp.sin(phase)) * math.sqrt(2.0 / count)
    edge = (row == 0) | (row == half)
    matrix = jnp.where(edge, jnp.cos(phase) * math.sqrt(1.0 / count), scaled)
    slots = jnp.arange(count)
    slot_wave = jnp.where(slots <= half, slots, slots - half)
    cosines = jnp.cos(slot_wave.astype(jnp.float32) * (2.0 * math.pi / count))
    return (matrix, cosines)


def along_spans(matrix, block):
    shape = block.shape
    flat = block.reshape(shape[0], -1)
    return jnp.dot(matrix, flat, precision=HIGHEST).reshape(shape)


def spread(block, count):
    rows, dofs = block.shape
    return block.reshape(rows, count, dofs // count).transpose(1, 0, 2)


def collect(pieces):
    count, rows, dofs = pieces.shape
    return pieces.transpose(1, 0, 2).reshape(1, rows, count * dofs)


def exchange(pieces):
    return lax.all_to_all(pieces, "span", split_axis=0, concat_axis=0, tiled=True)


def to_next(cells, step):
    count, parts = lax.axis_size("span"), lax.axis_size("elem")
    line = [s * parts + e for e in range(parts) for s in range(count)]
    pairs = list(zip(line, line[1:]))
    if step < 0:
        pairs = [(b, a) for a, b in pairs]
    return lax.ppermute(cells, ("span", "elem"), pairs)


def coefficients(ground, tension, stiff, offset, link, count, dofs):
    dof_dev = ground.shape[0]
    start = lax.axis_index("span") * dofs
    elem = lax.axis_index("elem")
    dof_all = dof_dev * lax.axis_size("elem")
    position = elem * dof_dev + jnp.arange(dof_dev)
    distance = jnp.arange(1, REACH + 1)[:, None]
    weights = jnp.where((offset == distance) & (position + distance < dof_all), stiff, 0.0)
    wire = jnp.where((distance == 1) & (position < dof_all - 1), tension, 0.0)
    weights = weights + wire
    pairs = [(i, i + 1) for i in range(lax.axis_size("elem") - 1)]
    left = lax.ppermute(weights[:, dof_dev - REACH :], "elem", pairs)
    weights = jnp.concatenate([left, weights], 1)
    weights = lax.dynamic_slice_in_dim(weights, start, dofs + REACH, 1)
    ground = lax.dynamic_slice_in_dim(ground, start, dofs, 0)
    link = lax.dynamic_slice_in_dim(link, start, dofs, 0)
    return weights, ground, link


def add_up(terms):
    total = terms[0]
    for term in terms[1:]:
        total = total + term
    return total


def scaled(factor, value):
    if abs(factor - 1.0) < 1e-12:
        return value
    return value * factor


def cosine_sums(a):
    n = len(a) - 1
    if n == 1:
        return [a[0] + a[1], a[0] - a[1]]
    half = n // 2
    even = cosine_sums([a[s] + a[n - s] for s in range(half)] + [a[half]])
    diff = [a[s] - a[n - s] for s in range(half)]
    out = [None] * (n + 1)
    out[0::2] = even
    for j in range(1, n, 2):
        out[j] = add_up([scaled(math.cos(math.pi * j * s / n), diff[s]) for s in range(half)])
    return out


def sine_sums(b):
    n = len(b) + 1
    if n == 1:
        return []
    half = n // 2
    at = [None] + list(b)
    even = sine_sums([at[s] - at[n - s] for s in range(1, half)])
    total = [None] + [at[s] + at[n - s] for s in range(1, half)] + [at[half]]
    out = [None] * (n + 1)
    for k, value in enumerate(even):
        out[2 * k + 2] = value
    for j in range(1, n, 2):
        terms = [(math.sin(math.pi * j * s / n), total[s]) for s in range(1, half + 1)]
        terms = [scaled(abs(f), t) if f > 0 else -scaled(abs(f), t) for f, t in terms]
        out[j] = add_up(terms)
    return out[1:n]


def slot_scales(count):
    edge, inner = math.sqrt(1.0 / count), math.sqrt(2.0 / count)
    return [edge if j in (0, count // 2) else inner for j in range(count)]


def to_slots(x):
    n = len(x)
    half = n // 2
    plus = [x[0]] + [x[s] + x[n - s] for s in range(1, half)] + [x[half]]
    minus = [x[s] - x[n - s] for s in range(1, half)]
    return cosine_sums(plus) + sine_sums(minus)


def to_spans(y):
    n = len(y)
    half = n // 2
    even = cosine_sums(y[: half + 1])
    odd = [None] + sine_sums(y[half + 1 :])
    out = [None] * n
    out[0], out[half] = even[0], even[half]
    for s in range(1, half):
        out[s] = even[s] + odd[s]
        out[n - s] = even[s] - odd[s]
    return out


def params(**kw):
    return pltpu.CompilerParams(vmem_limit_bytes=VMEM_LIMIT, **kw)


def spread_blocks(blocks, count, ranges):
    _, rows, dof_dev = blocks[0].shape
    dofs = dof_dev // count
    kinds = len(blocks)
    shape = (count, kinds * rows, sum(width for _, width in ranges))
    many = kinds * len(ranges)

    def kernel(*refs):
        out, held, come, go = refs[kinds:]
        arrivals = []
        for i in range(count):
            group, to = [], 0
            for first, width in ranges:
                for k in range(kinds):
                    copy = pltpu.make_async_copy(
                        refs[k].at[0, :, i * dofs + first : i * dofs + first + width],
                        held.at[i, k * rows : (k + 1) * rows, to : to + width],
                        come.at[i * many + len(group)],
                    )
                    copy.start()
                    group.append(copy)
                to += width
            arrivals.append(group)
        leaving = []
        for i, group in enumerate(arrivals):
            for copy in group:
                copy.wait()
            piece = pltpu.make_async_copy(held.at[i], out.at[i], go.at[i])
            piece.start()
            leaving.append(piece)
        for piece in leaving:
            piece.wait()

    whole = pl.BlockSpec(memory_space=pltpu.HBM)
    return pl.pallas_call(
        kernel,
        in_specs=[whole] * kinds,
        out_specs=whole,
        out_shape=pltpu.HBM(shape, jnp.float32),
        scratch_shapes=[
            pltpu.VMEM(shape, jnp.float32),
            pltpu.SemaphoreType.DMA((count * many,)),
            pltpu.SemaphoreType.DMA((count,)),
        ],
        compiler_params=pltpu.CompilerParams(vmem_limit_bytes=60 * 1024 * 1024),
        name="spread_blocks",
    )(*blocks)


def collect_blocks(early, late, middle):
    count, rows, early_width = early.shape
    dofs = early_width + LANES
    many = max(n for n in (1, 2, 4, 8) if count % n == 0)

    def kernel(first, last, block, residual):
        for i in range(many):
            at = i * dofs
            block[0, :, at : at + middle] = first[i, :, :middle]
            block[0, :, at + middle : at + middle + LANES] = last[i, :, dofs:]
            block[0, :, at + middle + LANES : at + dofs] = first[i, :, middle:]
            residual[0, :, at : at + dofs] = last[i, :, :dofs]

    return pl.pallas_call(
        kernel,
        grid=(count // many,),
        in_specs=[
            pl.BlockSpec((many, rows, early_width), lambda i: (i, 0, 0)),
            pl.BlockSpec((many, rows, dofs + LANES), lambda i: (i, 0, 0)),
        ],
        out_specs=[pl.BlockSpec((1, rows, many * dofs), lambda i: (0, 0, i))] * 2,
        out_shape=[pltpu.HBM((1, rows, count * dofs), jnp.float32)] * 2,
        compiler_params=params(),
        name="collect_blocks",
    )(early, late)


PARTS = 3


def bf16_parts(value):
    parts = []
    for i in range(PARTS):
        parts.append(value.astype(jnp.bfloat16))
        if i < PARTS - 1:
            value = value - parts[i].astype(jnp.float32)
    return parts


def project(stacked, rotation, dofs, tiles, prior=None):
    count, wide, _ = stacked.shape
    rows = rotation.shape[1]
    width = len(tiles) * LANES
    scales = slot_scales(count)
    groups = -(-count * REACH // LANES)
    per = LANES // REACH
    strip = 2 * ROWS

    def kernel(x, rot, *refs):
        refs = refs[1:] if prior is not None else refs
        proj, back = refs[:2]
        edges, scratch = (refs[2:4], refs[4:]) if prior is None else ((), refs[2:])
        held, split_rot, mine, sent, come, go = scratch[:6]
        split_slots = scratch[6:]
        arrivals = []
        for c in range(len(tiles)):
            copy = pltpu.make_async_copy(
                x.at[:, :, c * LANES : (c + 1) * LANES], held.at[c], come.at[c]
            )
            copy.start()
            arrivals.append(copy)

        def one(j, carry):
            for i, part in enumerate(bf16_parts(rot[j])):
                split_rot[j, i * rows : (i + 1) * rows, :] = part
            return carry

        lax.fori_loop(0, count, one, 0)
        for c, copy in enumerate(arrivals):
            copy.wait()

            def transform(r, carry, c=c):
                at = pl.ds(pl.multiple_of(r * strip, strip), strip)
                halves = []
                for h in range(2):
                    own = pl.ds(pl.multiple_of(r * strip + h * ROWS, ROWS), ROWS)
                    halves.append(to_slots([held[c, s, own, :] for s in range(count)]))
                for j in range(count):
                    value = jnp.concatenate([half[j] for half in halves], 0)
                    for part, ref in zip(bf16_parts(value), split_slots):
                        ref[j, at, c * LANES : (c + 1) * LANES] = part
                return carry

            lax.fori_loop(0, wide // strip, transform, 0)
        for j in range(count):
            total = None
            for i in range(PARTS - 1, -1, -1):
                terms = PARTS - i
                stacked_terms = jnp.dot(
                    split_rot[j, : terms * rows, :],
                    split_slots[i][j],
                    preferred_element_type=jnp.float32,
                )
                for q in range(terms - 1, -1, -1):
                    term = stacked_terms[q * rows : (q + 1) * rows]
                    total = term if total is None else total + term
            mine[j] = total
        leaving = []

        def leave(source, target, c, t, at):
            copy = pltpu.make_async_copy(
                source.at[:, :, c * LANES : (c + 1) * LANES],
                target.at[:, :, t * LANES : (t + 1) * LANES],
                go.at[at],
            )
            copy.start()
            leaving.append(copy)

        for c, t in enumerate(tiles):
            leave(mine, proj, c, t, c)
        for c in range(len(tiles)):
            lanes = slice(c * LANES, (c + 1) * LANES)

            def inverse(r, carry, lanes=lanes):
                at = pl.ds(pl.multiple_of(r * ROWS, ROWS), ROWS)
                out = to_spans([mine[j, at, lanes] * scales[j] for j in range(count)])
                for s in range(count):
                    sent[s, at, lanes] = out[s]
                return carry

            lax.fori_loop(0, rows // ROWS, inverse, 0)
            leave(sent, back, c, c, len(tiles) + c)
        lane = lax.broadcasted_iota(jnp.int32, (rows, LANES), 1)
        ends = ((0, 0), (len(tiles) - 1, LANES - REACH))
        for ref, (c, start) in zip(edges, ends):
            for g in range(groups):
                packed = jnp.zeros((rows, LANES), jnp.float32)
                for k in range(min(per, count - g * per)):
                    turn = (k * REACH - start) % LANES
                    value = mine[g * per + k, :, c * LANES : (c + 1) * LANES]
                    value = pltpu.roll(value, turn, 1) if turn else value
                    packed = jnp.where(lane // REACH == k, value, packed)
                ref[g] = packed
        for copy in leaving:
            copy.wait()

    whole = pl.BlockSpec(memory_space=pltpu.HBM)
    vmem = pl.BlockSpec(memory_space=pltpu.VMEM)
    field = pltpu.HBM((count, rows, dofs), jnp.float32)
    edge = jax.ShapeDtypeStruct((groups, rows, LANES), jnp.float32)
    sending = pltpu.HBM((count, rows, width), jnp.float32)
    first = prior is None
    passes = PARTS * (PARTS + 1) // 2
    cost = pl.CostEstimate(
        flops=2 * passes * count * wide * rows * width,
        bytes_accessed=4 * count * (wide + 2 * rows) * width,
        transcendentals=0,
    )
    return pl.pallas_call(
        kernel,
        in_specs=[whole, vmem] + ([] if first else [whole]),
        out_specs=[whole, whole] + ([vmem, vmem] if first else []),
        out_shape=[field, sending] + ([edge, edge] if first else []),
        input_output_aliases={} if first else {2: 0},
        cost_estimate=cost,
        scratch_shapes=[
            pltpu.VMEM((len(tiles), count, wide, LANES), jnp.float32),
            pltpu.VMEM((count, PARTS * rows, wide), jnp.bfloat16),
            pltpu.VMEM((count, rows, width), jnp.float32),
            pltpu.VMEM((count, rows, width), jnp.float32),
            pltpu.SemaphoreType.DMA((len(tiles),)),
            pltpu.SemaphoreType.DMA((2 * len(tiles),)),
        ]
        + [pltpu.VMEM((count, wide, width), jnp.bfloat16)] * PARTS,
        compiler_params=params(),
        name="project",
    )(stacked, rotation, *(() if first else (prior,)))


def stiffness(projected, before, after, bands, links):
    count, rows, dofs = projected.shape
    per = LANES // REACH
    tiles = dofs // LANES

    def kernel(x, left, right, band, lam, stiff, sums, energy, norm, matrix):
        row = lax.broadcasted_iota(jnp.int32, (LANES, LANES), 0)
        gap = row - lax.broadcasted_iota(jnp.int32, (LANES, LANES), 1)
        for t in range(tiles):
            at = slice(t * LANES, (t + 1) * LANES)
            here = jnp.where(gap == 0, band[16:17, at], 0.0)
            halo = jnp.zeros((LANES, LANES), jnp.float32)
            for d in range(1, REACH + 1):
                up, down = band[d - 1 : d, at], band[REACH + d - 1 : REACH + d, at]
                here = jnp.where(gap == d, -up, here)
                here = jnp.where(gap == -d, -down, here)
                halo = jnp.where(gap == d - LANES, -up, halo)
                halo = jnp.where(gap == LANES - d, -down, halo)
            matrix[t, :LANES, :] = here
            matrix[t, LANES:, :] = halo
        lane = lax.broadcasted_iota(jnp.int32, (rows, LANES), 1)

        def slot(j, carry):
            to = pl.ds(pl.multiple_of(j * rows, rows), rows)
            g, k = j // per, j % per
            low = pltpu.roll(left[g], (2 * LANES - REACH - REACH * k) % LANES, 1)
            high = pltpu.roll(right[g], (LANES - REACH * k) % LANES, 1)
            work = jnp.zeros((rows, LANES), jnp.float32)
            size = jnp.zeros((rows, LANES), jnp.float32)
            for t in range(tiles):
                at = slice(t * LANES, (t + 1) * LANES)
                here = x[j, :, at]
                previous = low if t == 0 else x[j, :, (t - 1) * LANES : t * LANES]
                following = high if t == tiles - 1 else x[j, :, (t + 1) * LANES : (t + 2) * LANES]
                halo = jnp.where(lane < LANES // 2, following, previous)
                total = jnp.dot(
                    jnp.concatenate([here, halo], 1),
                    matrix[t],
                    precision=HIGHEST,
                    preferred_element_type=jnp.float32,
                )
                total = total + (lam[j] * band[17:18, at]) * here
                stiff[j, :, at] = total
                work = work + total * here
                size = size + here * here
            energy[to, :] = work
            norm[to, :] = size
            return carry

        lax.fori_loop(0, count, slot, 0)
        ones = jnp.ones((ROWS, LANES), jnp.float32)
        for r, part in enumerate((energy, norm)):
            line = lax.dot_general(
                ones,
                part[...],
                (((1,), (1,)), ((), ())),
                precision=HIGHEST,
                preferred_element_type=jnp.float32,
            )
            sums[r : r + 1, :] = line[:1]

    vmem = pl.BlockSpec(memory_space=pltpu.VMEM)
    return pl.pallas_call(
        kernel,
        in_specs=[vmem, vmem, vmem, vmem, pl.BlockSpec(memory_space=pltpu.SMEM)],
        out_specs=[vmem, vmem],
        out_shape=[
            jax.ShapeDtypeStruct((count, rows, dofs), jnp.float32),
            jax.ShapeDtypeStruct((2, count * rows), jnp.float32),
        ],
        scratch_shapes=[
            pltpu.VMEM((count * rows, LANES), jnp.float32),
            pltpu.VMEM((count * rows, LANES), jnp.float32),
            pltpu.VMEM((tiles, 2 * LANES, LANES), jnp.float32),
        ],
        compiler_params=params(),
        name="stiffness",
    )(projected, before, after, bands, links)


def residual_back(projected, stiff, sums, late):
    count, rows, dofs = projected.shape
    scales = slot_scales(count)

    tiles = dofs // LANES

    def kernel(x, kx, total, extra, back, ritz, wide):
        @pl.when(pl.program_id(0) == 0)
        def _():
            value = total[0:1, :] / (total[1:2, :] + 1e-06)
            ritz[...] = value
            row = lax.broadcasted_iota(jnp.int32, (ROWS, count * rows), 0)
            first = jnp.where(row == 0, value, 0.0)
            ones = jnp.ones((ROWS, LANES), jnp.float32)
            spread_out = lax.dot_general(
                first,
                ones,
                (((0,), (0,)), ((), ())),
                precision=HIGHEST,
                preferred_element_type=jnp.float32,
            )
            wide[...] = spread_out

        def strip(r, carry):
            at = pl.ds(pl.multiple_of(r * ROWS, ROWS), ROWS)
            terms = []
            for j in range(count):
                to = pl.ds(pl.multiple_of(j * rows + r * ROWS, ROWS), ROWS)
                terms.append((kx[j, at, :] - wide[to, :] * x[j, at, :]) * scales[j])
            out = to_spans(terms)
            for s in range(count):
                back[s, at, :] = out[s]
            return carry

        @pl.when(pl.program_id(0) < tiles)
        def _():
            lax.fori_loop(0, rows // ROWS, strip, 0)

        @pl.when(pl.program_id(0) == tiles)
        def _():
            back[...] = extra[...]

    inner = pl.BlockSpec((count, rows, LANES), lambda t: (0, 0, jnp.minimum(t, tiles - 1)))
    cell = pl.BlockSpec((count, rows, LANES), lambda t: (0, 0, t))
    return pl.pallas_call(
        kernel,
        grid=(tiles + 1,),
        in_specs=[
            inner,
            inner,
            pl.BlockSpec((2, count * rows), lambda t: (0, 0)),
            pl.BlockSpec((count, rows, LANES), lambda t: (0, 0, 0)),
        ],
        out_specs=[cell, pl.BlockSpec((1, count * rows), lambda t: (0, 0))],
        out_shape=[
            pltpu.HBM((count, rows, dofs + LANES), jnp.float32),
            jax.ShapeDtypeStruct((1, count * rows), jnp.float32),
        ],
        scratch_shapes=[pltpu.VMEM((count * rows, LANES), jnp.float32)],
        compiler_params=params(),
        name="residual_back",
    )(projected, stiff, sums, late)


def halvings(axis):
    step = lax.axis_size(axis) // 2
    while step:
        yield step, [(i, i ^ step) for i in range(lax.axis_size(axis))]
        step //= 2


def exchange_step(held, step, pairs):
    other = lax.ppermute(held, "span", pairs)
    upper = (lax.axis_index("span") & step) != 0
    return jnp.stack([jnp.where(upper, other, held), jnp.where(upper, held, other)])


def in_order(held, steps):
    bits = [step for step, _ in steps][::-1]
    order = tuple(sorted(range(len(bits)), key=lambda d: -bits[d]))
    held = held.transpose(order + tuple(range(len(bits), held.ndim)))
    return held.reshape((-1,) + held.shape[len(bits) :])


def tiled_device(
    current_block,
    search_block,
    previous_block,
    ground_spring,
    wire_tension,
    dropper_stiff,
    dropper_offset,
    span_link,
    ritz_rotation,
):
    count = lax.axis_size("span")
    dofs = current_block.shape[2] // count
    rows = current_block.shape[1]
    steps = list(halvings("span"))
    tiles = list(range(dofs // LANES))
    middle = tiles[len(tiles) // 2]
    early = [t for t in tiles if t != middle]
    at = middle * LANES
    blocks = (current_block, search_block, previous_block)
    rotation = exchange_step(ritz_rotation[0].T, *steps[0])
    pieces = spread_blocks(blocks, count, [(0, at), (at + LANES, dofs - at - LANES)])
    pieces, rotation = lax.optimization_barrier((pieces, rotation))
    stacked = exchange(pieces)
    order = steps[2:] + steps[1:2]
    for step, pairs in order:
        rotation = exchange_step(rotation, step, pairs)
    rotation = in_order(rotation, [steps[0]] + order)
    scales = jnp.array(slot_scales(count), jnp.float32)[:, None, None]
    rotation = rotation * scales
    pieces = spread_blocks(blocks, count, [(at, LANES)])
    pieces, rotation = lax.optimization_barrier((pieces, rotation))
    stacked_late = exchange(pieces)
    weights, ground, link = coefficients(
        ground_spring, wire_tension, dropper_stiff, dropper_offset, span_link, count, dofs
    )
    up = weights[:, REACH:]
    down = [weights[d - 1, REACH - d : REACH - d + dofs] for d in range(1, REACH + 1)]
    down = jnp.stack(down)
    diagonal = ground + jnp.sum(up, 0) + jnp.sum(down, 0)
    bands = jnp.concatenate([up, down, diagonal[None], link[None]])
    links = 2.0 * (1.0 - fourier_rows(count)[1])
    projected, spans, head, tail = project(stacked, rotation, dofs, early)
    before, after = to_next(tail, 1), to_next(head, -1)
    spans, before, after = lax.optimization_barrier((spans, before, after))
    early_pieces = exchange(spans)
    projected, late = project(stacked_late, rotation, dofs, [middle], projected)
    stiff, sums = stiffness(projected, before, after, bands, links)
    for _, pairs in halvings("elem"):
        sums = sums + lax.ppermute(sums, "elem", pairs)
    for _, pairs in steps[::-1]:
        sums = sums + lax.ppermute(sums, "span", pairs)
    spans, ritz = residual_back(projected, stiff, sums, late)
    next_block, next_residual = collect_blocks(early_pieces, exchange(spans), at)
    ritz = lax.dynamic_slice_in_dim(ritz, lax.axis_index("span") * rows, rows, 1)
    return (next_block, next_residual, ritz)


def on_device(
    current_block,
    search_block,
    previous_block,
    ground_spring,
    wire_tension,
    dropper_stiff,
    dropper_offset,
    span_link,
    ritz_rotation,
):
    count = lax.axis_size("span")
    dof_dev = current_block.shape[2]
    dofs = dof_dev // count
    matrix, cosines = fourier_rows(count)
    blocks = (current_block, search_block, previous_block)
    stacked = exchange(jnp.concatenate([spread(b[0], count) for b in blocks], 1))
    rotation = lax.all_gather(ritz_rotation, "span", axis=0, tiled=True)
    weights, ground, link = coefficients(
        ground_spring, wire_tension, dropper_stiff, dropper_offset, span_link, count, dofs
    )
    slots = along_spans(matrix, stacked)
    projected = jnp.einsum("jvm,jvd->jmd", rotation, slots, precision=HIGHEST)
    back = matrix.T
    next_block = collect(exchange(along_spans(back, projected)))
    before = to_next(projected[:, :, dofs - REACH :], 1)
    after = to_next(projected[:, :, :REACH], -1)
    wide = jnp.concatenate([before, projected, after], 2)
    stiff = ground * projected
    near = wide[:, :, : REACH + dofs]
    for distance in range(1, REACH + 1):
        flux = weights[distance - 1] * (near - wide[:, :, distance : distance + REACH + dofs])
        stiff = stiff + flux[:, :, REACH:] - flux[:, :, REACH - distance : REACH - distance + dofs]
    stiff = stiff + (2.0 * (1.0 - cosines))[:, None, None] * link * projected
    sums = jnp.stack([jnp.sum(projected * stiff, 2), jnp.sum(projected * projected, 2)])
    sums = lax.psum(sums, ("elem", "span"))
    ritz = sums[0] / (sums[1] + 1e-06)
    residual = stiff - ritz[:, :, None] * projected
    next_residual = collect(exchange(along_spans(back, residual)))
    my_ritz = lax.dynamic_slice_in_dim(ritz, lax.axis_index("span"), 1, 0)
    return (next_block, next_residual, my_ritz)


def by_shape(*args):
    count, dof_dev = lax.axis_size("span"), args[0].shape[2]
    halves = count & (count - 1) == 0 and lax.axis_size("elem") in (1, 2, 4, 8, 16)
    if halves and count > 2 and dof_dev % (count * LANES) == 0 and dof_dev > 2 * count * LANES:
        return tiled_device(*args)
    return on_device(*args)


def solution(mesh):
    return jax.shard_map(
        by_shape,
        mesh=mesh,
        in_specs=(
            P("span", None, "elem"),
            P("span", None, "elem"),
            P("span", None, "elem"),
            P("elem"),
            P("elem"),
            P("elem"),
            P("elem"),
            P("elem"),
            P("span", None, None),
        ),
        out_specs=(P("span", None, "elem"), P("span", None, "elem"), P("span", None)),
        check_vma=False,
    )
```

```python
import math

import jax
import jax.numpy as jnp
from jax import lax
from jax.experimental import pallas as pl
from jax.experimental.pallas import tpu as pltpu
from jax.sharding import PartitionSpec as P

REACH = 8
LANES = 128
ROWS = 8
VMEM_LIMIT = 24 * 1024 * 1024
HIGHEST = lax.Precision.HIGHEST


def fourier_rows(count):
    row = jnp.arange(count)[:, None]
    col = jnp.arange(count)[None, :]
    half = count // 2
    wave = jnp.where(row <= half, row, row - half)
    phase = (wave * col % count).astype(jnp.float32) * (2.0 * math.pi / count)
    scaled = jnp.where(row <= half, jnp.cos(phase), jnp.sin(phase)) * math.sqrt(2.0 / count)
    edge = (row == 0) | (row == half)
    matrix = jnp.where(edge, jnp.cos(phase) * math.sqrt(1.0 / count), scaled)
    slots = jnp.arange(count)
    slot_wave = jnp.where(slots <= half, slots, slots - half)
    cosines = jnp.cos(slot_wave.astype(jnp.float32) * (2.0 * math.pi / count))
    return (matrix, cosines)


def along_spans(matrix, block):
    shape = block.shape
    flat = block.reshape(shape[0], -1)
    return jnp.dot(matrix, flat, precision=HIGHEST).reshape(shape)


def spread(block, count):
    rows, dofs = block.shape
    return block.reshape(rows, count, dofs // count).transpose(1, 0, 2)


def collect(pieces):
    count, rows, dofs = pieces.shape
    return pieces.transpose(1, 0, 2).reshape(1, rows, count * dofs)


def exchange(pieces):
    return lax.all_to_all(pieces, "span", split_axis=0, concat_axis=0, tiled=True)


def to_next(cells, step):
    count, parts = lax.axis_size("span"), lax.axis_size("elem")
    line = [s * parts + e for e in range(parts) for s in range(count)]
    pairs = list(zip(line, line[1:]))
    if step < 0:
        pairs = [(b, a) for a, b in pairs]
    return lax.ppermute(cells, ("span", "elem"), pairs)


def coefficients(ground, tension, stiff, offset, link, count, dofs):
    dof_dev = ground.shape[0]
    start = lax.axis_index("span") * dofs
    elem = lax.axis_index("elem")
    dof_all = dof_dev * lax.axis_size("elem")
    position = elem * dof_dev + jnp.arange(dof_dev)
    distance = jnp.arange(1, REACH + 1)[:, None]
    weights = jnp.where((offset == distance) & (position + distance < dof_all), stiff, 0.0)
    wire = jnp.where((distance == 1) & (position < dof_all - 1), tension, 0.0)
    weights = weights + wire
    pairs = [(i, i + 1) for i in range(lax.axis_size("elem") - 1)]
    left = lax.ppermute(weights[:, dof_dev - REACH :], "elem", pairs)
    weights = jnp.concatenate([left, weights], 1)
    weights = lax.dynamic_slice_in_dim(weights, start, dofs + REACH, 1)
    ground = lax.dynamic_slice_in_dim(ground, start, dofs, 0)
    link = lax.dynamic_slice_in_dim(link, start, dofs, 0)
    return weights, ground, link


def add_up(terms):
    total = terms[0]
    for term in terms[1:]:
        total = total + term
    return total


def scaled(factor, value):
    if abs(factor - 1.0) < 1e-12:
        return value
    return value * factor


def cosine_sums(a):
    n = len(a) - 1
    if n == 1:
        return [a[0] + a[1], a[0] - a[1]]
    half = n // 2
    even = cosine_sums([a[s] + a[n - s] for s in range(half)] + [a[half]])
    diff = [a[s] - a[n - s] for s in range(half)]
    out = [None] * (n + 1)
    out[0::2] = even
    for j in range(1, n, 2):
        out[j] = add_up([scaled(math.cos(math.pi * j * s / n), diff[s]) for s in range(half)])
    return out


def sine_sums(b):
    n = len(b) + 1
    if n == 1:
        return []
    half = n // 2
    at = [None] + list(b)
    even = sine_sums([at[s] - at[n - s] for s in range(1, half)])
    total = [None] + [at[s] + at[n - s] for s in range(1, half)] + [at[half]]
    out = [None] * (n + 1)
    for k, value in enumerate(even):
        out[2 * k + 2] = value
    for j in range(1, n, 2):
        terms = [(math.sin(math.pi * j * s / n), total[s]) for s in range(1, half + 1)]
        terms = [scaled(abs(f), t) if f > 0 else -scaled(abs(f), t) for f, t in terms]
        out[j] = add_up(terms)
    return out[1:n]


def slot_scales(count):
    edge, inner = math.sqrt(1.0 / count), math.sqrt(2.0 / count)
    return [edge if j in (0, count // 2) else inner for j in range(count)]


def to_slots(x):
    n = len(x)
    half = n // 2
    plus = [x[0]] + [x[s] + x[n - s] for s in range(1, half)] + [x[half]]
    minus = [x[s] - x[n - s] for s in range(1, half)]
    return cosine_sums(plus) + sine_sums(minus)


def to_spans(y):
    n = len(y)
    half = n // 2
    even = cosine_sums(y[: half + 1])
    odd = [None] + sine_sums(y[half + 1 :])
    out = [None] * n
    out[0], out[half] = even[0], even[half]
    for s in range(1, half):
        out[s] = even[s] + odd[s]
        out[n - s] = even[s] - odd[s]
    return out


def params(**kw):
    return pltpu.CompilerParams(vmem_limit_bytes=VMEM_LIMIT, **kw)


def spread_blocks(blocks, count, ranges):
    _, rows, dof_dev = blocks[0].shape
    dofs = dof_dev // count
    kinds = len(blocks)
    shape = (count, kinds * rows, sum(width for _, width in ranges))
    many = kinds * len(ranges)

    def kernel(*refs):
        out, held, come, go = refs[kinds:]
        arrivals = []
        for i in range(count):
            group, to = [], 0
            for first, width in ranges:
                for k in range(kinds):
                    copy = pltpu.make_async_copy(
                        refs[k].at[0, :, i * dofs + first : i * dofs + first + width],
                        held.at[i, k * rows : (k + 1) * rows, to : to + width],
                        come.at[i * many + len(group)],
                    )
                    copy.start()
                    group.append(copy)
                to += width
            arrivals.append(group)
        leaving = []
        for i, group in enumerate(arrivals):
            for copy in group:
                copy.wait()
            piece = pltpu.make_async_copy(held.at[i], out.at[i], go.at[i])
            piece.start()
            leaving.append(piece)
        for piece in leaving:
            piece.wait()

    whole = pl.BlockSpec(memory_space=pltpu.HBM)
    return pl.pallas_call(
        kernel,
        in_specs=[whole] * kinds,
        out_specs=whole,
        out_shape=pltpu.HBM(shape, jnp.float32),
        scratch_shapes=[
            pltpu.VMEM(shape, jnp.float32),
            pltpu.SemaphoreType.DMA((count * many,)),
            pltpu.SemaphoreType.DMA((count,)),
        ],
        compiler_params=pltpu.CompilerParams(vmem_limit_bytes=60 * 1024 * 1024),
        name="spread_blocks",
    )(*blocks)


def collect_early(early, middle):
    count, rows, early_width = early.shape
    dofs = early_width + LANES
    many = max(n for n in (1, 2, 4, 8) if count % n == 0)

    def kernel(first, block):
        for i in range(many):
            at = i * dofs
            block[0, :, at : at + middle] = first[i, :, :middle]
            block[0, :, at + middle + LANES : at + dofs] = first[i, :, middle:]

    return pl.pallas_call(
        kernel,
        grid=(count // many,),
        in_specs=[pl.BlockSpec((many, rows, early_width), lambda i: (i, 0, 0))],
        out_specs=pl.BlockSpec((1, rows, many * dofs), lambda i: (0, 0, i)),
        out_shape=pltpu.HBM((1, rows, count * dofs), jnp.float32),
        compiler_params=params(),
        name="collect_early",
    )(early)


def collect_late(late, block, middle):
    count, rows, width = late.shape
    dofs = width - LANES
    many = max(n for n in (1, 2, 4, 8) if count % n == 0)

    def kernel(last, _, residual, whole, sem):
        copies = []
        for i in range(many):
            at = (pl.program_id(0) * many + i) * dofs + middle
            copy = pltpu.make_async_copy(
                last.at[i, :, pl.ds(dofs, LANES)],
                whole.at[0, :, pl.ds(pl.multiple_of(at, LANES), LANES)],
                sem.at[i],
            )
            copy.start()
            copies.append(copy)
        for i in range(many):
            residual[0, :, i * dofs : (i + 1) * dofs] = last[i, :, :dofs]
        for copy in copies:
            copy.wait()

    place = pl.BlockSpec(memory_space=pltpu.HBM)
    shape = pltpu.HBM((1, rows, count * dofs), jnp.float32)
    return pl.pallas_call(
        kernel,
        grid=(count // many,),
        in_specs=[pl.BlockSpec((many, rows, width), lambda i: (i, 0, 0)), place],
        out_specs=[pl.BlockSpec((1, rows, many * dofs), lambda i: (0, 0, i)), place],
        out_shape=[shape, shape],
        input_output_aliases={1: 1},
        scratch_shapes=[pltpu.SemaphoreType.DMA((many,))],
        compiler_params=params(),
        name="collect_late",
    )(late, block)


PARTS = 3


def bf16_parts(value):
    parts = []
    for i in range(PARTS):
        parts.append(value.astype(jnp.bfloat16))
        if i < PARTS - 1:
            value = value - parts[i].astype(jnp.float32)
    return parts


def project(stacked, rotation, dofs, tiles, prior=None):
    count, wide, _ = stacked.shape
    rows = rotation.shape[1]
    width = len(tiles) * LANES
    scales = slot_scales(count)
    groups = -(-count * REACH // LANES)
    per = LANES // REACH
    strip = 2 * ROWS

    def kernel(x, rot, *refs):
        refs = refs[1:] if prior is not None else refs
        proj, back = refs[:2]
        edges, scratch = (refs[2:4], refs[4:]) if prior is None else ((), refs[2:])
        held, split_rot, mine, sent, come, go = scratch[:6]
        split_slots = scratch[6:]
        arrivals = []
        for c in range(len(tiles)):
            copy = pltpu.make_async_copy(
                x.at[:, :, c * LANES : (c + 1) * LANES], held.at[c], come.at[c]
            )
            copy.start()
            arrivals.append(copy)

        def one(j, carry):
            for i, part in enumerate(bf16_parts(rot[j])):
                split_rot[j, i * rows : (i + 1) * rows, :] = part
            return carry

        lax.fori_loop(0, count, one, 0)
        for c, copy in enumerate(arrivals):
            copy.wait()

            def transform(r, carry, c=c):
                at = pl.ds(pl.multiple_of(r * strip, strip), strip)
                halves = []
                for h in range(2):
                    own = pl.ds(pl.multiple_of(r * strip + h * ROWS, ROWS), ROWS)
                    halves.append(to_slots([held[c, s, own, :] for s in range(count)]))
                for j in range(count):
                    value = jnp.concatenate([half[j] for half in halves], 0)
                    for part, ref in zip(bf16_parts(value), split_slots):
                        ref[j, at, c * LANES : (c + 1) * LANES] = part
                return carry

            lax.fori_loop(0, wide // strip, transform, 0)
        for j in range(count):
            total = None
            for i in range(PARTS - 1, -1, -1):
                terms = PARTS - i
                stacked_terms = jnp.dot(
                    split_rot[j, : terms * rows, :],
                    split_slots[i][j],
                    preferred_element_type=jnp.float32,
                )
                for q in range(terms - 1, -1, -1):
                    term = stacked_terms[q * rows : (q + 1) * rows]
                    total = term if total is None else total + term
            mine[j] = total
        leaving = []

        def leave(source, target, c, t, at):
            copy = pltpu.make_async_copy(
                source.at[:, :, c * LANES : (c + 1) * LANES],
                target.at[:, :, t * LANES : (t + 1) * LANES],
                go.at[at],
            )
            copy.start()
            leaving.append(copy)

        for c, t in enumerate(tiles):
            leave(mine, proj, c, t, c)
        for c in range(len(tiles)):
            lanes = slice(c * LANES, (c + 1) * LANES)

            def inverse(r, carry, lanes=lanes):
                at = pl.ds(pl.multiple_of(r * ROWS, ROWS), ROWS)
                out = to_spans([mine[j, at, lanes] * scales[j] for j in range(count)])
                for s in range(count):
                    sent[s, at, lanes] = out[s]
                return carry

            lax.fori_loop(0, rows // ROWS, inverse, 0)
            leave(sent, back, c, c, len(tiles) + c)
        lane = lax.broadcasted_iota(jnp.int32, (rows, LANES), 1)
        ends = ((0, 0), (len(tiles) - 1, LANES - REACH))
        for ref, (c, start) in zip(edges, ends):
            for g in range(groups):
                packed = jnp.zeros((rows, LANES), jnp.float32)
                for k in range(min(per, count - g * per)):
                    turn = (k * REACH - start) % LANES
                    value = mine[g * per + k, :, c * LANES : (c + 1) * LANES]
                    value = pltpu.roll(value, turn, 1) if turn else value
                    packed = jnp.where(lane // REACH == k, value, packed)
                ref[g] = packed
        for copy in leaving:
            copy.wait()

    whole = pl.BlockSpec(memory_space=pltpu.HBM)
    vmem = pl.BlockSpec(memory_space=pltpu.VMEM)
    field = pltpu.HBM((count, rows, dofs), jnp.float32)
    edge = jax.ShapeDtypeStruct((groups, rows, LANES), jnp.float32)
    sending = pltpu.HBM((count, rows, width), jnp.float32)
    first = prior is None
    passes = PARTS * (PARTS + 1) // 2
    cost = pl.CostEstimate(
        flops=2 * passes * count * wide * rows * width,
        bytes_accessed=4 * count * (wide + 2 * rows) * width,
        transcendentals=0,
    )
    return pl.pallas_call(
        kernel,
        in_specs=[whole, vmem] + ([] if first else [whole]),
        out_specs=[whole, whole] + ([vmem, vmem] if first else []),
        out_shape=[field, sending] + ([edge, edge] if first else []),
        input_output_aliases={} if first else {2: 0},
        cost_estimate=cost,
        scratch_shapes=[
            pltpu.VMEM((len(tiles), count, wide, LANES), jnp.float32),
            pltpu.VMEM((count, PARTS * rows, wide), jnp.bfloat16),
            pltpu.VMEM((count, rows, width), jnp.float32),
            pltpu.VMEM((count, rows, width), jnp.float32),
            pltpu.SemaphoreType.DMA((len(tiles),)),
            pltpu.SemaphoreType.DMA((2 * len(tiles),)),
        ]
        + [pltpu.VMEM((count, wide, width), jnp.bfloat16)] * PARTS,
        compiler_params=params(),
        name="project",
    )(stacked, rotation, *(() if first else (prior,)))


def stiffness(projected, before, after, bands, links):
    count, rows, dofs = projected.shape
    per = LANES // REACH
    tiles = dofs // LANES

    def kernel(x, left, right, band, lam, stiff, sums, energy, norm, matrix):
        row = lax.broadcasted_iota(jnp.int32, (LANES, LANES), 0)
        gap = row - lax.broadcasted_iota(jnp.int32, (LANES, LANES), 1)
        for t in range(tiles):
            at = slice(t * LANES, (t + 1) * LANES)
            here = jnp.where(gap == 0, band[16:17, at], 0.0)
            halo = jnp.zeros((LANES, LANES), jnp.float32)
            for d in range(1, REACH + 1):
                up, down = band[d - 1 : d, at], band[REACH + d - 1 : REACH + d, at]
                here = jnp.where(gap == d, -up, here)
                here = jnp.where(gap == -d, -down, here)
                halo = jnp.where(gap == d - LANES, -up, halo)
                halo = jnp.where(gap == LANES - d, -down, halo)
            matrix[t, :LANES, :] = here
            matrix[t, LANES:, :] = halo
        lane = lax.broadcasted_iota(jnp.int32, (rows, LANES), 1)

        def slot(j, carry):
            to = pl.ds(pl.multiple_of(j * rows, rows), rows)
            g, k = j // per, j % per
            low = pltpu.roll(left[g], (2 * LANES - REACH - REACH * k) % LANES, 1)
            high = pltpu.roll(right[g], (LANES - REACH * k) % LANES, 1)
            work = jnp.zeros((rows, LANES), jnp.float32)
            size = jnp.zeros((rows, LANES), jnp.float32)
            for t in range(tiles):
                at = slice(t * LANES, (t + 1) * LANES)
                here = x[j, :, at]
                previous = low if t == 0 else x[j, :, (t - 1) * LANES : t * LANES]
                following = high if t == tiles - 1 else x[j, :, (t + 1) * LANES : (t + 2) * LANES]
                halo = jnp.where(lane < LANES // 2, following, previous)
                total = jnp.dot(
                    jnp.concatenate([here, halo], 1),
                    matrix[t],
                    precision=HIGHEST,
                    preferred_element_type=jnp.float32,
                )
                total = total + (lam[j] * band[17:18, at]) * here
                stiff[j, :, at] = total
                work = work + total * here
                size = size + here * here
            energy[to, :] = work
            norm[to, :] = size
            return carry

        lax.fori_loop(0, count, slot, 0)
        ones = jnp.ones((ROWS, LANES), jnp.float32)
        for r, part in enumerate((energy, norm)):
            line = lax.dot_general(
                ones,
                part[...],
                (((1,), (1,)), ((), ())),
                precision=HIGHEST,
                preferred_element_type=jnp.float32,
            )
            sums[r : r + 1, :] = line[:1]

    vmem = pl.BlockSpec(memory_space=pltpu.VMEM)
    return pl.pallas_call(
        kernel,
        in_specs=[vmem, vmem, vmem, vmem, pl.BlockSpec(memory_space=pltpu.SMEM)],
        out_specs=[vmem, vmem],
        out_shape=[
            jax.ShapeDtypeStruct((count, rows, dofs), jnp.float32),
            jax.ShapeDtypeStruct((2, count * rows), jnp.float32),
        ],
        scratch_shapes=[
            pltpu.VMEM((count * rows, LANES), jnp.float32),
            pltpu.VMEM((count * rows, LANES), jnp.float32),
            pltpu.VMEM((tiles, 2 * LANES, LANES), jnp.float32),
        ],
        compiler_params=params(),
        name="stiffness",
    )(projected, before, after, bands, links)


def residual_back(projected, stiff, sums, late):
    count, rows, dofs = projected.shape
    scales = slot_scales(count)

    tiles = dofs // LANES

    def kernel(x, kx, total, extra, back, ritz, wide):
        @pl.when(pl.program_id(0) == 0)
        def _():
            value = total[0:1, :] / (total[1:2, :] + 1e-06)
            ritz[...] = value
            row = lax.broadcasted_iota(jnp.int32, (ROWS, count * rows), 0)
            first = jnp.where(row == 0, value, 0.0)
            ones = jnp.ones((ROWS, LANES), jnp.float32)
            spread_out = lax.dot_general(
                first,
                ones,
                (((0,), (0,)), ((), ())),
                precision=HIGHEST,
                preferred_element_type=jnp.float32,
            )
            wide[...] = spread_out

        def strip(r, carry):
            at = pl.ds(pl.multiple_of(r * ROWS, ROWS), ROWS)
            terms = []
            for j in range(count):
                to = pl.ds(pl.multiple_of(j * rows + r * ROWS, ROWS), ROWS)
                terms.append((kx[j, at, :] - wide[to, :] * x[j, at, :]) * scales[j])
            out = to_spans(terms)
            for s in range(count):
                back[s, at, :] = out[s]
            return carry

        @pl.when(pl.program_id(0) < tiles)
        def _():
            lax.fori_loop(0, rows // ROWS, strip, 0)

        @pl.when(pl.program_id(0) == tiles)
        def _():
            back[...] = extra[...]

    inner = pl.BlockSpec((count, rows, LANES), lambda t: (0, 0, jnp.minimum(t, tiles - 1)))
    cell = pl.BlockSpec((count, rows, LANES), lambda t: (0, 0, t))
    return pl.pallas_call(
        kernel,
        grid=(tiles + 1,),
        in_specs=[
            inner,
            inner,
            pl.BlockSpec((2, count * rows), lambda t: (0, 0)),
            pl.BlockSpec((count, rows, LANES), lambda t: (0, 0, 0)),
        ],
        out_specs=[cell, pl.BlockSpec((1, count * rows), lambda t: (0, 0))],
        out_shape=[
            pltpu.HBM((count, rows, dofs + LANES), jnp.float32),
            jax.ShapeDtypeStruct((1, count * rows), jnp.float32),
        ],
        scratch_shapes=[pltpu.VMEM((count * rows, LANES), jnp.float32)],
        compiler_params=params(),
        name="residual_back",
    )(projected, stiff, sums, late)


def halvings(axis):
    step = lax.axis_size(axis) // 2
    while step:
        yield step, [(i, i ^ step) for i in range(lax.axis_size(axis))]
        step //= 2


def exchange_step(held, step, pairs):
    other = lax.ppermute(held, "span", pairs)
    upper = (lax.axis_index("span") & step) != 0
    return jnp.stack([jnp.where(upper, other, held), jnp.where(upper, held, other)])


def in_order(held, steps):
    bits = [step for step, _ in steps][::-1]
    order = tuple(sorted(range(len(bits)), key=lambda d: -bits[d]))
    held = held.transpose(order + tuple(range(len(bits), held.ndim)))
    return held.reshape((-1,) + held.shape[len(bits) :])


def tiled_device(
    current_block,
    search_block,
    previous_block,
    ground_spring,
    wire_tension,
    dropper_stiff,
    dropper_offset,
    span_link,
    ritz_rotation,
):
    count = lax.axis_size("span")
    dofs = current_block.shape[2] // count
    rows = current_block.shape[1]
    steps = list(halvings("span"))
    tiles = list(range(dofs // LANES))
    middle = tiles[len(tiles) // 2]
    early = [t for t in tiles if t != middle]
    at = middle * LANES
    blocks = (current_block, search_block, previous_block)
    rotation = exchange_step(ritz_rotation[0].T, *steps[0])
    pieces = spread_blocks(blocks, count, [(0, at), (at + LANES, dofs - at - LANES)])
    pieces, rotation = lax.optimization_barrier((pieces, rotation))
    stacked = exchange(pieces)
    order = steps[2:] + steps[1:2]
    for step, pairs in order:
        rotation = exchange_step(rotation, step, pairs)
    rotation = in_order(rotation, [steps[0]] + order)
    scales = jnp.array(slot_scales(count), jnp.float32)[:, None, None]
    rotation = rotation * scales
    pieces = spread_blocks(blocks, count, [(at, LANES)])
    pieces, rotation = lax.optimization_barrier((pieces, rotation))
    stacked_late = exchange(pieces)
    weights, ground, link = coefficients(
        ground_spring, wire_tension, dropper_stiff, dropper_offset, span_link, count, dofs
    )
    up = weights[:, REACH:]
    down = [weights[d - 1, REACH - d : REACH - d + dofs] for d in range(1, REACH + 1)]
    down = jnp.stack(down)
    diagonal = ground + jnp.sum(up, 0) + jnp.sum(down, 0)
    bands = jnp.concatenate([up, down, diagonal[None], link[None]])
    links = 2.0 * (1.0 - fourier_rows(count)[1])
    projected, spans, head, tail = project(stacked, rotation, dofs, early)
    before, after = to_next(tail, 1), to_next(head, -1)
    spans, before, after = lax.optimization_barrier((spans, before, after))
    early_pieces = exchange(spans)
    projected, late = project(stacked_late, rotation, dofs, [middle], projected)
    stiff, sums = stiffness(projected, before, after, bands, links)
    for _, pairs in halvings("elem"):
        sums = sums + lax.ppermute(sums, "elem", pairs)
    for _, pairs in steps[::-1]:
        sums = sums + lax.ppermute(sums, "span", pairs)
    spans, ritz = residual_back(projected, stiff, sums, late)
    next_block = collect_early(early_pieces, at)
    next_residual, next_block = collect_late(exchange(spans), next_block, at)
    ritz = lax.dynamic_slice_in_dim(ritz, lax.axis_index("span") * rows, rows, 1)
    return (next_block, next_residual, ritz)


def on_device(
    current_block,
    search_block,
    previous_block,
    ground_spring,
    wire_tension,
    dropper_stiff,
    dropper_offset,
    span_link,
    ritz_rotation,
):
    count = lax.axis_size("span")
    dof_dev = current_block.shape[2]
    dofs = dof_dev // count
    matrix, cosines = fourier_rows(count)
    blocks = (current_block, search_block, previous_block)
    stacked = exchange(jnp.concatenate([spread(b[0], count) for b in blocks], 1))
    rotation = lax.all_gather(ritz_rotation, "span", axis=0, tiled=True)
    weights, ground, link = coefficients(
        ground_spring, wire_tension, dropper_stiff, dropper_offset, span_link, count, dofs
    )
    slots = along_spans(matrix, stacked)
    projected = jnp.einsum("jvm,jvd->jmd", rotation, slots, precision=HIGHEST)
    back = matrix.T
    next_block = collect(exchange(along_spans(back, projected)))
    before = to_next(projected[:, :, dofs - REACH :], 1)
    after = to_next(projected[:, :, :REACH], -1)
    wide = jnp.concatenate([before, projected, after], 2)
    stiff = ground * projected
    near = wide[:, :, : REACH + dofs]
    for distance in range(1, REACH + 1):
        flux = weights[distance - 1] * (near - wide[:, :, distance : distance + REACH + dofs])
        stiff = stiff + flux[:, :, REACH:] - flux[:, :, REACH - distance : REACH - distance + dofs]
    stiff = stiff + (2.0 * (1.0 - cosines))[:, None, None] * link * projected
    sums = jnp.stack([jnp.sum(projected * stiff, 2), jnp.sum(projected * projected, 2)])
    sums = lax.psum(sums, ("elem", "span"))
    ritz = sums[0] / (sums[1] + 1e-06)
    residual = stiff - ritz[:, :, None] * projected
    next_residual = collect(exchange(along_spans(back, residual)))
    my_ritz = lax.dynamic_slice_in_dim(ritz, lax.axis_index("span"), 1, 0)
    return (next_block, next_residual, my_ritz)


def by_shape(*args):
    count, dof_dev = lax.axis_size("span"), args[0].shape[2]
    halves = count & (count - 1) == 0 and lax.axis_size("elem") in (1, 2, 4, 8, 16)
    if halves and count > 2 and dof_dev % (count * LANES) == 0 and dof_dev > 2 * count * LANES:
        return tiled_device(*args)
    return on_device(*args)


def solution(mesh):
    return jax.shard_map(
        by_shape,
        mesh=mesh,
        in_specs=(
            P("span", None, "elem"),
            P("span", None, "elem"),
            P("span", None, "elem"),
            P("elem"),
            P("elem"),
            P("elem"),
            P("elem"),
            P("elem"),
            P("span", None, None),
        ),
        out_specs=(P("span", None, "elem"), P("span", None, "elem"), P("span", None)),
        check_vma=False,
    )
```

```python
import math

import jax
import jax.numpy as jnp
from jax import lax
from jax.experimental import pallas as pl
from jax.experimental.pallas import tpu as pltpu
from jax.sharding import PartitionSpec as P

REACH = 8
LANES = 128
ROWS = 8
VMEM_LIMIT = 24 * 1024 * 1024
HIGHEST = lax.Precision.HIGHEST


def fourier_rows(count):
    row = jnp.arange(count)[:, None]
    col = jnp.arange(count)[None, :]
    half = count // 2
    wave = jnp.where(row <= half, row, row - half)
    phase = (wave * col % count).astype(jnp.float32) * (2.0 * math.pi / count)
    scaled = jnp.where(row <= half, jnp.cos(phase), jnp.sin(phase)) * math.sqrt(2.0 / count)
    edge = (row == 0) | (row == half)
    matrix = jnp.where(edge, jnp.cos(phase) * math.sqrt(1.0 / count), scaled)
    slots = jnp.arange(count)
    slot_wave = jnp.where(slots <= half, slots, slots - half)
    cosines = jnp.cos(slot_wave.astype(jnp.float32) * (2.0 * math.pi / count))
    return (matrix, cosines)


def along_spans(matrix, block):
    shape = block.shape
    flat = block.reshape(shape[0], -1)
    return jnp.dot(matrix, flat, precision=HIGHEST).reshape(shape)


def spread(block, count):
    rows, dofs = block.shape
    return block.reshape(rows, count, dofs // count).transpose(1, 0, 2)


def collect(pieces):
    count, rows, dofs = pieces.shape
    return pieces.transpose(1, 0, 2).reshape(1, rows, count * dofs)


def exchange(pieces):
    return lax.all_to_all(pieces, "span", split_axis=0, concat_axis=0, tiled=True)


def to_next(cells, step):
    count, parts = lax.axis_size("span"), lax.axis_size("elem")
    line = [s * parts + e for e in range(parts) for s in range(count)]
    pairs = list(zip(line, line[1:]))
    if step < 0:
        pairs = [(b, a) for a, b in pairs]
    return lax.ppermute(cells, ("span", "elem"), pairs)


def coefficients(ground, tension, stiff, offset, link, count, dofs):
    dof_dev = ground.shape[0]
    start = lax.axis_index("span") * dofs
    elem = lax.axis_index("elem")
    dof_all = dof_dev * lax.axis_size("elem")
    position = elem * dof_dev + jnp.arange(dof_dev)
    distance = jnp.arange(1, REACH + 1)[:, None]
    weights = jnp.where((offset == distance) & (position + distance < dof_all), stiff, 0.0)
    wire = jnp.where((distance == 1) & (position < dof_all - 1), tension, 0.0)
    weights = weights + wire
    pairs = [(i, i + 1) for i in range(lax.axis_size("elem") - 1)]
    left = lax.ppermute(weights[:, dof_dev - REACH :], "elem", pairs)
    weights = jnp.concatenate([left, weights], 1)
    weights = lax.dynamic_slice_in_dim(weights, start, dofs + REACH, 1)
    ground = lax.dynamic_slice_in_dim(ground, start, dofs, 0)
    link = lax.dynamic_slice_in_dim(link, start, dofs, 0)
    return weights, ground, link


def add_up(terms):
    total = terms[0]
    for term in terms[1:]:
        total = total + term
    return total


def scaled(factor, value):
    if abs(factor - 1.0) < 1e-12:
        return value
    return value * factor


def cosine_sums(a):
    n = len(a) - 1
    if n == 1:
        return [a[0] + a[1], a[0] - a[1]]
    half = n // 2
    even = cosine_sums([a[s] + a[n - s] for s in range(half)] + [a[half]])
    diff = [a[s] - a[n - s] for s in range(half)]
    out = [None] * (n + 1)
    out[0::2] = even
    for j in range(1, n, 2):
        out[j] = add_up([scaled(math.cos(math.pi * j * s / n), diff[s]) for s in range(half)])
    return out


def sine_sums(b):
    n = len(b) + 1
    if n == 1:
        return []
    half = n // 2
    at = [None] + list(b)
    even = sine_sums([at[s] - at[n - s] for s in range(1, half)])
    total = [None] + [at[s] + at[n - s] for s in range(1, half)] + [at[half]]
    out = [None] * (n + 1)
    for k, value in enumerate(even):
        out[2 * k + 2] = value
    for j in range(1, n, 2):
        terms = [(math.sin(math.pi * j * s / n), total[s]) for s in range(1, half + 1)]
        terms = [scaled(abs(f), t) if f > 0 else -scaled(abs(f), t) for f, t in terms]
        out[j] = add_up(terms)
    return out[1:n]


def slot_scales(count):
    edge, inner = math.sqrt(1.0 / count), math.sqrt(2.0 / count)
    return [edge if j in (0, count // 2) else inner for j in range(count)]


def to_slots(x):
    n = len(x)
    half = n // 2
    plus = [x[0]] + [x[s] + x[n - s] for s in range(1, half)] + [x[half]]
    minus = [x[s] - x[n - s] for s in range(1, half)]
    return cosine_sums(plus) + sine_sums(minus)


def to_spans(y):
    n = len(y)
    half = n // 2
    even = cosine_sums(y[: half + 1])
    odd = [None] + sine_sums(y[half + 1 :])
    out = [None] * n
    out[0], out[half] = even[0], even[half]
    for s in range(1, half):
        out[s] = even[s] + odd[s]
        out[n - s] = even[s] - odd[s]
    return out


def params(**kw):
    return pltpu.CompilerParams(vmem_limit_bytes=VMEM_LIMIT, **kw)


def spread_blocks(blocks, count, ranges):
    _, rows, dof_dev = blocks[0].shape
    dofs = dof_dev // count
    kinds = len(blocks)
    shape = (count, kinds * rows, sum(width for _, width in ranges))
    many = kinds * len(ranges)

    def kernel(*refs):
        out, held, come, go = refs[kinds:]
        arrivals = []
        for i in range(count):
            group, to = [], 0
            for first, width in ranges:
                for k in range(kinds):
                    copy = pltpu.make_async_copy(
                        refs[k].at[0, :, i * dofs + first : i * dofs + first + width],
                        held.at[i, k * rows : (k + 1) * rows, to : to + width],
                        come.at[i * many + len(group)],
                    )
                    copy.start()
                    group.append(copy)
                to += width
            arrivals.append(group)
        leaving = []
        for i, group in enumerate(arrivals):
            for copy in group:
                copy.wait()
            piece = pltpu.make_async_copy(held.at[i], out.at[i], go.at[i])
            piece.start()
            leaving.append(piece)
        for piece in leaving:
            piece.wait()

    whole = pl.BlockSpec(memory_space=pltpu.HBM)
    return pl.pallas_call(
        kernel,
        in_specs=[whole] * kinds,
        out_specs=whole,
        out_shape=pltpu.HBM(shape, jnp.float32),
        scratch_shapes=[
            pltpu.VMEM(shape, jnp.float32),
            pltpu.SemaphoreType.DMA((count * many,)),
            pltpu.SemaphoreType.DMA((count,)),
        ],
        compiler_params=pltpu.CompilerParams(vmem_limit_bytes=60 * 1024 * 1024),
        name="spread_blocks",
    )(*blocks)


def collect_early(early, middle):
    count, rows, early_width = early.shape
    dofs = early_width + LANES
    many = max(n for n in (1, 2, 4, 8) if count % n == 0)

    def kernel(first, block):
        for i in range(many):
            at = i * dofs
            block[0, :, at : at + middle] = first[i, :, :middle]
            block[0, :, at + middle + LANES : at + dofs] = first[i, :, middle:]

    return pl.pallas_call(
        kernel,
        grid=(count // many,),
        in_specs=[pl.BlockSpec((many, rows, early_width), lambda i: (i, 0, 0))],
        out_specs=pl.BlockSpec((1, rows, many * dofs), lambda i: (0, 0, i)),
        out_shape=pltpu.HBM((1, rows, count * dofs), jnp.float32),
        compiler_params=params(),
        name="collect_early",
    )(early)


def collect_late(late, block, middle):
    count, rows, width = late.shape
    dofs = width - LANES
    many = max(n for n in (1, 2, 4, 8) if count % n == 0)

    def kernel(last, _, residual, whole, sem):
        copies = []
        for i in range(many):
            at = (pl.program_id(0) * many + i) * dofs + middle
            copy = pltpu.make_async_copy(
                last.at[i, :, pl.ds(dofs, LANES)],
                whole.at[0, :, pl.ds(pl.multiple_of(at, LANES), LANES)],
                sem.at[i],
            )
            copy.start()
            copies.append(copy)
        for i in range(many):
            residual[0, :, i * dofs : (i + 1) * dofs] = last[i, :, :dofs]
        for copy in copies:
            copy.wait()

    place = pl.BlockSpec(memory_space=pltpu.HBM)
    shape = pltpu.HBM((1, rows, count * dofs), jnp.float32)
    return pl.pallas_call(
        kernel,
        grid=(count // many,),
        in_specs=[pl.BlockSpec((many, rows, width), lambda i: (i, 0, 0)), place],
        out_specs=[pl.BlockSpec((1, rows, many * dofs), lambda i: (0, 0, i)), place],
        out_shape=[shape, shape],
        input_output_aliases={1: 1},
        scratch_shapes=[pltpu.SemaphoreType.DMA((many,))],
        compiler_params=params(),
        name="collect_late",
    )(late, block)


PARTS = 3


def bf16_parts(value):
    parts = []
    for i in range(PARTS):
        parts.append(value.astype(jnp.bfloat16))
        if i < PARTS - 1:
            value = value - parts[i].astype(jnp.float32)
    return parts


def project(stacked, rotation, dofs, tiles, prior=None):
    count, wide, _ = stacked.shape
    rows = rotation.shape[1]
    width = len(tiles) * LANES
    scales = slot_scales(count)
    groups = -(-count * REACH // LANES)
    per = LANES // REACH
    strip = 2 * ROWS

    def kernel(x, rot, *refs):
        refs = refs[1:] if prior is not None else refs
        proj, back = refs[:2]
        edges, scratch = (refs[2:4], refs[4:]) if prior is None else ((), refs[2:])
        held, split_rot, mine, sent, come, go = scratch[:6]
        split_slots = scratch[6:]
        arrivals = []
        for c in range(len(tiles)):
            copy = pltpu.make_async_copy(
                x.at[:, :, c * LANES : (c + 1) * LANES], held.at[c], come.at[c]
            )
            copy.start()
            arrivals.append(copy)

        def one(j, carry):
            for i, part in enumerate(bf16_parts(rot[j])):
                split_rot[j, i * rows : (i + 1) * rows, :] = part
            return carry

        lax.fori_loop(0, count, one, 0)
        for c, copy in enumerate(arrivals):
            copy.wait()

            def transform(r, carry, c=c):
                at = pl.ds(pl.multiple_of(r * strip, strip), strip)
                halves = []
                for h in range(2):
                    own = pl.ds(pl.multiple_of(r * strip + h * ROWS, ROWS), ROWS)
                    halves.append(to_slots([held[c, s, own, :] for s in range(count)]))
                for j in range(count):
                    value = jnp.concatenate([half[j] for half in halves], 0)
                    for part, ref in zip(bf16_parts(value), split_slots):
                        ref[j, at, c * LANES : (c + 1) * LANES] = part
                return carry

            lax.fori_loop(0, wide // strip, transform, 0)
        for j in range(count):
            total = None
            for i in range(PARTS - 1, -1, -1):
                terms = PARTS - i
                stacked_terms = jnp.dot(
                    split_rot[j, : terms * rows, :],
                    split_slots[i][j],
                    preferred_element_type=jnp.float32,
                )
                for q in range(terms - 1, -1, -1):
                    term = stacked_terms[q * rows : (q + 1) * rows]
                    total = term if total is None else total + term
            mine[j] = total
        leaving = []

        def leave(source, target, c, t, at):
            copy = pltpu.make_async_copy(
                source.at[:, :, c * LANES : (c + 1) * LANES],
                target.at[:, :, t * LANES : (t + 1) * LANES],
                go.at[at],
            )
            copy.start()
            leaving.append(copy)

        for c, t in enumerate(tiles):
            leave(mine, proj, c, t, c)
        for c in range(len(tiles)):
            lanes = slice(c * LANES, (c + 1) * LANES)

            def inverse(r, carry, lanes=lanes):
                at = pl.ds(pl.multiple_of(r * ROWS, ROWS), ROWS)
                out = to_spans([mine[j, at, lanes] * scales[j] for j in range(count)])
                for s in range(count):
                    sent[s, at, lanes] = out[s]
                return carry

            lax.fori_loop(0, rows // ROWS, inverse, 0)
            leave(sent, back, c, c, len(tiles) + c)
        lane = lax.broadcasted_iota(jnp.int32, (rows, LANES), 1)
        ends = ((0, 0), (len(tiles) - 1, LANES - REACH))
        for ref, (c, start) in zip(edges, ends):
            for g in range(groups):
                packed = jnp.zeros((rows, LANES), jnp.float32)
                for k in range(min(per, count - g * per)):
                    turn = (k * REACH - start) % LANES
                    value = mine[g * per + k, :, c * LANES : (c + 1) * LANES]
                    value = pltpu.roll(value, turn, 1) if turn else value
                    packed = jnp.where(lane // REACH == k, value, packed)
                ref[g] = packed
        for copy in leaving:
            copy.wait()

    whole = pl.BlockSpec(memory_space=pltpu.HBM)
    vmem = pl.BlockSpec(memory_space=pltpu.VMEM)
    field = pltpu.HBM((count, rows, dofs), jnp.float32)
    edge = jax.ShapeDtypeStruct((groups, rows, LANES), jnp.float32)
    sending = pltpu.HBM((count, rows, width), jnp.float32)
    first = prior is None
    passes = PARTS * (PARTS + 1) // 2
    cost = pl.CostEstimate(
        flops=2 * passes * count * wide * rows * width,
        bytes_accessed=4 * count * (wide + 2 * rows) * width,
        transcendentals=0,
    )
    return pl.pallas_call(
        kernel,
        in_specs=[whole, vmem] + ([] if first else [whole]),
        out_specs=[whole, whole] + ([vmem, vmem] if first else []),
        out_shape=[field, sending] + ([edge, edge] if first else []),
        input_output_aliases={} if first else {2: 0},
        cost_estimate=cost,
        scratch_shapes=[
            pltpu.VMEM((len(tiles), count, wide, LANES), jnp.float32),
            pltpu.VMEM((count, PARTS * rows, wide), jnp.bfloat16),
            pltpu.VMEM((count, rows, width), jnp.float32),
            pltpu.VMEM((count, rows, width), jnp.float32),
            pltpu.SemaphoreType.DMA((len(tiles),)),
            pltpu.SemaphoreType.DMA((2 * len(tiles),)),
        ]
        + [pltpu.VMEM((count, wide, width), jnp.bfloat16)] * PARTS,
        compiler_params=params(),
        name="project",
    )(stacked, rotation, *(() if first else (prior,)))


def stiffness(projected, before, after, bands, links):
    count, rows, dofs = projected.shape
    per = LANES // REACH
    tiles = dofs // LANES

    def kernel(x, left, right, band, lam, stiff, sums, energy, norm, matrix):
        row = lax.broadcasted_iota(jnp.int32, (LANES, LANES), 0)
        gap = row - lax.broadcasted_iota(jnp.int32, (LANES, LANES), 1)
        for t in range(tiles):
            at = slice(t * LANES, (t + 1) * LANES)
            here = jnp.where(gap == 0, band[16:17, at], 0.0)
            halo = jnp.zeros((LANES, LANES), jnp.float32)
            for d in range(1, REACH + 1):
                up, down = band[d - 1 : d, at], band[REACH + d - 1 : REACH + d, at]
                here = jnp.where(gap == d, -up, here)
                here = jnp.where(gap == -d, -down, here)
                halo = jnp.where(gap == d - LANES, -up, halo)
                halo = jnp.where(gap == LANES - d, -down, halo)
            matrix[t, :LANES, :] = here
            matrix[t, LANES:, :] = halo
        lane = lax.broadcasted_iota(jnp.int32, (rows, LANES), 1)

        def slot(j, carry):
            to = pl.ds(pl.multiple_of(j * rows, rows), rows)
            g, k = j // per, j % per
            low = pltpu.roll(left[g], (2 * LANES - REACH - REACH * k) % LANES, 1)
            high = pltpu.roll(right[g], (LANES - REACH * k) % LANES, 1)
            work = jnp.zeros((rows, LANES), jnp.float32)
            size = jnp.zeros((rows, LANES), jnp.float32)
            for t in range(tiles):
                at = slice(t * LANES, (t + 1) * LANES)
                here = x[j, :, at]
                previous = low if t == 0 else x[j, :, (t - 1) * LANES : t * LANES]
                following = high if t == tiles - 1 else x[j, :, (t + 1) * LANES : (t + 2) * LANES]
                halo = jnp.where(lane < LANES // 2, following, previous)
                total = jnp.dot(
                    jnp.concatenate([here, halo], 1),
                    matrix[t],
                    precision=HIGHEST,
                    preferred_element_type=jnp.float32,
                )
                total = total + (lam[j] * band[17:18, at]) * here
                stiff[j, :, at] = total
                work = work + total * here
                size = size + here * here
            energy[to, :] = work
            norm[to, :] = size
            return carry

        lax.fori_loop(0, count, slot, 0)
        ones = jnp.ones((ROWS, LANES), jnp.float32)
        for r, part in enumerate((energy, norm)):
            line = lax.dot_general(
                ones,
                part[...],
                (((1,), (1,)), ((), ())),
                precision=HIGHEST,
                preferred_element_type=jnp.float32,
            )
            sums[r : r + 1, :] = line[:1]

    vmem = pl.BlockSpec(memory_space=pltpu.VMEM)
    return pl.pallas_call(
        kernel,
        in_specs=[vmem, vmem, vmem, vmem, pl.BlockSpec(memory_space=pltpu.SMEM)],
        out_specs=[vmem, vmem],
        out_shape=[
            jax.ShapeDtypeStruct((count, rows, dofs), jnp.float32),
            jax.ShapeDtypeStruct((2, count * rows), jnp.float32),
        ],
        scratch_shapes=[
            pltpu.VMEM((count * rows, LANES), jnp.float32),
            pltpu.VMEM((count * rows, LANES), jnp.float32),
            pltpu.VMEM((tiles, 2 * LANES, LANES), jnp.float32),
        ],
        compiler_params=params(),
        name="stiffness",
    )(projected, before, after, bands, links)


def residual_back(projected, stiff, sums, late):
    count, rows, dofs = projected.shape
    scales = slot_scales(count)

    tiles = dofs // LANES

    def kernel(x, kx, total, extra, back, ritz, wide):
        @pl.when(pl.program_id(0) == 0)
        def _():
            value = total[0:1, :] / (total[1:2, :] + 1e-06)
            ritz[...] = value
            row = lax.broadcasted_iota(jnp.int32, (ROWS, count * rows), 0)
            first = jnp.where(row == 0, value, 0.0)
            ones = jnp.ones((ROWS, LANES), jnp.float32)
            spread_out = lax.dot_general(
                first,
                ones,
                (((0,), (0,)), ((), ())),
                precision=HIGHEST,
                preferred_element_type=jnp.float32,
            )
            wide[...] = spread_out

        def strip(r, carry):
            at = pl.ds(pl.multiple_of(r * ROWS, ROWS), ROWS)
            terms = []
            for j in range(count):
                to = pl.ds(pl.multiple_of(j * rows + r * ROWS, ROWS), ROWS)
                terms.append((kx[j, at, :] - wide[to, :] * x[j, at, :]) * scales[j])
            out = to_spans(terms)
            for s in range(count):
                back[s, at, :] = out[s]
            return carry

        @pl.when(pl.program_id(0) < tiles)
        def _():
            lax.fori_loop(0, rows // ROWS, strip, 0)

        @pl.when(pl.program_id(0) == tiles)
        def _():
            back[...] = extra[...]

    inner = pl.BlockSpec((count, rows, LANES), lambda t: (0, 0, jnp.minimum(t, tiles - 1)))
    cell = pl.BlockSpec((count, rows, LANES), lambda t: (0, 0, t))
    return pl.pallas_call(
        kernel,
        grid=(tiles + 1,),
        in_specs=[
            inner,
            inner,
            pl.BlockSpec((2, count * rows), lambda t: (0, 0)),
            pl.BlockSpec((count, rows, LANES), lambda t: (0, 0, 0)),
        ],
        out_specs=[cell, pl.BlockSpec((1, count * rows), lambda t: (0, 0))],
        out_shape=[
            pltpu.HBM((count, rows, dofs + LANES), jnp.float32),
            jax.ShapeDtypeStruct((1, count * rows), jnp.float32),
        ],
        scratch_shapes=[pltpu.VMEM((count * rows, LANES), jnp.float32)],
        compiler_params=params(),
        name="residual_back",
    )(projected, stiff, sums, late)


def halvings(axis):
    step = lax.axis_size(axis) // 2
    while step:
        yield step, [(i, i ^ step) for i in range(lax.axis_size(axis))]
        step //= 2


def exchange_step(held, step, pairs):
    other = lax.ppermute(held, "span", pairs)
    upper = (lax.axis_index("span") & step) != 0
    return jnp.stack([jnp.where(upper, other, held), jnp.where(upper, held, other)])


def exchange_bits(held, steps):
    bits = len(steps)
    tail = held.shape[1:]
    held = held.reshape((2,) * bits + tail)

    def halves(held, step, d):
        upper = (lax.axis_index("span") & step) != 0
        low, high = (lax.index_in_dim(held, side, d, keepdims=False) for side in (0, 1))
        return jnp.where(upper, high, low), jnp.where(upper, low, high)

    def join(mine, other, step, pairs, d):
        upper = (lax.axis_index("span") & step) != 0
        got = lax.ppermute(other, "span", pairs)
        return jnp.stack([jnp.where(upper, got, mine), jnp.where(upper, mine, got)], d)

    near = steps[::-1]
    for k, (step, pairs) in enumerate(near[:-1]):
        d = bits - 1 - k
        held = join(*halves(held, step, d), step, pairs, d)
    step, pairs = near[-1]
    mine, other = halves(held, step, 0)

    def finish(mine, other):
        return join(mine, other, step, pairs, 0).reshape((-1,) + tail)

    return mine, other, finish


def in_order(held, steps):
    bits = [step for step, _ in steps][::-1]
    order = tuple(sorted(range(len(bits)), key=lambda d: -bits[d]))
    held = held.transpose(order + tuple(range(len(bits), held.ndim)))
    return held.reshape((-1,) + held.shape[len(bits) :])


def tiled_device(
    current_block,
    search_block,
    previous_block,
    ground_spring,
    wire_tension,
    dropper_stiff,
    dropper_offset,
    span_link,
    ritz_rotation,
):
    count = lax.axis_size("span")
    dofs = current_block.shape[2] // count
    rows = current_block.shape[1]
    steps = list(halvings("span"))
    tiles = list(range(dofs // LANES))
    middle = tiles[len(tiles) // 2]
    early = [t for t in tiles if t != middle]
    at = middle * LANES
    blocks = (current_block, search_block, previous_block)
    rotation = exchange_step(ritz_rotation[0].T, *steps[0])
    pieces = spread_blocks(blocks, count, [(0, at), (at + LANES, dofs - at - LANES)])
    pieces, rotation = lax.optimization_barrier((pieces, rotation))
    stacked = exchange(pieces)
    order = steps[2:] + steps[1:2]
    for step, pairs in order:
        rotation = exchange_step(rotation, step, pairs)
    rotation = in_order(rotation, [steps[0]] + order)
    scales = jnp.array(slot_scales(count), jnp.float32)[:, None, None]
    rotation = rotation * scales
    pieces = spread_blocks(blocks, count, [(at, LANES)])
    mine, other, finish = exchange_bits(pieces, steps)
    rotation, mine, other = lax.optimization_barrier((rotation, mine, other))
    stacked_late = finish(mine, other)
    weights, ground, link = coefficients(
        ground_spring, wire_tension, dropper_stiff, dropper_offset, span_link, count, dofs
    )
    up = weights[:, REACH:]
    down = [weights[d - 1, REACH - d : REACH - d + dofs] for d in range(1, REACH + 1)]
    down = jnp.stack(down)
    diagonal = ground + jnp.sum(up, 0) + jnp.sum(down, 0)
    bands = jnp.concatenate([up, down, diagonal[None], link[None]])
    links = 2.0 * (1.0 - fourier_rows(count)[1])
    projected, spans, head, tail = project(stacked, rotation, dofs, early)
    before, after = to_next(tail, 1), to_next(head, -1)
    spans, before, after, stacked_late = lax.optimization_barrier(
        (spans, before, after, stacked_late)
    )
    early_pieces = exchange(spans)
    projected, late = project(stacked_late, rotation, dofs, [middle], projected)
    stiff, sums = stiffness(projected, before, after, bands, links)
    for _, pairs in halvings("elem"):
        sums = sums + lax.ppermute(sums, "elem", pairs)
    for _, pairs in steps[::-1]:
        sums = sums + lax.ppermute(sums, "span", pairs)
    spans, ritz = residual_back(projected, stiff, sums, late)
    next_block = collect_early(early_pieces, at)
    next_residual, next_block = collect_late(exchange(spans), next_block, at)
    ritz = lax.dynamic_slice_in_dim(ritz, lax.axis_index("span") * rows, rows, 1)
    return (next_block, next_residual, ritz)


def on_device(
    current_block,
    search_block,
    previous_block,
    ground_spring,
    wire_tension,
    dropper_stiff,
    dropper_offset,
    span_link,
    ritz_rotation,
):
    count = lax.axis_size("span")
    dof_dev = current_block.shape[2]
    dofs = dof_dev // count
    matrix, cosines = fourier_rows(count)
    blocks = (current_block, search_block, previous_block)
    stacked = exchange(jnp.concatenate([spread(b[0], count) for b in blocks], 1))
    rotation = lax.all_gather(ritz_rotation, "span", axis=0, tiled=True)
    weights, ground, link = coefficients(
        ground_spring, wire_tension, dropper_stiff, dropper_offset, span_link, count, dofs
    )
    slots = along_spans(matrix, stacked)
    projected = jnp.einsum("jvm,jvd->jmd", rotation, slots, precision=HIGHEST)
    back = matrix.T
    next_block = collect(exchange(along_spans(back, projected)))
    before = to_next(projected[:, :, dofs - REACH :], 1)
    after = to_next(projected[:, :, :REACH], -1)
    wide = jnp.concatenate([before, projected, after], 2)
    stiff = ground * projected
    near = wide[:, :, : REACH + dofs]
    for distance in range(1, REACH + 1):
        flux = weights[distance - 1] * (near - wide[:, :, distance : distance + REACH + dofs])
        stiff = stiff + flux[:, :, REACH:] - flux[:, :, REACH - distance : REACH - distance + dofs]
    stiff = stiff + (2.0 * (1.0 - cosines))[:, None, None] * link * projected
    sums = jnp.stack([jnp.sum(projected * stiff, 2), jnp.sum(projected * projected, 2)])
    sums = lax.psum(sums, ("elem", "span"))
    ritz = sums[0] / (sums[1] + 1e-06)
    residual = stiff - ritz[:, :, None] * projected
    next_residual = collect(exchange(along_spans(back, residual)))
    my_ritz = lax.dynamic_slice_in_dim(ritz, lax.axis_index("span"), 1, 0)
    return (next_block, next_residual, my_ritz)


def by_shape(*args):
    count, dof_dev = lax.axis_size("span"), args[0].shape[2]
    halves = count & (count - 1) == 0 and lax.axis_size("elem") in (1, 2, 4, 8, 16)
    if halves and count > 2 and dof_dev % (count * LANES) == 0 and dof_dev > 2 * count * LANES:
        return tiled_device(*args)
    return on_device(*args)


def solution(mesh):
    return jax.shard_map(
        by_shape,
        mesh=mesh,
        in_specs=(
            P("span", None, "elem"),
            P("span", None, "elem"),
            P("span", None, "elem"),
            P("elem"),
            P("elem"),
            P("elem"),
            P("elem"),
            P("elem"),
            P("span", None, None),
        ),
        out_specs=(P("span", None, "elem"), P("span", None, "elem"), P("span", None)),
        check_vma=False,
    )
```

```python
import math

import jax
import jax.numpy as jnp
from jax import lax
from jax.experimental import pallas as pl
from jax.experimental.pallas import tpu as pltpu
from jax.sharding import PartitionSpec as P

REACH = 8
LANES = 128
ROWS = 8
VMEM_LIMIT = 24 * 1024 * 1024
HIGHEST = lax.Precision.HIGHEST


def fourier_rows(count):
    row = jnp.arange(count)[:, None]
    col = jnp.arange(count)[None, :]
    half = count // 2
    wave = jnp.where(row <= half, row, row - half)
    phase = (wave * col % count).astype(jnp.float32) * (2.0 * math.pi / count)
    scaled = jnp.where(row <= half, jnp.cos(phase), jnp.sin(phase)) * math.sqrt(2.0 / count)
    edge = (row == 0) | (row == half)
    matrix = jnp.where(edge, jnp.cos(phase) * math.sqrt(1.0 / count), scaled)
    slots = jnp.arange(count)
    slot_wave = jnp.where(slots <= half, slots, slots - half)
    cosines = jnp.cos(slot_wave.astype(jnp.float32) * (2.0 * math.pi / count))
    return (matrix, cosines)


def along_spans(matrix, block):
    shape = block.shape
    flat = block.reshape(shape[0], -1)
    return jnp.dot(matrix, flat, precision=HIGHEST).reshape(shape)


def spread(block, count):
    rows, dofs = block.shape
    return block.reshape(rows, count, dofs // count).transpose(1, 0, 2)


def collect(pieces):
    count, rows, dofs = pieces.shape
    return pieces.transpose(1, 0, 2).reshape(1, rows, count * dofs)


def exchange(pieces):
    return lax.all_to_all(pieces, "span", split_axis=0, concat_axis=0, tiled=True)


def to_next(cells, step):
    count, parts = lax.axis_size("span"), lax.axis_size("elem")
    line = [s * parts + e for e in range(parts) for s in range(count)]
    pairs = list(zip(line, line[1:]))
    if step < 0:
        pairs = [(b, a) for a, b in pairs]
    return lax.ppermute(cells, ("span", "elem"), pairs)


def coefficients(ground, tension, stiff, offset, link, count, dofs):
    dof_dev = ground.shape[0]
    start = lax.axis_index("span") * dofs
    elem = lax.axis_index("elem")
    dof_all = dof_dev * lax.axis_size("elem")
    position = elem * dof_dev + jnp.arange(dof_dev)
    distance = jnp.arange(1, REACH + 1)[:, None]
    weights = jnp.where((offset == distance) & (position + distance < dof_all), stiff, 0.0)
    wire = jnp.where((distance == 1) & (position < dof_all - 1), tension, 0.0)
    weights = weights + wire
    pairs = [(i, i + 1) for i in range(lax.axis_size("elem") - 1)]
    left = lax.ppermute(weights[:, dof_dev - REACH :], "elem", pairs)
    weights = jnp.concatenate([left, weights], 1)
    weights = lax.dynamic_slice_in_dim(weights, start, dofs + REACH, 1)
    ground = lax.dynamic_slice_in_dim(ground, start, dofs, 0)
    link = lax.dynamic_slice_in_dim(link, start, dofs, 0)
    return weights, ground, link


def add_up(terms):
    total = terms[0]
    for term in terms[1:]:
        total = total + term
    return total


def scaled(factor, value):
    if abs(factor - 1.0) < 1e-12:
        return value
    return value * factor


def cosine_sums(a):
    n = len(a) - 1
    if n == 1:
        return [a[0] + a[1], a[0] - a[1]]
    half = n // 2
    even = cosine_sums([a[s] + a[n - s] for s in range(half)] + [a[half]])
    diff = [a[s] - a[n - s] for s in range(half)]
    out = [None] * (n + 1)
    out[0::2] = even
    for j in range(1, n, 2):
        out[j] = add_up([scaled(math.cos(math.pi * j * s / n), diff[s]) for s in range(half)])
    return out


def sine_sums(b):
    n = len(b) + 1
    if n == 1:
        return []
    half = n // 2
    at = [None] + list(b)
    even = sine_sums([at[s] - at[n - s] for s in range(1, half)])
    total = [None] + [at[s] + at[n - s] for s in range(1, half)] + [at[half]]
    out = [None] * (n + 1)
    for k, value in enumerate(even):
        out[2 * k + 2] = value
    for j in range(1, n, 2):
        terms = [(math.sin(math.pi * j * s / n), total[s]) for s in range(1, half + 1)]
        terms = [scaled(abs(f), t) if f > 0 else -scaled(abs(f), t) for f, t in terms]
        out[j] = add_up(terms)
    return out[1:n]


def slot_scales(count):
    edge, inner = math.sqrt(1.0 / count), math.sqrt(2.0 / count)
    return [edge if j in (0, count // 2) else inner for j in range(count)]


def to_slots(x):
    n = len(x)
    half = n // 2
    plus = [x[0]] + [x[s] + x[n - s] for s in range(1, half)] + [x[half]]
    minus = [x[s] - x[n - s] for s in range(1, half)]
    return cosine_sums(plus) + sine_sums(minus)


def to_spans(y):
    n = len(y)
    half = n // 2
    even = cosine_sums(y[: half + 1])
    odd = [None] + sine_sums(y[half + 1 :])
    out = [None] * n
    out[0], out[half] = even[0], even[half]
    for s in range(1, half):
        out[s] = even[s] + odd[s]
        out[n - s] = even[s] - odd[s]
    return out


def params(**kw):
    return pltpu.CompilerParams(vmem_limit_bytes=VMEM_LIMIT, **kw)


def spread_blocks(blocks, count, ranges):
    _, rows, dof_dev = blocks[0].shape
    dofs = dof_dev // count
    kinds = len(blocks)
    shape = (count, kinds * rows, sum(width for _, width in ranges))
    many = kinds * len(ranges)

    def kernel(*refs):
        out, held, come, go = refs[kinds:]
        arrivals = []
        for i in range(count):
            group, to = [], 0
            for first, width in ranges:
                for k in range(kinds):
                    copy = pltpu.make_async_copy(
                        refs[k].at[0, :, i * dofs + first : i * dofs + first + width],
                        held.at[i, k * rows : (k + 1) * rows, to : to + width],
                        come.at[i * many + len(group)],
                    )
                    copy.start()
                    group.append(copy)
                to += width
            arrivals.append(group)
        leaving = []
        for i, group in enumerate(arrivals):
            for copy in group:
                copy.wait()
            piece = pltpu.make_async_copy(held.at[i], out.at[i], go.at[i])
            piece.start()
            leaving.append(piece)
        for piece in leaving:
            piece.wait()

    whole = pl.BlockSpec(memory_space=pltpu.HBM)
    return pl.pallas_call(
        kernel,
        in_specs=[whole] * kinds,
        out_specs=whole,
        out_shape=pltpu.HBM(shape, jnp.float32),
        scratch_shapes=[
            pltpu.VMEM(shape, jnp.float32),
            pltpu.SemaphoreType.DMA((count * many,)),
            pltpu.SemaphoreType.DMA((count,)),
        ],
        compiler_params=pltpu.CompilerParams(vmem_limit_bytes=60 * 1024 * 1024),
        name="spread_blocks",
    )(*blocks)


def collect_early(early, middle):
    count, rows, early_width = early.shape
    dofs = early_width + LANES
    many = max(n for n in (1, 2, 4, 8) if count % n == 0)

    def kernel(first, block):
        for i in range(many):
            at = i * dofs
            block[0, :, at : at + middle] = first[i, :, :middle]
            block[0, :, at + middle + LANES : at + dofs] = first[i, :, middle:]

    return pl.pallas_call(
        kernel,
        grid=(count // many,),
        in_specs=[pl.BlockSpec((many, rows, early_width), lambda i: (i, 0, 0))],
        out_specs=pl.BlockSpec((1, rows, many * dofs), lambda i: (0, 0, i)),
        out_shape=pltpu.HBM((1, rows, count * dofs), jnp.float32),
        compiler_params=params(),
        name="collect_early",
    )(early)


def collect_late(late, block, middle):
    count, rows, width = late.shape
    dofs = width - LANES
    many = max(n for n in (1, 2, 4, 8) if count % n == 0)

    def kernel(last, _, residual, whole, sem):
        copies = []
        for i in range(many):
            at = (pl.program_id(0) * many + i) * dofs + middle
            copy = pltpu.make_async_copy(
                last.at[i, :, pl.ds(dofs, LANES)],
                whole.at[0, :, pl.ds(pl.multiple_of(at, LANES), LANES)],
                sem.at[i],
            )
            copy.start()
            copies.append(copy)
        for i in range(many):
            residual[0, :, i * dofs : (i + 1) * dofs] = last[i, :, :dofs]
        for copy in copies:
            copy.wait()

    place = pl.BlockSpec(memory_space=pltpu.HBM)
    shape = pltpu.HBM((1, rows, count * dofs), jnp.float32)
    return pl.pallas_call(
        kernel,
        grid=(count // many,),
        in_specs=[pl.BlockSpec((many, rows, width), lambda i: (i, 0, 0)), place],
        out_specs=[pl.BlockSpec((1, rows, many * dofs), lambda i: (0, 0, i)), place],
        out_shape=[shape, shape],
        input_output_aliases={1: 1},
        scratch_shapes=[pltpu.SemaphoreType.DMA((many,))],
        compiler_params=params(),
        name="collect_late",
    )(late, block)


PARTS = 3


def bf16_parts(value):
    parts = []
    for i in range(PARTS):
        parts.append(value.astype(jnp.bfloat16))
        if i < PARTS - 1:
            value = value - parts[i].astype(jnp.float32)
    return parts


def project(stacked, rotation, dofs, tiles, prior=None):
    count, wide, _ = stacked.shape
    rows = rotation.shape[1]
    width = len(tiles) * LANES
    scales = slot_scales(count)
    groups = -(-count * REACH // LANES)
    per = LANES // REACH
    strip = 2 * ROWS

    def kernel(x, rot, *refs):
        refs = refs[1:] if prior is not None else refs
        proj, back = refs[:2]
        edges, scratch = (refs[2:4], refs[4:]) if prior is None else ((), refs[2:])
        held, split_rot, mine, sent, come, go = scratch[:6]
        split_slots = scratch[6:]
        arrivals = []
        for c in range(len(tiles)):
            copy = pltpu.make_async_copy(
                x.at[:, :, c * LANES : (c + 1) * LANES], held.at[c], come.at[c]
            )
            copy.start()
            arrivals.append(copy)

        def one(j, carry):
            for i, part in enumerate(bf16_parts(rot[j])):
                split_rot[j, i * rows : (i + 1) * rows, :] = part
            return carry

        lax.fori_loop(0, count, one, 0)
        for c, copy in enumerate(arrivals):
            copy.wait()

            def transform(r, carry, c=c):
                at = pl.ds(pl.multiple_of(r * strip, strip), strip)
                halves = []
                for h in range(2):
                    own = pl.ds(pl.multiple_of(r * strip + h * ROWS, ROWS), ROWS)
                    halves.append(to_slots([held[c, s, own, :] for s in range(count)]))
                for j in range(count):
                    value = jnp.concatenate([half[j] for half in halves], 0)
                    for part, ref in zip(bf16_parts(value), split_slots):
                        ref[j, at, c * LANES : (c + 1) * LANES] = part
                return carry

            lax.fori_loop(0, wide // strip, transform, 0)
        for j in range(count):
            total = None
            for i in range(PARTS - 1, -1, -1):
                terms = PARTS - i
                stacked_terms = jnp.dot(
                    split_rot[j, : terms * rows, :],
                    split_slots[i][j],
                    preferred_element_type=jnp.float32,
                )
                for q in range(terms - 1, -1, -1):
                    term = stacked_terms[q * rows : (q + 1) * rows]
                    total = term if total is None else total + term
            mine[j] = total
        leaving = []

        def leave(source, target, c, t, at):
            copy = pltpu.make_async_copy(
                source.at[:, :, c * LANES : (c + 1) * LANES],
                target.at[:, :, t * LANES : (t + 1) * LANES],
                go.at[at],
            )
            copy.start()
            leaving.append(copy)

        for c, t in enumerate(tiles):
            leave(mine, proj, c, t, c)
        for c in range(len(tiles)):
            lanes = slice(c * LANES, (c + 1) * LANES)

            def inverse(r, carry, lanes=lanes):
                at = pl.ds(pl.multiple_of(r * ROWS, ROWS), ROWS)
                out = to_spans([mine[j, at, lanes] * scales[j] for j in range(count)])
                for s in range(count):
                    sent[s, at, lanes] = out[s]
                return carry

            lax.fori_loop(0, rows // ROWS, inverse, 0)
            leave(sent, back, c, c, len(tiles) + c)
        lane = lax.broadcasted_iota(jnp.int32, (rows, LANES), 1)
        ends = ((0, 0), (len(tiles) - 1, LANES - REACH))
        for ref, (c, start) in zip(edges, ends):
            for g in range(groups):
                packed = jnp.zeros((rows, LANES), jnp.float32)
                for k in range(min(per, count - g * per)):
                    turn = (k * REACH - start) % LANES
                    value = mine[g * per + k, :, c * LANES : (c + 1) * LANES]
                    value = pltpu.roll(value, turn, 1) if turn else value
                    packed = jnp.where(lane // REACH == k, value, packed)
                ref[g] = packed
        for copy in leaving:
            copy.wait()

    whole = pl.BlockSpec(memory_space=pltpu.HBM)
    vmem = pl.BlockSpec(memory_space=pltpu.VMEM)
    field = pltpu.HBM((count, rows, dofs), jnp.float32)
    edge = jax.ShapeDtypeStruct((groups, rows, LANES), jnp.float32)
    sending = pltpu.HBM((count, rows, width), jnp.float32)
    first = prior is None
    passes = PARTS * (PARTS + 1) // 2
    cost = pl.CostEstimate(
        flops=2 * passes * count * wide * rows * width,
        bytes_accessed=4 * count * (wide + 2 * rows) * width,
        transcendentals=0,
    )
    return pl.pallas_call(
        kernel,
        in_specs=[whole, vmem] + ([] if first else [whole]),
        out_specs=[whole, whole] + ([vmem, vmem] if first else []),
        out_shape=[field, sending] + ([edge, edge] if first else []),
        input_output_aliases={} if first else {2: 0},
        cost_estimate=cost,
        scratch_shapes=[
            pltpu.VMEM((len(tiles), count, wide, LANES), jnp.float32),
            pltpu.VMEM((count, PARTS * rows, wide), jnp.bfloat16),
            pltpu.VMEM((count, rows, width), jnp.float32),
            pltpu.VMEM((count, rows, width), jnp.float32),
            pltpu.SemaphoreType.DMA((len(tiles),)),
            pltpu.SemaphoreType.DMA((2 * len(tiles),)),
        ]
        + [pltpu.VMEM((count, wide, width), jnp.bfloat16)] * PARTS,
        compiler_params=params(),
        name="project",
    )(stacked, rotation, *(() if first else (prior,)))


def stiffness(projected, before, after, bands, links):
    count, rows, dofs = projected.shape
    per = LANES // REACH
    tiles = dofs // LANES

    def kernel(x, left, right, band, lam, stiff, sums, energy, norm, matrix):
        row = lax.broadcasted_iota(jnp.int32, (LANES, LANES), 0)
        gap = row - lax.broadcasted_iota(jnp.int32, (LANES, LANES), 1)
        for t in range(tiles):
            at = slice(t * LANES, (t + 1) * LANES)
            here = jnp.where(gap == 0, band[16:17, at], 0.0)
            halo = jnp.zeros((LANES, LANES), jnp.float32)
            for d in range(1, REACH + 1):
                up, down = band[d - 1 : d, at], band[REACH + d - 1 : REACH + d, at]
                here = jnp.where(gap == d, -up, here)
                here = jnp.where(gap == -d, -down, here)
                halo = jnp.where(gap == d - LANES, -up, halo)
                halo = jnp.where(gap == LANES - d, -down, halo)
            matrix[t, :LANES, :] = here
            matrix[t, LANES:, :] = halo
        lane = lax.broadcasted_iota(jnp.int32, (rows, LANES), 1)

        def slot(j, carry):
            to = pl.ds(pl.multiple_of(j * rows, rows), rows)
            g, k = j // per, j % per
            low = pltpu.roll(left[g], (2 * LANES - REACH - REACH * k) % LANES, 1)
            high = pltpu.roll(right[g], (LANES - REACH * k) % LANES, 1)
            work = jnp.zeros((rows, LANES), jnp.float32)
            size = jnp.zeros((rows, LANES), jnp.float32)
            for t in range(tiles):
                at = slice(t * LANES, (t + 1) * LANES)
                here = x[j, :, at]
                previous = low if t == 0 else x[j, :, (t - 1) * LANES : t * LANES]
                following = high if t == tiles - 1 else x[j, :, (t + 1) * LANES : (t + 2) * LANES]
                halo = jnp.where(lane < LANES // 2, following, previous)
                total = jnp.dot(
                    jnp.concatenate([here, halo], 1),
                    matrix[t],
                    precision=HIGHEST,
                    preferred_element_type=jnp.float32,
                )
                total = total + (lam[j] * band[17:18, at]) * here
                stiff[j, :, at] = total
                work = work + total * here
                size = size + here * here
            energy[to, :] = work
            norm[to, :] = size
            return carry

        lax.fori_loop(0, count, slot, 0)
        ones = jnp.ones((ROWS, LANES), jnp.float32)
        for r, part in enumerate((energy, norm)):
            line = lax.dot_general(
                ones,
                part[...],
                (((1,), (1,)), ((), ())),
                precision=HIGHEST,
                preferred_element_type=jnp.float32,
            )
            sums[r : r + 1, :] = line[:1]

    vmem = pl.BlockSpec(memory_space=pltpu.VMEM)
    return pl.pallas_call(
        kernel,
        in_specs=[vmem, vmem, vmem, vmem, pl.BlockSpec(memory_space=pltpu.SMEM)],
        out_specs=[vmem, vmem],
        out_shape=[
            jax.ShapeDtypeStruct((count, rows, dofs), jnp.float32),
            jax.ShapeDtypeStruct((2, count * rows), jnp.float32),
        ],
        scratch_shapes=[
            pltpu.VMEM((count * rows, LANES), jnp.float32),
            pltpu.VMEM((count * rows, LANES), jnp.float32),
            pltpu.VMEM((tiles, 2 * LANES, LANES), jnp.float32),
        ],
        compiler_params=params(),
        name="stiffness",
    )(projected, before, after, bands, links)


def residual_back(projected, stiff, sums, late):
    count, rows, dofs = projected.shape
    scales = slot_scales(count)

    tiles = dofs // LANES

    def kernel(x, kx, total, extra, back, ritz, wide):
        @pl.when(pl.program_id(0) == 0)
        def _():
            value = total[0:1, :] / (total[1:2, :] + 1e-06)
            ritz[...] = value
            row = lax.broadcasted_iota(jnp.int32, (ROWS, count * rows), 0)
            first = jnp.where(row == 0, value, 0.0)
            ones = jnp.ones((ROWS, LANES), jnp.float32)
            spread_out = lax.dot_general(
                first,
                ones,
                (((0,), (0,)), ((), ())),
                precision=HIGHEST,
                preferred_element_type=jnp.float32,
            )
            wide[...] = spread_out

        def strip(r, carry):
            at = pl.ds(pl.multiple_of(r * ROWS, ROWS), ROWS)
            terms = []
            for j in range(count):
                to = pl.ds(pl.multiple_of(j * rows + r * ROWS, ROWS), ROWS)
                terms.append((kx[j, at, :] - wide[to, :] * x[j, at, :]) * scales[j])
            out = to_spans(terms)
            for s in range(count):
                back[s, at, :] = out[s]
            return carry

        @pl.when(pl.program_id(0) < tiles)
        def _():
            lax.fori_loop(0, rows // ROWS, strip, 0)

        @pl.when(pl.program_id(0) == tiles)
        def _():
            back[...] = extra[...]

    inner = pl.BlockSpec((count, rows, LANES), lambda t: (0, 0, jnp.minimum(t, tiles - 1)))
    cell = pl.BlockSpec((count, rows, LANES), lambda t: (0, 0, t))
    return pl.pallas_call(
        kernel,
        grid=(tiles + 1,),
        in_specs=[
            inner,
            inner,
            pl.BlockSpec((2, count * rows), lambda t: (0, 0)),
            pl.BlockSpec((count, rows, LANES), lambda t: (0, 0, 0)),
        ],
        out_specs=[cell, pl.BlockSpec((1, count * rows), lambda t: (0, 0))],
        out_shape=[
            pltpu.HBM((count, rows, dofs + LANES), jnp.float32),
            jax.ShapeDtypeStruct((1, count * rows), jnp.float32),
        ],
        scratch_shapes=[pltpu.VMEM((count * rows, LANES), jnp.float32)],
        compiler_params=params(),
        name="residual_back",
    )(projected, stiff, sums, late)


def halvings(axis):
    step = lax.axis_size(axis) // 2
    while step:
        yield step, [(i, i ^ step) for i in range(lax.axis_size(axis))]
        step //= 2


def exchange_step(held, step, pairs):
    other = lax.ppermute(held, "span", pairs)
    upper = (lax.axis_index("span") & step) != 0
    return jnp.stack([jnp.where(upper, other, held), jnp.where(upper, held, other)])


def exchange_bits(held, steps):
    bits = len(steps)
    tail = held.shape[1:]
    held = held.reshape((2,) * bits + tail)

    def halves(held, step, d):
        upper = (lax.axis_index("span") & step) != 0
        low, high = (lax.index_in_dim(held, side, d, keepdims=False) for side in (0, 1))
        return jnp.where(upper, high, low), jnp.where(upper, low, high)

    def join(mine, other, step, pairs, d):
        upper = (lax.axis_index("span") & step) != 0
        got = lax.ppermute(other, "span", pairs)
        return jnp.stack([jnp.where(upper, got, mine), jnp.where(upper, mine, got)], d)

    near = steps[::-1]
    for k, (step, pairs) in enumerate(near[:-1]):
        d = bits - 1 - k
        held = join(*halves(held, step, d), step, pairs, d)
    step, pairs = near[-1]
    mine, other = halves(held, step, 0)

    def finish(mine, other):
        return join(mine, other, step, pairs, 0).reshape((-1,) + tail)

    return mine, other, finish


def in_order(held, steps):
    bits = [step for step, _ in steps][::-1]
    order = tuple(sorted(range(len(bits)), key=lambda d: -bits[d]))
    held = held.transpose(order + tuple(range(len(bits), held.ndim)))
    return held.reshape((-1,) + held.shape[len(bits) :])


def tiled_device(
    current_block,
    search_block,
    previous_block,
    ground_spring,
    wire_tension,
    dropper_stiff,
    dropper_offset,
    span_link,
    ritz_rotation,
):
    count = lax.axis_size("span")
    dofs = current_block.shape[2] // count
    rows = current_block.shape[1]
    steps = list(halvings("span"))
    tiles = list(range(dofs // LANES))
    middle = tiles[len(tiles) // 2]
    early = [t for t in tiles if t != middle]
    at = middle * LANES
    blocks = (current_block, search_block, previous_block)
    rotation = exchange_step(ritz_rotation[0].T, *steps[0])
    pieces = spread_blocks(blocks, count, [(0, at), (at + LANES, dofs - at - LANES)])
    pieces, rotation = lax.optimization_barrier((pieces, rotation))
    stacked = exchange(pieces)
    order = steps[2:] + steps[1:2]
    for step, pairs in order:
        rotation = exchange_step(rotation, step, pairs)
    rotation = in_order(rotation, [steps[0]] + order)
    scales = jnp.array(slot_scales(count), jnp.float32)[:, None, None]
    rotation = rotation * scales
    pieces = spread_blocks(blocks, count, [(at, LANES)])
    mine, other, finish = exchange_bits(pieces, steps)
    rotation, mine, other = lax.optimization_barrier((rotation, mine, other))
    stacked_late = finish(mine, other)
    weights, ground, link = coefficients(
        ground_spring, wire_tension, dropper_stiff, dropper_offset, span_link, count, dofs
    )
    up = weights[:, REACH:]
    down = [weights[d - 1, REACH - d : REACH - d + dofs] for d in range(1, REACH + 1)]
    down = jnp.stack(down)
    diagonal = ground + jnp.sum(up, 0) + jnp.sum(down, 0)
    bands = jnp.concatenate([up, down, diagonal[None], link[None]])
    links = 2.0 * (1.0 - fourier_rows(count)[1])
    projected, spans, head, tail = project(stacked, rotation, dofs, early)
    before, after = to_next(tail, 1), to_next(head, -1)
    spans, before, after = lax.optimization_barrier((spans, before, after))
    early_pieces = exchange(spans)
    projected, late = project(stacked_late, rotation, dofs, [middle], projected)
    stiff, sums = stiffness(projected, before, after, bands, links)
    for _, pairs in halvings("elem"):
        sums = sums + lax.ppermute(sums, "elem", pairs)
    for _, pairs in steps[::-1]:
        sums = sums + lax.ppermute(sums, "span", pairs)
    spans, ritz = residual_back(projected, stiff, sums, late)
    next_block = collect_early(early_pieces, at)
    next_residual, next_block = collect_late(exchange(spans), next_block, at)
    ritz = lax.dynamic_slice_in_dim(ritz, lax.axis_index("span") * rows, rows, 1)
    return (next_block, next_residual, ritz)


def on_device(
    current_block,
    search_block,
    previous_block,
    ground_spring,
    wire_tension,
    dropper_stiff,
    dropper_offset,
    span_link,
    ritz_rotation,
):
    count = lax.axis_size("span")
    dof_dev = current_block.shape[2]
    dofs = dof_dev // count
    matrix, cosines = fourier_rows(count)
    blocks = (current_block, search_block, previous_block)
    stacked = exchange(jnp.concatenate([spread(b[0], count) for b in blocks], 1))
    rotation = lax.all_gather(ritz_rotation, "span", axis=0, tiled=True)
    weights, ground, link = coefficients(
        ground_spring, wire_tension, dropper_stiff, dropper_offset, span_link, count, dofs
    )
    slots = along_spans(matrix, stacked)
    projected = jnp.einsum("jvm,jvd->jmd", rotation, slots, precision=HIGHEST)
    back = matrix.T
    next_block = collect(exchange(along_spans(back, projected)))
    before = to_next(projected[:, :, dofs - REACH :], 1)
    after = to_next(projected[:, :, :REACH], -1)
    wide = jnp.concatenate([before, projected, after], 2)
    stiff = ground * projected
    near = wide[:, :, : REACH + dofs]
    for distance in range(1, REACH + 1):
        flux = weights[distance - 1] * (near - wide[:, :, distance : distance + REACH + dofs])
        stiff = stiff + flux[:, :, REACH:] - flux[:, :, REACH - distance : REACH - distance + dofs]
    stiff = stiff + (2.0 * (1.0 - cosines))[:, None, None] * link * projected
    sums = jnp.stack([jnp.sum(projected * stiff, 2), jnp.sum(projected * projected, 2)])
    sums = lax.psum(sums, ("elem", "span"))
    ritz = sums[0] / (sums[1] + 1e-06)
    residual = stiff - ritz[:, :, None] * projected
    next_residual = collect(exchange(along_spans(back, residual)))
    my_ritz = lax.dynamic_slice_in_dim(ritz, lax.axis_index("span"), 1, 0)
    return (next_block, next_residual, my_ritz)


def by_shape(*args):
    count, dof_dev = lax.axis_size("span"), args[0].shape[2]
    halves = count & (count - 1) == 0 and lax.axis_size("elem") in (1, 2, 4, 8, 16)
    if halves and count > 2 and dof_dev % (count * LANES) == 0 and dof_dev > 2 * count * LANES:
        return tiled_device(*args)
    return on_device(*args)


def solution(mesh):
    return jax.shard_map(
        by_shape,
        mesh=mesh,
        in_specs=(
            P("span", None, "elem"),
            P("span", None, "elem"),
            P("span", None, "elem"),
            P("elem"),
            P("elem"),
            P("elem"),
            P("elem"),
            P("elem"),
            P("span", None, None),
        ),
        out_specs=(P("span", None, "elem"), P("span", None, "elem"), P("span", None)),
        check_vma=False,
    )
```

```python
import math

import jax
import jax.numpy as jnp
from jax import lax
from jax.experimental import pallas as pl
from jax.experimental.pallas import tpu as pltpu
from jax.sharding import PartitionSpec as P

REACH = 8
LANES = 128
ROWS = 8
VMEM_LIMIT = 24 * 1024 * 1024
VMEM_MOST = 61_500_000
HIGHEST = lax.Precision.HIGHEST


def fourier_rows(count):
    row = jnp.arange(count)[:, None]
    col = jnp.arange(count)[None, :]
    half = count // 2
    wave = jnp.where(row <= half, row, row - half)
    phase = (wave * col % count).astype(jnp.float32) * (2.0 * math.pi / count)
    scaled = jnp.where(row <= half, jnp.cos(phase), jnp.sin(phase)) * math.sqrt(2.0 / count)
    edge = (row == 0) | (row == half)
    matrix = jnp.where(edge, jnp.cos(phase) * math.sqrt(1.0 / count), scaled)
    slots = jnp.arange(count)
    slot_wave = jnp.where(slots <= half, slots, slots - half)
    cosines = jnp.cos(slot_wave.astype(jnp.float32) * (2.0 * math.pi / count))
    return (matrix, cosines)


def along_spans(matrix, block):
    shape = block.shape
    flat = block.reshape(shape[0], -1)
    return jnp.dot(matrix, flat, precision=HIGHEST).reshape(shape)


def spread(block, count):
    rows, dofs = block.shape
    return block.reshape(rows, count, dofs // count).transpose(1, 0, 2)


def collect(pieces):
    count, rows, dofs = pieces.shape
    return pieces.transpose(1, 0, 2).reshape(1, rows, count * dofs)


def exchange(pieces):
    return lax.all_to_all(pieces, "span", split_axis=0, concat_axis=0, tiled=True)


def to_next(cells, step):
    count, parts = lax.axis_size("span"), lax.axis_size("elem")
    line = [s * parts + e for e in range(parts) for s in range(count)]
    pairs = list(zip(line, line[1:]))
    if step < 0:
        pairs = [(b, a) for a, b in pairs]
    return lax.ppermute(cells, ("span", "elem"), pairs)


def coefficients(ground, tension, stiff, offset, link, count, dofs):
    dof_dev = ground.shape[0]
    start = lax.axis_index("span") * dofs
    elem = lax.axis_index("elem")
    dof_all = dof_dev * lax.axis_size("elem")
    position = elem * dof_dev + jnp.arange(dof_dev)
    distance = jnp.arange(1, REACH + 1)[:, None]
    weights = jnp.where((offset == distance) & (position + distance < dof_all), stiff, 0.0)
    wire = jnp.where((distance == 1) & (position < dof_all - 1), tension, 0.0)
    weights = weights + wire
    pairs = [(i, i + 1) for i in range(lax.axis_size("elem") - 1)]
    left = lax.ppermute(weights[:, dof_dev - REACH :], "elem", pairs)
    weights = jnp.concatenate([left, weights], 1)
    weights = lax.dynamic_slice_in_dim(weights, start, dofs + REACH, 1)
    ground = lax.dynamic_slice_in_dim(ground, start, dofs, 0)
    link = lax.dynamic_slice_in_dim(link, start, dofs, 0)
    return weights, ground, link


def add_up(terms):
    total = terms[0]
    for term in terms[1:]:
        total = total + term
    return total


def scaled(factor, value):
    if abs(factor - 1.0) < 1e-12:
        return value
    return value * factor


def cosine_sums(a):
    n = len(a) - 1
    if n == 1:
        return [a[0] + a[1], a[0] - a[1]]
    half = n // 2
    even = cosine_sums([a[s] + a[n - s] for s in range(half)] + [a[half]])
    diff = [a[s] - a[n - s] for s in range(half)]
    out = [None] * (n + 1)
    out[0::2] = even
    for j in range(1, n, 2):
        out[j] = add_up([scaled(math.cos(math.pi * j * s / n), diff[s]) for s in range(half)])
    return out


def sine_sums(b):
    n = len(b) + 1
    if n == 1:
        return []
    half = n // 2
    at = [None] + list(b)
    even = sine_sums([at[s] - at[n - s] for s in range(1, half)])
    total = [None] + [at[s] + at[n - s] for s in range(1, half)] + [at[half]]
    out = [None] * (n + 1)
    for k, value in enumerate(even):
        out[2 * k + 2] = value
    for j in range(1, n, 2):
        terms = [(math.sin(math.pi * j * s / n), total[s]) for s in range(1, half + 1)]
        terms = [scaled(abs(f), t) if f > 0 else -scaled(abs(f), t) for f, t in terms]
        out[j] = add_up(terms)
    return out[1:n]


def slot_scales(count):
    edge, inner = math.sqrt(1.0 / count), math.sqrt(2.0 / count)
    return [edge if j in (0, count // 2) else inner for j in range(count)]


def to_slots(x):
    n = len(x)
    half = n // 2
    plus = [x[0]] + [x[s] + x[n - s] for s in range(1, half)] + [x[half]]
    minus = [x[s] - x[n - s] for s in range(1, half)]
    return cosine_sums(plus) + sine_sums(minus)


def to_spans(y):
    n = len(y)
    half = n // 2
    even = cosine_sums(y[: half + 1])
    odd = [None] + sine_sums(y[half + 1 :])
    out = [None] * n
    out[0], out[half] = even[0], even[half]
    for s in range(1, half):
        out[s] = even[s] + odd[s]
        out[n - s] = even[s] - odd[s]
    return out


def params(limit=VMEM_LIMIT):
    return pltpu.CompilerParams(vmem_limit_bytes=limit)


def spread_blocks(blocks, count, ranges):
    _, rows, dof_dev = blocks[0].shape
    dofs = dof_dev // count
    kinds = len(blocks)
    shape = (count, kinds * rows, sum(width for _, width in ranges))
    many = kinds * len(ranges)

    def kernel(*refs):
        out, held, come, go = refs[kinds:]
        arrivals = []
        for i in range(count):
            group, to = [], 0
            for first, width in ranges:
                for k in range(kinds):
                    copy = pltpu.make_async_copy(
                        refs[k].at[0, :, i * dofs + first : i * dofs + first + width],
                        held.at[i, k * rows : (k + 1) * rows, to : to + width],
                        come.at[i * many + len(group)],
                    )
                    copy.start()
                    group.append(copy)
                to += width
            arrivals.append(group)
        leaving = []
        for i, group in enumerate(arrivals):
            for copy in group:
                copy.wait()
            piece = pltpu.make_async_copy(held.at[i], out.at[i], go.at[i])
            piece.start()
            leaving.append(piece)
        for piece in leaving:
            piece.wait()

    whole = pl.BlockSpec(memory_space=pltpu.HBM)
    return pl.pallas_call(
        kernel,
        in_specs=[whole] * kinds,
        out_specs=whole,
        out_shape=pltpu.HBM(shape, jnp.float32),
        scratch_shapes=[
            pltpu.VMEM(shape, jnp.float32),
            pltpu.SemaphoreType.DMA((count * many,)),
            pltpu.SemaphoreType.DMA((count,)),
        ],
        compiler_params=params(VMEM_MOST),
        name="spread_blocks",
    )(*blocks)


def collect_early(early, middle):
    count, rows, early_width = early.shape
    dofs = early_width + LANES
    many = max(n for n in (1, 2, 4, 8) if count % n == 0)

    def kernel(first, block):
        for i in range(many):
            at = i * dofs
            block[0, :, at : at + middle] = first[i, :, :middle]
            block[0, :, at + middle + LANES : at + dofs] = first[i, :, middle:]

    return pl.pallas_call(
        kernel,
        grid=(count // many,),
        in_specs=[pl.BlockSpec((many, rows, early_width), lambda i: (i, 0, 0))],
        out_specs=pl.BlockSpec((1, rows, many * dofs), lambda i: (0, 0, i)),
        out_shape=pltpu.HBM((1, rows, count * dofs), jnp.float32),
        compiler_params=params(VMEM_MOST),
        name="collect_early",
    )(early)


def collect_late(late, block, middle):
    count, rows, width = late.shape
    dofs = width - LANES
    many = max(n for n in (1, 2, 4, 8) if count % n == 0)

    def kernel(last, _, residual, whole, sem):
        copies = []
        for i in range(many):
            at = (pl.program_id(0) * many + i) * dofs + middle
            copy = pltpu.make_async_copy(
                last.at[i, :, pl.ds(dofs, LANES)],
                whole.at[0, :, pl.ds(pl.multiple_of(at, LANES), LANES)],
                sem.at[i],
            )
            copy.start()
            copies.append(copy)
        for i in range(many):
            residual[0, :, i * dofs : (i + 1) * dofs] = last[i, :, :dofs]
        for copy in copies:
            copy.wait()

    place = pl.BlockSpec(memory_space=pltpu.HBM)
    shape = pltpu.HBM((1, rows, count * dofs), jnp.float32)
    return pl.pallas_call(
        kernel,
        grid=(count // many,),
        in_specs=[pl.BlockSpec((many, rows, width), lambda i: (i, 0, 0)), place],
        out_specs=[pl.BlockSpec((1, rows, many * dofs), lambda i: (0, 0, i)), place],
        out_shape=[shape, shape],
        input_output_aliases={1: 1},
        scratch_shapes=[pltpu.SemaphoreType.DMA((many,))],
        compiler_params=params(),
        name="collect_late",
    )(late, block)


PARTS = 3


def bf16_parts(value):
    parts = []
    for i in range(PARTS):
        parts.append(value.astype(jnp.bfloat16))
        if i < PARTS - 1:
            value = value - parts[i].astype(jnp.float32)
    return parts


def project(stacked, rotation, dofs, tiles, prior=None):
    count, wide, _ = stacked.shape
    rows = rotation.shape[1]
    width = len(tiles) * LANES
    scales = slot_scales(count)
    groups = -(-count * REACH // LANES)
    per = LANES // REACH
    strip = 2 * ROWS

    def kernel(x, rot, *refs):
        refs = refs[1:] if prior is not None else refs
        proj, back = refs[:2]
        edges, scratch = (refs[2:4], refs[4:]) if prior is None else ((), refs[2:])
        held, split_rot, mine, sent, come, go = scratch[:6]
        split_slots = scratch[6:]
        arrivals = []
        for c in range(len(tiles)):
            copy = pltpu.make_async_copy(
                x.at[:, :, c * LANES : (c + 1) * LANES], held.at[c], come.at[c]
            )
            copy.start()
            arrivals.append(copy)

        def one(j, carry):
            for i, part in enumerate(bf16_parts(rot[j])):
                split_rot[j, i * rows : (i + 1) * rows, :] = part
            return carry

        lax.fori_loop(0, count, one, 0)
        for c, copy in enumerate(arrivals):
            copy.wait()

            def transform(r, carry, c=c):
                at = pl.ds(pl.multiple_of(r * strip, strip), strip)
                halves = []
                for h in range(2):
                    own = pl.ds(pl.multiple_of(r * strip + h * ROWS, ROWS), ROWS)
                    halves.append(to_slots([held[c, s, own, :] for s in range(count)]))
                for j in range(count):
                    value = jnp.concatenate([half[j] for half in halves], 0)
                    for part, ref in zip(bf16_parts(value), split_slots):
                        ref[j, at, c * LANES : (c + 1) * LANES] = part
                return carry

            lax.fori_loop(0, wide // strip, transform, 0)
        for j in range(count):
            total = None
            for i in range(PARTS - 1, -1, -1):
                terms = PARTS - i
                stacked_terms = jnp.dot(
                    split_rot[j, : terms * rows, :],
                    split_slots[i][j],
                    preferred_element_type=jnp.float32,
                )
                for q in range(terms - 1, -1, -1):
                    term = stacked_terms[q * rows : (q + 1) * rows]
                    total = term if total is None else total + term
            mine[j] = total
        leaving = []

        def leave(source, target, c, t, at):
            copy = pltpu.make_async_copy(
                source.at[:, :, c * LANES : (c + 1) * LANES],
                target.at[:, :, t * LANES : (t + 1) * LANES],
                go.at[at],
            )
            copy.start()
            leaving.append(copy)

        for c, t in enumerate(tiles):
            leave(mine, proj, c, t, c)
        for c in range(len(tiles)):
            lanes = slice(c * LANES, (c + 1) * LANES)

            def inverse(r, carry, lanes=lanes):
                at = pl.ds(pl.multiple_of(r * ROWS, ROWS), ROWS)
                out = to_spans([mine[j, at, lanes] * scales[j] for j in range(count)])
                for s in range(count):
                    sent[s, at, lanes] = out[s]
                return carry

            lax.fori_loop(0, rows // ROWS, inverse, 0)
            leave(sent, back, c, c, len(tiles) + c)
        lane = lax.broadcasted_iota(jnp.int32, (rows, LANES), 1)
        ends = ((0, 0), (len(tiles) - 1, LANES - REACH))
        for ref, (c, start) in zip(edges, ends):
            for g in range(groups):
                packed = jnp.zeros((rows, LANES), jnp.float32)
                for k in range(min(per, count - g * per)):
                    turn = (k * REACH - start) % LANES
                    value = mine[g * per + k, :, c * LANES : (c + 1) * LANES]
                    value = pltpu.roll(value, turn, 1) if turn else value
                    packed = jnp.where(lane // REACH == k, value, packed)
                ref[g] = packed
        for copy in leaving:
            copy.wait()

    whole = pl.BlockSpec(memory_space=pltpu.HBM)
    vmem = pl.BlockSpec(memory_space=pltpu.VMEM)
    field = pltpu.HBM((count, rows, dofs), jnp.float32)
    edge = jax.ShapeDtypeStruct((groups, rows, LANES), jnp.float32)
    sending = pltpu.HBM((count, rows, width), jnp.float32)
    first = prior is None
    passes = PARTS * (PARTS + 1) // 2
    cost = pl.CostEstimate(
        flops=2 * passes * count * wide * rows * width,
        bytes_accessed=4 * count * (wide + 2 * rows) * width,
        transcendentals=0,
    )
    return pl.pallas_call(
        kernel,
        in_specs=[whole, vmem] + ([] if first else [whole]),
        out_specs=[whole, whole] + ([vmem, vmem] if first else []),
        out_shape=[field, sending] + ([edge, edge] if first else []),
        input_output_aliases={} if first else {2: 0},
        cost_estimate=cost,
        scratch_shapes=[
            pltpu.VMEM((len(tiles), count, wide, LANES), jnp.float32),
            pltpu.VMEM((count, PARTS * rows, wide), jnp.bfloat16),
            pltpu.VMEM((count, rows, width), jnp.float32),
            pltpu.VMEM((count, rows, width), jnp.float32),
            pltpu.SemaphoreType.DMA((len(tiles),)),
            pltpu.SemaphoreType.DMA((2 * len(tiles),)),
        ]
        + [pltpu.VMEM((count, wide, width), jnp.bfloat16)] * PARTS,
        compiler_params=params(VMEM_MOST),
        name="project",
    )(stacked, rotation, *(() if first else (prior,)))


def stiffness(projected, before, after, bands, links):
    count, rows, dofs = projected.shape
    per = LANES // REACH
    tiles = dofs // LANES

    def kernel(x, left, right, band, lam, stiff, sums, energy, norm, matrix):
        row = lax.broadcasted_iota(jnp.int32, (LANES, LANES), 0)
        gap = row - lax.broadcasted_iota(jnp.int32, (LANES, LANES), 1)
        for t in range(tiles):
            at = slice(t * LANES, (t + 1) * LANES)
            here = jnp.where(gap == 0, band[16:17, at], 0.0)
            halo = jnp.zeros((LANES, LANES), jnp.float32)
            for d in range(1, REACH + 1):
                up, down = band[d - 1 : d, at], band[REACH + d - 1 : REACH + d, at]
                here = jnp.where(gap == d, -up, here)
                here = jnp.where(gap == -d, -down, here)
                halo = jnp.where(gap == d - LANES, -up, halo)
                halo = jnp.where(gap == LANES - d, -down, halo)
            matrix[t, :LANES, :] = here
            matrix[t, LANES:, :] = halo
        lane = lax.broadcasted_iota(jnp.int32, (rows, LANES), 1)

        def slot(j, carry):
            to = pl.ds(pl.multiple_of(j * rows, rows), rows)
            g, k = j // per, j % per
            low = pltpu.roll(left[g], (2 * LANES - REACH - REACH * k) % LANES, 1)
            high = pltpu.roll(right[g], (LANES - REACH * k) % LANES, 1)
            work = jnp.zeros((rows, LANES), jnp.float32)
            size = jnp.zeros((rows, LANES), jnp.float32)
            for t in range(tiles):
                at = slice(t * LANES, (t + 1) * LANES)
                here = x[j, :, at]
                previous = low if t == 0 else x[j, :, (t - 1) * LANES : t * LANES]
                following = high if t == tiles - 1 else x[j, :, (t + 1) * LANES : (t + 2) * LANES]
                halo = jnp.where(lane < LANES // 2, following, previous)
                total = jnp.dot(
                    jnp.concatenate([here, halo], 1),
                    matrix[t],
                    precision=HIGHEST,
                    preferred_element_type=jnp.float32,
                )
                total = total + (lam[j] * band[17:18, at]) * here
                stiff[j, :, at] = total
                work = work + total * here
                size = size + here * here
            energy[to, :] = work
            norm[to, :] = size
            return carry

        lax.fori_loop(0, count, slot, 0)
        ones = jnp.ones((ROWS, LANES), jnp.float32)
        for r, part in enumerate((energy, norm)):
            line = lax.dot_general(
                ones,
                part[...],
                (((1,), (1,)), ((), ())),
                precision=HIGHEST,
                preferred_element_type=jnp.float32,
            )
            sums[r : r + 1, :] = line[:1]

    vmem = pl.BlockSpec(memory_space=pltpu.VMEM)
    return pl.pallas_call(
        kernel,
        in_specs=[vmem, vmem, vmem, vmem, pl.BlockSpec(memory_space=pltpu.SMEM)],
        out_specs=[vmem, vmem],
        out_shape=[
            jax.ShapeDtypeStruct((count, rows, dofs), jnp.float32),
            jax.ShapeDtypeStruct((2, count * rows), jnp.float32),
        ],
        scratch_shapes=[
            pltpu.VMEM((count * rows, LANES), jnp.float32),
            pltpu.VMEM((count * rows, LANES), jnp.float32),
            pltpu.VMEM((tiles, 2 * LANES, LANES), jnp.float32),
        ],
        compiler_params=params(),
        name="stiffness",
    )(projected, before, after, bands, links)


def residual_back(projected, stiff, sums, late):
    count, rows, dofs = projected.shape
    scales = slot_scales(count)
    tiles = dofs // LANES

    def kernel(x, kx, total, extra, back, ritz, wide, sent, go):
        leaving = [pltpu.make_async_copy(extra, back.at[:, :, dofs : dofs + LANES], go.at[tiles])]
        leaving[0].start()
        value = total[0:1, :] / (total[1:2, :] + 1e-06)
        ritz[...] = value
        row = lax.broadcasted_iota(jnp.int32, (2 * ROWS, count * rows), 0)
        stack = jnp.zeros((2 * ROWS, count * rows), jnp.float32)
        for i, part in enumerate(bf16_parts(value)):
            stack = jnp.where(row == i, part.astype(jnp.float32), stack)
        wide[...] = lax.dot_general(
            stack.astype(jnp.bfloat16),
            jnp.ones((2 * ROWS, LANES), jnp.bfloat16),
            (((0,), (0,)), ((), ())),
            preferred_element_type=jnp.float32,
        )
        for t in range(tiles):
            lanes = slice(t * LANES, (t + 1) * LANES)

            def strip(r, carry, lanes=lanes):
                at = pl.ds(pl.multiple_of(r * ROWS, ROWS), ROWS)
                terms = []
                for j in range(count):
                    to = pl.ds(pl.multiple_of(j * rows + r * ROWS, ROWS), ROWS)
                    terms.append((kx[j, at, lanes] - wide[to, :] * x[j, at, lanes]) * scales[j])
                out = to_spans(terms)
                for s in range(count):
                    sent[s, at, lanes] = out[s]
                return carry

            lax.fori_loop(0, rows // ROWS, strip, 0)
            copy = pltpu.make_async_copy(sent.at[:, :, lanes], back.at[:, :, lanes], go.at[t])
            copy.start()
            leaving.append(copy)
        for copy in leaving:
            copy.wait()

    vmem = pl.BlockSpec(memory_space=pltpu.VMEM)
    return pl.pallas_call(
        kernel,
        in_specs=[vmem] * 4,
        out_specs=[pl.BlockSpec(memory_space=pltpu.HBM), vmem],
        out_shape=[
            pltpu.HBM((count, rows, dofs + LANES), jnp.float32),
            jax.ShapeDtypeStruct((1, count * rows), jnp.float32),
        ],
        scratch_shapes=[
            pltpu.VMEM((count * rows, LANES), jnp.float32),
            pltpu.VMEM((count, rows, dofs), jnp.float32),
            pltpu.SemaphoreType.DMA((tiles + 1,)),
        ],
        compiler_params=params(),
        name="residual_back",
    )(projected, stiff, sums, late)


def halvings(axis):
    step = lax.axis_size(axis) // 2
    while step:
        yield step, [(i, i ^ step) for i in range(lax.axis_size(axis))]
        step //= 2


def exchange_step(held, step, pairs):
    other = lax.ppermute(held, "span", pairs)
    upper = (lax.axis_index("span") & step) != 0
    return jnp.stack([jnp.where(upper, other, held), jnp.where(upper, held, other)])


def in_order(held, steps):
    bits = [step for step, _ in steps][::-1]
    order = tuple(sorted(range(len(bits)), key=lambda d: -bits[d]))
    held = held.transpose(order + tuple(range(len(bits), held.ndim)))
    return held.reshape((-1,) + held.shape[len(bits) :])


def tiled_device(
    current_block,
    search_block,
    previous_block,
    ground_spring,
    wire_tension,
    dropper_stiff,
    dropper_offset,
    span_link,
    ritz_rotation,
):
    count = lax.axis_size("span")
    dofs = current_block.shape[2] // count
    rows = current_block.shape[1]
    steps = list(halvings("span"))
    tiles = list(range(dofs // LANES))
    middle = tiles[len(tiles) // 2]
    early = [t for t in tiles if t != middle]
    at = middle * LANES
    blocks = (current_block, search_block, previous_block)
    rotation = exchange_step(ritz_rotation[0].T, *steps[0])
    pieces = spread_blocks(blocks, count, [(0, at), (at + LANES, dofs - at - LANES)])
    pieces, rotation = lax.optimization_barrier((pieces, rotation))
    stacked = exchange(pieces)
    order = steps[2:] + steps[1:2]
    for step, pairs in order:
        rotation = exchange_step(rotation, step, pairs)
    rotation = in_order(rotation, [steps[0]] + order)
    scales = jnp.array(slot_scales(count), jnp.float32)[:, None, None]
    rotation = rotation * scales
    pieces = spread_blocks(blocks, count, [(at, LANES)])
    pieces, rotation = lax.optimization_barrier((pieces, rotation))
    stacked_late = exchange(pieces)
    weights, ground, link = coefficients(
        ground_spring, wire_tension, dropper_stiff, dropper_offset, span_link, count, dofs
    )
    up = weights[:, REACH:]
    down = [weights[d - 1, REACH - d : REACH - d + dofs] for d in range(1, REACH + 1)]
    down = jnp.stack(down)
    diagonal = ground + jnp.sum(up, 0) + jnp.sum(down, 0)
    bands = jnp.concatenate([up, down, diagonal[None], link[None]])
    links = 2.0 * (1.0 - fourier_rows(count)[1])
    projected, spans, head, tail = project(stacked, rotation, dofs, early)
    before, after = to_next(tail, 1), to_next(head, -1)
    spans, before, after = lax.optimization_barrier((spans, before, after))
    early_pieces = exchange(spans)
    projected, late = project(stacked_late, rotation, dofs, [middle], projected)
    stiff, sums = stiffness(projected, before, after, bands, links)
    for _, pairs in halvings("elem"):
        sums = sums + lax.ppermute(sums, "elem", pairs)
    for _, pairs in steps[::-1]:
        sums = sums + lax.ppermute(sums, "span", pairs)
    spans, ritz = residual_back(projected, stiff, sums, late)
    next_block = collect_early(early_pieces, at)
    next_residual, next_block = collect_late(exchange(spans), next_block, at)
    ritz = lax.dynamic_slice_in_dim(ritz, lax.axis_index("span") * rows, rows, 1)
    return (next_block, next_residual, ritz)


def on_device(
    current_block,
    search_block,
    previous_block,
    ground_spring,
    wire_tension,
    dropper_stiff,
    dropper_offset,
    span_link,
    ritz_rotation,
):
    count = lax.axis_size("span")
    dof_dev = current_block.shape[2]
    dofs = dof_dev // count
    matrix, cosines = fourier_rows(count)
    blocks = (current_block, search_block, previous_block)
    stacked = exchange(jnp.concatenate([spread(b[0], count) for b in blocks], 1))
    rotation = lax.all_gather(ritz_rotation, "span", axis=0, tiled=True)
    weights, ground, link = coefficients(
        ground_spring, wire_tension, dropper_stiff, dropper_offset, span_link, count, dofs
    )
    slots = along_spans(matrix, stacked)
    projected = jnp.einsum("jvm,jvd->jmd", rotation, slots, precision=HIGHEST)
    back = matrix.T
    next_block = collect(exchange(along_spans(back, projected)))
    before = to_next(projected[:, :, dofs - REACH :], 1)
    after = to_next(projected[:, :, :REACH], -1)
    wide = jnp.concatenate([before, projected, after], 2)
    stiff = ground * projected
    near = wide[:, :, : REACH + dofs]
    for distance in range(1, REACH + 1):
        flux = weights[distance - 1] * (near - wide[:, :, distance : distance + REACH + dofs])
        stiff = stiff + flux[:, :, REACH:] - flux[:, :, REACH - distance : REACH - distance + dofs]
    stiff = stiff + (2.0 * (1.0 - cosines))[:, None, None] * link * projected
    sums = jnp.stack([jnp.sum(projected * stiff, 2), jnp.sum(projected * projected, 2)])
    sums = lax.psum(sums, ("elem", "span"))
    ritz = sums[0] / (sums[1] + 1e-06)
    residual = stiff - ritz[:, :, None] * projected
    next_residual = collect(exchange(along_spans(back, residual)))
    my_ritz = lax.dynamic_slice_in_dim(ritz, lax.axis_index("span"), 1, 0)
    return (next_block, next_residual, my_ritz)


def by_shape(*args):
    count, dof_dev = lax.axis_size("span"), args[0].shape[2]
    halves = count & (count - 1) == 0 and lax.axis_size("elem") in (1, 2, 4, 8, 16)
    if halves and count > 2 and dof_dev % (count * LANES) == 0 and dof_dev > 2 * count * LANES:
        return tiled_device(*args)
    return on_device(*args)


def solution(mesh):
    return jax.shard_map(
        by_shape,
        mesh=mesh,
        in_specs=(
            P("span", None, "elem"),
            P("span", None, "elem"),
            P("span", None, "elem"),
            P("elem"),
            P("elem"),
            P("elem"),
            P("elem"),
            P("elem"),
            P("span", None, None),
        ),
        out_specs=(P("span", None, "elem"), P("span", None, "elem"), P("span", None)),
        check_vma=False,
    )
```

```python
import math

import jax
import jax.numpy as jnp
from jax import lax
from jax.experimental import pallas as pl
from jax.experimental.pallas import tpu as pltpu
from jax.sharding import PartitionSpec as P

REACH = 8
LANES = 128
ROWS = 8
VMEM_LIMIT = 24 * 1024 * 1024
VMEM_MOST = 61_500_000
HIGHEST = lax.Precision.HIGHEST


def fourier_rows(count):
    row = jnp.arange(count)[:, None]
    col = jnp.arange(count)[None, :]
    half = count // 2
    wave = jnp.where(row <= half, row, row - half)
    phase = (wave * col % count).astype(jnp.float32) * (2.0 * math.pi / count)
    scaled = jnp.where(row <= half, jnp.cos(phase), jnp.sin(phase)) * math.sqrt(2.0 / count)
    edge = (row == 0) | (row == half)
    matrix = jnp.where(edge, jnp.cos(phase) * math.sqrt(1.0 / count), scaled)
    slots = jnp.arange(count)
    slot_wave = jnp.where(slots <= half, slots, slots - half)
    cosines = jnp.cos(slot_wave.astype(jnp.float32) * (2.0 * math.pi / count))
    return (matrix, cosines)


def along_spans(matrix, block):
    shape = block.shape
    flat = block.reshape(shape[0], -1)
    return jnp.dot(matrix, flat, precision=HIGHEST).reshape(shape)


def spread(block, count):
    rows, dofs = block.shape
    return block.reshape(rows, count, dofs // count).transpose(1, 0, 2)


def collect(pieces):
    count, rows, dofs = pieces.shape
    return pieces.transpose(1, 0, 2).reshape(1, rows, count * dofs)


def exchange(pieces):
    return lax.all_to_all(pieces, "span", split_axis=0, concat_axis=0, tiled=True)


def to_next(cells, step):
    count, parts = lax.axis_size("span"), lax.axis_size("elem")
    line = [s * parts + e for e in range(parts) for s in range(count)]
    pairs = list(zip(line, line[1:]))
    if step < 0:
        pairs = [(b, a) for a, b in pairs]
    return lax.ppermute(cells, ("span", "elem"), pairs)


def coefficients(ground, tension, stiff, offset, link, count, dofs):
    dof_dev = ground.shape[0]
    start = lax.axis_index("span") * dofs
    elem = lax.axis_index("elem")
    dof_all = dof_dev * lax.axis_size("elem")
    position = elem * dof_dev + jnp.arange(dof_dev)
    distance = jnp.arange(1, REACH + 1)[:, None]
    weights = jnp.where((offset == distance) & (position + distance < dof_all), stiff, 0.0)
    wire = jnp.where((distance == 1) & (position < dof_all - 1), tension, 0.0)
    weights = weights + wire
    pairs = [(i, i + 1) for i in range(lax.axis_size("elem") - 1)]
    left = lax.ppermute(weights[:, dof_dev - REACH :], "elem", pairs)
    weights = jnp.concatenate([left, weights], 1)
    weights = lax.dynamic_slice_in_dim(weights, start, dofs + REACH, 1)
    ground = lax.dynamic_slice_in_dim(ground, start, dofs, 0)
    link = lax.dynamic_slice_in_dim(link, start, dofs, 0)
    return weights, ground, link


def add_up(terms):
    total = terms[0]
    for term in terms[1:]:
        total = total + term
    return total


def scaled(factor, value):
    if abs(factor - 1.0) < 1e-12:
        return value
    return value * factor


def cosine_sums(a):
    n = len(a) - 1
    if n == 1:
        return [a[0] + a[1], a[0] - a[1]]
    half = n // 2
    even = cosine_sums([a[s] + a[n - s] for s in range(half)] + [a[half]])
    diff = [a[s] - a[n - s] for s in range(half)]
    out = [None] * (n + 1)
    out[0::2] = even
    for j in range(1, n, 2):
        out[j] = add_up([scaled(math.cos(math.pi * j * s / n), diff[s]) for s in range(half)])
    return out


def sine_sums(b):
    n = len(b) + 1
    if n == 1:
        return []
    half = n // 2
    at = [None] + list(b)
    even = sine_sums([at[s] - at[n - s] for s in range(1, half)])
    total = [None] + [at[s] + at[n - s] for s in range(1, half)] + [at[half]]
    out = [None] * (n + 1)
    for k, value in enumerate(even):
        out[2 * k + 2] = value
    for j in range(1, n, 2):
        terms = [(math.sin(math.pi * j * s / n), total[s]) for s in range(1, half + 1)]
        terms = [scaled(abs(f), t) if f > 0 else -scaled(abs(f), t) for f, t in terms]
        out[j] = add_up(terms)
    return out[1:n]


def slot_scales(count):
    edge, inner = math.sqrt(1.0 / count), math.sqrt(2.0 / count)
    return [edge if j in (0, count // 2) else inner for j in range(count)]


def to_slots(x):
    n = len(x)
    half = n // 2
    plus = [x[0]] + [x[s] + x[n - s] for s in range(1, half)] + [x[half]]
    minus = [x[s] - x[n - s] for s in range(1, half)]
    return cosine_sums(plus) + sine_sums(minus)


def to_spans(y):
    n = len(y)
    half = n // 2
    even = cosine_sums(y[: half + 1])
    odd = [None] + sine_sums(y[half + 1 :])
    out = [None] * n
    out[0], out[half] = even[0], even[half]
    for s in range(1, half):
        out[s] = even[s] + odd[s]
        out[n - s] = even[s] - odd[s]
    return out


def params(limit=VMEM_LIMIT):
    return pltpu.CompilerParams(vmem_limit_bytes=limit)


def spread_blocks(blocks, count, ranges):
    _, rows, dof_dev = blocks[0].shape
    dofs = dof_dev // count
    kinds = len(blocks)
    shape = (count, kinds * rows, sum(width for _, width in ranges))
    many = kinds * len(ranges)

    def kernel(*refs):
        out, held, come, go = refs[kinds:]
        arrivals = []
        for i in range(count):
            group, to = [], 0
            for first, width in ranges:
                for k in range(kinds):
                    copy = pltpu.make_async_copy(
                        refs[k].at[0, :, i * dofs + first : i * dofs + first + width],
                        held.at[i, k * rows : (k + 1) * rows, to : to + width],
                        come.at[i * many + len(group)],
                    )
                    copy.start()
                    group.append(copy)
                to += width
            arrivals.append(group)
        leaving = []
        for i, group in enumerate(arrivals):
            for copy in group:
                copy.wait()
            piece = pltpu.make_async_copy(held.at[i], out.at[i], go.at[i])
            piece.start()
            leaving.append(piece)
        for piece in leaving:
            piece.wait()

    whole = pl.BlockSpec(memory_space=pltpu.HBM)
    return pl.pallas_call(
        kernel,
        in_specs=[whole] * kinds,
        out_specs=whole,
        out_shape=pltpu.HBM(shape, jnp.float32),
        scratch_shapes=[
            pltpu.VMEM(shape, jnp.float32),
            pltpu.SemaphoreType.DMA((count * many,)),
            pltpu.SemaphoreType.DMA((count,)),
        ],
        compiler_params=params(VMEM_MOST),
        name="spread_blocks",
    )(*blocks)


def collect_early(early, middle):
    count, rows, early_width = early.shape
    dofs = early_width + LANES
    many = max(n for n in (1, 2, 4, 8) if count % n == 0)

    def kernel(first, block):
        for i in range(many):
            at = i * dofs
            block[0, :, at : at + middle] = first[i, :, :middle]
            block[0, :, at + middle + LANES : at + dofs] = first[i, :, middle:]

    return pl.pallas_call(
        kernel,
        grid=(count // many,),
        in_specs=[pl.BlockSpec((many, rows, early_width), lambda i: (i, 0, 0))],
        out_specs=pl.BlockSpec((1, rows, many * dofs), lambda i: (0, 0, i)),
        out_shape=pltpu.HBM((1, rows, count * dofs), jnp.float32),
        compiler_params=params(VMEM_MOST),
        name="collect_early",
    )(early)


def collect_late(late, block, middle):
    count, rows, width = late.shape
    dofs = width - LANES
    many = max(n for n in (1, 2, 4, 8) if count % n == 0)

    def kernel(last, _, residual, whole, sem):
        copies = []
        for i in range(many):
            at = (pl.program_id(0) * many + i) * dofs + middle
            copy = pltpu.make_async_copy(
                last.at[i, :, pl.ds(dofs, LANES)],
                whole.at[0, :, pl.ds(pl.multiple_of(at, LANES), LANES)],
                sem.at[i],
            )
            copy.start()
            copies.append(copy)
        for i in range(many):
            residual[0, :, i * dofs : (i + 1) * dofs] = last[i, :, :dofs]
        for copy in copies:
            copy.wait()

    place = pl.BlockSpec(memory_space=pltpu.HBM)
    shape = pltpu.HBM((1, rows, count * dofs), jnp.float32)
    return pl.pallas_call(
        kernel,
        grid=(count // many,),
        in_specs=[pl.BlockSpec((many, rows, width), lambda i: (i, 0, 0)), place],
        out_specs=[pl.BlockSpec((1, rows, many * dofs), lambda i: (0, 0, i)), place],
        out_shape=[shape, shape],
        input_output_aliases={1: 1},
        scratch_shapes=[pltpu.SemaphoreType.DMA((many,))],
        compiler_params=params(),
        name="collect_late",
    )(late, block)


PARTS = 3


def bf16_parts(value):
    parts = []
    for i in range(PARTS):
        parts.append(value.astype(jnp.bfloat16))
        if i < PARTS - 1:
            value = value - parts[i].astype(jnp.float32)
    return parts


def project(stacked, rotation, dofs, tiles, prior=None):
    count, wide, _ = stacked.shape
    rows = rotation.shape[1]
    width = len(tiles) * LANES
    scales = slot_scales(count)
    groups = -(-count * REACH // LANES)
    per = LANES // REACH
    strip = 2 * ROWS

    def kernel(x, rot, *refs):
        refs = refs[1:] if prior is not None else refs
        proj, back = refs[:2]
        edges, scratch = (refs[2:4], refs[4:]) if prior is None else ((), refs[2:])
        held, split_rot, mine, sent, come, go = scratch[:6]
        split_slots = scratch[6:]
        arrivals = []
        for c in range(len(tiles)):
            copy = pltpu.make_async_copy(
                x.at[:, :, c * LANES : (c + 1) * LANES], held.at[c], come.at[c]
            )
            copy.start()
            arrivals.append(copy)

        def one(j, carry):
            for i, part in enumerate(bf16_parts(rot[j])):
                split_rot[j, i * rows : (i + 1) * rows, :] = part
            return carry

        lax.fori_loop(0, count, one, 0)
        for c, copy in enumerate(arrivals):
            copy.wait()

            def transform(r, carry, c=c):
                at = pl.ds(pl.multiple_of(r * strip, strip), strip)
                halves = []
                for h in range(2):
                    own = pl.ds(pl.multiple_of(r * strip + h * ROWS, ROWS), ROWS)
                    halves.append(to_slots([held[c, s, own, :] for s in range(count)]))
                for j in range(count):
                    value = jnp.concatenate([half[j] for half in halves], 0)
                    for part, ref in zip(bf16_parts(value), split_slots):
                        ref[j, at, c * LANES : (c + 1) * LANES] = part
                return carry

            lax.fori_loop(0, wide // strip, transform, 0)
        for j in range(count):
            total = None
            for i in range(PARTS - 1, -1, -1):
                terms = PARTS - i
                stacked_terms = jnp.dot(
                    split_rot[j, : terms * rows, :],
                    split_slots[i][j],
                    preferred_element_type=jnp.float32,
                )
                for q in range(terms - 1, -1, -1):
                    term = stacked_terms[q * rows : (q + 1) * rows]
                    total = term if total is None else total + term
            mine[j] = total
        leaving = []

        def leave(source, target, c, t, at):
            copy = pltpu.make_async_copy(
                source.at[:, :, c * LANES : (c + 1) * LANES],
                target.at[:, :, t * LANES : (t + 1) * LANES],
                go.at[at],
            )
            copy.start()
            leaving.append(copy)

        for c, t in enumerate(tiles):
            leave(mine, proj, c, t, c)
        for c in range(len(tiles)):
            lanes = slice(c * LANES, (c + 1) * LANES)

            def inverse(r, carry, lanes=lanes):
                at = pl.ds(pl.multiple_of(r * ROWS, ROWS), ROWS)
                out = to_spans([mine[j, at, lanes] * scales[j] for j in range(count)])
                for s in range(count):
                    sent[s, at, lanes] = out[s]
                return carry

            lax.fori_loop(0, rows // ROWS, inverse, 0)
            leave(sent, back, c, c, len(tiles) + c)
        lane = lax.broadcasted_iota(jnp.int32, (rows, LANES), 1)
        ends = ((0, 0), (len(tiles) - 1, LANES - REACH))
        for ref, (c, start) in zip(edges, ends):
            for g in range(groups):
                packed = jnp.zeros((rows, LANES), jnp.float32)
                for k in range(min(per, count - g * per)):
                    turn = (k * REACH - start) % LANES
                    value = mine[g * per + k, :, c * LANES : (c + 1) * LANES]
                    value = pltpu.roll(value, turn, 1) if turn else value
                    packed = jnp.where(lane // REACH == k, value, packed)
                ref[g] = packed
        for copy in leaving:
            copy.wait()

    whole = pl.BlockSpec(memory_space=pltpu.HBM)
    vmem = pl.BlockSpec(memory_space=pltpu.VMEM)
    field = pltpu.HBM((count, rows, dofs), jnp.float32)
    edge = jax.ShapeDtypeStruct((groups, rows, LANES), jnp.float32)
    sending = pltpu.HBM((count, rows, width), jnp.float32)
    first = prior is None
    passes = PARTS * (PARTS + 1) // 2
    cost = pl.CostEstimate(
        flops=2 * passes * count * wide * rows * width,
        bytes_accessed=4 * count * (wide + 2 * rows) * width,
        transcendentals=0,
    )
    return pl.pallas_call(
        kernel,
        in_specs=[whole, vmem] + ([] if first else [whole]),
        out_specs=[whole, whole] + ([vmem, vmem] if first else []),
        out_shape=[field, sending] + ([edge, edge] if first else []),
        input_output_aliases={} if first else {2: 0},
        cost_estimate=cost,
        scratch_shapes=[
            pltpu.VMEM((len(tiles), count, wide, LANES), jnp.float32),
            pltpu.VMEM((count, PARTS * rows, wide), jnp.bfloat16),
            pltpu.VMEM((count, rows, width), jnp.float32),
            pltpu.VMEM((count, rows, width), jnp.float32),
            pltpu.SemaphoreType.DMA((len(tiles),)),
            pltpu.SemaphoreType.DMA((2 * len(tiles),)),
        ]
        + [pltpu.VMEM((count, wide, width), jnp.bfloat16)] * PARTS,
        compiler_params=params(VMEM_MOST),
        name="project",
    )(stacked, rotation, *(() if first else (prior,)))


def stiffness(projected, before, after, bands, links):
    count, rows, dofs = projected.shape
    per = LANES // REACH
    tiles = dofs // LANES

    def kernel(x, left, right, band, lam, stiff, sums, energy, norm, matrix):
        row = lax.broadcasted_iota(jnp.int32, (LANES, LANES), 0)
        gap = row - lax.broadcasted_iota(jnp.int32, (LANES, LANES), 1)
        for t in range(tiles):
            at = slice(t * LANES, (t + 1) * LANES)
            here = jnp.where(gap == 0, band[16:17, at], 0.0)
            halo = jnp.zeros((LANES, LANES), jnp.float32)
            for d in range(1, REACH + 1):
                up, down = band[d - 1 : d, at], band[REACH + d - 1 : REACH + d, at]
                here = jnp.where(gap == d, -up, here)
                here = jnp.where(gap == -d, -down, here)
                halo = jnp.where(gap == d - LANES, -up, halo)
                halo = jnp.where(gap == LANES - d, -down, halo)
            matrix[t, :LANES, :] = here
            matrix[t, LANES:, :] = halo
        lane = lax.broadcasted_iota(jnp.int32, (rows, LANES), 1)

        def slot(j, carry):
            to = pl.ds(pl.multiple_of(j * rows, rows), rows)
            g, k = j // per, j % per
            low = pltpu.roll(left[g], (2 * LANES - REACH - REACH * k) % LANES, 1)
            high = pltpu.roll(right[g], (LANES - REACH * k) % LANES, 1)
            work = jnp.zeros((rows, LANES), jnp.float32)
            size = jnp.zeros((rows, LANES), jnp.float32)
            for t in range(tiles):
                at = slice(t * LANES, (t + 1) * LANES)
                here = x[j, :, at]
                previous = low if t == 0 else x[j, :, (t - 1) * LANES : t * LANES]
                following = high if t == tiles - 1 else x[j, :, (t + 1) * LANES : (t + 2) * LANES]
                halo = jnp.where(lane < LANES // 2, following, previous)
                total = jnp.dot(
                    jnp.concatenate([here, halo], 1),
                    matrix[t],
                    precision=HIGHEST,
                    preferred_element_type=jnp.float32,
                )
                total = total + (lam[j] * band[17:18, at]) * here
                stiff[j, :, at] = total
                work = work + total * here
                size = size + here * here
            energy[to, :] = work
            norm[to, :] = size
            return carry

        lax.fori_loop(0, count, slot, 0)
        ones = jnp.ones((ROWS, LANES), jnp.float32)
        for r, part in enumerate((energy, norm)):
            line = lax.dot_general(
                ones,
                part[...],
                (((1,), (1,)), ((), ())),
                precision=HIGHEST,
                preferred_element_type=jnp.float32,
            )
            sums[r : r + 1, :] = line[:1]

    vmem = pl.BlockSpec(memory_space=pltpu.VMEM)
    return pl.pallas_call(
        kernel,
        in_specs=[vmem, vmem, vmem, vmem, pl.BlockSpec(memory_space=pltpu.SMEM)],
        out_specs=[vmem, vmem],
        out_shape=[
            jax.ShapeDtypeStruct((count, rows, dofs), jnp.float32),
            jax.ShapeDtypeStruct((2, count * rows), jnp.float32),
        ],
        scratch_shapes=[
            pltpu.VMEM((count * rows, LANES), jnp.float32),
            pltpu.VMEM((count * rows, LANES), jnp.float32),
            pltpu.VMEM((tiles, 2 * LANES, LANES), jnp.float32),
        ],
        compiler_params=params(),
        name="stiffness",
    )(projected, before, after, bands, links)


def residual_back(projected, stiff, sums, late):
    count, rows, dofs = projected.shape
    scales = slot_scales(count)
    tiles = dofs // LANES

    def kernel(x, kx, total, extra, back, ritz, wide, sent, go):
        leaving = [pltpu.make_async_copy(extra, back.at[:, :, dofs : dofs + LANES], go.at[tiles])]
        leaving[0].start()
        value = total[0:1, :] / (total[1:2, :] + 1e-06)
        ritz[...] = value
        row = lax.broadcasted_iota(jnp.int32, (2 * ROWS, count * rows), 0)
        stack = jnp.zeros((2 * ROWS, count * rows), jnp.float32)
        for i, part in enumerate(bf16_parts(value)):
            stack = jnp.where(row == i, part.astype(jnp.float32), stack)
        wide[...] = lax.dot_general(
            stack.astype(jnp.bfloat16),
            jnp.ones((2 * ROWS, LANES), jnp.bfloat16),
            (((0,), (0,)), ((), ())),
            preferred_element_type=jnp.float32,
        )
        for t in range(tiles):
            lanes = slice(t * LANES, (t + 1) * LANES)

            def strip(r, carry, lanes=lanes):
                at = pl.ds(pl.multiple_of(r * ROWS, ROWS), ROWS)
                terms = []
                for j in range(count):
                    to = pl.ds(pl.multiple_of(j * rows + r * ROWS, ROWS), ROWS)
                    terms.append((kx[j, at, lanes] - wide[to, :] * x[j, at, lanes]) * scales[j])
                out = to_spans(terms)
                for s in range(count):
                    sent[s, at, lanes] = out[s]
                return carry

            lax.fori_loop(0, rows // ROWS, strip, 0)
            copy = pltpu.make_async_copy(sent.at[:, :, lanes], back.at[:, :, lanes], go.at[t])
            copy.start()
            leaving.append(copy)
        for copy in leaving:
            copy.wait()

    vmem = pl.BlockSpec(memory_space=pltpu.VMEM)
    return pl.pallas_call(
        kernel,
        in_specs=[vmem] * 4,
        out_specs=[pl.BlockSpec(memory_space=pltpu.HBM), vmem],
        out_shape=[
            pltpu.HBM((count, rows, dofs + LANES), jnp.float32),
            jax.ShapeDtypeStruct((1, count * rows), jnp.float32),
        ],
        scratch_shapes=[
            pltpu.VMEM((count * rows, LANES), jnp.float32),
            pltpu.VMEM((count, rows, dofs), jnp.float32),
            pltpu.SemaphoreType.DMA((tiles + 1,)),
        ],
        compiler_params=params(),
        name="residual_back",
    )(projected, stiff, sums, late)


def halvings(axis):
    step = lax.axis_size(axis) // 2
    while step:
        yield step, [(i, i ^ step) for i in range(lax.axis_size(axis))]
        step //= 2


def exchange_step(held, step, pairs):
    other = lax.ppermute(held, "span", pairs)
    upper = (lax.axis_index("span") & step) != 0
    return jnp.stack([jnp.where(upper, other, held), jnp.where(upper, held, other)])


def in_order(held, steps):
    bits = [step for step, _ in steps][::-1]
    order = tuple(sorted(range(len(bits)), key=lambda d: -bits[d]))
    held = held.transpose(order + tuple(range(len(bits), held.ndim)))
    return held.reshape((-1,) + held.shape[len(bits) :])


def tiled_device(
    current_block,
    search_block,
    previous_block,
    ground_spring,
    wire_tension,
    dropper_stiff,
    dropper_offset,
    span_link,
    ritz_rotation,
):
    count = lax.axis_size("span")
    dofs = current_block.shape[2] // count
    rows = current_block.shape[1]
    steps = list(halvings("span"))
    tiles = list(range(dofs // LANES))
    middle = tiles[len(tiles) // 2]
    early = [t for t in tiles if t != middle]
    at = middle * LANES
    blocks = (current_block, search_block, previous_block)
    rotation = exchange_step(ritz_rotation[0].T, *steps[0])
    pieces = spread_blocks(blocks, count, [(0, at), (at + LANES, dofs - at - LANES)])
    pieces, rotation = lax.optimization_barrier((pieces, rotation))
    stacked = exchange(pieces)
    order = steps[2:] + steps[1:2]
    for step, pairs in order:
        rotation = exchange_step(rotation, step, pairs)
    rotation = in_order(rotation, [steps[0]] + order)
    scales = jnp.array(slot_scales(count), jnp.float32)[:, None, None]
    rotation = rotation * scales
    weights, ground, link = coefficients(
        ground_spring, wire_tension, dropper_stiff, dropper_offset, span_link, count, dofs
    )
    up = weights[:, REACH:]
    down = [weights[d - 1, REACH - d : REACH - d + dofs] for d in range(1, REACH + 1)]
    down = jnp.stack(down)
    diagonal = ground + jnp.sum(up, 0) + jnp.sum(down, 0)
    bands = jnp.concatenate([up, down, diagonal[None], link[None]])
    links = 2.0 * (1.0 - fourier_rows(count)[1])
    pieces = spread_blocks(blocks, count, [(at, LANES)])
    pieces, rotation, bands = lax.optimization_barrier((pieces, rotation, bands))
    stacked_late = exchange(pieces)
    projected, spans, head, tail = project(stacked, rotation, dofs, early)
    before, after = to_next(tail, 1), to_next(head, -1)
    spans, before, after = lax.optimization_barrier((spans, before, after))
    early_pieces = exchange(spans)
    projected, late = project(stacked_late, rotation, dofs, [middle], projected)
    stiff, sums = stiffness(projected, before, after, bands, links)
    for _, pairs in halvings("elem"):
        sums = sums + lax.ppermute(sums, "elem", pairs)
    for _, pairs in steps[::-1]:
        sums = sums + lax.ppermute(sums, "span", pairs)
    spans, ritz = residual_back(projected, stiff, sums, late)
    next_block = collect_early(early_pieces, at)
    next_residual, next_block = collect_late(exchange(spans), next_block, at)
    ritz = lax.dynamic_slice_in_dim(ritz, lax.axis_index("span") * rows, rows, 1)
    return (next_block, next_residual, ritz)


def on_device(
    current_block,
    search_block,
    previous_block,
    ground_spring,
    wire_tension,
    dropper_stiff,
    dropper_offset,
    span_link,
    ritz_rotation,
):
    count = lax.axis_size("span")
    dof_dev = current_block.shape[2]
    dofs = dof_dev // count
    matrix, cosines = fourier_rows(count)
    blocks = (current_block, search_block, previous_block)
    stacked = exchange(jnp.concatenate([spread(b[0], count) for b in blocks], 1))
    rotation = lax.all_gather(ritz_rotation, "span", axis=0, tiled=True)
    weights, ground, link = coefficients(
        ground_spring, wire_tension, dropper_stiff, dropper_offset, span_link, count, dofs
    )
    slots = along_spans(matrix, stacked)
    projected = jnp.einsum("jvm,jvd->jmd", rotation, slots, precision=HIGHEST)
    back = matrix.T
    next_block = collect(exchange(along_spans(back, projected)))
    before = to_next(projected[:, :, dofs - REACH :], 1)
    after = to_next(projected[:, :, :REACH], -1)
    wide = jnp.concatenate([before, projected, after], 2)
    stiff = ground * projected
    near = wide[:, :, : REACH + dofs]
    for distance in range(1, REACH + 1):
        flux = weights[distance - 1] * (near - wide[:, :, distance : distance + REACH + dofs])
        stiff = stiff + flux[:, :, REACH:] - flux[:, :, REACH - distance : REACH - distance + dofs]
    stiff = stiff + (2.0 * (1.0 - cosines))[:, None, None] * link * projected
    sums = jnp.stack([jnp.sum(projected * stiff, 2), jnp.sum(projected * projected, 2)])
    sums = lax.psum(sums, ("elem", "span"))
    ritz = sums[0] / (sums[1] + 1e-06)
    residual = stiff - ritz[:, :, None] * projected
    next_residual = collect(exchange(along_spans(back, residual)))
    my_ritz = lax.dynamic_slice_in_dim(ritz, lax.axis_index("span"), 1, 0)
    return (next_block, next_residual, my_ritz)


def by_shape(*args):
    count, dof_dev = lax.axis_size("span"), args[0].shape[2]
    halves = count & (count - 1) == 0 and lax.axis_size("elem") in (1, 2, 4, 8, 16)
    if halves and count > 2 and dof_dev % (count * LANES) == 0 and dof_dev > 2 * count * LANES:
        return tiled_device(*args)
    return on_device(*args)


def solution(mesh):
    return jax.shard_map(
        by_shape,
        mesh=mesh,
        in_specs=(
            P("span", None, "elem"),
            P("span", None, "elem"),
            P("span", None, "elem"),
            P("elem"),
            P("elem"),
            P("elem"),
            P("elem"),
            P("elem"),
            P("span", None, None),
        ),
        out_specs=(P("span", None, "elem"), P("span", None, "elem"), P("span", None)),
        check_vma=False,
    )
```

```python
import math

import jax
import jax.numpy as jnp
from jax import lax
from jax.experimental import pallas as pl
from jax.experimental.pallas import tpu as pltpu
from jax.sharding import PartitionSpec as P

REACH = 8
LANES = 128
ROWS = 8
VMEM_LIMIT = 24 * 1024 * 1024
VMEM_MOST = 61_500_000
HIGHEST = lax.Precision.HIGHEST


def fourier_rows(count):
    row = jnp.arange(count)[:, None]
    col = jnp.arange(count)[None, :]
    half = count // 2
    wave = jnp.where(row <= half, row, row - half)
    phase = (wave * col % count).astype(jnp.float32) * (2.0 * math.pi / count)
    scaled = jnp.where(row <= half, jnp.cos(phase), jnp.sin(phase)) * math.sqrt(2.0 / count)
    edge = (row == 0) | (row == half)
    matrix = jnp.where(edge, jnp.cos(phase) * math.sqrt(1.0 / count), scaled)
    slots = jnp.arange(count)
    slot_wave = jnp.where(slots <= half, slots, slots - half)
    cosines = jnp.cos(slot_wave.astype(jnp.float32) * (2.0 * math.pi / count))
    return (matrix, cosines)


def along_spans(matrix, block):
    shape = block.shape
    flat = block.reshape(shape[0], -1)
    return jnp.dot(matrix, flat, precision=HIGHEST).reshape(shape)


def spread(block, count):
    rows, dofs = block.shape
    return block.reshape(rows, count, dofs // count).transpose(1, 0, 2)


def collect(pieces):
    count, rows, dofs = pieces.shape
    return pieces.transpose(1, 0, 2).reshape(1, rows, count * dofs)


def exchange(pieces):
    return lax.all_to_all(pieces, "span", split_axis=0, concat_axis=0, tiled=True)


def to_next(cells, step):
    count, parts = lax.axis_size("span"), lax.axis_size("elem")
    line = [s * parts + e for e in range(parts) for s in range(count)]
    pairs = list(zip(line, line[1:]))
    if step < 0:
        pairs = [(b, a) for a, b in pairs]
    return lax.ppermute(cells, ("span", "elem"), pairs)


def coefficients(ground, tension, stiff, offset, link, count, dofs):
    dof_dev = ground.shape[0]
    start = lax.axis_index("span") * dofs
    elem = lax.axis_index("elem")
    dof_all = dof_dev * lax.axis_size("elem")
    position = elem * dof_dev + jnp.arange(dof_dev)
    distance = jnp.arange(1, REACH + 1)[:, None]
    weights = jnp.where((offset == distance) & (position + distance < dof_all), stiff, 0.0)
    wire = jnp.where((distance == 1) & (position < dof_all - 1), tension, 0.0)
    weights = weights + wire
    pairs = [(i, i + 1) for i in range(lax.axis_size("elem") - 1)]
    left = lax.ppermute(weights[:, dof_dev - REACH :], "elem", pairs)
    weights = jnp.concatenate([left, weights], 1)
    weights = lax.dynamic_slice_in_dim(weights, start, dofs + REACH, 1)
    ground = lax.dynamic_slice_in_dim(ground, start, dofs, 0)
    link = lax.dynamic_slice_in_dim(link, start, dofs, 0)
    return weights, ground, link


def add_up(terms):
    total = terms[0]
    for term in terms[1:]:
        total = total + term
    return total


def scaled(factor, value):
    if abs(factor - 1.0) < 1e-12:
        return value
    return value * factor


def cosine_sums(a):
    n = len(a) - 1
    if n == 1:
        return [a[0] + a[1], a[0] - a[1]]
    half = n // 2
    even = cosine_sums([a[s] + a[n - s] for s in range(half)] + [a[half]])
    diff = [a[s] - a[n - s] for s in range(half)]
    out = [None] * (n + 1)
    out[0::2] = even
    for j in range(1, n, 2):
        out[j] = add_up([scaled(math.cos(math.pi * j * s / n), diff[s]) for s in range(half)])
    return out


def sine_sums(b):
    n = len(b) + 1
    if n == 1:
        return []
    half = n // 2
    at = [None] + list(b)
    even = sine_sums([at[s] - at[n - s] for s in range(1, half)])
    total = [None] + [at[s] + at[n - s] for s in range(1, half)] + [at[half]]
    out = [None] * (n + 1)
    for k, value in enumerate(even):
        out[2 * k + 2] = value
    for j in range(1, n, 2):
        terms = [(math.sin(math.pi * j * s / n), total[s]) for s in range(1, half + 1)]
        terms = [scaled(abs(f), t) if f > 0 else -scaled(abs(f), t) for f, t in terms]
        out[j] = add_up(terms)
    return out[1:n]


def slot_scales(count):
    edge, inner = math.sqrt(1.0 / count), math.sqrt(2.0 / count)
    return [edge if j in (0, count // 2) else inner for j in range(count)]


def to_slots(x):
    n = len(x)
    half = n // 2
    plus = [x[0]] + [x[s] + x[n - s] for s in range(1, half)] + [x[half]]
    minus = [x[s] - x[n - s] for s in range(1, half)]
    return cosine_sums(plus) + sine_sums(minus)


def to_spans(y):
    n = len(y)
    half = n // 2
    even = cosine_sums(y[: half + 1])
    odd = [None] + sine_sums(y[half + 1 :])
    out = [None] * n
    out[0], out[half] = even[0], even[half]
    for s in range(1, half):
        out[s] = even[s] + odd[s]
        out[n - s] = even[s] - odd[s]
    return out


def params(limit=VMEM_LIMIT):
    return pltpu.CompilerParams(vmem_limit_bytes=limit)


def spread_blocks(blocks, count, ranges):
    _, rows, dof_dev = blocks[0].shape
    dofs = dof_dev // count
    kinds = len(blocks)
    shape = (count, kinds * rows, sum(width for _, width in ranges))
    many = kinds * len(ranges)

    def kernel(*refs):
        out, held, come, go = refs[kinds:]
        arrivals = []
        for i in range(count):
            group, to = [], 0
            for first, width in ranges:
                for k in range(kinds):
                    copy = pltpu.make_async_copy(
                        refs[k].at[0, :, i * dofs + first : i * dofs + first + width],
                        held.at[i, k * rows : (k + 1) * rows, to : to + width],
                        come.at[i * many + len(group)],
                    )
                    copy.start()
                    group.append(copy)
                to += width
            arrivals.append(group)
        leaving = []
        for i, group in enumerate(arrivals):
            for copy in group:
                copy.wait()
            piece = pltpu.make_async_copy(held.at[i], out.at[i], go.at[i])
            piece.start()
            leaving.append(piece)
        for piece in leaving:
            piece.wait()

    whole = pl.BlockSpec(memory_space=pltpu.HBM)
    return pl.pallas_call(
        kernel,
        in_specs=[whole] * kinds,
        out_specs=whole,
        out_shape=pltpu.HBM(shape, jnp.float32),
        scratch_shapes=[
            pltpu.VMEM(shape, jnp.float32),
            pltpu.SemaphoreType.DMA((count * many,)),
            pltpu.SemaphoreType.DMA((count,)),
        ],
        compiler_params=params(VMEM_MOST),
        name="spread_blocks",
    )(*blocks)


def collect_early(early, middle):
    count, rows, early_width = early.shape
    dofs = early_width + LANES
    many = max(n for n in (1, 2, 4, 8) if count % n == 0)

    def kernel(first, block):
        for i in range(many):
            at = i * dofs
            block[0, :, at : at + middle] = first[i, :, :middle]
            block[0, :, at + middle + LANES : at + dofs] = first[i, :, middle:]

    return pl.pallas_call(
        kernel,
        grid=(count // many,),
        in_specs=[pl.BlockSpec((many, rows, early_width), lambda i: (i, 0, 0))],
        out_specs=pl.BlockSpec((1, rows, many * dofs), lambda i: (0, 0, i)),
        out_shape=pltpu.HBM((1, rows, count * dofs), jnp.float32),
        compiler_params=params(VMEM_MOST),
        name="collect_early",
    )(early)


def collect_late(late, block, middle):
    count, rows, width = late.shape
    dofs = width - LANES

    def kernel(last, _, residual, whole, sem):
        copies = []
        for i in range(count):
            at = i * dofs + middle
            copies.append(
                pltpu.make_async_copy(
                    last.at[i, :, :dofs],
                    residual.at[0, :, i * dofs : (i + 1) * dofs],
                    sem.at[2 * i],
                )
            )
            copies.append(
                pltpu.make_async_copy(
                    last.at[i, :, dofs:width], whole.at[0, :, at : at + LANES], sem.at[2 * i + 1]
                )
            )
        for copy in copies:
            copy.start()
        for copy in copies:
            copy.wait()

    place = pl.BlockSpec(memory_space=pltpu.HBM)
    shape = pltpu.HBM((1, rows, count * dofs), jnp.float32)
    return pl.pallas_call(
        kernel,
        in_specs=[pl.BlockSpec(memory_space=pltpu.VMEM), place],
        out_specs=[place, place],
        out_shape=[shape, shape],
        input_output_aliases={1: 1},
        scratch_shapes=[pltpu.SemaphoreType.DMA((2 * count,))],
        compiler_params=params(),
        name="collect_late",
    )(late, block)


PARTS = 3


def bf16_parts(value):
    parts = []
    for i in range(PARTS):
        parts.append(value.astype(jnp.bfloat16))
        if i < PARTS - 1:
            value = value - parts[i].astype(jnp.float32)
    return parts


def project(stacked, rotation, dofs, tiles, prior=None):
    count, wide, _ = stacked.shape
    rows = rotation.shape[1]
    width = len(tiles) * LANES
    scales = slot_scales(count)
    groups = -(-count * REACH // LANES)
    per = LANES // REACH
    strip = 2 * ROWS

    def kernel(x, rot, *refs):
        refs = refs[1:] if prior is not None else refs
        proj, back = refs[:2]
        edges, scratch = (refs[2:4], refs[4:]) if prior is None else ((), refs[2:])
        held, split_rot, mine, sent, come, go = scratch[:6]
        split_slots = scratch[6:]
        arrivals = []
        for c in range(len(tiles)):
            copy = pltpu.make_async_copy(
                x.at[:, :, c * LANES : (c + 1) * LANES], held.at[c], come.at[c]
            )
            copy.start()
            arrivals.append(copy)

        def one(j, carry):
            for i, part in enumerate(bf16_parts(rot[j])):
                split_rot[j, i * rows : (i + 1) * rows, :] = part
            return carry

        lax.fori_loop(0, count, one, 0)
        for c, copy in enumerate(arrivals):
            copy.wait()

            def transform(r, carry, c=c):
                at = pl.ds(pl.multiple_of(r * strip, strip), strip)
                halves = []
                for h in range(2):
                    own = pl.ds(pl.multiple_of(r * strip + h * ROWS, ROWS), ROWS)
                    halves.append(to_slots([held[c, s, own, :] for s in range(count)]))
                for j in range(count):
                    value = jnp.concatenate([half[j] for half in halves], 0)
                    for part, ref in zip(bf16_parts(value), split_slots):
                        ref[j, at, c * LANES : (c + 1) * LANES] = part
                return carry

            lax.fori_loop(0, wide // strip, transform, 0)
        for j in range(count):
            total = None
            for i in range(PARTS - 1, -1, -1):
                terms = PARTS - i
                stacked_terms = jnp.dot(
                    split_rot[j, : terms * rows, :],
                    split_slots[i][j],
                    preferred_element_type=jnp.float32,
                )
                for q in range(terms - 1, -1, -1):
                    term = stacked_terms[q * rows : (q + 1) * rows]
                    total = term if total is None else total + term
            mine[j] = total
        leaving = []

        def leave(source, target, c, t, at):
            copy = pltpu.make_async_copy(
                source.at[:, :, c * LANES : (c + 1) * LANES],
                target.at[:, :, t * LANES : (t + 1) * LANES],
                go.at[at],
            )
            copy.start()
            leaving.append(copy)

        for c, t in enumerate(tiles):
            leave(mine, proj, c, t, c)
        for c in range(len(tiles)):
            lanes = slice(c * LANES, (c + 1) * LANES)

            def inverse(r, carry, lanes=lanes):
                at = pl.ds(pl.multiple_of(r * ROWS, ROWS), ROWS)
                out = to_spans([mine[j, at, lanes] * scales[j] for j in range(count)])
                for s in range(count):
                    sent[s, at, lanes] = out[s]
                return carry

            lax.fori_loop(0, rows // ROWS, inverse, 0)
            leave(sent, back, c, c, len(tiles) + c)
        lane = lax.broadcasted_iota(jnp.int32, (rows, LANES), 1)
        ends = ((0, 0), (len(tiles) - 1, LANES - REACH))
        for ref, (c, start) in zip(edges, ends):
            for g in range(groups):
                packed = jnp.zeros((rows, LANES), jnp.float32)
                for k in range(min(per, count - g * per)):
                    turn = (k * REACH - start) % LANES
                    value = mine[g * per + k, :, c * LANES : (c + 1) * LANES]
                    value = pltpu.roll(value, turn, 1) if turn else value
                    packed = jnp.where(lane // REACH == k, value, packed)
                ref[g] = packed
        for copy in leaving:
            copy.wait()

    whole = pl.BlockSpec(memory_space=pltpu.HBM)
    vmem = pl.BlockSpec(memory_space=pltpu.VMEM)
    field = pltpu.HBM((count, rows, dofs), jnp.float32)
    edge = jax.ShapeDtypeStruct((groups, rows, LANES), jnp.float32)
    sending = pltpu.HBM((count, rows, width), jnp.float32)
    first = prior is None
    passes = PARTS * (PARTS + 1) // 2
    cost = pl.CostEstimate(
        flops=2 * passes * count * wide * rows * width,
        bytes_accessed=4 * count * (wide + 2 * rows) * width,
        transcendentals=0,
    )
    return pl.pallas_call(
        kernel,
        in_specs=[whole, vmem] + ([] if first else [whole]),
        out_specs=[whole, whole] + ([vmem, vmem] if first else []),
        out_shape=[field, sending] + ([edge, edge] if first else []),
        input_output_aliases={} if first else {2: 0},
        cost_estimate=cost,
        scratch_shapes=[
            pltpu.VMEM((len(tiles), count, wide, LANES), jnp.float32),
            pltpu.VMEM((count, PARTS * rows, wide), jnp.bfloat16),
            pltpu.VMEM((count, rows, width), jnp.float32),
            pltpu.VMEM((count, rows, width), jnp.float32),
            pltpu.SemaphoreType.DMA((len(tiles),)),
            pltpu.SemaphoreType.DMA((2 * len(tiles),)),
        ]
        + [pltpu.VMEM((count, wide, width), jnp.bfloat16)] * PARTS,
        compiler_params=params(65_400_000),
        name="project",
    )(stacked, rotation, *(() if first else (prior,)))


def stiffness(projected, before, after, bands, links):
    count, rows, dofs = projected.shape
    per = LANES // REACH
    tiles = dofs // LANES

    def kernel(x, left, right, band, lam, stiff, sums, energy, norm, matrix):
        row = lax.broadcasted_iota(jnp.int32, (LANES, LANES), 0)
        gap = row - lax.broadcasted_iota(jnp.int32, (LANES, LANES), 1)
        for t in range(tiles):
            at = slice(t * LANES, (t + 1) * LANES)
            here = jnp.where(gap == 0, band[16:17, at], 0.0)
            halo = jnp.zeros((LANES, LANES), jnp.float32)
            for d in range(1, REACH + 1):
                up, down = band[d - 1 : d, at], band[REACH + d - 1 : REACH + d, at]
                here = jnp.where(gap == d, -up, here)
                here = jnp.where(gap == -d, -down, here)
                halo = jnp.where(gap == d - LANES, -up, halo)
                halo = jnp.where(gap == LANES - d, -down, halo)
            matrix[t, :LANES, :] = here
            matrix[t, LANES:, :] = halo
        lane = lax.broadcasted_iota(jnp.int32, (rows, LANES), 1)

        def slot(j, carry):
            to = pl.ds(pl.multiple_of(j * rows, rows), rows)
            g, k = j // per, j % per
            low = pltpu.roll(left[g], (2 * LANES - REACH - REACH * k) % LANES, 1)
            high = pltpu.roll(right[g], (LANES - REACH * k) % LANES, 1)
            work = jnp.zeros((rows, LANES), jnp.float32)
            size = jnp.zeros((rows, LANES), jnp.float32)
            for t in range(tiles):
                at = slice(t * LANES, (t + 1) * LANES)
                here = x[j, :, at]
                previous = low if t == 0 else x[j, :, (t - 1) * LANES : t * LANES]
                following = high if t == tiles - 1 else x[j, :, (t + 1) * LANES : (t + 2) * LANES]
                halo = jnp.where(lane < LANES // 2, following, previous)
                total = jnp.dot(
                    jnp.concatenate([here, halo], 1),
                    matrix[t],
                    precision=HIGHEST,
                    preferred_element_type=jnp.float32,
                )
                total = total + (lam[j] * band[17:18, at]) * here
                stiff[j, :, at] = total
                work = work + total * here
                size = size + here * here
            energy[to, :] = work
            norm[to, :] = size
            return carry

        lax.fori_loop(0, count, slot, 0)
        ones = jnp.ones((ROWS, LANES), jnp.float32)
        for r, part in enumerate((energy, norm)):
            line = lax.dot_general(
                ones,
                part[...],
                (((1,), (1,)), ((), ())),
                precision=HIGHEST,
                preferred_element_type=jnp.float32,
            )
            sums[r : r + 1, :] = line[:1]

    vmem = pl.BlockSpec(memory_space=pltpu.VMEM)
    return pl.pallas_call(
        kernel,
        in_specs=[vmem, vmem, vmem, vmem, pl.BlockSpec(memory_space=pltpu.SMEM)],
        out_specs=[vmem, vmem],
        out_shape=[
            jax.ShapeDtypeStruct((count, rows, dofs), jnp.float32),
            jax.ShapeDtypeStruct((2, count * rows), jnp.float32),
        ],
        scratch_shapes=[
            pltpu.VMEM((count * rows, LANES), jnp.float32),
            pltpu.VMEM((count * rows, LANES), jnp.float32),
            pltpu.VMEM((tiles, 2 * LANES, LANES), jnp.float32),
        ],
        compiler_params=params(),
        name="stiffness",
    )(projected, before, after, bands, links)


def residual_back(projected, stiff, sums, late):
    count, rows, dofs = projected.shape
    scales = slot_scales(count)
    tiles = dofs // LANES

    def kernel(x, kx, total, extra, back, ritz, wide, sent, go):
        leaving = [pltpu.make_async_copy(extra, back.at[:, :, dofs : dofs + LANES], go.at[tiles])]
        leaving[0].start()
        value = total[0:1, :] / (total[1:2, :] + 1e-06)
        ritz[...] = value
        row = lax.broadcasted_iota(jnp.int32, (2 * ROWS, count * rows), 0)
        stack = jnp.zeros((2 * ROWS, count * rows), jnp.float32)
        for i, part in enumerate(bf16_parts(value)):
            stack = jnp.where(row == i, part.astype(jnp.float32), stack)
        wide[...] = lax.dot_general(
            stack.astype(jnp.bfloat16),
            jnp.ones((2 * ROWS, LANES), jnp.bfloat16),
            (((0,), (0,)), ((), ())),
            preferred_element_type=jnp.float32,
        )
        for t in range(tiles):
            lanes = slice(t * LANES, (t + 1) * LANES)

            def strip(r, carry, lanes=lanes):
                at = pl.ds(pl.multiple_of(r * ROWS, ROWS), ROWS)
                terms = []
                for j in range(count):
                    to = pl.ds(pl.multiple_of(j * rows + r * ROWS, ROWS), ROWS)
                    terms.append((kx[j, at, lanes] - wide[to, :] * x[j, at, lanes]) * scales[j])
                out = to_spans(terms)
                for s in range(count):
                    sent[s, at, lanes] = out[s]
                return carry

            lax.fori_loop(0, rows // ROWS, strip, 0)
            copy = pltpu.make_async_copy(sent.at[:, :, lanes], back.at[:, :, lanes], go.at[t])
            copy.start()
            leaving.append(copy)
        for copy in leaving:
            copy.wait()

    vmem = pl.BlockSpec(memory_space=pltpu.VMEM)
    return pl.pallas_call(
        kernel,
        in_specs=[vmem] * 4,
        out_specs=[pl.BlockSpec(memory_space=pltpu.HBM), vmem],
        out_shape=[
            pltpu.HBM((count, rows, dofs + LANES), jnp.float32),
            jax.ShapeDtypeStruct((1, count * rows), jnp.float32),
        ],
        scratch_shapes=[
            pltpu.VMEM((count * rows, LANES), jnp.float32),
            pltpu.VMEM((count, rows, dofs), jnp.float32),
            pltpu.SemaphoreType.DMA((tiles + 1,)),
        ],
        compiler_params=params(60_500_000),
        name="residual_back",
    )(projected, stiff, sums, late)


def halvings(axis):
    step = lax.axis_size(axis) // 2
    while step:
        yield step, [(i, i ^ step) for i in range(lax.axis_size(axis))]
        step //= 2


def exchange_step(held, step, pairs):
    other = lax.ppermute(held, "span", pairs)
    upper = (lax.axis_index("span") & step) != 0
    return jnp.stack([jnp.where(upper, other, held), jnp.where(upper, held, other)])


def in_order(held, steps):
    bits = [step for step, _ in steps][::-1]
    order = tuple(sorted(range(len(bits)), key=lambda d: -bits[d]))
    held = held.transpose(order + tuple(range(len(bits), held.ndim)))
    return held.reshape((-1,) + held.shape[len(bits) :])


def tiled_device(
    current_block,
    search_block,
    previous_block,
    ground_spring,
    wire_tension,
    dropper_stiff,
    dropper_offset,
    span_link,
    ritz_rotation,
):
    count = lax.axis_size("span")
    dofs = current_block.shape[2] // count
    rows = current_block.shape[1]
    steps = list(halvings("span"))
    tiles = list(range(dofs // LANES))
    middle = tiles[len(tiles) // 2]
    early = [t for t in tiles if t != middle]
    at = middle * LANES
    blocks = (current_block, search_block, previous_block)
    rotation = exchange_step(ritz_rotation[0].T, *steps[0])
    pieces = spread_blocks(blocks, count, [(0, at), (at + LANES, dofs - at - LANES)])
    pieces, rotation = lax.optimization_barrier((pieces, rotation))
    stacked = exchange(pieces)
    order = steps[2:] + steps[1:2]
    for step, pairs in order:
        rotation = exchange_step(rotation, step, pairs)
    rotation = in_order(rotation, [steps[0]] + order)
    scales = jnp.array(slot_scales(count), jnp.float32)[:, None, None]
    rotation = rotation * scales
    weights, ground, link = coefficients(
        ground_spring, wire_tension, dropper_stiff, dropper_offset, span_link, count, dofs
    )
    up = weights[:, REACH:]
    down = [weights[d - 1, REACH - d : REACH - d + dofs] for d in range(1, REACH + 1)]
    down = jnp.stack(down)
    diagonal = ground + jnp.sum(up, 0) + jnp.sum(down, 0)
    bands = jnp.concatenate([up, down, diagonal[None], link[None]])
    links = 2.0 * (1.0 - fourier_rows(count)[1])
    pieces = spread_blocks(blocks, count, [(at, LANES)])
    pieces, rotation, bands = lax.optimization_barrier((pieces, rotation, bands))
    stacked_late = exchange(pieces)
    projected, spans, head, tail = project(stacked, rotation, dofs, early)
    before, after = to_next(tail, 1), to_next(head, -1)
    spans, before, after = lax.optimization_barrier((spans, before, after))
    early_pieces = exchange(spans)
    projected, late = project(stacked_late, rotation, dofs, [middle], projected)
    stiff, sums = stiffness(projected, before, after, bands, links)
    for _, pairs in halvings("elem"):
        sums = sums + lax.ppermute(sums, "elem", pairs)
    for _, pairs in steps[::-1]:
        sums = sums + lax.ppermute(sums, "span", pairs)
    spans, ritz = residual_back(projected, stiff, sums, late)
    next_block = collect_early(early_pieces, at)
    next_residual, next_block = collect_late(exchange(spans), next_block, at)
    ritz = lax.dynamic_slice_in_dim(ritz, lax.axis_index("span") * rows, rows, 1)
    return (next_block, next_residual, ritz)


def on_device(
    current_block,
    search_block,
    previous_block,
    ground_spring,
    wire_tension,
    dropper_stiff,
    dropper_offset,
    span_link,
    ritz_rotation,
):
    count = lax.axis_size("span")
    dof_dev = current_block.shape[2]
    dofs = dof_dev // count
    matrix, cosines = fourier_rows(count)
    blocks = (current_block, search_block, previous_block)
    stacked = exchange(jnp.concatenate([spread(b[0], count) for b in blocks], 1))
    rotation = lax.all_gather(ritz_rotation, "span", axis=0, tiled=True)
    weights, ground, link = coefficients(
        ground_spring, wire_tension, dropper_stiff, dropper_offset, span_link, count, dofs
    )
    slots = along_spans(matrix, stacked)
    projected = jnp.einsum("jvm,jvd->jmd", rotation, slots, precision=HIGHEST)
    back = matrix.T
    next_block = collect(exchange(along_spans(back, projected)))
    before = to_next(projected[:, :, dofs - REACH :], 1)
    after = to_next(projected[:, :, :REACH], -1)
    wide = jnp.concatenate([before, projected, after], 2)
    stiff = ground * projected
    near = wide[:, :, : REACH + dofs]
    for distance in range(1, REACH + 1):
        flux = weights[distance - 1] * (near - wide[:, :, distance : distance + REACH + dofs])
        stiff = stiff + flux[:, :, REACH:] - flux[:, :, REACH - distance : REACH - distance + dofs]
    stiff = stiff + (2.0 * (1.0 - cosines))[:, None, None] * link * projected
    sums = jnp.stack([jnp.sum(projected * stiff, 2), jnp.sum(projected * projected, 2)])
    sums = lax.psum(sums, ("elem", "span"))
    ritz = sums[0] / (sums[1] + 1e-06)
    residual = stiff - ritz[:, :, None] * projected
    next_residual = collect(exchange(along_spans(back, residual)))
    my_ritz = lax.dynamic_slice_in_dim(ritz, lax.axis_index("span"), 1, 0)
    return (next_block, next_residual, my_ritz)


def by_shape(*args):
    count, dof_dev = lax.axis_size("span"), args[0].shape[2]
    halves = count & (count - 1) == 0 and lax.axis_size("elem") in (1, 2, 4, 8, 16)
    if halves and count > 2 and dof_dev % (count * LANES) == 0 and dof_dev > 2 * count * LANES:
        return tiled_device(*args)
    return on_device(*args)


def solution(mesh):
    return jax.shard_map(
        by_shape,
        mesh=mesh,
        in_specs=(
            P("span", None, "elem"),
            P("span", None, "elem"),
            P("span", None, "elem"),
            P("elem"),
            P("elem"),
            P("elem"),
            P("elem"),
            P("elem"),
            P("span", None, None),
        ),
        out_specs=(P("span", None, "elem"), P("span", None, "elem"), P("span", None)),
        check_vma=False,
    )
```

```python
import math

import jax
import jax.numpy as jnp
from jax import lax
from jax.experimental import pallas as pl
from jax.experimental.pallas import tpu as pltpu
from jax.sharding import PartitionSpec as P

REACH = 8
LANES = 128
ROWS = 8
VMEM_LIMIT = 24 * 1024 * 1024
VMEM_MOST = 61_500_000
HIGHEST = lax.Precision.HIGHEST


def fourier_rows(count):
    row = jnp.arange(count)[:, None]
    col = jnp.arange(count)[None, :]
    half = count // 2
    wave = jnp.where(row <= half, row, row - half)
    phase = (wave * col % count).astype(jnp.float32) * (2.0 * math.pi / count)
    scaled = jnp.where(row <= half, jnp.cos(phase), jnp.sin(phase)) * math.sqrt(2.0 / count)
    edge = (row == 0) | (row == half)
    matrix = jnp.where(edge, jnp.cos(phase) * math.sqrt(1.0 / count), scaled)
    slots = jnp.arange(count)
    slot_wave = jnp.where(slots <= half, slots, slots - half)
    cosines = jnp.cos(slot_wave.astype(jnp.float32) * (2.0 * math.pi / count))
    return (matrix, cosines)


def along_spans(matrix, block):
    shape = block.shape
    flat = block.reshape(shape[0], -1)
    return jnp.dot(matrix, flat, precision=HIGHEST).reshape(shape)


def spread(block, count):
    rows, dofs = block.shape
    return block.reshape(rows, count, dofs // count).transpose(1, 0, 2)


def collect(pieces):
    count, rows, dofs = pieces.shape
    return pieces.transpose(1, 0, 2).reshape(1, rows, count * dofs)


def exchange(pieces):
    return lax.all_to_all(pieces, "span", split_axis=0, concat_axis=0, tiled=True)


def to_next(cells, step):
    count, parts = lax.axis_size("span"), lax.axis_size("elem")
    line = [s * parts + e for e in range(parts) for s in range(count)]
    pairs = list(zip(line, line[1:]))
    if step < 0:
        pairs = [(b, a) for a, b in pairs]
    return lax.ppermute(cells, ("span", "elem"), pairs)


def coefficients(ground, tension, stiff, offset, link, count, dofs):
    dof_dev = ground.shape[0]
    start = lax.axis_index("span") * dofs
    elem = lax.axis_index("elem")
    dof_all = dof_dev * lax.axis_size("elem")
    position = elem * dof_dev + jnp.arange(dof_dev)
    distance = jnp.arange(1, REACH + 1)[:, None]
    weights = jnp.where((offset == distance) & (position + distance < dof_all), stiff, 0.0)
    wire = jnp.where((distance == 1) & (position < dof_all - 1), tension, 0.0)
    weights = weights + wire
    pairs = [(i, i + 1) for i in range(lax.axis_size("elem") - 1)]
    left = lax.ppermute(weights[:, dof_dev - REACH :], "elem", pairs)
    weights = jnp.concatenate([left, weights], 1)
    weights = lax.dynamic_slice_in_dim(weights, start, dofs + REACH, 1)
    ground = lax.dynamic_slice_in_dim(ground, start, dofs, 0)
    link = lax.dynamic_slice_in_dim(link, start, dofs, 0)
    return weights, ground, link


def add_up(terms):
    total = terms[0]
    for term in terms[1:]:
        total = total + term
    return total


def scaled(factor, value):
    if abs(factor - 1.0) < 1e-12:
        return value
    return value * factor


def cosine_sums(a):
    n = len(a) - 1
    if n == 1:
        return [a[0] + a[1], a[0] - a[1]]
    half = n // 2
    even = cosine_sums([a[s] + a[n - s] for s in range(half)] + [a[half]])
    diff = [a[s] - a[n - s] for s in range(half)]
    out = [None] * (n + 1)
    out[0::2] = even
    for j in range(1, n, 2):
        out[j] = add_up([scaled(math.cos(math.pi * j * s / n), diff[s]) for s in range(half)])
    return out


def sine_sums(b):
    n = len(b) + 1
    if n == 1:
        return []
    half = n // 2
    at = [None] + list(b)
    even = sine_sums([at[s] - at[n - s] for s in range(1, half)])
    total = [None] + [at[s] + at[n - s] for s in range(1, half)] + [at[half]]
    out = [None] * (n + 1)
    for k, value in enumerate(even):
        out[2 * k + 2] = value
    for j in range(1, n, 2):
        terms = [(math.sin(math.pi * j * s / n), total[s]) for s in range(1, half + 1)]
        terms = [scaled(abs(f), t) if f > 0 else -scaled(abs(f), t) for f, t in terms]
        out[j] = add_up(terms)
    return out[1:n]


def slot_scales(count):
    edge, inner = math.sqrt(1.0 / count), math.sqrt(2.0 / count)
    return [edge if j in (0, count // 2) else inner for j in range(count)]


def to_slots(x):
    n = len(x)
    half = n // 2
    plus = [x[0]] + [x[s] + x[n - s] for s in range(1, half)] + [x[half]]
    minus = [x[s] - x[n - s] for s in range(1, half)]
    return cosine_sums(plus) + sine_sums(minus)


def to_spans(y):
    n = len(y)
    half = n // 2
    even = cosine_sums(y[: half + 1])
    odd = [None] + sine_sums(y[half + 1 :])
    out = [None] * n
    out[0], out[half] = even[0], even[half]
    for s in range(1, half):
        out[s] = even[s] + odd[s]
        out[n - s] = even[s] - odd[s]
    return out


def params(limit=VMEM_LIMIT):
    return pltpu.CompilerParams(vmem_limit_bytes=limit)


def spread_blocks(blocks, count, ranges):
    _, rows, dof_dev = blocks[0].shape
    dofs = dof_dev // count
    kinds = len(blocks)
    shape = (count, kinds * rows, sum(width for _, width in ranges))
    many = kinds * len(ranges)

    def kernel(*refs):
        out, held, come, go = refs[kinds:]
        arrivals = []
        for i in range(count):
            group, to = [], 0
            for first, width in ranges:
                for k in range(kinds):
                    copy = pltpu.make_async_copy(
                        refs[k].at[0, :, i * dofs + first : i * dofs + first + width],
                        held.at[i, k * rows : (k + 1) * rows, to : to + width],
                        come.at[i * many + len(group)],
                    )
                    copy.start()
                    group.append(copy)
                to += width
            arrivals.append(group)
        leaving = []
        for i, group in enumerate(arrivals):
            for copy in group:
                copy.wait()
            piece = pltpu.make_async_copy(held.at[i], out.at[i], go.at[i])
            piece.start()
            leaving.append(piece)
        for piece in leaving:
            piece.wait()

    whole = pl.BlockSpec(memory_space=pltpu.HBM)
    return pl.pallas_call(
        kernel,
        in_specs=[whole] * kinds,
        out_specs=whole,
        out_shape=pltpu.HBM(shape, jnp.float32),
        scratch_shapes=[
            pltpu.VMEM(shape, jnp.float32),
            pltpu.SemaphoreType.DMA((count * many,)),
            pltpu.SemaphoreType.DMA((count,)),
        ],
        compiler_params=params(VMEM_MOST),
        name="spread_blocks",
    )(*blocks)


def collect_early(early, middle):
    count, rows, early_width = early.shape
    dofs = early_width + LANES
    many = max(n for n in (1, 2, 4, 8) if count % n == 0)

    def kernel(first, block):
        for i in range(many):
            at = i * dofs
            block[0, :, at : at + middle] = first[i, :, :middle]
            block[0, :, at + middle + LANES : at + dofs] = first[i, :, middle:]

    return pl.pallas_call(
        kernel,
        grid=(count // many,),
        in_specs=[pl.BlockSpec((many, rows, early_width), lambda i: (i, 0, 0))],
        out_specs=pl.BlockSpec((1, rows, many * dofs), lambda i: (0, 0, i)),
        out_shape=pltpu.HBM((1, rows, count * dofs), jnp.float32),
        compiler_params=params(VMEM_MOST),
        name="collect_early",
    )(early)


def collect_late(late, block, middle):
    count, rows, width = late.shape
    dofs = width - LANES

    def kernel(last, _, residual, whole, sem):
        copies = []
        for i in range(count):
            at = i * dofs + middle
            copies.append(
                pltpu.make_async_copy(
                    last.at[i, :, :dofs],
                    residual.at[0, :, i * dofs : (i + 1) * dofs],
                    sem.at[2 * i],
                )
            )
            copies.append(
                pltpu.make_async_copy(
                    last.at[i, :, dofs:width], whole.at[0, :, at : at + LANES], sem.at[2 * i + 1]
                )
            )
        for copy in copies:
            copy.start()
        for copy in copies:
            copy.wait()

    place = pl.BlockSpec(memory_space=pltpu.HBM)
    shape = pltpu.HBM((1, rows, count * dofs), jnp.float32)
    return pl.pallas_call(
        kernel,
        in_specs=[pl.BlockSpec(memory_space=pltpu.VMEM), place],
        out_specs=[place, place],
        out_shape=[shape, shape],
        input_output_aliases={1: 1},
        scratch_shapes=[pltpu.SemaphoreType.DMA((2 * count,))],
        compiler_params=params(),
        name="collect_late",
    )(late, block)


PARTS = 3


def bf16_parts(value):
    parts = []
    for i in range(PARTS):
        parts.append(value.astype(jnp.bfloat16))
        if i < PARTS - 1:
            value = value - parts[i].astype(jnp.float32)
    return parts


def project(stacked, rotation, dofs, tiles, prior=None):
    count, wide, _ = stacked.shape
    rows = rotation.shape[1]
    width = len(tiles) * LANES
    scales = slot_scales(count)
    groups = -(-count * REACH // LANES)
    per = LANES // REACH
    strip = 2 * ROWS

    def kernel(x, rot, *refs):
        refs = refs[1:] if prior is not None else refs
        proj, back = refs[:2]
        edges, scratch = (refs[2:4], refs[4:]) if prior is None else ((), refs[2:])
        held, split_rot, mine, sent, come, go = scratch[:6]
        split_slots = scratch[6:]
        arrivals = []
        for c in range(len(tiles)):
            copy = pltpu.make_async_copy(
                x.at[:, :, c * LANES : (c + 1) * LANES], held.at[c], come.at[c]
            )
            copy.start()
            arrivals.append(copy)

        def one(j, carry):
            for i, part in enumerate(bf16_parts(rot[j])):
                split_rot[j, i * rows : (i + 1) * rows, :] = part
            return carry

        lax.fori_loop(0, count, one, 0)
        for c, copy in enumerate(arrivals):
            copy.wait()

            def transform(r, carry, c=c):
                at = pl.ds(pl.multiple_of(r * strip, strip), strip)
                halves = []
                for h in range(2):
                    own = pl.ds(pl.multiple_of(r * strip + h * ROWS, ROWS), ROWS)
                    halves.append(to_slots([held[c, s, own, :] for s in range(count)]))
                for j in range(count):
                    value = jnp.concatenate([half[j] for half in halves], 0)
                    for part, ref in zip(bf16_parts(value), split_slots):
                        ref[j, at, c * LANES : (c + 1) * LANES] = part
                return carry

            lax.fori_loop(0, wide // strip, transform, 0)
        for j in range(count):
            total = None
            for i in range(PARTS - 1, -1, -1):
                terms = PARTS - i
                stacked_terms = jnp.dot(
                    split_rot[j, : terms * rows, :],
                    split_slots[i][j],
                    preferred_element_type=jnp.float32,
                )
                for q in range(terms - 1, -1, -1):
                    term = stacked_terms[q * rows : (q + 1) * rows]
                    total = term if total is None else total + term
            mine[j] = total
        leaving = []

        def leave(source, target, c, t, at):
            copy = pltpu.make_async_copy(
                source.at[:, :, c * LANES : (c + 1) * LANES],
                target.at[:, :, t * LANES : (t + 1) * LANES],
                go.at[at],
            )
            copy.start()
            leaving.append(copy)

        for c, t in enumerate(tiles):
            leave(mine, proj, c, t, c)
        for c in range(len(tiles)):
            lanes = slice(c * LANES, (c + 1) * LANES)

            def inverse(r, carry, lanes=lanes):
                at = pl.ds(pl.multiple_of(r * ROWS, ROWS), ROWS)
                out = to_spans([mine[j, at, lanes] * scales[j] for j in range(count)])
                for s in range(count):
                    sent[s, at, lanes] = out[s]
                return carry

            lax.fori_loop(0, rows // ROWS, inverse, 0)
            leave(sent, back, c, c, len(tiles) + c)
        lane = lax.broadcasted_iota(jnp.int32, (rows, LANES), 1)
        ends = ((0, 0), (len(tiles) - 1, LANES - REACH))
        for ref, (c, start) in zip(edges, ends):
            for g in range(groups):
                packed = jnp.zeros((rows, LANES), jnp.float32)
                for k in range(min(per, count - g * per)):
                    turn = (k * REACH - start) % LANES
                    value = mine[g * per + k, :, c * LANES : (c + 1) * LANES]
                    value = pltpu.roll(value, turn, 1) if turn else value
                    packed = jnp.where(lane // REACH == k, value, packed)
                ref[g] = packed
        for copy in leaving:
            copy.wait()

    whole = pl.BlockSpec(memory_space=pltpu.HBM)
    vmem = pl.BlockSpec(memory_space=pltpu.VMEM)
    field = pltpu.HBM((count, rows, dofs), jnp.float32)
    edge = jax.ShapeDtypeStruct((groups, rows, LANES), jnp.float32)
    sending = pltpu.HBM((count, rows, width), jnp.float32)
    first = prior is None
    passes = PARTS * (PARTS + 1) // 2
    cost = pl.CostEstimate(
        flops=2 * passes * count * wide * rows * width,
        bytes_accessed=4 * count * (wide + 2 * rows) * width,
        transcendentals=0,
    )
    return pl.pallas_call(
        kernel,
        in_specs=[whole, vmem] + ([] if first else [whole]),
        out_specs=[whole, whole] + ([vmem, vmem] if first else []),
        out_shape=[field, sending] + ([edge, edge] if first else []),
        input_output_aliases={} if first else {2: 0},
        cost_estimate=cost,
        scratch_shapes=[
            pltpu.VMEM((len(tiles), count, wide, LANES), jnp.float32),
            pltpu.VMEM((count, PARTS * rows, wide), jnp.bfloat16),
            pltpu.VMEM((count, rows, width), jnp.float32),
            pltpu.VMEM((count, rows, width), jnp.float32),
            pltpu.SemaphoreType.DMA((len(tiles),)),
            pltpu.SemaphoreType.DMA((2 * len(tiles),)),
        ]
        + [pltpu.VMEM((count, wide, width), jnp.bfloat16)] * PARTS,
        compiler_params=params(65_400_000),
        name="project",
    )(stacked, rotation, *(() if first else (prior,)))


def stiffness(projected, before, after, bands, links):
    count, rows, dofs = projected.shape
    per = LANES // REACH
    tiles = dofs // LANES

    def kernel(x, left, right, band, lam, stiff, sums, energy, norm, matrix):
        row = lax.broadcasted_iota(jnp.int32, (LANES, LANES), 0)
        gap = row - lax.broadcasted_iota(jnp.int32, (LANES, LANES), 1)
        for t in range(tiles):
            at = slice(t * LANES, (t + 1) * LANES)
            here = jnp.where(gap == 0, band[16:17, at], 0.0)
            halo = jnp.zeros((LANES, LANES), jnp.float32)
            for d in range(1, REACH + 1):
                up, down = band[d - 1 : d, at], band[REACH + d - 1 : REACH + d, at]
                here = jnp.where(gap == d, -up, here)
                here = jnp.where(gap == -d, -down, here)
                halo = jnp.where(gap == d - LANES, -up, halo)
                halo = jnp.where(gap == LANES - d, -down, halo)
            matrix[t, :LANES, :] = here
            matrix[t, LANES:, :] = halo
        lane = lax.broadcasted_iota(jnp.int32, (rows, LANES), 1)

        def slot(j, carry):
            to = pl.ds(pl.multiple_of(j * rows, rows), rows)
            g, k = j // per, j % per
            low = pltpu.roll(left[g], (2 * LANES - REACH - REACH * k) % LANES, 1)
            high = pltpu.roll(right[g], (LANES - REACH * k) % LANES, 1)
            work = jnp.zeros((rows, LANES), jnp.float32)
            size = jnp.zeros((rows, LANES), jnp.float32)
            for t in range(tiles):
                at = slice(t * LANES, (t + 1) * LANES)
                here = x[j, :, at]
                previous = low if t == 0 else x[j, :, (t - 1) * LANES : t * LANES]
                following = high if t == tiles - 1 else x[j, :, (t + 1) * LANES : (t + 2) * LANES]
                halo = jnp.where(lane < LANES // 2, following, previous)
                total = jnp.dot(
                    jnp.concatenate([here, halo], 1),
                    matrix[t],
                    precision=HIGHEST,
                    preferred_element_type=jnp.float32,
                )
                total = total + (lam[j] * band[17:18, at]) * here
                stiff[j, :, at] = total
                work = work + total * here
                size = size + here * here
            energy[to, :] = work
            norm[to, :] = size
            return carry

        lax.fori_loop(0, count, slot, 0)
        ones = jnp.ones((ROWS, LANES), jnp.float32)
        for r, part in enumerate((energy, norm)):
            line = lax.dot_general(
                ones,
                part[...],
                (((1,), (1,)), ((), ())),
                precision=HIGHEST,
                preferred_element_type=jnp.float32,
            )
            sums[r : r + 1, :] = line[:1]

    vmem = pl.BlockSpec(memory_space=pltpu.VMEM)
    return pl.pallas_call(
        kernel,
        in_specs=[vmem, vmem, vmem, vmem, pl.BlockSpec(memory_space=pltpu.SMEM)],
        out_specs=[vmem, vmem],
        out_shape=[
            jax.ShapeDtypeStruct((count, rows, dofs), jnp.float32),
            jax.ShapeDtypeStruct((2, count * rows), jnp.float32),
        ],
        scratch_shapes=[
            pltpu.VMEM((count * rows, LANES), jnp.float32),
            pltpu.VMEM((count * rows, LANES), jnp.float32),
            pltpu.VMEM((tiles, 2 * LANES, LANES), jnp.float32),
        ],
        compiler_params=params(),
        name="stiffness",
    )(projected, before, after, bands, links)


def residual_back(projected, stiff, sums, late):
    count, rows, dofs = projected.shape
    scales = slot_scales(count)
    tiles = dofs // LANES

    def kernel(x, kx, total, extra, back, ritz, wide, sent, go):
        leaving = [pltpu.make_async_copy(extra, back.at[:, :, dofs : dofs + LANES], go.at[tiles])]
        leaving[0].start()
        value = total[0:1, :] / (total[1:2, :] + 1e-06)
        ritz[...] = value
        row = lax.broadcasted_iota(jnp.int32, (2 * ROWS, count * rows), 0)
        stack = jnp.zeros((2 * ROWS, count * rows), jnp.float32)
        for i, part in enumerate(bf16_parts(value)):
            stack = jnp.where(row == i, part.astype(jnp.float32), stack)
        wide[...] = lax.dot_general(
            stack.astype(jnp.bfloat16),
            jnp.ones((2 * ROWS, LANES), jnp.bfloat16),
            (((0,), (0,)), ((), ())),
            preferred_element_type=jnp.float32,
        )
        for t in range(tiles):
            lanes = slice(t * LANES, (t + 1) * LANES)

            def strip(r, carry, lanes=lanes):
                at = pl.ds(pl.multiple_of(r * ROWS, ROWS), ROWS)
                terms = []
                for j in range(count):
                    to = pl.ds(pl.multiple_of(j * rows + r * ROWS, ROWS), ROWS)
                    terms.append((kx[j, at, lanes] - wide[to, :] * x[j, at, lanes]) * scales[j])
                out = to_spans(terms)
                for s in range(count):
                    sent[s, at, lanes] = out[s]
                return carry

            lax.fori_loop(0, rows // ROWS, strip, 0)
            copy = pltpu.make_async_copy(sent.at[:, :, lanes], back.at[:, :, lanes], go.at[t])
            copy.start()
            leaving.append(copy)
        for copy in leaving:
            copy.wait()

    vmem = pl.BlockSpec(memory_space=pltpu.VMEM)
    return pl.pallas_call(
        kernel,
        in_specs=[vmem] * 4,
        out_specs=[pl.BlockSpec(memory_space=pltpu.HBM), vmem],
        out_shape=[
            pltpu.HBM((count, rows, dofs + LANES), jnp.float32),
            jax.ShapeDtypeStruct((1, count * rows), jnp.float32),
        ],
        scratch_shapes=[
            pltpu.VMEM((count * rows, LANES), jnp.float32),
            pltpu.VMEM((count, rows, dofs), jnp.float32),
            pltpu.SemaphoreType.DMA((tiles + 1,)),
        ],
        compiler_params=params(57_400_000),
        name="residual_back",
    )(projected, stiff, sums, late)


def halvings(axis):
    step = lax.axis_size(axis) // 2
    while step:
        yield step, [(i, i ^ step) for i in range(lax.axis_size(axis))]
        step //= 2


def exchange_step(held, step, pairs):
    other = lax.ppermute(held, "span", pairs)
    upper = (lax.axis_index("span") & step) != 0
    return jnp.stack([jnp.where(upper, other, held), jnp.where(upper, held, other)])


def in_order(held, steps):
    bits = [step for step, _ in steps][::-1]
    order = tuple(sorted(range(len(bits)), key=lambda d: -bits[d]))
    held = held.transpose(order + tuple(range(len(bits), held.ndim)))
    return held.reshape((-1,) + held.shape[len(bits) :])


def tiled_device(
    current_block,
    search_block,
    previous_block,
    ground_spring,
    wire_tension,
    dropper_stiff,
    dropper_offset,
    span_link,
    ritz_rotation,
):
    count = lax.axis_size("span")
    dofs = current_block.shape[2] // count
    rows = current_block.shape[1]
    steps = list(halvings("span"))
    tiles = list(range(dofs // LANES))
    middle = tiles[len(tiles) // 2]
    early = [t for t in tiles if t != middle]
    at = middle * LANES
    blocks = (current_block, search_block, previous_block)
    rotation = exchange_step(ritz_rotation[0].T, *steps[0])
    pieces = spread_blocks(blocks, count, [(0, at), (at + LANES, dofs - at - LANES)])
    pieces, rotation = lax.optimization_barrier((pieces, rotation))
    stacked = exchange(pieces)
    order = steps[2:] + steps[1:2]
    for step, pairs in order:
        rotation = exchange_step(rotation, step, pairs)
    rotation = in_order(rotation, [steps[0]] + order)
    scales = jnp.array(slot_scales(count), jnp.float32)[:, None, None]
    rotation = rotation * scales
    weights, ground, link = coefficients(
        ground_spring, wire_tension, dropper_stiff, dropper_offset, span_link, count, dofs
    )
    up = weights[:, REACH:]
    down = [weights[d - 1, REACH - d : REACH - d + dofs] for d in range(1, REACH + 1)]
    down = jnp.stack(down)
    diagonal = ground + jnp.sum(up, 0) + jnp.sum(down, 0)
    bands = jnp.concatenate([up, down, diagonal[None], link[None]])
    links = 2.0 * (1.0 - fourier_rows(count)[1])
    pieces = spread_blocks(blocks, count, [(at, LANES)])
    pieces, rotation, bands = lax.optimization_barrier((pieces, rotation, bands))
    stacked_late = exchange(pieces)
    projected, spans, head, tail = project(stacked, rotation, dofs, early)
    before, after = to_next(tail, 1), to_next(head, -1)
    spans, before, after = lax.optimization_barrier((spans, before, after))
    early_pieces = exchange(spans)
    projected, late = project(stacked_late, rotation, dofs, [middle], projected)
    stiff, sums = stiffness(projected, before, after, bands, links)
    for _, pairs in halvings("elem"):
        sums = sums + lax.ppermute(sums, "elem", pairs)
    for _, pairs in steps[::-1]:
        sums = sums + lax.ppermute(sums, "span", pairs)
    spans, ritz = residual_back(projected, stiff, sums, late)
    next_block = collect_early(early_pieces, at)
    next_residual, next_block = collect_late(exchange(spans), next_block, at)
    ritz = lax.dynamic_slice_in_dim(ritz, lax.axis_index("span") * rows, rows, 1)
    return (next_block, next_residual, ritz)


def on_device(
    current_block,
    search_block,
    previous_block,
    ground_spring,
    wire_tension,
    dropper_stiff,
    dropper_offset,
    span_link,
    ritz_rotation,
):
    count = lax.axis_size("span")
    dof_dev = current_block.shape[2]
    dofs = dof_dev // count
    matrix, cosines = fourier_rows(count)
    blocks = (current_block, search_block, previous_block)
    stacked = exchange(jnp.concatenate([spread(b[0], count) for b in blocks], 1))
    rotation = lax.all_gather(ritz_rotation, "span", axis=0, tiled=True)
    weights, ground, link = coefficients(
        ground_spring, wire_tension, dropper_stiff, dropper_offset, span_link, count, dofs
    )
    slots = along_spans(matrix, stacked)
    projected = jnp.einsum("jvm,jvd->jmd", rotation, slots, precision=HIGHEST)
    back = matrix.T
    next_block = collect(exchange(along_spans(back, projected)))
    before = to_next(projected[:, :, dofs - REACH :], 1)
    after = to_next(projected[:, :, :REACH], -1)
    wide = jnp.concatenate([before, projected, after], 2)
    stiff = ground * projected
    near = wide[:, :, : REACH + dofs]
    for distance in range(1, REACH + 1):
        flux = weights[distance - 1] * (near - wide[:, :, distance : distance + REACH + dofs])
        stiff = stiff + flux[:, :, REACH:] - flux[:, :, REACH - distance : REACH - distance + dofs]
    stiff = stiff + (2.0 * (1.0 - cosines))[:, None, None] * link * projected
    sums = jnp.stack([jnp.sum(projected * stiff, 2), jnp.sum(projected * projected, 2)])
    sums = lax.psum(sums, ("elem", "span"))
    ritz = sums[0] / (sums[1] + 1e-06)
    residual = stiff - ritz[:, :, None] * projected
    next_residual = collect(exchange(along_spans(back, residual)))
    my_ritz = lax.dynamic_slice_in_dim(ritz, lax.axis_index("span"), 1, 0)
    return (next_block, next_residual, my_ritz)


def by_shape(*args):
    count, dof_dev = lax.axis_size("span"), args[0].shape[2]
    halves = count & (count - 1) == 0 and lax.axis_size("elem") in (1, 2, 4, 8, 16)
    if halves and count > 2 and dof_dev % (count * LANES) == 0 and dof_dev > 2 * count * LANES:
        return tiled_device(*args)
    return on_device(*args)


def solution(mesh):
    return jax.shard_map(
        by_shape,
        mesh=mesh,
        in_specs=(
            P("span", None, "elem"),
            P("span", None, "elem"),
            P("span", None, "elem"),
            P("elem"),
            P("elem"),
            P("elem"),
            P("elem"),
            P("elem"),
            P("span", None, None),
        ),
        out_specs=(P("span", None, "elem"), P("span", None, "elem"), P("span", None)),
        check_vma=False,
    )
```

```python
import math

import jax
import jax.numpy as jnp
from jax import lax
from jax.experimental import pallas as pl
from jax.experimental.pallas import tpu as pltpu
from jax.sharding import PartitionSpec as P

REACH = 8
LANES = 128
ROWS = 8
VMEM_LIMIT = 24 * 1024 * 1024
VMEM_MOST = 61_500_000
HIGHEST = lax.Precision.HIGHEST


def fourier_rows(count):
    row = jnp.arange(count)[:, None]
    col = jnp.arange(count)[None, :]
    half = count // 2
    wave = jnp.where(row <= half, row, row - half)
    phase = (wave * col % count).astype(jnp.float32) * (2.0 * math.pi / count)
    scaled = jnp.where(row <= half, jnp.cos(phase), jnp.sin(phase)) * math.sqrt(2.0 / count)
    edge = (row == 0) | (row == half)
    matrix = jnp.where(edge, jnp.cos(phase) * math.sqrt(1.0 / count), scaled)
    slots = jnp.arange(count)
    slot_wave = jnp.where(slots <= half, slots, slots - half)
    cosines = jnp.cos(slot_wave.astype(jnp.float32) * (2.0 * math.pi / count))
    return (matrix, cosines)


def along_spans(matrix, block):
    shape = block.shape
    flat = block.reshape(shape[0], -1)
    return jnp.dot(matrix, flat, precision=HIGHEST).reshape(shape)


def spread(block, count):
    rows, dofs = block.shape
    return block.reshape(rows, count, dofs // count).transpose(1, 0, 2)


def collect(pieces):
    count, rows, dofs = pieces.shape
    return pieces.transpose(1, 0, 2).reshape(1, rows, count * dofs)


def exchange(pieces):
    return lax.all_to_all(pieces, "span", split_axis=0, concat_axis=0, tiled=True)


def to_next(cells, step):
    count, parts = lax.axis_size("span"), lax.axis_size("elem")
    line = [s * parts + e for e in range(parts) for s in range(count)]
    pairs = list(zip(line, line[1:]))
    if step < 0:
        pairs = [(b, a) for a, b in pairs]
    return lax.ppermute(cells, ("span", "elem"), pairs)


def coefficients(ground, tension, stiff, offset, link, count, dofs):
    dof_dev = ground.shape[0]
    start = lax.axis_index("span") * dofs
    elem = lax.axis_index("elem")
    dof_all = dof_dev * lax.axis_size("elem")
    position = elem * dof_dev + jnp.arange(dof_dev)
    distance = jnp.arange(1, REACH + 1)[:, None]
    weights = jnp.where((offset == distance) & (position + distance < dof_all), stiff, 0.0)
    wire = jnp.where((distance == 1) & (position < dof_all - 1), tension, 0.0)
    weights = weights + wire
    pairs = [(i, i + 1) for i in range(lax.axis_size("elem") - 1)]
    left = lax.ppermute(weights[:, dof_dev - REACH :], "elem", pairs)
    weights = jnp.concatenate([left, weights], 1)
    weights = lax.dynamic_slice_in_dim(weights, start, dofs + REACH, 1)
    ground = lax.dynamic_slice_in_dim(ground, start, dofs, 0)
    link = lax.dynamic_slice_in_dim(link, start, dofs, 0)
    return weights, ground, link


def add_up(terms):
    total = terms[0]
    for term in terms[1:]:
        total = total + term
    return total


def scaled(factor, value):
    if abs(factor - 1.0) < 1e-12:
        return value
    return value * factor


def cosine_sums(a):
    n = len(a) - 1
    if n == 1:
        return [a[0] + a[1], a[0] - a[1]]
    half = n // 2
    even = cosine_sums([a[s] + a[n - s] for s in range(half)] + [a[half]])
    diff = [a[s] - a[n - s] for s in range(half)]
    out = [None] * (n + 1)
    out[0::2] = even
    for j in range(1, n, 2):
        out[j] = add_up([scaled(math.cos(math.pi * j * s / n), diff[s]) for s in range(half)])
    return out


def sine_sums(b):
    n = len(b) + 1
    if n == 1:
        return []
    half = n // 2
    at = [None] + list(b)
    even = sine_sums([at[s] - at[n - s] for s in range(1, half)])
    total = [None] + [at[s] + at[n - s] for s in range(1, half)] + [at[half]]
    out = [None] * (n + 1)
    for k, value in enumerate(even):
        out[2 * k + 2] = value
    for j in range(1, n, 2):
        terms = [(math.sin(math.pi * j * s / n), total[s]) for s in range(1, half + 1)]
        terms = [scaled(abs(f), t) if f > 0 else -scaled(abs(f), t) for f, t in terms]
        out[j] = add_up(terms)
    return out[1:n]


def slot_scales(count):
    edge, inner = math.sqrt(1.0 / count), math.sqrt(2.0 / count)
    return [edge if j in (0, count // 2) else inner for j in range(count)]


def to_slots(x):
    n = len(x)
    half = n // 2
    plus = [x[0]] + [x[s] + x[n - s] for s in range(1, half)] + [x[half]]
    minus = [x[s] - x[n - s] for s in range(1, half)]
    return cosine_sums(plus) + sine_sums(minus)


def to_spans(y):
    n = len(y)
    half = n // 2
    even = cosine_sums(y[: half + 1])
    odd = [None] + sine_sums(y[half + 1 :])
    out = [None] * n
    out[0], out[half] = even[0], even[half]
    for s in range(1, half):
        out[s] = even[s] + odd[s]
        out[n - s] = even[s] - odd[s]
    return out


def params(limit=VMEM_LIMIT):
    return pltpu.CompilerParams(vmem_limit_bytes=limit)


def spread_blocks(blocks, count, ranges):
    _, rows, dof_dev = blocks[0].shape
    dofs = dof_dev // count
    kinds = len(blocks)
    shape = (count, kinds * rows, sum(width for _, width in ranges))
    many = kinds * len(ranges)

    def kernel(*refs):
        out, held, come, go = refs[kinds:]
        arrivals = []
        for i in range(count):
            group, to = [], 0
            for first, width in ranges:
                for k in range(kinds):
                    copy = pltpu.make_async_copy(
                        refs[k].at[0, :, i * dofs + first : i * dofs + first + width],
                        held.at[i, k * rows : (k + 1) * rows, to : to + width],
                        come.at[i * many + len(group)],
                    )
                    copy.start()
                    group.append(copy)
                to += width
            arrivals.append(group)
        leaving = []
        for i, group in enumerate(arrivals):
            for copy in group:
                copy.wait()
            piece = pltpu.make_async_copy(held.at[i], out.at[i], go.at[i])
            piece.start()
            leaving.append(piece)
        for piece in leaving:
            piece.wait()

    whole = pl.BlockSpec(memory_space=pltpu.HBM)
    return pl.pallas_call(
        kernel,
        in_specs=[whole] * kinds,
        out_specs=whole,
        out_shape=pltpu.HBM(shape, jnp.float32),
        scratch_shapes=[
            pltpu.VMEM(shape, jnp.float32),
            pltpu.SemaphoreType.DMA((count * many,)),
            pltpu.SemaphoreType.DMA((count,)),
        ],
        compiler_params=params(VMEM_MOST),
        name="spread_blocks",
    )(*blocks)


def collect_early(early, middle):
    count, rows, early_width = early.shape
    dofs = early_width + LANES
    many = max(n for n in (1, 2, 4, 8) if count % n == 0)

    def kernel(first, block):
        for i in range(many):
            at = i * dofs
            block[0, :, at : at + middle] = first[i, :, :middle]
            block[0, :, at + middle + LANES : at + dofs] = first[i, :, middle:]

    return pl.pallas_call(
        kernel,
        grid=(count // many,),
        in_specs=[pl.BlockSpec((many, rows, early_width), lambda i: (i, 0, 0))],
        out_specs=pl.BlockSpec((1, rows, many * dofs), lambda i: (0, 0, i)),
        out_shape=pltpu.HBM((1, rows, count * dofs), jnp.float32),
        compiler_params=params(VMEM_MOST),
        name="collect_early",
    )(early)


def collect_late(late, block, middle):
    count, rows, width = late.shape
    dofs = width - LANES

    def kernel(last, _, residual, whole, sem):
        copies = []
        for i in range(count):
            at = i * dofs + middle
            copies.append(
                pltpu.make_async_copy(
                    last.at[i, :, :dofs],
                    residual.at[0, :, i * dofs : (i + 1) * dofs],
                    sem.at[2 * i],
                )
            )
            copies.append(
                pltpu.make_async_copy(
                    last.at[i, :, dofs:width], whole.at[0, :, at : at + LANES], sem.at[2 * i + 1]
                )
            )
        for copy in copies:
            copy.start()
        for copy in copies:
            copy.wait()

    place = pl.BlockSpec(memory_space=pltpu.HBM)
    shape = pltpu.HBM((1, rows, count * dofs), jnp.float32)
    return pl.pallas_call(
        kernel,
        in_specs=[pl.BlockSpec(memory_space=pltpu.VMEM), place],
        out_specs=[place, place],
        out_shape=[shape, shape],
        input_output_aliases={1: 1},
        scratch_shapes=[pltpu.SemaphoreType.DMA((2 * count,))],
        compiler_params=params(),
        name="collect_late",
    )(late, block)


PARTS = 3


def bf16_parts(value):
    parts = []
    for i in range(PARTS):
        parts.append(value.astype(jnp.bfloat16))
        if i < PARTS - 1:
            value = value - parts[i].astype(jnp.float32)
    return parts


def project(stacked, rotation, dofs, tiles, prior=None):
    count, wide, _ = stacked.shape
    rows = rotation.shape[1]
    width = len(tiles) * LANES
    scales = slot_scales(count)
    groups = -(-count * REACH // LANES)
    per = LANES // REACH
    strip = 2 * ROWS

    def kernel(x, rot, *refs):
        refs = refs[1:] if prior is not None else refs
        proj, back = refs[:2]
        edges, scratch = (refs[2:4], refs[4:]) if prior is None else ((), refs[2:])
        held, split_rot, mine, sent, come, go = scratch[:6]
        split_slots = scratch[6:]
        arrivals = []
        for c in range(len(tiles)):
            copy = pltpu.make_async_copy(
                x.at[:, :, c * LANES : (c + 1) * LANES], held.at[c], come.at[c]
            )
            copy.start()
            arrivals.append(copy)

        def one(j, carry):
            for i, part in enumerate(bf16_parts(rot[j])):
                split_rot[j, i * rows : (i + 1) * rows, :] = part
            return carry

        lax.fori_loop(0, count, one, 0)
        for c, copy in enumerate(arrivals):
            copy.wait()

            def transform(r, carry, c=c):
                at = pl.ds(pl.multiple_of(r * strip, strip), strip)
                halves = []
                for h in range(2):
                    own = pl.ds(pl.multiple_of(r * strip + h * ROWS, ROWS), ROWS)
                    halves.append(to_slots([held[c, s, own, :] for s in range(count)]))
                for j in range(count):
                    value = jnp.concatenate([half[j] for half in halves], 0)
                    for part, ref in zip(bf16_parts(value), split_slots):
                        ref[j, at, c * LANES : (c + 1) * LANES] = part
                return carry

            lax.fori_loop(0, wide // strip, transform, 0)
        for j in range(count):
            total = None
            for i in range(PARTS - 1, -1, -1):
                terms = PARTS - i
                stacked_terms = jnp.dot(
                    split_rot[j, : terms * rows, :],
                    split_slots[i][j],
                    preferred_element_type=jnp.float32,
                )
                for q in range(terms - 1, -1, -1):
                    term = stacked_terms[q * rows : (q + 1) * rows]
                    total = term if total is None else total + term
            mine[j] = total
        leaving = []

        def leave(source, target, c, t, at):
            copy = pltpu.make_async_copy(
                source.at[:, :, c * LANES : (c + 1) * LANES],
                target.at[:, :, t * LANES : (t + 1) * LANES],
                go.at[at],
            )
            copy.start()
            leaving.append(copy)

        for c, t in enumerate(tiles):
            leave(mine, proj, c, t, c)
        for c in range(len(tiles)):
            lanes = slice(c * LANES, (c + 1) * LANES)

            def inverse(r, carry, lanes=lanes):
                at = pl.ds(pl.multiple_of(r * ROWS, ROWS), ROWS)
                out = to_spans([mine[j, at, lanes] * scales[j] for j in range(count)])
                for s in range(count):
                    sent[s, at, lanes] = out[s]
                return carry

            lax.fori_loop(0, rows // ROWS, inverse, 0)
            leave(sent, back, c, c, len(tiles) + c)
        lane = lax.broadcasted_iota(jnp.int32, (rows, LANES), 1)
        ends = ((0, 0), (len(tiles) - 1, LANES - REACH))
        for ref, (c, start) in zip(edges, ends):
            for g in range(groups):
                packed = jnp.zeros((rows, LANES), jnp.float32)
                for k in range(min(per, count - g * per)):
                    turn = (k * REACH - start) % LANES
                    value = mine[g * per + k, :, c * LANES : (c + 1) * LANES]
                    value = pltpu.roll(value, turn, 1) if turn else value
                    packed = jnp.where(lane // REACH == k, value, packed)
                ref[g] = packed
        for copy in leaving:
            copy.wait()

    whole = pl.BlockSpec(memory_space=pltpu.HBM)
    vmem = pl.BlockSpec(memory_space=pltpu.VMEM)
    field = pltpu.HBM((count, rows, dofs), jnp.float32)
    edge = jax.ShapeDtypeStruct((groups, rows, LANES), jnp.float32)
    sending = pltpu.HBM((count, rows, width), jnp.float32)
    first = prior is None
    passes = PARTS * (PARTS + 1) // 2
    cost = pl.CostEstimate(
        flops=2 * passes * count * wide * rows * width,
        bytes_accessed=4 * count * (wide + 2 * rows) * width,
        transcendentals=0,
    )
    return pl.pallas_call(
        kernel,
        in_specs=[whole, vmem] + ([] if first else [whole]),
        out_specs=[whole, whole] + ([vmem, vmem] if first else []),
        out_shape=[field, sending] + ([edge, edge] if first else []),
        input_output_aliases={} if first else {2: 0},
        cost_estimate=cost,
        scratch_shapes=[
            pltpu.VMEM((len(tiles), count, wide, LANES), jnp.float32),
            pltpu.VMEM((count, PARTS * rows, wide), jnp.bfloat16),
            pltpu.VMEM((count, rows, width), jnp.float32),
            pltpu.VMEM((count, rows, width), jnp.float32),
            pltpu.SemaphoreType.DMA((len(tiles),)),
            pltpu.SemaphoreType.DMA((2 * len(tiles),)),
        ]
        + [pltpu.VMEM((count, wide, width), jnp.bfloat16)] * PARTS,
        compiler_params=params(65_400_000),
        name="project",
    )(stacked, rotation, *(() if first else (prior,)))


def stiffness(projected, before, after, bands, links):
    count, rows, dofs = projected.shape
    per = LANES // REACH
    tiles = dofs // LANES

    def kernel(x, left, right, band, lam, stiff, sums, energy, norm, matrix):
        row = lax.broadcasted_iota(jnp.int32, (LANES, LANES), 0)
        gap = row - lax.broadcasted_iota(jnp.int32, (LANES, LANES), 1)
        for t in range(tiles):
            at = slice(t * LANES, (t + 1) * LANES)
            here = jnp.where(gap == 0, band[16:17, at], 0.0)
            halo = jnp.zeros((LANES, LANES), jnp.float32)
            for d in range(1, REACH + 1):
                up, down = band[d - 1 : d, at], band[REACH + d - 1 : REACH + d, at]
                here = jnp.where(gap == d, -up, here)
                here = jnp.where(gap == -d, -down, here)
                halo = jnp.where(gap == d - LANES, -up, halo)
                halo = jnp.where(gap == LANES - d, -down, halo)
            matrix[t, :LANES, :] = here
            matrix[t, LANES:, :] = halo
        lane = lax.broadcasted_iota(jnp.int32, (rows, LANES), 1)

        def slot(j, carry):
            to = pl.ds(pl.multiple_of(j * rows, rows), rows)
            g, k = j // per, j % per
            low = pltpu.roll(left[g], (2 * LANES - REACH - REACH * k) % LANES, 1)
            high = pltpu.roll(right[g], (LANES - REACH * k) % LANES, 1)
            work = jnp.zeros((rows, LANES), jnp.float32)
            size = jnp.zeros((rows, LANES), jnp.float32)
            for t in range(tiles):
                at = slice(t * LANES, (t + 1) * LANES)
                here = x[j, :, at]
                previous = low if t == 0 else x[j, :, (t - 1) * LANES : t * LANES]
                following = high if t == tiles - 1 else x[j, :, (t + 1) * LANES : (t + 2) * LANES]
                halo = jnp.where(lane < LANES // 2, following, previous)
                total = jnp.dot(
                    jnp.concatenate([here, halo], 1),
                    matrix[t],
                    precision=HIGHEST,
                    preferred_element_type=jnp.float32,
                )
                total = total + (lam[j] * band[17:18, at]) * here
                stiff[j, :, at] = total
                work = work + total * here
                size = size + here * here
            energy[to, :] = work
            norm[to, :] = size
            return carry

        lax.fori_loop(0, count, slot, 0)
        ones = jnp.ones((ROWS, LANES), jnp.float32)
        for r, part in enumerate((energy, norm)):
            line = lax.dot_general(
                ones,
                part[...],
                (((1,), (1,)), ((), ())),
                precision=HIGHEST,
                preferred_element_type=jnp.float32,
            )
            sums[r : r + 1, :] = line[:1]

    vmem = pl.BlockSpec(memory_space=pltpu.VMEM)
    return pl.pallas_call(
        kernel,
        in_specs=[vmem, vmem, vmem, vmem, pl.BlockSpec(memory_space=pltpu.SMEM)],
        out_specs=[vmem, vmem],
        out_shape=[
            jax.ShapeDtypeStruct((count, rows, dofs), jnp.float32),
            jax.ShapeDtypeStruct((2, count * rows), jnp.float32),
        ],
        scratch_shapes=[
            pltpu.VMEM((count * rows, LANES), jnp.float32),
            pltpu.VMEM((count * rows, LANES), jnp.float32),
            pltpu.VMEM((tiles, 2 * LANES, LANES), jnp.float32),
        ],
        compiler_params=params(),
        name="stiffness",
    )(projected, before, after, bands, links)


def residual_back(projected, stiff, sums, late):
    count, rows, dofs = projected.shape
    scales = slot_scales(count)
    tiles = dofs // LANES

    def kernel(x, kx, total, extra, back, ritz, wide, sent, go):
        leaving = [pltpu.make_async_copy(extra, back.at[:, :, dofs : dofs + LANES], go.at[tiles])]
        leaving[0].start()
        value = total[0:1, :] / (total[1:2, :] + 1e-06)
        ritz[...] = value
        row = lax.broadcasted_iota(jnp.int32, (2 * ROWS, count * rows), 0)
        stack = jnp.zeros((2 * ROWS, count * rows), jnp.float32)
        for i, part in enumerate(bf16_parts(value)):
            stack = jnp.where(row == i, part.astype(jnp.float32), stack)
        wide[...] = lax.dot_general(
            stack.astype(jnp.bfloat16),
            jnp.ones((2 * ROWS, LANES), jnp.bfloat16),
            (((0,), (0,)), ((), ())),
            preferred_element_type=jnp.float32,
        )
        for t in range(tiles):
            lanes = slice(t * LANES, (t + 1) * LANES)

            def strip(r, carry, lanes=lanes):
                at = pl.ds(pl.multiple_of(r * ROWS, ROWS), ROWS)
                terms = []
                for j in range(count):
                    to = pl.ds(pl.multiple_of(j * rows + r * ROWS, ROWS), ROWS)
                    terms.append((kx[j, at, lanes] - wide[to, :] * x[j, at, lanes]) * scales[j])
                out = to_spans(terms)
                for s in range(count):
                    sent[s, at, lanes] = out[s]
                return carry

            lax.fori_loop(0, rows // ROWS, strip, 0)
            copy = pltpu.make_async_copy(sent.at[:, :, lanes], back.at[:, :, lanes], go.at[t])
            copy.start()
            leaving.append(copy)
        for copy in leaving:
            copy.wait()

    vmem = pl.BlockSpec(memory_space=pltpu.VMEM)
    return pl.pallas_call(
        kernel,
        in_specs=[vmem] * 4,
        out_specs=[pl.BlockSpec(memory_space=pltpu.HBM), vmem],
        out_shape=[
            pltpu.HBM((count, rows, dofs + LANES), jnp.float32),
            jax.ShapeDtypeStruct((1, count * rows), jnp.float32),
        ],
        scratch_shapes=[
            pltpu.VMEM((count * rows, LANES), jnp.float32),
            pltpu.VMEM((count, rows, dofs), jnp.float32),
            pltpu.SemaphoreType.DMA((tiles + 1,)),
        ],
        compiler_params=params(),
        name="residual_back",
    )(projected, stiff, sums, late)


def halvings(axis):
    step = lax.axis_size(axis) // 2
    while step:
        yield step, [(i, i ^ step) for i in range(lax.axis_size(axis))]
        step //= 2


def exchange_step(held, step, pairs):
    other = lax.ppermute(held, "span", pairs)
    upper = (lax.axis_index("span") & step) != 0
    return jnp.stack([jnp.where(upper, other, held), jnp.where(upper, held, other)])


def in_order(held, steps):
    bits = [step for step, _ in steps][::-1]
    order = tuple(sorted(range(len(bits)), key=lambda d: -bits[d]))
    held = held.transpose(order + tuple(range(len(bits), held.ndim)))
    return held.reshape((-1,) + held.shape[len(bits) :])


def tiled_device(
    current_block,
    search_block,
    previous_block,
    ground_spring,
    wire_tension,
    dropper_stiff,
    dropper_offset,
    span_link,
    ritz_rotation,
):
    count = lax.axis_size("span")
    dofs = current_block.shape[2] // count
    rows = current_block.shape[1]
    steps = list(halvings("span"))
    tiles = list(range(dofs // LANES))
    middle = tiles[len(tiles) // 2]
    early = [t for t in tiles if t != middle]
    at = middle * LANES
    blocks = (current_block, search_block, previous_block)
    rotation = exchange_step(ritz_rotation[0].T, *steps[0])
    pieces = spread_blocks(blocks, count, [(0, at), (at + LANES, dofs - at - LANES)])
    pieces, rotation = lax.optimization_barrier((pieces, rotation))
    stacked = exchange(pieces)
    order = steps[2:] + steps[1:2]
    for step, pairs in order:
        rotation = exchange_step(rotation, step, pairs)
    rotation = in_order(rotation, [steps[0]] + order)
    scales = jnp.array(slot_scales(count), jnp.float32)[:, None, None]
    rotation = rotation * scales
    weights, ground, link = coefficients(
        ground_spring, wire_tension, dropper_stiff, dropper_offset, span_link, count, dofs
    )
    up = weights[:, REACH:]
    down = [weights[d - 1, REACH - d : REACH - d + dofs] for d in range(1, REACH + 1)]
    down = jnp.stack(down)
    diagonal = ground + jnp.sum(up, 0) + jnp.sum(down, 0)
    bands = jnp.concatenate([up, down, diagonal[None], link[None]])
    links = 2.0 * (1.0 - fourier_rows(count)[1])
    pieces = spread_blocks(blocks, count, [(at, LANES)])
    pieces, rotation, bands = lax.optimization_barrier((pieces, rotation, bands))
    stacked_late = exchange(pieces)
    projected, spans, head, tail = project(stacked, rotation, dofs, early)
    before, after = to_next(tail, 1), to_next(head, -1)
    spans, before, after = lax.optimization_barrier((spans, before, after))
    early_pieces = exchange(spans)
    projected, late = project(stacked_late, rotation, dofs, [middle], projected)
    stiff, sums = stiffness(projected, before, after, bands, links)
    for _, pairs in halvings("elem"):
        sums = sums + lax.ppermute(sums, "elem", pairs)
    for _, pairs in steps[::-1]:
        sums = sums + lax.ppermute(sums, "span", pairs)
    spans, ritz = residual_back(projected, stiff, sums, late)
    next_block = collect_early(early_pieces, at)
    next_residual, next_block = collect_late(exchange(spans), next_block, at)
    ritz = lax.dynamic_slice_in_dim(ritz, lax.axis_index("span") * rows, rows, 1)
    return (next_block, next_residual, ritz)


def on_device(
    current_block,
    search_block,
    previous_block,
    ground_spring,
    wire_tension,
    dropper_stiff,
    dropper_offset,
    span_link,
    ritz_rotation,
):
    count = lax.axis_size("span")
    dof_dev = current_block.shape[2]
    dofs = dof_dev // count
    matrix, cosines = fourier_rows(count)
    blocks = (current_block, search_block, previous_block)
    stacked = exchange(jnp.concatenate([spread(b[0], count) for b in blocks], 1))
    rotation = lax.all_gather(ritz_rotation, "span", axis=0, tiled=True)
    weights, ground, link = coefficients(
        ground_spring, wire_tension, dropper_stiff, dropper_offset, span_link, count, dofs
    )
    slots = along_spans(matrix, stacked)
    projected = jnp.einsum("jvm,jvd->jmd", rotation, slots, precision=HIGHEST)
    back = matrix.T
    next_block = collect(exchange(along_spans(back, projected)))
    before = to_next(projected[:, :, dofs - REACH :], 1)
    after = to_next(projected[:, :, :REACH], -1)
    wide = jnp.concatenate([before, projected, after], 2)
    stiff = ground * projected
    near = wide[:, :, : REACH + dofs]
    for distance in range(1, REACH + 1):
        flux = weights[distance - 1] * (near - wide[:, :, distance : distance + REACH + dofs])
        stiff = stiff + flux[:, :, REACH:] - flux[:, :, REACH - distance : REACH - distance + dofs]
    stiff = stiff + (2.0 * (1.0 - cosines))[:, None, None] * link * projected
    sums = jnp.stack([jnp.sum(projected * stiff, 2), jnp.sum(projected * projected, 2)])
    sums = lax.psum(sums, ("elem", "span"))
    ritz = sums[0] / (sums[1] + 1e-06)
    residual = stiff - ritz[:, :, None] * projected
    next_residual = collect(exchange(along_spans(back, residual)))
    my_ritz = lax.dynamic_slice_in_dim(ritz, lax.axis_index("span"), 1, 0)
    return (next_block, next_residual, my_ritz)


def by_shape(*args):
    count, dof_dev = lax.axis_size("span"), args[0].shape[2]
    halves = count & (count - 1) == 0 and lax.axis_size("elem") in (1, 2, 4, 8, 16)
    if halves and count > 2 and dof_dev % (count * LANES) == 0 and dof_dev > 2 * count * LANES:
        return tiled_device(*args)
    return on_device(*args)


def solution(mesh):
    return jax.shard_map(
        by_shape,
        mesh=mesh,
        in_specs=(
            P("span", None, "elem"),
            P("span", None, "elem"),
            P("span", None, "elem"),
            P("elem"),
            P("elem"),
            P("elem"),
            P("elem"),
            P("elem"),
            P("span", None, None),
        ),
        out_specs=(P("span", None, "elem"), P("span", None, "elem"), P("span", None)),
        check_vma=False,
    )
```

```python
import math

import jax
import jax.numpy as jnp
from jax import lax
from jax.experimental import pallas as pl
from jax.experimental.pallas import tpu as pltpu
from jax.sharding import PartitionSpec as P

REACH = 8
LANES = 128
ROWS = 8
VMEM_LIMIT = 24 * 1024 * 1024
VMEM_MOST = 61_500_000
HIGHEST = lax.Precision.HIGHEST


def fourier_rows(count):
    row = jnp.arange(count)[:, None]
    col = jnp.arange(count)[None, :]
    half = count // 2
    wave = jnp.where(row <= half, row, row - half)
    phase = (wave * col % count).astype(jnp.float32) * (2.0 * math.pi / count)
    scaled = jnp.where(row <= half, jnp.cos(phase), jnp.sin(phase)) * math.sqrt(2.0 / count)
    edge = (row == 0) | (row == half)
    matrix = jnp.where(edge, jnp.cos(phase) * math.sqrt(1.0 / count), scaled)
    slots = jnp.arange(count)
    slot_wave = jnp.where(slots <= half, slots, slots - half)
    cosines = jnp.cos(slot_wave.astype(jnp.float32) * (2.0 * math.pi / count))
    return (matrix, cosines)


def along_spans(matrix, block):
    shape = block.shape
    flat = block.reshape(shape[0], -1)
    return jnp.dot(matrix, flat, precision=HIGHEST).reshape(shape)


def spread(block, count):
    rows, dofs = block.shape
    return block.reshape(rows, count, dofs // count).transpose(1, 0, 2)


def collect(pieces):
    count, rows, dofs = pieces.shape
    return pieces.transpose(1, 0, 2).reshape(1, rows, count * dofs)


def exchange(pieces):
    return lax.all_to_all(pieces, "span", split_axis=0, concat_axis=0, tiled=True)


def to_next(cells, step):
    count, parts = lax.axis_size("span"), lax.axis_size("elem")
    line = [s * parts + e for e in range(parts) for s in range(count)]
    pairs = list(zip(line, line[1:]))
    if step < 0:
        pairs = [(b, a) for a, b in pairs]
    return lax.ppermute(cells, ("span", "elem"), pairs)


def coefficients(ground, tension, stiff, offset, link, count, dofs):
    dof_dev = ground.shape[0]
    start = lax.axis_index("span") * dofs
    elem = lax.axis_index("elem")
    dof_all = dof_dev * lax.axis_size("elem")
    position = elem * dof_dev + jnp.arange(dof_dev)
    distance = jnp.arange(1, REACH + 1)[:, None]
    weights = jnp.where((offset == distance) & (position + distance < dof_all), stiff, 0.0)
    wire = jnp.where((distance == 1) & (position < dof_all - 1), tension, 0.0)
    weights = weights + wire
    pairs = [(i, i + 1) for i in range(lax.axis_size("elem") - 1)]
    left = lax.ppermute(weights[:, dof_dev - REACH :], "elem", pairs)
    weights = jnp.concatenate([left, weights], 1)
    weights = lax.dynamic_slice_in_dim(weights, start, dofs + REACH, 1)
    ground = lax.dynamic_slice_in_dim(ground, start, dofs, 0)
    link = lax.dynamic_slice_in_dim(link, start, dofs, 0)
    return weights, ground, link


def add_up(terms):
    total = terms[0]
    for term in terms[1:]:
        total = total + term
    return total


def scaled(factor, value):
    if abs(factor - 1.0) < 1e-12:
        return value
    return value * factor


def cosine_sums(a):
    n = len(a) - 1
    if n == 1:
        return [a[0] + a[1], a[0] - a[1]]
    half = n // 2
    even = cosine_sums([a[s] + a[n - s] for s in range(half)] + [a[half]])
    diff = [a[s] - a[n - s] for s in range(half)]
    out = [None] * (n + 1)
    out[0::2] = even
    for j in range(1, n, 2):
        out[j] = add_up([scaled(math.cos(math.pi * j * s / n), diff[s]) for s in range(half)])
    return out


def sine_sums(b):
    n = len(b) + 1
    if n == 1:
        return []
    half = n // 2
    at = [None] + list(b)
    even = sine_sums([at[s] - at[n - s] for s in range(1, half)])
    total = [None] + [at[s] + at[n - s] for s in range(1, half)] + [at[half]]
    out = [None] * (n + 1)
    for k, value in enumerate(even):
        out[2 * k + 2] = value
    for j in range(1, n, 2):
        terms = [(math.sin(math.pi * j * s / n), total[s]) for s in range(1, half + 1)]
        terms = [scaled(abs(f), t) if f > 0 else -scaled(abs(f), t) for f, t in terms]
        out[j] = add_up(terms)
    return out[1:n]


def slot_scales(count):
    edge, inner = math.sqrt(1.0 / count), math.sqrt(2.0 / count)
    return [edge if j in (0, count // 2) else inner for j in range(count)]


def to_slots(x):
    n = len(x)
    half = n // 2
    plus = [x[0]] + [x[s] + x[n - s] for s in range(1, half)] + [x[half]]
    minus = [x[s] - x[n - s] for s in range(1, half)]
    return cosine_sums(plus) + sine_sums(minus)


def to_spans(y):
    n = len(y)
    half = n // 2
    even = cosine_sums(y[: half + 1])
    odd = [None] + sine_sums(y[half + 1 :])
    out = [None] * n
    out[0], out[half] = even[0], even[half]
    for s in range(1, half):
        out[s] = even[s] + odd[s]
        out[n - s] = even[s] - odd[s]
    return out


def params(limit=VMEM_LIMIT):
    return pltpu.CompilerParams(vmem_limit_bytes=limit)


def spread_blocks(blocks, count, ranges):
    _, rows, dof_dev = blocks[0].shape
    dofs = dof_dev // count
    kinds = len(blocks)
    shape = (count, kinds * rows, sum(width for _, width in ranges))
    many = kinds * len(ranges)

    def kernel(*refs):
        out, held, come, go = refs[kinds:]
        arrivals = []
        for i in range(count):
            group, to = [], 0
            for first, width in ranges:
                for k in range(kinds):
                    copy = pltpu.make_async_copy(
                        refs[k].at[0, :, i * dofs + first : i * dofs + first + width],
                        held.at[i, k * rows : (k + 1) * rows, to : to + width],
                        come.at[i * many + len(group)],
                    )
                    copy.start()
                    group.append(copy)
                to += width
            arrivals.append(group)
        leaving = []
        for i, group in enumerate(arrivals):
            for copy in group:
                copy.wait()
            piece = pltpu.make_async_copy(held.at[i], out.at[i], go.at[i])
            piece.start()
            leaving.append(piece)
        for piece in leaving:
            piece.wait()

    whole = pl.BlockSpec(memory_space=pltpu.HBM)
    return pl.pallas_call(
        kernel,
        in_specs=[whole] * kinds,
        out_specs=whole,
        out_shape=pltpu.HBM(shape, jnp.float32),
        scratch_shapes=[
            pltpu.VMEM(shape, jnp.float32),
            pltpu.SemaphoreType.DMA((count * many,)),
            pltpu.SemaphoreType.DMA((count,)),
        ],
        compiler_params=params(VMEM_MOST),
        name="spread_blocks",
    )(*blocks)


def collect_early(early, middle):
    count, rows, early_width = early.shape
    dofs = early_width + LANES
    many = max(n for n in (1, 2, 4, 8) if count % n == 0)

    def kernel(first, block):
        for i in range(many):
            at = i * dofs
            block[0, :, at : at + middle] = first[i, :, :middle]
            block[0, :, at + middle + LANES : at + dofs] = first[i, :, middle:]

    return pl.pallas_call(
        kernel,
        grid=(count // many,),
        in_specs=[pl.BlockSpec((many, rows, early_width), lambda i: (i, 0, 0))],
        out_specs=pl.BlockSpec((1, rows, many * dofs), lambda i: (0, 0, i)),
        out_shape=pltpu.HBM((1, rows, count * dofs), jnp.float32),
        compiler_params=params(VMEM_MOST),
        name="collect_early",
    )(early)


def collect_late(late, block, middle):
    count, rows, width = late.shape
    dofs = width - LANES

    def kernel(last, _, residual, whole, sem):
        copies = []
        for i in range(count):
            at = i * dofs + middle
            copies.append(
                pltpu.make_async_copy(
                    last.at[i, :, :dofs],
                    residual.at[0, :, i * dofs : (i + 1) * dofs],
                    sem.at[2 * i],
                )
            )
            copies.append(
                pltpu.make_async_copy(
                    last.at[i, :, dofs:width], whole.at[0, :, at : at + LANES], sem.at[2 * i + 1]
                )
            )
        for copy in copies:
            copy.start()
        for copy in copies:
            copy.wait()

    place = pl.BlockSpec(memory_space=pltpu.HBM)
    shape = pltpu.HBM((1, rows, count * dofs), jnp.float32)
    return pl.pallas_call(
        kernel,
        in_specs=[pl.BlockSpec(memory_space=pltpu.VMEM), place],
        out_specs=[place, place],
        out_shape=[shape, shape],
        input_output_aliases={1: 1},
        scratch_shapes=[pltpu.SemaphoreType.DMA((2 * count,))],
        compiler_params=params(),
        name="collect_late",
    )(late, block)


PARTS = 3


def bf16_parts(value):
    parts = []
    for i in range(PARTS):
        parts.append(value.astype(jnp.bfloat16))
        if i < PARTS - 1:
            value = value - parts[i].astype(jnp.float32)
    return parts


def project(stacked, rotation, dofs, tiles, prior=None):
    count, wide, _ = stacked.shape
    rows = rotation.shape[1]
    width = len(tiles) * LANES
    scales = slot_scales(count)
    groups = -(-count * REACH // LANES)
    per = LANES // REACH
    strip = 2 * ROWS

    def kernel(x, rot, *refs):
        refs = refs[1:] if prior is not None else refs
        proj, back = refs[:2]
        edges, scratch = (refs[2:4], refs[4:]) if prior is None else ((), refs[2:])
        held, split_rot, mine, sent, come, go = scratch[:6]
        split_slots = scratch[6:]
        arrivals = []
        for c in range(len(tiles)):
            copy = pltpu.make_async_copy(
                x.at[:, :, c * LANES : (c + 1) * LANES], held.at[c], come.at[c]
            )
            copy.start()
            arrivals.append(copy)

        def one(j, carry):
            for i, part in enumerate(bf16_parts(rot[j])):
                split_rot[j, i * rows : (i + 1) * rows, :] = part
            return carry

        lax.fori_loop(0, count, one, 0)
        for c, copy in enumerate(arrivals):
            copy.wait()

            def transform(r, carry, c=c):
                at = pl.ds(pl.multiple_of(r * strip, strip), strip)
                halves = []
                for h in range(2):
                    own = pl.ds(pl.multiple_of(r * strip + h * ROWS, ROWS), ROWS)
                    halves.append(to_slots([held[c, s, own, :] for s in range(count)]))
                for j in range(count):
                    value = jnp.concatenate([half[j] for half in halves], 0)
                    for part, ref in zip(bf16_parts(value), split_slots):
                        ref[j, at, c * LANES : (c + 1) * LANES] = part
                return carry

            lax.fori_loop(0, wide // strip, transform, 0)
        for j in range(count):
            total = None
            for i in range(PARTS - 1, -1, -1):
                terms = PARTS - i
                stacked_terms = jnp.dot(
                    split_rot[j, : terms * rows, :],
                    split_slots[i][j],
                    preferred_element_type=jnp.float32,
                )
                for q in range(terms - 1, -1, -1):
                    term = stacked_terms[q * rows : (q + 1) * rows]
                    total = term if total is None else total + term
            mine[j] = total
        leaving = []

        def leave(source, target, c, t, at):
            copy = pltpu.make_async_copy(
                source.at[:, :, c * LANES : (c + 1) * LANES],
                target.at[:, :, t * LANES : (t + 1) * LANES],
                go.at[at],
            )
            copy.start()
            leaving.append(copy)

        for c, t in enumerate(tiles):
            leave(mine, proj, c, t, c)
        for c in range(len(tiles)):
            lanes = slice(c * LANES, (c + 1) * LANES)

            def inverse(r, carry, lanes=lanes):
                at = pl.ds(pl.multiple_of(r * ROWS, ROWS), ROWS)
                out = to_spans([mine[j, at, lanes] * scales[j] for j in range(count)])
                for s in range(count):
                    sent[s, at, lanes] = out[s]
                return carry

            lax.fori_loop(0, rows // ROWS, inverse, 0)
            leave(sent, back, c, c, len(tiles) + c)
        lane = lax.broadcasted_iota(jnp.int32, (rows, LANES), 1)
        ends = ((0, 0), (len(tiles) - 1, LANES - REACH))
        for ref, (c, start) in zip(edges, ends):
            for g in range(groups):
                packed = jnp.zeros((rows, LANES), jnp.float32)
                for k in range(min(per, count - g * per)):
                    turn = (k * REACH - start) % LANES
                    value = mine[g * per + k, :, c * LANES : (c + 1) * LANES]
                    value = pltpu.roll(value, turn, 1) if turn else value
                    packed = jnp.where(lane // REACH == k, value, packed)
                ref[g] = packed
        for copy in leaving:
            copy.wait()

    whole = pl.BlockSpec(memory_space=pltpu.HBM)
    vmem = pl.BlockSpec(memory_space=pltpu.VMEM)
    field = pltpu.HBM((count, rows, dofs), jnp.float32)
    edge = jax.ShapeDtypeStruct((groups, rows, LANES), jnp.float32)
    sending = pltpu.HBM((count, rows, width), jnp.float32)
    first = prior is None
    passes = PARTS * (PARTS + 1) // 2
    cost = pl.CostEstimate(
        flops=2 * passes * count * wide * rows * width,
        bytes_accessed=4 * count * (wide + 2 * rows) * width,
        transcendentals=0,
    )
    return pl.pallas_call(
        kernel,
        in_specs=[whole, vmem] + ([] if first else [whole]),
        out_specs=[whole, whole] + ([vmem, vmem] if first else []),
        out_shape=[field, sending] + ([edge, edge] if first else []),
        input_output_aliases={} if first else {2: 0},
        cost_estimate=cost,
        scratch_shapes=[
            pltpu.VMEM((len(tiles), count, wide, LANES), jnp.float32),
            pltpu.VMEM((count, PARTS * rows, wide), jnp.bfloat16),
            pltpu.VMEM((count, rows, width), jnp.float32),
            pltpu.VMEM((count, rows, width), jnp.float32),
            pltpu.SemaphoreType.DMA((len(tiles),)),
            pltpu.SemaphoreType.DMA((2 * len(tiles),)),
        ]
        + [pltpu.VMEM((count, wide, width), jnp.bfloat16)] * PARTS,
        compiler_params=params(65_400_000),
        name="project",
    )(stacked, rotation, *(() if first else (prior,)))


def stiffness(projected, before, after, bands, links):
    count, rows, dofs = projected.shape
    per = LANES // REACH
    tiles = dofs // LANES

    def kernel(x, left, right, band, lam, stiff, sums, energy, norm, matrix):
        row = lax.broadcasted_iota(jnp.int32, (LANES, LANES), 0)
        gap = row - lax.broadcasted_iota(jnp.int32, (LANES, LANES), 1)
        for t in range(tiles):
            at = slice(t * LANES, (t + 1) * LANES)
            here = jnp.where(gap == 0, band[16:17, at], 0.0)
            halo = jnp.zeros((LANES, LANES), jnp.float32)
            for d in range(1, REACH + 1):
                up, down = band[d - 1 : d, at], band[REACH + d - 1 : REACH + d, at]
                here = jnp.where(gap == d, -up, here)
                here = jnp.where(gap == -d, -down, here)
                halo = jnp.where(gap == d - LANES, -up, halo)
                halo = jnp.where(gap == LANES - d, -down, halo)
            matrix[t, :LANES, :] = here
            matrix[t, LANES:, :] = halo
        lane = lax.broadcasted_iota(jnp.int32, (rows, LANES), 1)

        def slot(j, carry):
            to = pl.ds(pl.multiple_of(j * rows, rows), rows)
            g, k = j // per, j % per
            low = pltpu.roll(left[g], (2 * LANES - REACH - REACH * k) % LANES, 1)
            high = pltpu.roll(right[g], (LANES - REACH * k) % LANES, 1)
            work = jnp.zeros((rows, LANES), jnp.float32)
            size = jnp.zeros((rows, LANES), jnp.float32)
            for t in range(tiles):
                at = slice(t * LANES, (t + 1) * LANES)
                here = x[j, :, at]
                previous = low if t == 0 else x[j, :, (t - 1) * LANES : t * LANES]
                following = high if t == tiles - 1 else x[j, :, (t + 1) * LANES : (t + 2) * LANES]
                halo = jnp.where(lane < LANES // 2, following, previous)
                total = jnp.dot(
                    jnp.concatenate([here, halo], 1),
                    matrix[t],
                    precision=HIGHEST,
                    preferred_element_type=jnp.float32,
                )
                total = total + (lam[j] * band[17:18, at]) * here
                stiff[j, :, at] = total
                work = work + total * here
                size = size + here * here
            energy[to, :] = work
            norm[to, :] = size
            return carry

        lax.fori_loop(0, count, slot, 0)
        ones = jnp.ones((ROWS, LANES), jnp.float32)
        for r, part in enumerate((energy, norm)):
            line = lax.dot_general(
                ones,
                part[...],
                (((1,), (1,)), ((), ())),
                precision=HIGHEST,
                preferred_element_type=jnp.float32,
            )
            sums[r : r + 1, :] = line[:1]

    vmem = pl.BlockSpec(memory_space=pltpu.VMEM)
    return pl.pallas_call(
        kernel,
        in_specs=[vmem, vmem, vmem, vmem, pl.BlockSpec(memory_space=pltpu.SMEM)],
        out_specs=[vmem, vmem],
        out_shape=[
            jax.ShapeDtypeStruct((count, rows, dofs), jnp.float32),
            jax.ShapeDtypeStruct((2, count * rows), jnp.float32),
        ],
        scratch_shapes=[
            pltpu.VMEM((count * rows, LANES), jnp.float32),
            pltpu.VMEM((count * rows, LANES), jnp.float32),
            pltpu.VMEM((tiles, 2 * LANES, LANES), jnp.float32),
        ],
        compiler_params=params(),
        name="stiffness",
    )(projected, before, after, bands, links)


def residual_back(projected, stiff, sums, late):
    count, rows, dofs = projected.shape
    scales = slot_scales(count)
    tiles = dofs // LANES

    def kernel(x, kx, total, extra, back, ritz, wide, sent, go):
        leaving = [pltpu.make_async_copy(extra, back.at[:, :, dofs : dofs + LANES], go.at[tiles])]
        leaving[0].start()
        value = total[0:1, :] / (total[1:2, :] + 1e-06)
        ritz[...] = value
        row = lax.broadcasted_iota(jnp.int32, (2 * ROWS, count * rows), 0)
        stack = jnp.zeros((2 * ROWS, count * rows), jnp.float32)
        for i, part in enumerate(bf16_parts(value)):
            stack = jnp.where(row == i, part.astype(jnp.float32), stack)
        wide[...] = lax.dot_general(
            stack.astype(jnp.bfloat16),
            jnp.ones((2 * ROWS, LANES), jnp.bfloat16),
            (((0,), (0,)), ((), ())),
            preferred_element_type=jnp.float32,
        )
        for t in range(tiles):
            lanes = slice(t * LANES, (t + 1) * LANES)

            def strip(r, carry, lanes=lanes):
                at = pl.ds(pl.multiple_of(r * ROWS, ROWS), ROWS)
                terms = []
                for j in range(count):
                    to = pl.ds(pl.multiple_of(j * rows + r * ROWS, ROWS), ROWS)
                    terms.append((kx[j, at, lanes] - wide[to, :] * x[j, at, lanes]) * scales[j])
                out = to_spans(terms)
                for s in range(count):
                    sent[s, at, lanes] = out[s]
                return carry

            lax.fori_loop(0, rows // ROWS, strip, 0)
            copy = pltpu.make_async_copy(sent.at[:, :, lanes], back.at[:, :, lanes], go.at[t])
            copy.start()
            leaving.append(copy)
        for copy in leaving:
            copy.wait()

    vmem = pl.BlockSpec(memory_space=pltpu.VMEM)
    return pl.pallas_call(
        kernel,
        in_specs=[vmem] * 4,
        out_specs=[pl.BlockSpec(memory_space=pltpu.HBM), vmem],
        out_shape=[
            pltpu.HBM((count, rows, dofs + LANES), jnp.float32),
            jax.ShapeDtypeStruct((1, count * rows), jnp.float32),
        ],
        scratch_shapes=[
            pltpu.VMEM((count * rows, LANES), jnp.float32),
            pltpu.VMEM((count, rows, dofs), jnp.float32),
            pltpu.SemaphoreType.DMA((tiles + 1,)),
        ],
        compiler_params=params(),
        name="residual_back",
    )(projected, stiff, sums, late)


def halvings(axis):
    step = lax.axis_size(axis) // 2
    while step:
        yield step, [(i, i ^ step) for i in range(lax.axis_size(axis))]
        step //= 2


def exchange_step(held, step, pairs):
    other = lax.ppermute(held, "span", pairs)
    upper = (lax.axis_index("span") & step) != 0
    return jnp.stack([jnp.where(upper, other, held), jnp.where(upper, held, other)])


def in_order(held, steps):
    bits = [step for step, _ in steps][::-1]
    order = tuple(sorted(range(len(bits)), key=lambda d: -bits[d]))
    held = held.transpose(order + tuple(range(len(bits), held.ndim)))
    return held.reshape((-1,) + held.shape[len(bits) :])


def tiled_device(
    current_block,
    search_block,
    previous_block,
    ground_spring,
    wire_tension,
    dropper_stiff,
    dropper_offset,
    span_link,
    ritz_rotation,
):
    count = lax.axis_size("span")
    dofs = current_block.shape[2] // count
    rows = current_block.shape[1]
    steps = list(halvings("span"))
    tiles = list(range(dofs // LANES))
    middle = tiles[len(tiles) // 2]
    early = [t for t in tiles if t != middle]
    at = middle * LANES
    blocks = (current_block, search_block, previous_block)
    rotation = exchange_step(ritz_rotation[0].T, *steps[0])
    pieces = spread_blocks(blocks, count, [(0, at), (at + LANES, dofs - at - LANES)])
    pieces, rotation = lax.optimization_barrier((pieces, rotation))
    stacked = exchange(pieces)
    order = steps[2:] + steps[1:2]
    for step, pairs in order:
        rotation = exchange_step(rotation, step, pairs)
    rotation = in_order(rotation, [steps[0]] + order)
    scales = jnp.array(slot_scales(count), jnp.float32)[:, None, None]
    rotation = rotation * scales
    weights, ground, link = coefficients(
        ground_spring, wire_tension, dropper_stiff, dropper_offset, span_link, count, dofs
    )
    up = weights[:, REACH:]
    down = [weights[d - 1, REACH - d : REACH - d + dofs] for d in range(1, REACH + 1)]
    down = jnp.stack(down)
    diagonal = ground + jnp.sum(up, 0) + jnp.sum(down, 0)
    bands = jnp.concatenate([up, down, diagonal[None], link[None]])
    links = 2.0 * (1.0 - fourier_rows(count)[1])
    pieces = spread_blocks(blocks, count, [(at, LANES)])
    pieces, rotation, bands = lax.optimization_barrier((pieces, rotation, bands))
    stacked_late = exchange(pieces)
    projected, spans, head, tail = project(stacked, rotation, dofs, early)
    before, after = to_next(tail, 1), to_next(head, -1)
    spans, before, after = lax.optimization_barrier((spans, before, after))
    early_pieces = exchange(spans)
    projected, late = project(stacked_late, rotation, dofs, [middle], projected)
    stiff, sums = stiffness(projected, before, after, bands, links)
    for _, pairs in halvings("elem"):
        sums = sums + lax.ppermute(sums, "elem", pairs)
    for _, pairs in steps[:1:-1]:
        sums = sums + lax.ppermute(sums, "span", pairs)
    (far, _), (near, _) = steps[:2]
    sums = sums + add_up(
        [
            lax.ppermute(sums, "span", [(i, i ^ flip) for i in range(count)])
            for flip in (far | near, far, near)
        ]
    )
    spans, ritz = residual_back(projected, stiff, sums, late)
    next_block = collect_early(early_pieces, at)
    next_residual, next_block = collect_late(exchange(spans), next_block, at)
    ritz = lax.dynamic_slice_in_dim(ritz, lax.axis_index("span") * rows, rows, 1)
    return (next_block, next_residual, ritz)


def on_device(
    current_block,
    search_block,
    previous_block,
    ground_spring,
    wire_tension,
    dropper_stiff,
    dropper_offset,
    span_link,
    ritz_rotation,
):
    count = lax.axis_size("span")
    dof_dev = current_block.shape[2]
    dofs = dof_dev // count
    matrix, cosines = fourier_rows(count)
    blocks = (current_block, search_block, previous_block)
    stacked = exchange(jnp.concatenate([spread(b[0], count) for b in blocks], 1))
    rotation = lax.all_gather(ritz_rotation, "span", axis=0, tiled=True)
    weights, ground, link = coefficients(
        ground_spring, wire_tension, dropper_stiff, dropper_offset, span_link, count, dofs
    )
    slots = along_spans(matrix, stacked)
    projected = jnp.einsum("jvm,jvd->jmd", rotation, slots, precision=HIGHEST)
    back = matrix.T
    next_block = collect(exchange(along_spans(back, projected)))
    before = to_next(projected[:, :, dofs - REACH :], 1)
    after = to_next(projected[:, :, :REACH], -1)
    wide = jnp.concatenate([before, projected, after], 2)
    stiff = ground * projected
    near = wide[:, :, : REACH + dofs]
    for distance in range(1, REACH + 1):
        flux = weights[distance - 1] * (near - wide[:, :, distance : distance + REACH + dofs])
        stiff = stiff + flux[:, :, REACH:] - flux[:, :, REACH - distance : REACH - distance + dofs]
    stiff = stiff + (2.0 * (1.0 - cosines))[:, None, None] * link * projected
    sums = jnp.stack([jnp.sum(projected * stiff, 2), jnp.sum(projected * projected, 2)])
    sums = lax.psum(sums, ("elem", "span"))
    ritz = sums[0] / (sums[1] + 1e-06)
    residual = stiff - ritz[:, :, None] * projected
    next_residual = collect(exchange(along_spans(back, residual)))
    my_ritz = lax.dynamic_slice_in_dim(ritz, lax.axis_index("span"), 1, 0)
    return (next_block, next_residual, my_ritz)


def by_shape(*args):
    count, dof_dev = lax.axis_size("span"), args[0].shape[2]
    halves = count & (count - 1) == 0 and lax.axis_size("elem") in (1, 2, 4, 8, 16)
    if halves and count > 2 and dof_dev % (count * LANES) == 0 and dof_dev > 2 * count * LANES:
        return tiled_device(*args)
    return on_device(*args)


def solution(mesh):
    return jax.shard_map(
        by_shape,
        mesh=mesh,
        in_specs=(
            P("span", None, "elem"),
            P("span", None, "elem"),
            P("span", None, "elem"),
            P("elem"),
            P("elem"),
            P("elem"),
            P("elem"),
            P("elem"),
            P("span", None, None),
        ),
        out_specs=(P("span", None, "elem"), P("span", None, "elem"), P("span", None)),
        check_vma=False,
    )
```

```python
import math

import jax
import jax.numpy as jnp
from jax import lax
from jax.experimental import pallas as pl
from jax.experimental.pallas import tpu as pltpu
from jax.sharding import PartitionSpec as P

REACH = 8
LANES = 128
ROWS = 8
VMEM_LIMIT = 24 * 1024 * 1024
VMEM_MOST = 61_500_000
HIGHEST = lax.Precision.HIGHEST


def fourier_rows(count):
    row = jnp.arange(count)[:, None]
    col = jnp.arange(count)[None, :]
    half = count // 2
    wave = jnp.where(row <= half, row, row - half)
    phase = (wave * col % count).astype(jnp.float32) * (2.0 * math.pi / count)
    scaled = jnp.where(row <= half, jnp.cos(phase), jnp.sin(phase)) * math.sqrt(2.0 / count)
    edge = (row == 0) | (row == half)
    matrix = jnp.where(edge, jnp.cos(phase) * math.sqrt(1.0 / count), scaled)
    slots = jnp.arange(count)
    slot_wave = jnp.where(slots <= half, slots, slots - half)
    cosines = jnp.cos(slot_wave.astype(jnp.float32) * (2.0 * math.pi / count))
    return (matrix, cosines)


def along_spans(matrix, block):
    shape = block.shape
    flat = block.reshape(shape[0], -1)
    return jnp.dot(matrix, flat, precision=HIGHEST).reshape(shape)


def spread(block, count):
    rows, dofs = block.shape
    return block.reshape(rows, count, dofs // count).transpose(1, 0, 2)


def collect(pieces):
    count, rows, dofs = pieces.shape
    return pieces.transpose(1, 0, 2).reshape(1, rows, count * dofs)


def exchange(pieces):
    return lax.all_to_all(pieces, "span", split_axis=0, concat_axis=0, tiled=True)


def to_next(cells, step):
    count, parts = lax.axis_size("span"), lax.axis_size("elem")
    line = [s * parts + e for e in range(parts) for s in range(count)]
    pairs = list(zip(line, line[1:]))
    if step < 0:
        pairs = [(b, a) for a, b in pairs]
    return lax.ppermute(cells, ("span", "elem"), pairs)


def coefficients(ground, tension, stiff, offset, link, count, dofs):
    dof_dev = ground.shape[0]
    start = lax.axis_index("span") * dofs
    elem = lax.axis_index("elem")
    dof_all = dof_dev * lax.axis_size("elem")
    position = elem * dof_dev + jnp.arange(dof_dev)
    distance = jnp.arange(1, REACH + 1)[:, None]
    weights = jnp.where((offset == distance) & (position + distance < dof_all), stiff, 0.0)
    wire = jnp.where((distance == 1) & (position < dof_all - 1), tension, 0.0)
    weights = weights + wire
    pairs = [(i, i + 1) for i in range(lax.axis_size("elem") - 1)]
    left = lax.ppermute(weights[:, dof_dev - REACH :], "elem", pairs)
    weights = jnp.concatenate([left, weights], 1)
    weights = lax.dynamic_slice_in_dim(weights, start, dofs + REACH, 1)
    ground = lax.dynamic_slice_in_dim(ground, start, dofs, 0)
    link = lax.dynamic_slice_in_dim(link, start, dofs, 0)
    return weights, ground, link


def add_up(terms):
    total = terms[0]
    for term in terms[1:]:
        total = total + term
    return total


def scaled(factor, value):
    if abs(factor - 1.0) < 1e-12:
        return value
    return value * factor


def cosine_sums(a):
    n = len(a) - 1
    if n == 1:
        return [a[0] + a[1], a[0] - a[1]]
    half = n // 2
    even = cosine_sums([a[s] + a[n - s] for s in range(half)] + [a[half]])
    diff = [a[s] - a[n - s] for s in range(half)]
    out = [None] * (n + 1)
    out[0::2] = even
    for j in range(1, n, 2):
        out[j] = add_up([scaled(math.cos(math.pi * j * s / n), diff[s]) for s in range(half)])
    return out


def sine_sums(b):
    n = len(b) + 1
    if n == 1:
        return []
    half = n // 2
    at = [None] + list(b)
    even = sine_sums([at[s] - at[n - s] for s in range(1, half)])
    total = [None] + [at[s] + at[n - s] for s in range(1, half)] + [at[half]]
    out = [None] * (n + 1)
    for k, value in enumerate(even):
        out[2 * k + 2] = value
    for j in range(1, n, 2):
        terms = [(math.sin(math.pi * j * s / n), total[s]) for s in range(1, half + 1)]
        terms = [scaled(abs(f), t) if f > 0 else -scaled(abs(f), t) for f, t in terms]
        out[j] = add_up(terms)
    return out[1:n]


def slot_scales(count):
    edge, inner = math.sqrt(1.0 / count), math.sqrt(2.0 / count)
    return [edge if j in (0, count // 2) else inner for j in range(count)]


def to_slots(x):
    n = len(x)
    half = n // 2
    plus = [x[0]] + [x[s] + x[n - s] for s in range(1, half)] + [x[half]]
    minus = [x[s] - x[n - s] for s in range(1, half)]
    return cosine_sums(plus) + sine_sums(minus)


def to_spans(y):
    n = len(y)
    half = n // 2
    even = cosine_sums(y[: half + 1])
    odd = [None] + sine_sums(y[half + 1 :])
    out = [None] * n
    out[0], out[half] = even[0], even[half]
    for s in range(1, half):
        out[s] = even[s] + odd[s]
        out[n - s] = even[s] - odd[s]
    return out


def params(limit=VMEM_LIMIT):
    return pltpu.CompilerParams(vmem_limit_bytes=limit)


def spread_blocks(blocks, count, ranges):
    _, rows, dof_dev = blocks[0].shape
    dofs = dof_dev // count
    kinds = len(blocks)
    shape = (count, kinds * rows, sum(width for _, width in ranges))
    many = kinds * len(ranges)

    def kernel(*refs):
        out, held, come, go = refs[kinds:]
        ahead = min(4, count)

        def fetch(i):
            group, to = [], 0
            for first, width in ranges:
                for k in range(kinds):
                    copy = pltpu.make_async_copy(
                        refs[k].at[0, :, i * dofs + first : i * dofs + first + width],
                        held.at[i, k * rows : (k + 1) * rows, to : to + width],
                        come.at[i * many + len(group)],
                    )
                    copy.start()
                    group.append(copy)
                to += width
            return group

        arrivals = [fetch(i) for i in range(ahead)]
        leaving = []
        for i in range(count):
            if i + ahead < count:
                arrivals.append(fetch(i + ahead))
            for copy in arrivals[i]:
                copy.wait()
            piece = pltpu.make_async_copy(held.at[i], out.at[i], go.at[i])
            piece.start()
            leaving.append(piece)
        for piece in leaving:
            piece.wait()

    whole = pl.BlockSpec(memory_space=pltpu.HBM)
    return pl.pallas_call(
        kernel,
        in_specs=[whole] * kinds,
        out_specs=whole,
        out_shape=pltpu.HBM(shape, jnp.float32),
        scratch_shapes=[
            pltpu.VMEM(shape, jnp.float32),
            pltpu.SemaphoreType.DMA((count * many,)),
            pltpu.SemaphoreType.DMA((count,)),
        ],
        compiler_params=params(VMEM_MOST),
        name="spread_blocks",
    )(*blocks)


def collect_early(early, middle):
    count, rows, early_width = early.shape
    dofs = early_width + LANES
    many = max(n for n in (1, 2, 4, 8) if count % n == 0)

    def kernel(first, block):
        for i in range(many):
            at = i * dofs
            block[0, :, at : at + middle] = first[i, :, :middle]
            block[0, :, at + middle + LANES : at + dofs] = first[i, :, middle:]

    return pl.pallas_call(
        kernel,
        grid=(count // many,),
        in_specs=[pl.BlockSpec((many, rows, early_width), lambda i: (i, 0, 0))],
        out_specs=pl.BlockSpec((1, rows, many * dofs), lambda i: (0, 0, i)),
        out_shape=pltpu.HBM((1, rows, count * dofs), jnp.float32),
        compiler_params=params(VMEM_MOST),
        name="collect_early",
    )(early)


def collect_late(late, block, middle):
    count, rows, width = late.shape
    dofs = width - LANES

    def kernel(last, _, residual, whole, sem):
        copies = []
        for i in range(count):
            at = i * dofs + middle
            copies.append(
                pltpu.make_async_copy(
                    last.at[i, :, :dofs],
                    residual.at[0, :, i * dofs : (i + 1) * dofs],
                    sem.at[2 * i],
                )
            )
            copies.append(
                pltpu.make_async_copy(
                    last.at[i, :, dofs:width], whole.at[0, :, at : at + LANES], sem.at[2 * i + 1]
                )
            )
        for copy in copies:
            copy.start()
        for copy in copies:
            copy.wait()

    place = pl.BlockSpec(memory_space=pltpu.HBM)
    shape = pltpu.HBM((1, rows, count * dofs), jnp.float32)
    return pl.pallas_call(
        kernel,
        in_specs=[pl.BlockSpec(memory_space=pltpu.VMEM), place],
        out_specs=[place, place],
        out_shape=[shape, shape],
        input_output_aliases={1: 1},
        scratch_shapes=[pltpu.SemaphoreType.DMA((2 * count,))],
        compiler_params=params(),
        name="collect_late",
    )(late, block)


PARTS = 3


def bf16_parts(value):
    parts = []
    for i in range(PARTS):
        parts.append(value.astype(jnp.bfloat16))
        if i < PARTS - 1:
            value = value - parts[i].astype(jnp.float32)
    return parts


def project(stacked, rotation, dofs, tiles, prior=None):
    count, wide, _ = stacked.shape
    rows = rotation.shape[1]
    width = len(tiles) * LANES
    scales = slot_scales(count)
    groups = -(-count * REACH // LANES)
    per = LANES // REACH
    strip = 2 * ROWS

    def kernel(x, rot, *refs):
        refs = refs[1:] if prior is not None else refs
        proj, back = refs[:2]
        edges, scratch = (refs[2:4], refs[4:]) if prior is None else ((), refs[2:])
        held, split_rot, mine, sent, come, go = scratch[:6]
        split_slots = scratch[6:]
        arrivals = []
        for c in range(len(tiles)):
            copy = pltpu.make_async_copy(
                x.at[:, :, c * LANES : (c + 1) * LANES], held.at[c], come.at[c]
            )
            copy.start()
            arrivals.append(copy)

        def one(j, carry):
            for i, part in enumerate(bf16_parts(rot[j])):
                split_rot[j, i * rows : (i + 1) * rows, :] = part
            return carry

        lax.fori_loop(0, count, one, 0)
        for c, copy in enumerate(arrivals):
            copy.wait()

            def transform(r, carry, c=c):
                at = pl.ds(pl.multiple_of(r * strip, strip), strip)
                halves = []
                for h in range(2):
                    own = pl.ds(pl.multiple_of(r * strip + h * ROWS, ROWS), ROWS)
                    halves.append(to_slots([held[c, s, own, :] for s in range(count)]))
                for j in range(count):
                    value = jnp.concatenate([half[j] for half in halves], 0)
                    for part, ref in zip(bf16_parts(value), split_slots):
                        ref[j, at, c * LANES : (c + 1) * LANES] = part
                return carry

            lax.fori_loop(0, wide // strip, transform, 0)
        for j in range(count):
            total = None
            for i in range(PARTS - 1, -1, -1):
                terms = PARTS - i
                stacked_terms = jnp.dot(
                    split_rot[j, : terms * rows, :],
                    split_slots[i][j],
                    preferred_element_type=jnp.float32,
                )
                for q in range(terms - 1, -1, -1):
                    term = stacked_terms[q * rows : (q + 1) * rows]
                    total = term if total is None else total + term
            mine[j] = total
        leaving = []

        def leave(source, target, c, t, at):
            copy = pltpu.make_async_copy(
                source.at[:, :, c * LANES : (c + 1) * LANES],
                target.at[:, :, t * LANES : (t + 1) * LANES],
                go.at[at],
            )
            copy.start()
            leaving.append(copy)

        for c, t in enumerate(tiles):
            leave(mine, proj, c, t, c)
        for c in range(len(tiles)):
            lanes = slice(c * LANES, (c + 1) * LANES)

            def inverse(r, carry, lanes=lanes):
                at = pl.ds(pl.multiple_of(r * ROWS, ROWS), ROWS)
                out = to_spans([mine[j, at, lanes] * scales[j] for j in range(count)])
                for s in range(count):
                    sent[s, at, lanes] = out[s]
                return carry

            lax.fori_loop(0, rows // ROWS, inverse, 0)
            leave(sent, back, c, c, len(tiles) + c)
        lane = lax.broadcasted_iota(jnp.int32, (rows, LANES), 1)
        ends = ((0, 0), (len(tiles) - 1, LANES - REACH))
        for ref, (c, start) in zip(edges, ends):
            for g in range(groups):
                packed = jnp.zeros((rows, LANES), jnp.float32)
                for k in range(min(per, count - g * per)):
                    turn = (k * REACH - start) % LANES
                    value = mine[g * per + k, :, c * LANES : (c + 1) * LANES]
                    value = pltpu.roll(value, turn, 1) if turn else value
                    packed = jnp.where(lane // REACH == k, value, packed)
                ref[g] = packed
        for copy in leaving:
            copy.wait()

    whole = pl.BlockSpec(memory_space=pltpu.HBM)
    vmem = pl.BlockSpec(memory_space=pltpu.VMEM)
    field = pltpu.HBM((count, rows, dofs), jnp.float32)
    edge = jax.ShapeDtypeStruct((groups, rows, LANES), jnp.float32)
    sending = pltpu.HBM((count, rows, width), jnp.float32)
    first = prior is None
    passes = PARTS * (PARTS + 1) // 2
    cost = pl.CostEstimate(
        flops=2 * passes * count * wide * rows * width,
        bytes_accessed=4 * count * (wide + 2 * rows) * width,
        transcendentals=0,
    )
    return pl.pallas_call(
        kernel,
        in_specs=[whole, vmem] + ([] if first else [whole]),
        out_specs=[whole, whole] + ([vmem, vmem] if first else []),
        out_shape=[field, sending] + ([edge, edge] if first else []),
        input_output_aliases={} if first else {2: 0},
        cost_estimate=cost,
        scratch_shapes=[
            pltpu.VMEM((len(tiles), count, wide, LANES), jnp.float32),
            pltpu.VMEM((count, PARTS * rows, wide), jnp.bfloat16),
            pltpu.VMEM((count, rows, width), jnp.float32),
            pltpu.VMEM((count, rows, width), jnp.float32),
            pltpu.SemaphoreType.DMA((len(tiles),)),
            pltpu.SemaphoreType.DMA((2 * len(tiles),)),
        ]
        + [pltpu.VMEM((count, wide, width), jnp.bfloat16)] * PARTS,
        compiler_params=params(65_400_000),
        name="project",
    )(stacked, rotation, *(() if first else (prior,)))


def stiffness(projected, before, after, bands, links):
    count, rows, dofs = projected.shape
    per = LANES // REACH
    tiles = dofs // LANES

    def kernel(x, left, right, band, lam, stiff, sums, energy, norm, matrix):
        row = lax.broadcasted_iota(jnp.int32, (LANES, LANES), 0)
        gap = row - lax.broadcasted_iota(jnp.int32, (LANES, LANES), 1)
        for t in range(tiles):
            at = slice(t * LANES, (t + 1) * LANES)
            here = jnp.where(gap == 0, band[16:17, at], 0.0)
            halo = jnp.zeros((LANES, LANES), jnp.float32)
            for d in range(1, REACH + 1):
                up, down = band[d - 1 : d, at], band[REACH + d - 1 : REACH + d, at]
                here = jnp.where(gap == d, -up, here)
                here = jnp.where(gap == -d, -down, here)
                halo = jnp.where(gap == d - LANES, -up, halo)
                halo = jnp.where(gap == LANES - d, -down, halo)
            matrix[t, :LANES, :] = here
            matrix[t, LANES:, :] = halo
        lane = lax.broadcasted_iota(jnp.int32, (rows, LANES), 1)

        def slot(j, carry):
            to = pl.ds(pl.multiple_of(j * rows, rows), rows)
            g, k = j // per, j % per
            low = pltpu.roll(left[g], (2 * LANES - REACH - REACH * k) % LANES, 1)
            high = pltpu.roll(right[g], (LANES - REACH * k) % LANES, 1)
            work = jnp.zeros((rows, LANES), jnp.float32)
            size = jnp.zeros((rows, LANES), jnp.float32)
            for t in range(tiles):
                at = slice(t * LANES, (t + 1) * LANES)
                here = x[j, :, at]
                previous = low if t == 0 else x[j, :, (t - 1) * LANES : t * LANES]
                following = high if t == tiles - 1 else x[j, :, (t + 1) * LANES : (t + 2) * LANES]
                halo = jnp.where(lane < LANES // 2, following, previous)
                total = jnp.dot(
                    jnp.concatenate([here, halo], 1),
                    matrix[t],
                    precision=HIGHEST,
                    preferred_element_type=jnp.float32,
                )
                total = total + (lam[j] * band[17:18, at]) * here
                stiff[j, :, at] = total
                work = work + total * here
                size = size + here * here
            energy[to, :] = work
            norm[to, :] = size
            return carry

        lax.fori_loop(0, count, slot, 0)
        ones = jnp.ones((ROWS, LANES), jnp.float32)
        for r, part in enumerate((energy, norm)):
            line = lax.dot_general(
                ones,
                part[...],
                (((1,), (1,)), ((), ())),
                precision=HIGHEST,
                preferred_element_type=jnp.float32,
            )
            sums[r : r + 1, :] = line[:1]

    vmem = pl.BlockSpec(memory_space=pltpu.VMEM)
    return pl.pallas_call(
        kernel,
        in_specs=[vmem, vmem, vmem, vmem, pl.BlockSpec(memory_space=pltpu.SMEM)],
        out_specs=[vmem, vmem],
        out_shape=[
            jax.ShapeDtypeStruct((count, rows, dofs), jnp.float32),
            jax.ShapeDtypeStruct((2, count * rows), jnp.float32),
        ],
        scratch_shapes=[
            pltpu.VMEM((count * rows, LANES), jnp.float32),
            pltpu.VMEM((count * rows, LANES), jnp.float32),
            pltpu.VMEM((tiles, 2 * LANES, LANES), jnp.float32),
        ],
        compiler_params=params(),
        name="stiffness",
    )(projected, before, after, bands, links)


def residual_back(projected, stiff, sums, late):
    count, rows, dofs = projected.shape
    scales = slot_scales(count)
    tiles = dofs // LANES

    def kernel(x, kx, total, extra, back, ritz, wide, sent, go):
        leaving = [pltpu.make_async_copy(extra, back.at[:, :, dofs : dofs + LANES], go.at[tiles])]
        leaving[0].start()
        value = total[0:1, :] / (total[1:2, :] + 1e-06)
        ritz[...] = value
        row = lax.broadcasted_iota(jnp.int32, (2 * ROWS, count * rows), 0)
        stack = jnp.zeros((2 * ROWS, count * rows), jnp.float32)
        for i, part in enumerate(bf16_parts(value)):
            stack = jnp.where(row == i, part.astype(jnp.float32), stack)
        wide[...] = lax.dot_general(
            stack.astype(jnp.bfloat16),
            jnp.ones((2 * ROWS, LANES), jnp.bfloat16),
            (((0,), (0,)), ((), ())),
            preferred_element_type=jnp.float32,
        )
        for t in range(tiles):
            lanes = slice(t * LANES, (t + 1) * LANES)

            def strip(r, carry, lanes=lanes):
                at = pl.ds(pl.multiple_of(r * ROWS, ROWS), ROWS)
                terms = []
                for j in range(count):
                    to = pl.ds(pl.multiple_of(j * rows + r * ROWS, ROWS), ROWS)
                    terms.append((kx[j, at, lanes] - wide[to, :] * x[j, at, lanes]) * scales[j])
                out = to_spans(terms)
                for s in range(count):
                    sent[s, at, lanes] = out[s]
                return carry

            lax.fori_loop(0, rows // ROWS, strip, 0)
            copy = pltpu.make_async_copy(sent.at[:, :, lanes], back.at[:, :, lanes], go.at[t])
            copy.start()
            leaving.append(copy)
        for copy in leaving:
            copy.wait()

    vmem = pl.BlockSpec(memory_space=pltpu.VMEM)
    return pl.pallas_call(
        kernel,
        in_specs=[vmem] * 4,
        out_specs=[pl.BlockSpec(memory_space=pltpu.HBM), vmem],
        out_shape=[
            pltpu.HBM((count, rows, dofs + LANES), jnp.float32),
            jax.ShapeDtypeStruct((1, count * rows), jnp.float32),
        ],
        scratch_shapes=[
            pltpu.VMEM((count * rows, LANES), jnp.float32),
            pltpu.VMEM((count, rows, dofs), jnp.float32),
            pltpu.SemaphoreType.DMA((tiles + 1,)),
        ],
        compiler_params=params(),
        name="residual_back",
    )(projected, stiff, sums, late)


def halvings(axis):
    step = lax.axis_size(axis) // 2
    while step:
        yield step, [(i, i ^ step) for i in range(lax.axis_size(axis))]
        step //= 2


def exchange_step(held, step, pairs):
    other = lax.ppermute(held, "span", pairs)
    upper = (lax.axis_index("span") & step) != 0
    return jnp.stack([jnp.where(upper, other, held), jnp.where(upper, held, other)])


def in_order(held, steps):
    bits = [step for step, _ in steps][::-1]
    order = tuple(sorted(range(len(bits)), key=lambda d: -bits[d]))
    held = held.transpose(order + tuple(range(len(bits), held.ndim)))
    return held.reshape((-1,) + held.shape[len(bits) :])


def tiled_device(
    current_block,
    search_block,
    previous_block,
    ground_spring,
    wire_tension,
    dropper_stiff,
    dropper_offset,
    span_link,
    ritz_rotation,
):
    count = lax.axis_size("span")
    dofs = current_block.shape[2] // count
    rows = current_block.shape[1]
    steps = list(halvings("span"))
    tiles = list(range(dofs // LANES))
    middle = tiles[len(tiles) // 2]
    early = [t for t in tiles if t != middle]
    at = middle * LANES
    blocks = (current_block, search_block, previous_block)
    rotation = exchange_step(ritz_rotation[0].T, *steps[0])
    pieces = spread_blocks(blocks, count, [(0, at), (at + LANES, dofs - at - LANES)])
    pieces, rotation = lax.optimization_barrier((pieces, rotation))
    stacked = exchange(pieces)
    order = steps[2:] + steps[1:2]
    for step, pairs in order:
        rotation = exchange_step(rotation, step, pairs)
    rotation = in_order(rotation, [steps[0]] + order)
    scales = jnp.array(slot_scales(count), jnp.float32)[:, None, None]
    rotation = rotation * scales
    weights, ground, link = coefficients(
        ground_spring, wire_tension, dropper_stiff, dropper_offset, span_link, count, dofs
    )
    up = weights[:, REACH:]
    down = [weights[d - 1, REACH - d : REACH - d + dofs] for d in range(1, REACH + 1)]
    down = jnp.stack(down)
    diagonal = ground + jnp.sum(up, 0) + jnp.sum(down, 0)
    bands = jnp.concatenate([up, down, diagonal[None], link[None]])
    links = 2.0 * (1.0 - fourier_rows(count)[1])
    pieces = spread_blocks(blocks, count, [(at, LANES)])
    pieces, rotation, bands = lax.optimization_barrier((pieces, rotation, bands))
    stacked_late = exchange(pieces)
    projected, spans, head, tail = project(stacked, rotation, dofs, early)
    before, after = to_next(tail, 1), to_next(head, -1)
    spans, before, after = lax.optimization_barrier((spans, before, after))
    early_pieces = exchange(spans)
    projected, late = project(stacked_late, rotation, dofs, [middle], projected)
    stiff, sums = stiffness(projected, before, after, bands, links)
    for _, pairs in halvings("elem"):
        sums = sums + lax.ppermute(sums, "elem", pairs)
    for _, pairs in steps[:1:-1]:
        sums = sums + lax.ppermute(sums, "span", pairs)
    (far, _), (near, _) = steps[:2]
    sums = sums + add_up(
        [
            lax.ppermute(sums, "span", [(i, i ^ flip) for i in range(count)])
            for flip in (far | near, far, near)
        ]
    )
    spans, ritz = residual_back(projected, stiff, sums, late)
    next_block = collect_early(early_pieces, at)
    next_residual, next_block = collect_late(exchange(spans), next_block, at)
    ritz = lax.dynamic_slice_in_dim(ritz, lax.axis_index("span") * rows, rows, 1)
    return (next_block, next_residual, ritz)


def on_device(
    current_block,
    search_block,
    previous_block,
    ground_spring,
    wire_tension,
    dropper_stiff,
    dropper_offset,
    span_link,
    ritz_rotation,
):
    count = lax.axis_size("span")
    dof_dev = current_block.shape[2]
    dofs = dof_dev // count
    matrix, cosines = fourier_rows(count)
    blocks = (current_block, search_block, previous_block)
    stacked = exchange(jnp.concatenate([spread(b[0], count) for b in blocks], 1))
    rotation = lax.all_gather(ritz_rotation, "span", axis=0, tiled=True)
    weights, ground, link = coefficients(
        ground_spring, wire_tension, dropper_stiff, dropper_offset, span_link, count, dofs
    )
    slots = along_spans(matrix, stacked)
    projected = jnp.einsum("jvm,jvd->jmd", rotation, slots, precision=HIGHEST)
    back = matrix.T
    next_block = collect(exchange(along_spans(back, projected)))
    before = to_next(projected[:, :, dofs - REACH :], 1)
    after = to_next(projected[:, :, :REACH], -1)
    wide = jnp.concatenate([before, projected, after], 2)
    stiff = ground * projected
    near = wide[:, :, : REACH + dofs]
    for distance in range(1, REACH + 1):
        flux = weights[distance - 1] * (near - wide[:, :, distance : distance + REACH + dofs])
        stiff = stiff + flux[:, :, REACH:] - flux[:, :, REACH - distance : REACH - distance + dofs]
    stiff = stiff + (2.0 * (1.0 - cosines))[:, None, None] * link * projected
    sums = jnp.stack([jnp.sum(projected * stiff, 2), jnp.sum(projected * projected, 2)])
    sums = lax.psum(sums, ("elem", "span"))
    ritz = sums[0] / (sums[1] + 1e-06)
    residual = stiff - ritz[:, :, None] * projected
    next_residual = collect(exchange(along_spans(back, residual)))
    my_ritz = lax.dynamic_slice_in_dim(ritz, lax.axis_index("span"), 1, 0)
    return (next_block, next_residual, my_ritz)


def by_shape(*args):
    count, dof_dev = lax.axis_size("span"), args[0].shape[2]
    halves = count & (count - 1) == 0 and lax.axis_size("elem") in (1, 2, 4, 8, 16)
    if halves and count > 2 and dof_dev % (count * LANES) == 0 and dof_dev > 2 * count * LANES:
        return tiled_device(*args)
    return on_device(*args)


def solution(mesh):
    return jax.shard_map(
        by_shape,
        mesh=mesh,
        in_specs=(
            P("span", None, "elem"),
            P("span", None, "elem"),
            P("span", None, "elem"),
            P("elem"),
            P("elem"),
            P("elem"),
            P("elem"),
            P("elem"),
            P("span", None, None),
        ),
        out_specs=(P("span", None, "elem"), P("span", None, "elem"), P("span", None)),
        check_vma=False,
    )
```
